32 devices in a mesh: doc: 16 (over z, x, core), feat: 2 (over y).
Axes of the slice: x: 2, y: 2, z: 4, core: 2. Of those that a mesh axis runs over, the one named last changes fastest.
Arguments:
- col_ids: int32 [8192, 32], P('doc', 'feat'), may hold values from 0 to 4095
- col_vals: bfloat16 [8192, 32], P('doc', 'feat'), may hold values from 0.019897461 to 0.19921875
- left_vec: float32 [8192, 256], P('doc'), may hold values from -6 to 6
- right_vec: float32 [8192, 256], P(('feat', 'doc')), may hold values from -6 to 6
- search_dir: float32 [8192, 256], P(('feat', 'doc')), may hold values from -6 to 6
- solution: float32 [8192, 256], P(('feat', 'doc')), may hold values from -6 to 6
- alpha_prev: float32 [256], replicated, may hold values from 1 to 3
- phibar: float32 [256], replicated, may hold values from 0.5 to 2
- rhobar: float32 [256], replicated, may hold values from 0.5 to 3
Outputs:
- left_next: float32 [8192, 256], P('doc')
- right_next: float32 [8192, 256], P(('feat', 'doc'))
- search_next: float32 [8192, 256], P(('feat', 'doc'))
- solution_next: float32 [8192, 256], P(('feat', 'doc'))
- alpha_next: float32 [256], replicated
- phibar_next: float32 [256], replicated
- rhobar_next: float32 [256], replicated
The draws below stay inside these ranges and needn't reach their ends.
Inputs may be any that keep to these rules, and one draw needn't show every extreme that they name: `col_ids`: entries j of a row with the same j // 16 name columns of one feature block.
All inputs are finite; a program needn't handle non-finite values.
Results may differ from the reference program's by a relative error of at most 0.0003.
Values sent between devices are 32-bit elements; how exact they have to be, the bound alone decides.
No kernel may reach another device: no remote copies, remote signals or barrier semaphores. Data moves between devices by JAX's collectives and lax.ppermute only.
A program may use at most 64 MiB of HBM per device.

```python
import math
import jax
import jax.numpy as jnp
from jax import lax

FEAT_DEV = 4096
TGT = 256
K_DEV = 16
DOCS = 8192
FEAT = 8192
NNZ = 32


def touch_ends(array, own_key, smallest, top_value):
    place = [jax.random.randint(jax.random.fold_in(own_key, axis), (), 0, length) for axis, length in enumerate(array.shape)]
    widest = array.shape.index(max(array.shape))
    beside = place[:widest] + [(place[widest] + 1) % array.shape[widest]] + place[widest + 1:]
    return array.at[tuple(place)].set(smallest).at[tuple(beside)].set(top_value)


def block_levels(own_key, extent, pieces, smallest, top_value):
    def one(dim, shards_of):
        draws = jax.random.uniform(jax.random.fold_in(jax.random.fold_in(own_key, 6), dim), (shards_of,), jnp.float32, smallest / len(pieces), top_value / len(pieces))
        return jnp.repeat(jnp.exp(draws), extent[dim] // shards_of).reshape((-1,) + (1,) * (len(extent) - dim - 1))

    gain = one(*pieces[0])
    for cut in pieces[1:]:
        gain = gain * one(*cut)
    return gain


def noise(stream_key, dims, deviation, bound, cuts=(), held_as=jnp.bfloat16):
    array = deviation * jax.random.normal(stream_key, dims, jnp.float32)
    if cuts:
        array = array * block_levels(stream_key, dims, cuts, -0.22, 0.18)
    return jnp.clip(array, -bound, bound).astype(held_as)


def setup_inputs(seed: int = 0) -> dict:
    seeds = jax.random.split(jax.random.key(seed), 10)
    return {
        "col_ids": touch_ends(jax.random.randint(seeds[0], (DOCS, NNZ), 0, FEAT_DEV), jax.random.fold_in(seeds[0], 1), 0, FEAT_DEV - 1).astype(jnp.int32),
        "col_vals": jnp.clip(jnp.exp(math.log(0.19921875) - 2.3038113 * jax.random.uniform(seeds[1], (DOCS, NNZ), jnp.float32) ** block_levels(seeds[1], (DOCS, NNZ), ((0, 16), (1, 2)), -0.2, 0.2)), 0.019897461, 0.19921875).astype(jnp.bfloat16),
        "left_vec": noise(seeds[2], (DOCS, TGT), 1.0, 6.0, ((0, 16),), jnp.float32),
        "right_vec": noise(seeds[3], (FEAT, TGT), 1.0, 6.0, ((0, 32),), jnp.float32),
        "search_dir": noise(seeds[4], (FEAT, TGT), 1.0, 6.0, ((0, 32),), jnp.float32),
        "solution": noise(seeds[5], (FEAT, TGT), 1.0, 6.0, ((0, 32),), jnp.float32),
        "alpha_prev": jnp.clip(jax.random.uniform(seeds[6], (TGT,), jnp.float32, 1.0, 3.0), 1.0, 3.0),
        "phibar": jnp.clip(jax.random.uniform(seeds[7], (TGT,), jnp.float32, 0.5, 2.0), 0.5, 2.0),
        "rhobar": jnp.clip(jax.random.uniform(seeds[8], (TGT,), jnp.float32, 0.5, 3.0), 0.5, 3.0),
    }


epsilon = 1e-06

def forward(col_ids, col_vals, table):
    nrows, count = col_ids.shape
    step_rows = min(512, nrows)
    nblocks = nrows // step_rows
    ids_blocks = col_ids.reshape(nblocks, step_rows, count)
    vals_blocks = col_vals.reshape(nblocks, step_rows, count)

    def one_block(pair):
        index_rows, value_rows = pair
        picked = table[index_rows]
        return lax.optimization_barrier(jnp.sum(value_rows.astype(jnp.float32)[:, :, None] * picked, axis=1))
    return lax.map(one_block, (ids_blocks, vals_blocks)).reshape(nrows, table.shape[1])

def backward(col_ids, col_vals, rows_in, width):
    nrows, count = col_ids.shape
    step_rows = min(512, nrows)
    nblocks = nrows // step_rows
    ids_blocks = col_ids.reshape(nblocks, step_rows, count)
    vals_blocks = col_vals.reshape(nblocks, step_rows, count)
    rows_blocks = rows_in.reshape(nblocks, step_rows, rows_in.shape[1])

    def one_block(carry, triple):
        index_rows, value_rows, left_rows = triple
        terms = value_rows.astype(jnp.float32)[:, :, None] * left_rows[:, None, :]
        terms = terms.reshape(step_rows * count, left_rows.shape[1])
        added = jax.ops.segment_sum(terms, index_rows.reshape(-1), num_segments=width)
        return (carry + added, None)
    start = jnp.zeros((width, rows_in.shape[1]), jnp.float32)
    result, unused = lax.scan(one_block, start, (ids_blocks, vals_blocks, rows_blocks))
    return result

def reference(col_ids, col_vals, left_vec, right_vec, search_dir, solution, alpha_prev, phibar, rhobar):
    offsets = jnp.arange(NNZ, dtype=jnp.int32) // K_DEV * FEAT_DEV
    global_ids = (col_ids + offsets[None, :]).astype(jnp.int32)
    product = forward(global_ids, col_vals, right_vec)
    left_raw = product - alpha_prev[None, :] * left_vec
    beta_norm = jnp.sqrt(lax.optimization_barrier(jnp.mean(left_raw * left_raw, axis=0)) + epsilon)
    left_next = left_raw / beta_norm[None, :]
    right_raw = backward(global_ids, col_vals, left_next, FEAT) - beta_norm[None, :] * right_vec
    alpha_next = jnp.sqrt(lax.optimization_barrier(jnp.mean(right_raw * right_raw, axis=0)) + epsilon)
    right_next = right_raw / alpha_next[None, :]
    rho_val = jnp.sqrt(rhobar * rhobar + beta_norm * beta_norm)
    cosine = rhobar / rho_val
    sine_val = beta_norm / rho_val
    theta_val = sine_val * alpha_next
    rhobar_next = -cosine * alpha_next
    phi_val = cosine * phibar
    phibar_next = sine_val * phibar
    solution_next = solution + (phi_val / rho_val)[None, :] * search_dir
    search_next = right_next - (theta_val / rho_val)[None, :] * search_dir
    return (left_next, right_next, search_next, solution_next, alpha_next, phibar_next, rhobar_next)
```

```python
import functools

import jax
import jax.numpy as jnp
from jax import lax
from jax.experimental import pallas as pl
from jax.experimental.pallas import tpu as pltpu
from jax.sharding import PartitionSpec as P

epsilon = 1e-06
AXES = ("doc", "feat")
MIB = 1024 * 1024


Y_BIT, CORE_BIT, X_BIT, Z_SHIFT = 1, 2, 4, 3
NT = (((1,), (1,)), ((), ()))


def coords():
    d = lax.axis_index("doc")
    y = lax.axis_index("feat")
    return d, d >> 2, y


def full(shape):
    return pl.BlockSpec(shape, lambda *_: (0,) * len(shape))


def params(mib):
    return pltpu.CompilerParams(vmem_limit_bytes=mib * MIB)


def cost(flops, nbytes):
    return pl.CostEstimate(flops=int(flops), bytes_accessed=int(nbytes), transcendentals=0)


def f32(*shape):
    return jax.ShapeDtypeStruct(shape, jnp.float32)


def bf16(*shape):
    return jax.ShapeDtypeStruct(shape, jnp.bfloat16)


def right_kernel(right_ref, m0, m1, m2, m3, turned):
    _, z, _ = coords()
    cols = turned.shape[1]
    turned[...] = right_ref[...].T.reshape(turned.shape)
    for k, out in enumerate((m0, m1, m2, m3)):
        out[...] = turned[z ^ k]


def right_quarters(right):
    rows, cols = right.shape
    q = cols // 4
    return pl.pallas_call(
        right_kernel,
        out_shape=[f32(q, rows)] * 4,
        scratch_shapes=[pltpu.VMEM((4, q, rows), jnp.float32)],
        compiler_params=params(16),
        cost_estimate=cost(0, rows * cols * 8),
        name="right_quarters",
    )(right)


def left_kernel(left_ref, u0, u1, turned):
    _, z, y = coords()
    turned[...] = left_ref[...].T.reshape(turned.shape)
    for k1, out in enumerate((u0, u1)):
        out[...] = turned[2 * ((z >> 1) ^ k1) + y]


def left_quarters(left):
    rows, cols = left.shape
    q = cols // 4
    return pl.pallas_call(
        left_kernel,
        out_shape=[f32(q, rows)] * 2,
        scratch_shapes=[pltpu.VMEM((4, q, rows), jnp.float32)],
        compiler_params=params(16),
        cost_estimate=cost(0, rows * cols * 8),
        name="left_quarters",
    )(left)


def build_kernel(e00, e01, e10, e11, hi_ref, lo_ref):
    d, z, y = coords()
    half = pl.program_id(0)
    step = pl.program_id(1)
    rows = e00.shape[0] // 2
    iota = lax.broadcasted_iota(jnp.int32, (256, 256), 0).astype(jnp.float32).astype(jnp.bfloat16)
    lane_doc = lax.broadcasted_iota(jnp.int32, (8, 256), 1) >> 4
    one = jnp.ones((256, 256), jnp.bfloat16)
    zero = jnp.zeros((256, 256), jnp.bfloat16)

    def spread(row):
        wide = jnp.broadcast_to(row, (16, 256)).astype(jnp.bfloat16)
        return jnp.broadcast_to(wide[None], (16, 16, 256)).reshape(256, 256)

    for k0, (near, far) in enumerate(((e00, e10), (e01, e11))):
        y_rel = ((z & 1) ^ k0) ^ y
        at = pl.multiple_of(step * 8, 8)
        ids = jnp.where(half == 0, near[pl.ds(at, 8), :], far[pl.ds(at, 8), :])
        vals = jnp.where(half == 0, near[pl.ds(rows + at, 8), :], far[pl.ds(rows + at, 8), :])
        ids = ids.astype(jnp.int32)
        rel = (ids >> 8) ^ d
        block = ((rel & 1) << 3) | ((rel & 2) << 1) | (rel >> 2)
        code = (block * 16 + lane_doc).astype(jnp.float32)
        inner = (ids & 255).astype(jnp.float32)
        for t in range(8):
            pick = jnp.where(iota == spread(code[t : t + 1]), one, zero)
            weigh = jnp.where(iota == spread(inner[t : t + 1]), spread(vals[t : t + 1]), zero)
            dense = lax.dot_general(pick, weigh, NT, preferred_element_type=jnp.float32)
            high = dense.astype(jnp.bfloat16)
            low = (dense - high.astype(jnp.float32)).astype(jnp.bfloat16)
            high = high.reshape(16, 16, 256)
            low = low.reshape(16, 16, 256)
            for cc in range(2):
                to = pl.ds(cc * 16 + y_rel * 8, 8)
                hi_ref[to, 16 * t : 16 * t + 16, :] = high[8 * cc : 8 * cc + 8]
                lo_ref[to, 16 * t : 16 * t + 16, :] = low[8 * cc : 8 * cc + 8]


def build(entries):
    docs = entries[0].shape[0] // 2 * 16
    steps = docs // 128
    return pl.pallas_call(
        build_kernel,
        grid=(2, steps),
        in_specs=[full(entries[0].shape)] * 4,
        out_specs=[pl.BlockSpec((32, 128, 256), lambda a, s: (0, a * steps + s, 0))] * 2,
        out_shape=[bf16(32, 2 * docs, 256)] * 2,
        compiler_params=params(32),
        cost_estimate=cost(2 * 2 * docs * 2 * 16 * 256 * 256, 2 * docs * 8192 * 4),
        name="dense_rows",
    )(*entries)


def split_rows(value):
    high = value.astype(jnp.bfloat16)
    low = (value - high.astype(jnp.float32)).astype(jnp.bfloat16)
    return jnp.concatenate([high, low], axis=0)


def add_product(hi_ref, lo_ref, vec, total):
    both = split_rows(vec)
    total[...] += lax.dot_general(
        hi_ref[0], both, NT, preferred_element_type=jnp.float32
    ) + lax.dot_general(lo_ref[0], both, NT, preferred_element_type=jnp.float32)


def forward_kernel(per, count, first, hi_ref, lo_ref, *refs):
    vecs = refs[:count]
    if first:
        (total,) = refs[count:]
    else:
        before, total = refs[count:]
    step = pl.program_id(0)

    @pl.when(step == 0)
    def _():
        if first:
            total[...] = jnp.zeros_like(total)
        else:
            total[...] = before[...]

    for n in range(count):

        @pl.when(step // per == n)
        def _(n=n):
            add_product(hi_ref, lo_ref, vecs[n][step - n * per], total)


def a_spec(docs, block_of):
    return pl.BlockSpec((1, docs, 256), lambda s: (block_of(s), 0, 0))


def forward_part(hi, lo, vecs, before, block_of):
    docs = hi.shape[1]
    q = vecs[0].shape[1]
    per, count = vecs[0].shape[0], len(vecs)
    extra = [] if before is None else [before]
    return pl.pallas_call(
        functools.partial(forward_kernel, per, count, before is None),
        grid=(per * count,),
        in_specs=[a_spec(docs, block_of)] * 2
        + [full(v.shape) for v in vecs]
        + [full((docs, 2 * q))] * len(extra),
        out_specs=full((docs, 2 * q)),
        out_shape=f32(docs, 2 * q),
        compiler_params=params(32),
        cost_estimate=cost(4 * docs * 256 * 256 * per * count, 4 * docs * 256 * per * count),
        name="forward_part",
    )(hi, lo, *vecs, *extra)


def square_row(value, z, cols):
    squares = value * value
    ones = jnp.ones((8, value.shape[1]), jnp.float32)
    sums = lax.dot_general(
        ones,
        jnp.concatenate([squares] * 4, axis=0),
        NT,
        preferred_element_type=jnp.float32,
        precision=lax.Precision.HIGHEST,
    )
    lane = lax.broadcasted_iota(jnp.int32, (8, cols), 1)
    return jnp.where(lane // (cols // 4) == z, sums, 0.0)


def row_to_column(row):
    return jnp.broadcast_to(row, (128, row.shape[1])).T


def last_forward_kernel(per, count, hi_ref, lo_ref, *refs):
    vecs = refs[:count]
    before, u0, u1, alpha, l0, l1, both, sums, total, columns = refs[count:]
    step = pl.program_id(0)

    @pl.when(step == 0)
    def _():
        total[...] = before[...]
        columns[...] = row_to_column(alpha[...])

    for n in range(count):

        @pl.when(step // per == n)
        def _(n=n):
            add_product(hi_ref, lo_ref, vecs[n][step - n * per], total)

    @pl.when(step == per * count - 1)
    def _():
        _, z, _ = coords()
        q, docs = u0.shape
        turned = total[...].T
        product = turned[:q] + turned[q:]
        scale = columns[pl.ds(pl.multiple_of(z * q, q), q), :][:, 0:1]
        l0[...] = product[:, :docs] - scale * u0[...]
        l1[...] = product[:, docs:] - scale * u1[...]
        left = jnp.concatenate([l0[...], l1[...]], axis=1)
        both[...] = split_rows(left)
        sums[...] = square_row(left, z, sums.shape[1])


def last_forward(hi, lo, vecs, before, u0, u1, alpha, block_of):
    docs = hi.shape[1]
    q = vecs[0].shape[1]
    per, count = vecs[0].shape[0], len(vecs)
    return pl.pallas_call(
        functools.partial(last_forward_kernel, per, count),
        grid=(per * count,),
        in_specs=[a_spec(docs, block_of)] * 2
        + [full(v.shape) for v in vecs]
        + [full((docs, 2 * q)), full(u0.shape), full(u1.shape), full(alpha.shape)],
        out_specs=[full(u0.shape), full(u1.shape), full((2 * q, docs)), full((8, 4 * q))],
        out_shape=[f32(*u0.shape), f32(*u1.shape), bf16(2 * q, docs), f32(8, 4 * q)],
        scratch_shapes=[pltpu.VMEM((docs, 2 * q), jnp.float32), pltpu.VMEM((4 * q, 128), jnp.float32)],
        compiler_params=params(32),
        cost_estimate=cost(4 * docs * 256 * 256 * per * count, 4 * docs * 256 * per * count),
        name="last_forward",
    )(hi, lo, *vecs, before, u0, u1, alpha)


def backward_kernel(hi_ref, lo_ref, both_ref, out_ref):
    q = out_ref.shape[1]
    both = both_ref[...]
    got = jnp.dot(both, hi_ref[0], preferred_element_type=jnp.float32) + jnp.dot(
        both, lo_ref[0], preferred_element_type=jnp.float32
    )
    out_ref[0] = got[:q] + got[q:]


def backward_part(hi, lo, both, blocks, block_of):
    docs = hi.shape[1]
    q = both.shape[0] // 2
    return pl.pallas_call(
        backward_kernel,
        grid=(blocks,),
        in_specs=[a_spec(docs, block_of)] * 2 + [full(both.shape)],
        out_specs=pl.BlockSpec((1, q, 256), lambda s: (s, 0, 0)),
        out_shape=f32(blocks, q, 256),
        compiler_params=params(32),
        cost_estimate=cost(4 * docs * 256 * 256 * blocks, 4 * docs * 256 * blocks),
        name="backward_part",
    )(hi, lo, both)


def right_norm_kernel(docs_total, own, peer, r1, r2, r3, v0, v1, v2, v3, beta_sums, g0, g1, g2, g3, sums, columns):
    _, z, _ = coords()
    q = g0.shape[0]
    beta_row = jnp.sqrt(beta_sums[0:1, :] / docs_total + epsilon)
    columns[...] = row_to_column(beta_row)
    beta = columns[pl.ds(pl.multiple_of(z * q, q), q), :][:, 0:1]
    raws = []
    for k, (v, g) in enumerate(zip((v0, v1, v2, v3), (g0, g1, g2, g3))):
        total = ((own[k] + peer[k]) + r1[k]) + (r2[k] + r3[k])
        g[...] = total
        raws.append(total / beta - beta * v[...])
    sums[...] = square_row(jnp.concatenate(raws, axis=1), z, sums.shape[1])


def right_norm(docs_total, own, peer, received, quarters, beta_sums):
    q, rows = quarters[0].shape
    return pl.pallas_call(
        functools.partial(right_norm_kernel, docs_total),
        out_shape=[f32(q, rows)] * 4 + [f32(8, 4 * q)],
        scratch_shapes=[pltpu.VMEM((4 * q, 128), jnp.float32)],
        compiler_params=params(32),
        cost_estimate=cost(rows * q * 64, rows * q * 100),
        name="right_norm",
    )(own, peer, *received, *quarters, beta_sums)


def finish_kernel(docs_total, feat_total, g0, g1, g2, g3, a0, a1, a2, a3, beta_sums, right, search, phibar, rhobar,
                  right_out, search_out, alpha_out, phibar_out, rhobar_out, turned):
    _, z, _ = coords()
    for k, g in enumerate((g0, g1, g2, g3)):
        turned[z ^ k] = g[...]
    got = turned[...].reshape(-1, turned.shape[2]).T
    squares = (a0[0:1, :] + a1[0:1, :]) + (a2[0:1, :] + a3[0:1, :])
    alpha = jnp.sqrt(squares / feat_total + epsilon)
    beta = jnp.sqrt(beta_sums[0:1, :] / docs_total + epsilon)
    rho = jnp.sqrt(rhobar[...] * rhobar[...] + beta * beta)
    cosine = rhobar[...] / rho
    sine = beta / rho
    theta = sine * alpha
    rhobar_out[...] = -cosine * alpha
    phibar_out[...] = sine * phibar[...]
    alpha_out[...] = alpha
    following = (got / beta - beta * right[...]) / alpha
    right_out[...] = following
    search_out[...] = following - (theta / rho) * search[...]


def finish(docs_total, feat_total, pieces, alphas, beta_sums, right, search, phibar, rhobar):
    q, rows = pieces[0].shape
    return pl.pallas_call(
        functools.partial(finish_kernel, docs_total, feat_total),
        out_shape=[f32(*right.shape)] * 2 + [f32(1, 4 * q)] * 3,
        scratch_shapes=[pltpu.VMEM((4, q, rows), jnp.float32)],
        compiler_params=params(32),
        cost_estimate=cost(rows * q * 64, rows * q * 80),
        name="finish",
    )(*pieces, *alphas, beta_sums, right, search, phibar, rhobar)


def left_out_kernel(docs_total, p00, p01, p10, p11, beta_sums, search, solution, phibar, rhobar, left_out, solution_out, turned):
    _, z, y = coords()
    for k1, pair in enumerate(((p00, p01), (p10, p11))):
        for k0, piece in enumerate(pair):
            turned[2 * ((z >> 1) ^ k1) + (y ^ k0)] = piece[...]
    beta = jnp.sqrt(beta_sums[0:1, :] / docs_total + epsilon)
    left_out[...] = turned[...].reshape(-1, turned.shape[2]).T / beta
    rho = jnp.sqrt(rhobar[...] * rhobar[...] + beta * beta)
    phi = rhobar[...] / rho * phibar[...]
    solution_out[...] = solution[...] + (phi / rho) * search[...]


def left_out(docs_total, pieces, beta_sums, search, solution, phibar, rhobar):
    q, docs = pieces[0].shape
    return pl.pallas_call(
        functools.partial(left_out_kernel, docs_total),
        out_shape=[f32(docs, 4 * q), f32(*solution.shape)],
        scratch_shapes=[pltpu.VMEM((4, q, docs), jnp.float32)],
        compiler_params=params(32),
        cost_estimate=cost(docs * q * 16, docs * q * 60),
        name="left_out",
    )(*pieces, beta_sums, search, solution, phibar, rhobar)


def move(value, perm):
    return lax.ppermute(value, AXES, perm)


def swap(value, mask):
    return move(value, [(i, i ^ mask) for i in range(32)])


def doc_rounds():
    rounds = {}
    for k1 in range(2):
        for k0 in range(2):
            perm = []
            for i in range(32):
                z1, z0, y = i >> 4, (i >> 3) & 1, i & 1
                to = ((z1 ^ k1) << 4) | ((y ^ k0) << 3) | (i & 6) | z0
                perm.append((i, to))
            rounds[k1, k0] = perm
    return rounds


def small_sum(value):
    got = [value] + [swap(value, mask) for mask in range(1, 8)]
    while len(got) > 1:
        got = [a + b for a, b in zip(got[::2], got[1::2])]
    return got[0]


def along_z(value):
    return [value] + [swap(value, k << Z_SHIFT) for k in (1, 2, 3)]


def by_columns(
    col_ids, col_vals, left_vec, right_vec, search_dir, solution_vec, alpha_prev, phibar, rhobar
):
    docs_total = left_vec.shape[0] * 16
    feat_total = right_vec.shape[0] * 32
    alpha_row, phibar_row, rhobar_row = (v.reshape(1, -1) for v in (alpha_prev, phibar, rhobar))
    rounds = doc_rounds()

    entries = jnp.concatenate(
        [col_ids.astype(jnp.float32).reshape(-1, 256), col_vals.astype(jnp.float32).reshape(-1, 256)], axis=0
    )
    moved = [move(entries, rounds[k1, k0]) for k1 in range(2) for k0 in range(2)]

    mine = right_quarters(right_vec)
    quarters = [mine[0]] + [swap(mine[k], k << Z_SHIFT) for k in (1, 2, 3)]
    own = jnp.stack(quarters)

    turned = left_quarters(left_vec)
    u0, u1 = move(turned[0], rounds[0, 0]), move(turned[1], rounds[1, 0])

    plane = [swap(own, Y_BIT * (g >> 1) | X_BIT * (g & 1)) for g in (1, 2, 3)]
    own_peer = swap(own, CORE_BIT)
    plane_peer = [swap(p, CORE_BIT) for p in plane]

    hi, lo = build(moved)
    total = forward_part(hi, lo, [own, own_peer], None, lambda s: s + (s // 4) * 12)
    total = forward_part(hi, lo, plane, total, lambda s: s + 4)
    l0, l1, both, beta_part = last_forward(
        hi, lo, plane_peer, total, u0, u1, alpha_row, lambda s: s + 20
    )

    far = backward_part(hi, lo, both, 12, lambda s: s + 20)
    far_peer = swap(far, CORE_BIT)
    near = backward_part(hi, lo, both, 12, lambda s: s + 4)
    near_other = backward_part(hi, lo, both, 4, lambda s: s + 16)
    near_peer = swap(near_other, CORE_BIT)
    received = [
        swap(near[4 * g - 4 : 4 * g] + far_peer[4 * g - 4 : 4 * g], Y_BIT * (g >> 1) | X_BIT * (g & 1))
        for g in (1, 2, 3)
    ]
    near_own = backward_part(hi, lo, both, 4, lambda s: s)

    beta_all = along_z(small_sum(beta_part))
    beta_sums = (beta_all[0] + beta_all[1]) + (beta_all[2] + beta_all[3])
    pieces = [move(l, rounds_back) for l, rounds_back in (
        (l0, back(rounds[0, 0])), (l0, back(rounds[0, 1])), (l1, back(rounds[1, 0])), (l1, back(rounds[1, 1])))]
    left_next, solution_next = left_out(
        docs_total, pieces, beta_sums, search_dir, solution_vec, phibar_row, rhobar_row
    )

    *sent, alpha_part = right_norm(docs_total, near_own, near_peer, received, quarters, beta_sums)
    got = [sent[0]] + [swap(sent[k], k << Z_SHIFT) for k in (1, 2, 3)]
    alphas = along_z(small_sum(alpha_part))
    right_next, search_next, alpha_next, phibar_next, rhobar_next = finish(
        docs_total, feat_total, got, alphas, beta_sums, right_vec, search_dir, phibar_row, rhobar_row
    )
    return (
        left_next,
        right_next,
        search_next,
        solution_next,
        alpha_next.reshape(-1),
        phibar_next.reshape(-1),
        rhobar_next.reshape(-1),
    )


def back(perm):
    return [(b, a) for a, b in perm]


def forward(col_ids, col_vals, table):
    picked = table[col_ids]
    return jnp.sum(col_vals.astype(jnp.float32)[:, :, None] * picked, axis=1)


def backward(col_ids, col_vals, rows_in, width):
    terms = col_vals.astype(jnp.float32)[:, :, None] * rows_in[:, None, :]
    return jax.ops.segment_sum(
        terms.reshape(-1, rows_in.shape[1]), col_ids.reshape(-1), num_segments=width
    )


def by_blocks(
    col_ids, col_vals, left_vec, right_vec, search_dir, solution_vec, alpha_prev, phibar, rhobar
):
    n_feat = lax.axis_size("feat")
    n_doc = lax.axis_size("doc")
    docs_total = left_vec.shape[0] * n_doc
    feat_total = right_vec.shape[0] * n_doc * n_feat
    table = lax.all_gather(right_vec, "doc", axis=0, tiled=True)
    total = lax.psum(forward(col_ids, col_vals, table), "feat")
    left_raw = total - alpha_prev[None, :] * left_vec
    row_part = jnp.sum(left_raw * left_raw, axis=0)
    beta_norm = jnp.sqrt(lax.psum(row_part, "doc") / docs_total + epsilon)
    left_next = left_raw / beta_norm[None, :]
    feature_part = lax.psum_scatter(
        backward(col_ids, col_vals, left_next, table.shape[0]), "doc", scatter_dimension=0, tiled=True
    )
    right_raw = feature_part - beta_norm[None, :] * right_vec
    squares = lax.psum(jnp.sum(right_raw * right_raw, axis=0), AXES)
    alpha_next = jnp.sqrt(squares / feat_total + epsilon)
    right_next = right_raw / alpha_next[None, :]
    rho_val = jnp.sqrt(rhobar * rhobar + beta_norm * beta_norm)
    cosine = rhobar / rho_val
    sine_val = beta_norm / rho_val
    theta_val = sine_val * alpha_next
    phi_val = cosine * phibar
    solution_next = solution_vec + (phi_val / rho_val)[None, :] * search_dir
    search_next = right_next - (theta_val / rho_val)[None, :] * search_dir
    return (
        left_next,
        right_next,
        search_next,
        solution_next,
        alpha_next,
        sine_val * phibar,
        -cosine * alpha_next,
    )


def solution(mesh):
    small = mesh.shape["doc"] == 16 and mesh.shape["feat"] == 2
    rows = P(("feat", "doc"), None)
    return jax.shard_map(
        by_columns if small else by_blocks,
        mesh=mesh,
        in_specs=(P("doc", "feat"), P("doc", "feat"), P("doc", None), rows, rows, rows, P(), P(), P()),
        out_specs=(P("doc", None), rows, rows, rows, P(), P(), P()),
        check_vma=False,
    )
```

```python
import functools

import jax
import jax.numpy as jnp
from jax import lax
from jax.experimental import pallas as pl
from jax.experimental.pallas import tpu as pltpu
from jax.sharding import PartitionSpec as P

epsilon = 1e-06
AXES = ("doc", "feat")
MIB = 1024 * 1024


Y_BIT, CORE_BIT, X_BIT, Z_SHIFT = 1, 2, 4, 3
NT = (((1,), (1,)), ((), ()))


def coords():
    d = lax.axis_index("doc")
    y = lax.axis_index("feat")
    return d, d >> 2, y


def full(shape):
    return pl.BlockSpec(shape, lambda *_: (0,) * len(shape))


def params(mib):
    return pltpu.CompilerParams(vmem_limit_bytes=mib * MIB)


def cost(flops, nbytes):
    return pl.CostEstimate(flops=int(flops), bytes_accessed=int(nbytes), transcendentals=0)


def f32(*shape):
    return jax.ShapeDtypeStruct(shape, jnp.float32)


def bf16(*shape):
    return jax.ShapeDtypeStruct(shape, jnp.bfloat16)


def quarters_kernel(right_ref, left_ref, m0, m1, m2, m3, u0, u1, u2, u3, turned):
    _, z, y = coords()
    rows = right_ref.shape[0]
    half = left_ref.shape[0] // 2
    turned[...] = right_ref[...].T.reshape(turned.shape)
    for k, out in enumerate((m0, m1, m2, m3)):
        out[...] = turned[z ^ k]
    turned[...] = left_ref[pl.ds(pl.multiple_of(y * half, half), half), :].T.reshape(turned.shape)
    for k, out in enumerate((u0, u1, u2, u3)):
        out[...] = turned[z ^ k]


def quarters_of(right, left):
    rows, cols = right.shape
    q = cols // 4
    got = pl.pallas_call(
        quarters_kernel,
        out_shape=[f32(q, rows)] * 4 + [f32(q, left.shape[0] // 2)] * 4,
        scratch_shapes=[pltpu.VMEM((4, q, rows), jnp.float32)],
        compiler_params=params(8),
        cost_estimate=cost(0, rows * cols * 16),
        name="quarters",
    )(right, left)
    return got[:4], got[4:]


def halves_kernel(ids_ref, vals_ref, keep, send):
    _, _, y = coords()
    n = keep.shape[0] // 2
    for out, part in ((keep, y), (send, 1 - y)):
        at = pl.multiple_of(part * n, n)
        out[0:n, :] = ids_ref[pl.ds(at, n), :]
        out[n:, :] = vals_ref[pl.ds(at, n), :]


def halves_of(ids, vals):
    shape = f32(*ids.shape)
    return pl.pallas_call(
        halves_kernel,
        out_shape=[shape, shape],
        compiler_params=params(8),
        cost_estimate=cost(0, ids.size * 16),
        name="entry_halves",
    )(ids, vals)


def build_kernel(e0, e1, e2, e3, hi_ref, lo_ref):
    d, _, _ = coords()
    n = e0.shape[0] // 4
    steps = n // 8
    iota = lax.broadcasted_iota(jnp.int32, (256, 256), 0).astype(jnp.float32).astype(jnp.bfloat16)
    lane_doc = lax.broadcasted_iota(jnp.int32, (8, 256), 1) >> 4
    one = jnp.ones((256, 256), jnp.bfloat16)
    zero = jnp.zeros((256, 256), jnp.bfloat16)

    def spread(row):
        wide = jnp.broadcast_to(row, (16, 256)).astype(jnp.bfloat16)
        return jnp.broadcast_to(wide[None], (16, 16, 256)).reshape(256, 256)

    for k, entries in enumerate((e0, e1, e2, e3)):

        @pl.loop(0, steps)
        def _(step, k=k, entries=entries):
            for yy in range(2):
                at = pl.multiple_of(step * 8, 8)
                ids = entries[pl.ds(2 * n * yy + at, 8), :].astype(jnp.int32)
                vals = entries[pl.ds(2 * n * yy + n + at, 8), :]
                rel = (ids >> 8) ^ d
                block = ((rel & 1) << 3) | ((rel & 2) << 1) | (rel >> 2)
                code = (block * 16 + lane_doc).astype(jnp.float32)
                inner = (ids & 255).astype(jnp.float32)
                for t in range(8):
                    pick = jnp.where(iota == spread(code[t : t + 1]), one, zero)
                    weigh = jnp.where(iota == spread(inner[t : t + 1]), spread(vals[t : t + 1]), zero)
                    dense = lax.dot_general(pick, weigh, NT, preferred_element_type=jnp.float32)
                    high = dense.astype(jnp.bfloat16)
                    low = (dense - high.astype(jnp.float32)).astype(jnp.bfloat16)
                    high = high.reshape(16, 16, 256)
                    low = low.reshape(16, 16, 256)
                    docs = pl.ds(pl.multiple_of(k * 16 * n + step * 128 + 16 * t, 16), 16)
                    for cc in range(2):
                        to = slice(cc * 16 + yy * 8, cc * 16 + yy * 8 + 8)
                        hi_ref[to, docs, :] = high[8 * cc : 8 * cc + 8]
                        lo_ref[to, docs, :] = low[8 * cc : 8 * cc + 8]


def whole():
    return pl.BlockSpec(memory_space=pltpu.VMEM)


def build(entries):
    docs = 4 * (entries[0].shape[0] // 4 * 16)
    return pl.pallas_call(
        build_kernel,
        in_specs=[whole()] * 4,
        out_specs=[whole()] * 2,
        out_shape=[pltpu.VMEM((32, docs, 256), jnp.bfloat16)] * 2,
        compiler_params=params(12),
        cost_estimate=cost(2 * docs * 2 * 16 * 256 * 256, docs * 8192 * 4),
        name="dense_rows",
    )(*entries)


def split_rows(value):
    high = value.astype(jnp.bfloat16)
    low = (value - high.astype(jnp.float32)).astype(jnp.bfloat16)
    return jnp.concatenate([high, low], axis=0)


def add_products(hi_ref, lo_ref, first, vecs, total):
    for pair in range(0, 4, 2):
        lhs, rhs = [], []
        for k in (pair, pair + 1):
            both = split_rows(vecs[k])
            lhs += [hi_ref[first + k], lo_ref[first + k]]
            rhs += [both, both]
        total[...] += lax.dot_general(
            jnp.concatenate(lhs, axis=1), jnp.concatenate(rhs, axis=1), NT, preferred_element_type=jnp.float32
        )


def forward_kernel(blocks, has_before, hi_ref, lo_ref, *refs):
    count = len(blocks)
    vecs, total = refs[:count], refs[-1]
    total[...] = refs[count][...] if has_before else jnp.zeros_like(total)
    for n in range(count):
        add_products(hi_ref, lo_ref, blocks[n], vecs[n], total)


def forward_part(hi, lo, vecs, before, blocks):
    docs = hi.shape[1]
    q = vecs[0].shape[1]
    extra = [] if before is None else [before]
    n = 4 * len(blocks)
    return pl.pallas_call(
        functools.partial(forward_kernel, blocks, before is not None),
        in_specs=[whole()] * (2 + len(vecs) + len(extra)),
        out_specs=whole(),
        out_shape=f32(docs, 2 * q),
        compiler_params=params(12),
        cost_estimate=cost(8 * docs * 256 * 256 * n, 4 * docs * 256 * n),
        name="forward_part",
    )(hi, lo, *vecs, *extra)


def square_row(value, z, cols):
    squares = value * value
    ones = jnp.ones((8, value.shape[1]), jnp.float32)
    sums = lax.dot_general(
        ones,
        jnp.concatenate([squares] * 4, axis=0),
        NT,
        preferred_element_type=jnp.float32,
        precision=lax.Precision.HIGHEST,
    )
    lane = lax.broadcasted_iota(jnp.int32, (8, cols), 1)
    return jnp.where(lane // (cols // 4) == z, sums, 0.0)


def row_to_column(row):
    return jnp.broadcast_to(row, (128, row.shape[1])).T


def last_forward_kernel(blocks, hi_ref, lo_ref, *refs):
    count = len(blocks)
    vecs = refs[:count]
    before, u0, u1, u2, u3, alpha, l0, l1, l2, l3, both, sums, total, columns = refs[count:]
    _, z, _ = coords()
    q, docs = u0.shape
    total[...] = before[...]
    columns[...] = row_to_column(alpha[...])
    for n in range(count):
        add_products(hi_ref, lo_ref, blocks[n], vecs[n], total)
    turned = total[...].T
    product = turned[:q] + turned[q:]
    scale = columns[pl.ds(pl.multiple_of(z * q, q), q), :][:, 0:1]
    for k, (u, out) in enumerate(((u0, l0), (u1, l1), (u2, l2), (u3, l3))):
        out[...] = product[:, k * docs : (k + 1) * docs] - scale * u[...]
    left = jnp.concatenate([l0[...], l1[...], l2[...], l3[...]], axis=1)
    both[...] = split_rows(left)
    sums[...] = square_row(left, z, sums.shape[1])


def last_forward(hi, lo, vecs, before, lefts, alpha, blocks):
    docs = hi.shape[1]
    q = vecs[0].shape[1]
    n = 4 * len(blocks)
    got = pl.pallas_call(
        functools.partial(last_forward_kernel, blocks),
        in_specs=[whole()] * (2 + len(vecs) + 6),
        out_specs=[whole()] * 6,
        out_shape=[f32(*u.shape) for u in lefts] + [bf16(2 * q, docs), f32(8, 4 * q)],
        scratch_shapes=[pltpu.VMEM((docs, 2 * q), jnp.float32), pltpu.VMEM((4 * q, 128), jnp.float32)],
        compiler_params=params(12),
        cost_estimate=cost(8 * docs * 256 * 256 * n, 4 * docs * 256 * n),
        name="last_forward",
    )(hi, lo, *vecs, before, *lefts, alpha)
    return got[:4], got[4], got[5]


def backward_kernel(first, blocks, has_tail, hi_ref, lo_ref, both_ref, *refs):
    out_ref = refs[-1]
    both = both_ref[...]
    q = both.shape[0] // 2
    twice = jnp.concatenate([both, both], axis=1)
    for b in range(blocks):
        got = jnp.dot(
            twice,
            jnp.concatenate([hi_ref[first + b], lo_ref[first + b]], axis=0),
            preferred_element_type=jnp.float32,
        )
        out_ref[b * q : (b + 1) * q, :] = got[:q] + got[q:]
    if has_tail:
        out_ref[blocks * q :, :] = refs[0][...]


def backward_part(hi, lo, both, first, blocks, tail=None):
    docs = hi.shape[1]
    q = both.shape[0] // 2
    extra = [] if tail is None else [tail]
    rows = blocks * q + (0 if tail is None else tail.shape[0])
    return pl.pallas_call(
        functools.partial(backward_kernel, first, blocks, tail is not None),
        in_specs=[whole()] * (3 + len(extra)),
        out_specs=whole(),
        out_shape=f32(rows, 256),
        compiler_params=params(12),
        cost_estimate=cost(8 * docs * 256 * 256 * blocks, 4 * docs * 256 * blocks),
        name="backward_part",
    )(hi, lo, both, *extra)


def plane_kernel(near, far, beta, s1, s2, s3, beta_core):
    n = near.shape[0] // 3
    beta_core[...] = beta[...] + far[3 * n :, :]
    for g, out in enumerate((s1, s2, s3)):
        rows = slice(g * n, (g + 1) * n)
        out[0:n, :] = near[rows, :] + far[rows, :]
        out[n:, :] = beta_core[...]


def plane_sums(near, far, beta):
    rows = near.shape[0] // 3
    return pl.pallas_call(
        plane_kernel,
        out_shape=[f32(rows + 8, 256)] * 3 + [f32(8, 256)],
        compiler_params=params(8),
        cost_estimate=cost(near.size, near.size * 12),
        name="plane_sums",
    )(near, far, beta)


def right_norm_kernel(docs_total, own, peer, r1, r2, r3, beta_core, v0, v1, v2, v3, g0, g1, g2, g3, sums, columns):
    _, z, _ = coords()
    q = v0.shape[0]
    tail = slice(4 * q, 4 * q + 8)
    beta_sums = (beta_core[...] + r1[tail, :]) + (r2[tail, :] + r3[tail, :])
    columns[...] = row_to_column(jnp.sqrt(beta_sums[0:1, :] / docs_total + epsilon))
    beta = columns[pl.ds(pl.multiple_of(z * q, q), q), :][:, 0:1]
    raws = []
    for k, (v, g) in enumerate(zip((v0, v1, v2, v3), (g0, g1, g2, g3))):
        rows = slice(k * q, (k + 1) * q)
        total = ((own[rows, :] + peer[rows, :]) + r1[rows, :]) + (r2[rows, :] + r3[rows, :])
        g[0:q, :] = total
        g[q:, :] = beta_sums
        raws.append(total / beta - beta * v[...])
    sums[...] = square_row(jnp.concatenate(raws, axis=1), z, sums.shape[1])


def right_norm(docs_total, own, peer, received, beta_core, quarters):
    q, rows = quarters[0].shape
    got = pl.pallas_call(
        functools.partial(right_norm_kernel, docs_total),
        out_shape=[f32(q + 8, rows)] * 4 + [f32(8, 4 * q)],
        scratch_shapes=[pltpu.VMEM((4 * q, 128), jnp.float32)],
        compiler_params=params(12),
        cost_estimate=cost(rows * q * 64, rows * q * 100),
        name="right_norm",
    )(own, peer, *received, beta_core, *quarters)
    return got[:4], got[4]


def beta_of(pieces, q, docs_total):
    squares = [g[q : q + 1, :] for g in pieces]
    return jnp.sqrt(((squares[0] + squares[1]) + (squares[2] + squares[3])) / docs_total + epsilon)


def finish_kernel(docs_total, feat_total, g0, g1, g2, g3, a0, a1, a2, a3, right, search, phibar, rhobar,
                  right_out, search_out, alpha_out, phibar_out, rhobar_out, turned):
    _, z, _ = coords()
    q = turned.shape[1]
    for k, g in enumerate((g0, g1, g2, g3)):
        turned[z ^ k] = g[0:q, :]
    got = turned[...].reshape(-1, turned.shape[2]).T
    squares = (a0[0:1, :] + a1[0:1, :]) + (a2[0:1, :] + a3[0:1, :])
    alpha = jnp.sqrt(squares / feat_total + epsilon)
    beta = beta_of((g0, g1, g2, g3), q, docs_total)
    rho = jnp.sqrt(rhobar[...] * rhobar[...] + beta * beta)
    cosine = rhobar[...] / rho
    sine = beta / rho
    theta = sine * alpha
    rhobar_out[...] = -cosine * alpha
    phibar_out[...] = sine * phibar[...]
    alpha_out[...] = alpha
    following = (got / beta - beta * right[...]) / alpha
    right_out[...] = following
    search_out[...] = following - (theta / rho) * search[...]


def finish(docs_total, feat_total, pieces, alphas, right, search, phibar, rhobar):
    rows, cols = right.shape
    return pl.pallas_call(
        functools.partial(finish_kernel, docs_total, feat_total),
        out_shape=[f32(rows, cols)] * 2 + [f32(1, cols)] * 3,
        scratch_shapes=[pltpu.VMEM((4, cols // 4, rows), jnp.float32)],
        compiler_params=params(12),
        cost_estimate=cost(rows * cols * 16, rows * cols * 20),
        name="finish",
    )(*pieces, *alphas, right, search, phibar, rhobar)


def left_out_kernel(docs_total, own, other, g0, g1, g2, g3, search, solution, phibar, rhobar, left_out, solution_out, turned):
    _, z, y = coords()
    q, half = turned.shape[1:]
    beta = beta_of((g0, g1, g2, g3), q, docs_total)
    for part, ref in ((y, own), (1 - y, other)):
        for k in range(4):
            turned[z ^ k] = ref[k]
        left_out[pl.ds(pl.multiple_of(part * half, half), half), :] = turned[...].reshape(-1, half).T / beta
    rho = jnp.sqrt(rhobar[...] * rhobar[...] + beta * beta)
    phi = rhobar[...] / rho * phibar[...]
    solution_out[...] = solution[...] + (phi / rho) * search[...]


def left_out(docs_total, own, other, pieces, search, solution, phibar, rhobar):
    _, q, half = own.shape
    return pl.pallas_call(
        functools.partial(left_out_kernel, docs_total),
        out_shape=[f32(2 * half, 4 * q), f32(*solution.shape)],
        scratch_shapes=[pltpu.VMEM((4, q, half), jnp.float32)],
        compiler_params=params(12),
        cost_estimate=cost(half * q * 32, half * q * 120),
        name="left_out",
    )(own, other, *pieces, search, solution, phibar, rhobar)


def swap(value, mask):
    return lax.ppermute(value, AXES, [(i, i ^ mask) for i in range(32)])


def along_z(values):
    return [values[0]] + [swap(values[k], k << Z_SHIFT) for k in (1, 2, 3)]


def plane_mask(g):
    return Y_BIT * (g >> 1) | X_BIT * (g & 1)


def by_columns(
    col_ids, col_vals, left_vec, right_vec, search_dir, solution_vec, alpha_prev, phibar, rhobar
):
    docs_total = left_vec.shape[0] * 16
    feat_total = right_vec.shape[0] * 32
    alpha_row, phibar_row, rhobar_row = (v.reshape(1, -1) for v in (alpha_prev, phibar, rhobar))

    mine, lefts = quarters_of(right_vec, left_vec)
    quarters = along_z(mine)
    keep, send = halves_of(
        col_ids.astype(jnp.float32).reshape(-1, 256), col_vals.astype(jnp.float32).reshape(-1, 256)
    )
    entries = along_z([jnp.concatenate([keep, swap(send, Y_BIT)], axis=0)] * 4)
    own = jnp.stack(quarters)
    plane = [swap(own, plane_mask(g)) for g in (1, 2, 3)]
    own_peer = swap(own, CORE_BIT)
    lefts = along_z(lefts)

    hi, lo = build(entries)
    total = forward_part(hi, lo, [own, own_peer], None, (0, 16))
    plane_peer = [swap(p, CORE_BIT) for p in plane]
    total = forward_part(hi, lo, plane, total, (4, 8, 12))
    raws, both, beta_part = last_forward(hi, lo, plane_peer, total, lefts, alpha_row, (20, 24, 28))

    far_peer = swap(backward_part(hi, lo, both, 20, 12, beta_part), CORE_BIT)
    near = backward_part(hi, lo, both, 4, 12)
    *sent, beta_core = plane_sums(near, far_peer, beta_part)
    received = [swap(s, plane_mask(g)) for g, s in zip((1, 2, 3), sent)]
    near_peer = swap(backward_part(hi, lo, both, 16, 4), CORE_BIT)
    near_own = backward_part(hi, lo, both, 0, 4)

    near_own, *raws = lax.optimization_barrier((near_own, *raws))
    left_own = jnp.stack(along_z(raws))
    left_other = swap(left_own, Y_BIT)

    sent, alpha_part = right_norm(docs_total, near_own, near_peer, received, beta_core, quarters)
    got = along_z(sent)
    for mask in (CORE_BIT, X_BIT, Y_BIT):
        alpha_part = alpha_part + swap(alpha_part, mask)
    alphas = along_z([alpha_part] * 4)
    left_next, solution_next = left_out(
        docs_total, left_own, left_other, got, search_dir, solution_vec, phibar_row, rhobar_row
    )
    right_next, search_next, alpha_next, phibar_next, rhobar_next = finish(
        docs_total, feat_total, got, alphas, right_vec, search_dir, phibar_row, rhobar_row
    )
    return (
        left_next,
        right_next,
        search_next,
        solution_next,
        alpha_next.reshape(-1),
        phibar_next.reshape(-1),
        rhobar_next.reshape(-1),
    )


def forward(col_ids, col_vals, table):
    picked = table[col_ids]
    return jnp.sum(col_vals.astype(jnp.float32)[:, :, None] * picked, axis=1)


def backward(col_ids, col_vals, rows_in, width):
    terms = col_vals.astype(jnp.float32)[:, :, None] * rows_in[:, None, :]
    return jax.ops.segment_sum(
        terms.reshape(-1, rows_in.shape[1]), col_ids.reshape(-1), num_segments=width
    )


def by_blocks(
    col_ids, col_vals, left_vec, right_vec, search_dir, solution_vec, alpha_prev, phibar, rhobar
):
    n_feat = lax.axis_size("feat")
    n_doc = lax.axis_size("doc")
    docs_total = left_vec.shape[0] * n_doc
    feat_total = right_vec.shape[0] * n_doc * n_feat
    table = lax.all_gather(right_vec, "doc", axis=0, tiled=True)
    total = lax.psum(forward(col_ids, col_vals, table), "feat")
    left_raw = total - alpha_prev[None, :] * left_vec
    row_part = jnp.sum(left_raw * left_raw, axis=0)
    beta_norm = jnp.sqrt(lax.psum(row_part, "doc") / docs_total + epsilon)
    left_next = left_raw / beta_norm[None, :]
    feature_part = lax.psum_scatter(
        backward(col_ids, col_vals, left_next, table.shape[0]), "doc", scatter_dimension=0, tiled=True
    )
    right_raw = feature_part - beta_norm[None, :] * right_vec
    squares = lax.psum(jnp.sum(right_raw * right_raw, axis=0), AXES)
    alpha_next = jnp.sqrt(squares / feat_total + epsilon)
    right_next = right_raw / alpha_next[None, :]
    rho_val = jnp.sqrt(rhobar * rhobar + beta_norm * beta_norm)
    cosine = rhobar / rho_val
    sine_val = beta_norm / rho_val
    theta_val = sine_val * alpha_next
    phi_val = cosine * phibar
    solution_next = solution_vec + (phi_val / rho_val)[None, :] * search_dir
    search_next = right_next - (theta_val / rho_val)[None, :] * search_dir
    return (
        left_next,
        right_next,
        search_next,
        solution_next,
        alpha_next,
        sine_val * phibar,
        -cosine * alpha_next,
    )


def solution(mesh):
    small = mesh.shape["doc"] == 16 and mesh.shape["feat"] == 2
    rows = P(("feat", "doc"), None)
    return jax.shard_map(
        by_columns if small else by_blocks,
        mesh=mesh,
        in_specs=(P("doc", "feat"), P("doc", "feat"), P("doc", None), rows, rows, rows, P(), P(), P()),
        out_specs=(P("doc", None), rows, rows, rows, P(), P(), P()),
        check_vma=False,
    )
```

```python
import functools

import jax
import jax.numpy as jnp
from jax import lax
from jax.experimental import pallas as pl
from jax.experimental.pallas import tpu as pltpu
from jax.sharding import PartitionSpec as P

epsilon = 1e-06
AXES = ("doc", "feat")
MIB = 1024 * 1024


Y_BIT, CORE_BIT, X_BIT, Z_SHIFT = 1, 2, 4, 3
NT = (((1,), (1,)), ((), ()))


def coords():
    d = lax.axis_index("doc")
    y = lax.axis_index("feat")
    return d, d >> 2, y


def params(mib):
    return pltpu.CompilerParams(vmem_limit_bytes=mib * MIB)


def cost(flops, nbytes):
    return pl.CostEstimate(flops=int(flops), bytes_accessed=int(nbytes), transcendentals=0)


def f32(*shape):
    return jax.ShapeDtypeStruct(shape, jnp.float32)


def bf16(*shape):
    return jax.ShapeDtypeStruct(shape, jnp.bfloat16)


def quarters_kernel(ref, m0, m1, m2, m3, turned):
    _, z, _ = coords()
    turned[...] = ref[...].T.reshape(turned.shape)
    for k, out in enumerate((m0, m1, m2, m3)):
        out[...] = turned[z ^ k]


def quarters_of(value, name):
    rows, cols = value.shape
    q = cols // 4
    return pl.pallas_call(
        quarters_kernel,
        out_shape=[f32(q, rows)] * 4,
        scratch_shapes=[pltpu.VMEM((4, q, rows), jnp.float32)],
        compiler_params=params(8),
        cost_estimate=cost(0, rows * cols * 8),
        name=name,
    )(value)


def build_kernel(e0, e1, e2, e3, hi_ref, lo_ref):
    d, _, _ = coords()
    n = e0.shape[0] // 2
    iota = lax.broadcasted_iota(jnp.int32, (256, 256), 0).astype(jnp.float32).astype(jnp.bfloat16)
    lane_doc = lax.broadcasted_iota(jnp.int32, (8, 256), 1) >> 4
    one = jnp.ones((256, 256), jnp.bfloat16)
    zero = jnp.zeros((256, 256), jnp.bfloat16)

    def spread(row):
        wide = jnp.broadcast_to(row, (16, 256)).astype(jnp.bfloat16)
        return jnp.broadcast_to(wide[None], (16, 16, 256)).reshape(256, 256)

    for k, entries in enumerate((e0, e1, e2, e3)):

        @pl.loop(0, n // 8)
        def _(step, k=k, entries=entries):
            at = pl.multiple_of(step * 8, 8)
            ids = entries[pl.ds(at, 8), :].astype(jnp.int32)
            vals = entries[pl.ds(n + at, 8), :]
            rel = (ids >> 8) ^ d
            block = ((rel & 1) << 3) | ((rel & 2) << 1) | (rel >> 2)
            code = (block * 16 + lane_doc).astype(jnp.float32)
            inner = (ids & 255).astype(jnp.float32)
            for t in range(8):
                pick = jnp.where(iota == spread(code[t : t + 1]), one, zero)
                weigh = jnp.where(iota == spread(inner[t : t + 1]), spread(vals[t : t + 1]), zero)
                dense = lax.dot_general(pick, weigh, NT, preferred_element_type=jnp.float32)
                high = dense.astype(jnp.bfloat16)
                low = (dense - high.astype(jnp.float32)).astype(jnp.bfloat16)
                docs = pl.ds(pl.multiple_of(k * 16 * n + step * 128 + 16 * t, 16), 16)
                hi_ref[:, docs, :] = high.reshape(16, 16, 256)
                lo_ref[:, docs, :] = low.reshape(16, 16, 256)


def whole():
    return pl.BlockSpec(memory_space=pltpu.VMEM)


def build(entries):
    docs = 4 * (entries[0].shape[0] // 2 * 16)
    return pl.pallas_call(
        build_kernel,
        in_specs=[whole()] * 4,
        out_specs=[whole()] * 2,
        out_shape=[pltpu.VMEM((16, docs, 256), jnp.bfloat16)] * 2,
        compiler_params=params(12),
        cost_estimate=cost(2 * docs * 16 * 256 * 256, docs * 4096 * 4),
        name="dense_rows",
    )(*entries)


def split_rows(value):
    high = value.astype(jnp.bfloat16)
    low = (value - high.astype(jnp.float32)).astype(jnp.bfloat16)
    return jnp.concatenate([high, low], axis=0)


def block_product(hi_ref, lo_ref, docs, first, vecs):
    lhs, rhs = [], []
    for k in range(2):
        both = split_rows(vecs[k])
        lhs += [hi_ref[first + k, docs, :], lo_ref[first + k, docs, :]]
        rhs += [both, both]
    return lax.dot_general(
        jnp.concatenate(lhs, axis=1), jnp.concatenate(rhs, axis=1), NT, preferred_element_type=jnp.float32
    )


def add_products(hi_ref, lo_ref, docs, vecs, blocks, total):
    for vec, first in zip(vecs, blocks):
        for pair in (0, 2):
            total[...] += block_product(hi_ref, lo_ref, docs, first + pair, vec[pair : pair + 2])


def forward_kernel(blocks, hi_ref, lo_ref, v0, v1, total):
    total[...] = jnp.zeros_like(total)
    for half in range(2):
        n = total.shape[0] // 2
        docs = slice(half * n, (half + 1) * n)
        add_products(hi_ref, lo_ref, docs, (v0, v1), blocks, total.at[docs])


def forward_part(hi, lo, vecs, blocks):
    docs = hi.shape[1]
    q = vecs[0].shape[1]
    n = 4 * len(blocks)
    return pl.pallas_call(
        functools.partial(forward_kernel, blocks),
        in_specs=[whole()] * 4,
        out_specs=whole(),
        out_shape=f32(docs, 2 * q),
        compiler_params=params(12),
        cost_estimate=cost(8 * docs * 256 * 256 * n, 4 * docs * 256 * n),
        name="forward_part",
    )(hi, lo, *vecs)


def forward_half_kernel(half, blocks, hi_ref, lo_ref, v0, v1, before, out, total):
    n = total.shape[0]
    docs = slice(half * n, (half + 1) * n)
    total[...] = before[docs, :]
    add_products(hi_ref, lo_ref, docs, (v0, v1), blocks, total)
    turned = total[...].T
    q = out.shape[0]
    out[...] = turned[:q] + turned[q:]


def forward_half(hi, lo, vecs, before, blocks, half):
    docs = hi.shape[1] // 2
    q = vecs[0].shape[1]
    n = 4 * len(blocks)
    return pl.pallas_call(
        functools.partial(forward_half_kernel, half, blocks),
        in_specs=[whole()] * 5,
        out_specs=whole(),
        out_shape=f32(q, docs),
        scratch_shapes=[pltpu.VMEM((docs, 2 * q), jnp.float32)],
        compiler_params=params(12),
        cost_estimate=cost(8 * docs * 256 * 256 * n, 4 * docs * 256 * n),
        name="forward_half",
    )(hi, lo, *vecs, before)


def square_row(value, z, cols):
    q, n = value.shape
    sums = value[:, 0:128] * value[:, 0:128]
    for at in range(128, n, 128):
        sums = sums + value[:, at : at + 128] * value[:, at : at + 128]
    row = jnp.sum(jnp.concatenate([sums] * (128 // q), axis=0).T, axis=0, keepdims=True)
    row = jnp.broadcast_to(jnp.concatenate([row] * (cols // 128), axis=1), (8, cols))
    lane = lax.broadcasted_iota(jnp.int32, (8, cols), 1)
    return jnp.where(lane // q == z, row, 0.0)


def row_to_column(row):
    return jnp.broadcast_to(row, (128, row.shape[1])).T


def left_raw_kernel(has_before, mine, other, u0, u1, alpha, *refs):
    l0, l1, both, sums, columns = refs[-5:]
    _, z, _ = coords()
    q, docs = u0.shape
    columns[...] = row_to_column(alpha[...])
    scale = columns[pl.ds(pl.multiple_of(z * q, q), q), :][:, 0:1]
    for k, (u, out) in enumerate(((u0, l0), (u1, l1))):
        at = slice(k * docs, (k + 1) * docs)
        out[...] = (mine[:, at] + other[:, at]) - scale * u[...]
    left = jnp.concatenate([l0[...], l1[...]], axis=1)
    both[...] = split_rows(left)
    squares = square_row(left, z, sums.shape[1])
    sums[...] = refs[0][...] + squares if has_before else squares


def left_raw(mine, other, lefts, alpha, before=None):
    q, docs = lefts[0].shape
    extra = [] if before is None else [before]
    return pl.pallas_call(
        functools.partial(left_raw_kernel, before is not None),
        out_shape=[f32(q, docs)] * 2 + [bf16(2 * q, 2 * docs), f32(8, 4 * q)],
        scratch_shapes=[pltpu.VMEM((4 * q, 128), jnp.float32)],
        compiler_params=params(8),
        cost_estimate=cost(8 * q * docs, 40 * q * docs),
        name="left_raw",
    )(mine, other, *lefts, alpha, *extra)


def backward_kernel(half, first, blocks, parts, hi_ref, lo_ref, both_ref, *refs):
    out_ref = refs[-1]
    both = both_ref[...]
    q, n = both.shape[0] // 2, both.shape[1]
    docs = slice(half * n, (half + 1) * n)
    twice = jnp.concatenate([both, both], axis=1)
    for b in range(blocks):
        got = jnp.dot(
            twice,
            jnp.concatenate([hi_ref[first + b, docs, :], lo_ref[first + b, docs, :]], axis=0),
            preferred_element_type=jnp.float32,
        )
        got = got[:q] + got[q:]
        if "before" in parts:
            got = got + refs[0][(first + b) * q : (first + b + 1) * q, :]
        out_ref[b * q : (b + 1) * q, :] = got
    if "tail" in parts:
        out_ref[blocks * q :, :] = refs[-2][...]


def backward_part(hi, lo, both, half, first, blocks, before=None, tail=None):
    q, docs = both.shape[0] // 2, both.shape[1]
    extra = {"before": before, "tail": tail}
    extra = {name: value for name, value in extra.items() if value is not None}
    rows = blocks * q + (0 if tail is None else tail.shape[0])
    return pl.pallas_call(
        functools.partial(backward_kernel, half, first, blocks, tuple(extra)),
        in_specs=[whole()] * (3 + len(extra)),
        out_specs=whole(),
        out_shape=f32(rows, 256),
        compiler_params=params(12),
        cost_estimate=cost(8 * docs * 256 * 256 * blocks, 4 * docs * 256 * blocks),
        name="backward_part",
    )(hi, lo, both, *extra.values())


def far_sum_kernel(near, far, beta, send, keep, beta_core):
    n = keep.shape[0]
    beta_core[...] = beta[...] + far[2 * n :, :]
    send[0:n, :] = near[n:, :] + far[n : 2 * n, :]
    send[n:, :] = beta_core[...]
    keep[...] = near[0:n, :] + far[0:n, :]


def far_sums(near, far, beta):
    rows = near.shape[0] // 2
    return pl.pallas_call(
        far_sum_kernel,
        out_shape=[f32(rows + 8, 256), f32(rows, 256), f32(8, 256)],
        compiler_params=params(8),
        cost_estimate=cost(near.size, near.size * 12),
        name="far_sums",
    )(near, far, beta)


def right_norm_kernel(docs_total, keep, got, beta_core, v0, v1, v2, v3, g0, g1, g2, g3, sums, columns):
    _, z, _ = coords()
    q = v0.shape[0]
    beta_sums = beta_core[...] + got[4 * q :, :]
    columns[...] = row_to_column(jnp.sqrt(beta_sums[0:1, :] / docs_total + epsilon))
    beta = columns[pl.ds(pl.multiple_of(z * q, q), q), :][:, 0:1]
    raws = []
    for k, (v, g) in enumerate(zip((v0, v1, v2, v3), (g0, g1, g2, g3))):
        rows = slice(k * q, (k + 1) * q)
        total = keep[rows, :] + got[rows, :]
        g[0:q, :] = total
        g[q:, :] = beta_sums
        raws.append(total / beta - beta * v[...])
    sums[...] = square_row(jnp.concatenate(raws, axis=1), z, sums.shape[1])


def right_norm(docs_total, keep, got, beta_core, quarters):
    q, rows = quarters[0].shape
    out = pl.pallas_call(
        functools.partial(right_norm_kernel, docs_total),
        out_shape=[f32(q + 8, rows)] * 4 + [f32(8, 4 * q)],
        scratch_shapes=[pltpu.VMEM((4 * q, 128), jnp.float32)],
        compiler_params=params(8),
        cost_estimate=cost(rows * q * 64, rows * q * 100),
        name="right_norm",
    )(keep, got, beta_core, *quarters)
    return out[:4], out[4]


def beta_of(pieces, q, docs_total):
    squares = [g[q : q + 1, :] for g in pieces]
    return jnp.sqrt(((squares[0] + squares[1]) + (squares[2] + squares[3])) / docs_total + epsilon)


def finish_kernel(docs_total, feat_total, g0, g1, g2, g3, a0, a1, a2, a3, right, search, phibar, rhobar,
                  right_out, search_out, alpha_out, phibar_out, rhobar_out, turned):
    _, z, _ = coords()
    q = turned.shape[1]
    for k, g in enumerate((g0, g1, g2, g3)):
        turned[z ^ k] = g[0:q, :]
    got = turned[...].reshape(-1, turned.shape[2]).T
    squares = (a0[0:1, :] + a1[0:1, :]) + (a2[0:1, :] + a3[0:1, :])
    alpha = jnp.sqrt(squares / feat_total + epsilon)
    beta = beta_of((g0, g1, g2, g3), q, docs_total)
    rho = jnp.sqrt(rhobar[...] * rhobar[...] + beta * beta)
    cosine = rhobar[...] / rho
    sine = beta / rho
    theta = sine * alpha
    rhobar_out[...] = -cosine * alpha
    phibar_out[...] = sine * phibar[...]
    alpha_out[...] = alpha
    following = (got / beta - beta * right[...]) / alpha
    right_out[...] = following
    search_out[...] = following - (theta / rho) * search[...]


def finish(docs_total, feat_total, pieces, alphas, right, search, phibar, rhobar):
    rows, cols = right.shape
    return pl.pallas_call(
        functools.partial(finish_kernel, docs_total, feat_total),
        out_shape=[f32(rows, cols)] * 2 + [f32(1, cols)] * 3,
        scratch_shapes=[pltpu.VMEM((4, cols // 4, rows), jnp.float32)],
        compiler_params=params(8),
        cost_estimate=cost(rows * cols * 16, rows * cols * 20),
        name="finish",
    )(*pieces, *alphas, right, search, phibar, rhobar)


def left_out_kernel(docs_total, l0, l1, l2, l3, g0, g1, g2, g3, search, solution, phibar, rhobar, left_out, solution_out, turned):
    _, z, _ = coords()
    q, docs = turned.shape[1:]
    beta = beta_of((g0, g1, g2, g3), q, docs_total)
    for k, piece in enumerate((l0, l1, l2, l3)):
        turned[z ^ k] = piece[...]
    left_out[...] = turned[...].reshape(-1, docs).T / beta
    rho = jnp.sqrt(rhobar[...] * rhobar[...] + beta * beta)
    phi = rhobar[...] / rho * phibar[...]
    solution_out[...] = solution[...] + (phi / rho) * search[...]


def left_out(docs_total, lefts, pieces, search, solution, phibar, rhobar):
    q, docs = lefts[0].shape
    return pl.pallas_call(
        functools.partial(left_out_kernel, docs_total),
        out_shape=[f32(docs, 4 * q), f32(*solution.shape)],
        scratch_shapes=[pltpu.VMEM((4, q, docs), jnp.float32)],
        compiler_params=params(8),
        cost_estimate=cost(docs * q * 16, docs * q * 60),
        name="left_out",
    )(*lefts, *pieces, search, solution, phibar, rhobar)


def swap(value, mask):
    return lax.ppermute(value, AXES, [(i, i ^ mask) for i in range(32)])


def along_z(values):
    return [values[0]] + [swap(values[k], k << Z_SHIFT) for k in (1, 2, 3)]


def after(value, *earlier):
    return lax.optimization_barrier((value, *earlier))[0]


def by_columns(
    col_ids, col_vals, left_vec, right_vec, search_dir, solution_vec, alpha_prev, phibar, rhobar
):
    docs_total = left_vec.shape[0] * 16
    feat_total = right_vec.shape[0] * 32
    alpha_row, phibar_row, rhobar_row = (v.reshape(1, -1) for v in (alpha_prev, phibar, rhobar))

    mine = quarters_of(right_vec, "right_quarters")
    quarters = along_z(mine)
    ids, vals = col_ids.astype(jnp.float32), col_vals.astype(jnp.float32)
    entries = along_z([jnp.concatenate([ids.reshape(-1, 256), vals.reshape(-1, 256)], axis=0)] * 4)
    own = jnp.stack(quarters)
    own_x = swap(own, X_BIT)
    own_peer = swap(own, CORE_BIT)
    lefts = along_z(quarters_of(after(left_vec, own), "left_quarters"))

    hi, lo = build(entries)
    total = forward_part(hi, lo, [own, own_peer], (0, 8))
    vecs = [own_x, swap(own_x, CORE_BIT)]
    product = [forward_half(hi, lo, vecs, total, (4, 12), half) for half in range(2)]
    other = [swap(p, Y_BIT) for p in product]

    l0, l1, both0, beta0 = left_raw(product[0], other[0], lefts[:2], alpha_row)
    partial = backward_part(hi, lo, both0, 0, 0, 16)
    l2, l3, both1, beta1 = left_raw(product[1], other[1], lefts[2:], alpha_row, beta0)
    far = swap(backward_part(hi, lo, both1, 1, 8, 8, partial, beta1), CORE_BIT)
    near = backward_part(hi, lo, both1, 1, 0, 8, partial)
    send, keep, beta_core = far_sums(near, far, beta1)
    got = swap(send, X_BIT)
    left_pieces = along_z([l0, after(l1, partial), after(l2, keep), after(l3, keep)])

    sent, alpha_part = right_norm(docs_total, keep, got, beta_core, quarters)
    pieces = along_z(sent)
    for mask in (CORE_BIT, X_BIT, Y_BIT):
        alpha_part = alpha_part + swap(alpha_part, mask)
    alphas = along_z([alpha_part] * 4)
    left_next, solution_next = left_out(
        docs_total, left_pieces, pieces, search_dir, solution_vec, phibar_row, rhobar_row
    )
    right_next, search_next, alpha_next, phibar_next, rhobar_next = finish(
        docs_total, feat_total, pieces, alphas, right_vec, search_dir, phibar_row, rhobar_row
    )
    return (
        left_next,
        right_next,
        search_next,
        solution_next,
        alpha_next.reshape(-1),
        phibar_next.reshape(-1),
        rhobar_next.reshape(-1),
    )


def forward(col_ids, col_vals, table):
    picked = table[col_ids]
    return jnp.sum(col_vals.astype(jnp.float32)[:, :, None] * picked, axis=1)


def backward(col_ids, col_vals, rows_in, width):
    terms = col_vals.astype(jnp.float32)[:, :, None] * rows_in[:, None, :]
    return jax.ops.segment_sum(
        terms.reshape(-1, rows_in.shape[1]), col_ids.reshape(-1), num_segments=width
    )


def by_blocks(
    col_ids, col_vals, left_vec, right_vec, search_dir, solution_vec, alpha_prev, phibar, rhobar
):
    n_feat = lax.axis_size("feat")
    n_doc = lax.axis_size("doc")
    docs_total = left_vec.shape[0] * n_doc
    feat_total = right_vec.shape[0] * n_doc * n_feat
    table = lax.all_gather(right_vec, "doc", axis=0, tiled=True)
    total = lax.psum(forward(col_ids, col_vals, table), "feat")
    left_raw = total - alpha_prev[None, :] * left_vec
    row_part = jnp.sum(left_raw * left_raw, axis=0)
    beta_norm = jnp.sqrt(lax.psum(row_part, "doc") / docs_total + epsilon)
    left_next = left_raw / beta_norm[None, :]
    feature_part = lax.psum_scatter(
        backward(col_ids, col_vals, left_next, table.shape[0]), "doc", scatter_dimension=0, tiled=True
    )
    right_raw = feature_part - beta_norm[None, :] * right_vec
    squares = lax.psum(jnp.sum(right_raw * right_raw, axis=0), AXES)
    alpha_next = jnp.sqrt(squares / feat_total + epsilon)
    right_next = right_raw / alpha_next[None, :]
    rho_val = jnp.sqrt(rhobar * rhobar + beta_norm * beta_norm)
    cosine = rhobar / rho_val
    sine_val = beta_norm / rho_val
    theta_val = sine_val * alpha_next
    phi_val = cosine * phibar
    solution_next = solution_vec + (phi_val / rho_val)[None, :] * search_dir
    search_next = right_next - (theta_val / rho_val)[None, :] * search_dir
    return (
        left_next,
        right_next,
        search_next,
        solution_next,
        alpha_next,
        sine_val * phibar,
        -cosine * alpha_next,
    )


def solution(mesh):
    small = mesh.shape["doc"] == 16 and mesh.shape["feat"] == 2
    rows = P(("feat", "doc"), None)
    return jax.shard_map(
        by_columns if small else by_blocks,
        mesh=mesh,
        in_specs=(P("doc", "feat"), P("doc", "feat"), P("doc", None), rows, rows, rows, P(), P(), P()),
        out_specs=(P("doc", None), rows, rows, rows, P(), P(), P()),
        check_vma=False,
    )
```

```python
import functools

import jax
import jax.numpy as jnp
from jax import lax
from jax.experimental import pallas as pl
from jax.experimental.pallas import tpu as pltpu
from jax.sharding import PartitionSpec as P

epsilon = 1e-06
AXES = ("doc", "feat")
MIB = 1024 * 1024


Y_BIT, CORE_BIT, X_BIT, Z_SHIFT = 1, 2, 4, 3
PLANES = [list(range(first, first + 8)) for first in range(0, 32, 8)]
NT = (((1,), (1,)), ((), ()))


def coords():
    d = lax.axis_index("doc")
    y = lax.axis_index("feat")
    return d, d >> 2, y


def params(mib):
    return pltpu.CompilerParams(vmem_limit_bytes=mib * MIB)


def cost(flops, nbytes):
    return pl.CostEstimate(flops=int(flops), bytes_accessed=int(nbytes), transcendentals=0)


def f32(*shape):
    return jax.ShapeDtypeStruct(shape, jnp.float32)


def bf16(*shape):
    return jax.ShapeDtypeStruct(shape, jnp.bfloat16)


def quarters_kernel(right_ref, left_ref, m0, m1, m2, m3, turned):
    _, z, y = coords()
    q, rows = turned.shape[1:]
    for part in range(2):
        value = left_ref[pl.ds(pl.multiple_of(y * rows, rows), rows), :] if part else right_ref[...]
        turned[...] = value.T.reshape(turned.shape)
        for k, out in enumerate((m0, m1, m2, m3)):
            out[part * q : (part + 1) * q, :] = turned[z ^ k]


def quarters_of(right, left):
    rows, cols = right.shape
    q = cols // 4
    return pl.pallas_call(
        quarters_kernel,
        out_shape=[f32(2 * q, rows)] * 4,
        scratch_shapes=[pltpu.VMEM((4, q, rows), jnp.float32)],
        compiler_params=params(8),
        cost_estimate=cost(0, rows * cols * 16),
        name="quarters",
    )(right, left)


def stack_kernel(m0, m1, m2, m3, out):
    for k, m in enumerate((m0, m1, m2, m3)):
        out[k] = m[0 : out.shape[1], :]


def stack_right(messages):
    q, rows = messages[0].shape[0] // 2, messages[0].shape[1]
    return pl.pallas_call(
        stack_kernel,
        out_shape=f32(4, q, rows),
        compiler_params=params(8),
        cost_estimate=cost(0, 32 * q * rows),
        name="stack_right",
    )(*messages)


def build_kernel(e0, e1, e2, e3, hi_ref, lo_ref):
    d, _, _ = coords()
    n = e0.shape[0] // 2
    iota = lax.broadcasted_iota(jnp.int32, (256, 256), 0).astype(jnp.float32).astype(jnp.bfloat16)
    lane_doc = lax.broadcasted_iota(jnp.int32, (8, 256), 1) >> 4
    one = jnp.ones((256, 256), jnp.bfloat16)
    zero = jnp.zeros((256, 256), jnp.bfloat16)

    def spread(row):
        wide = jnp.broadcast_to(row, (16, 256)).astype(jnp.bfloat16)
        return jnp.broadcast_to(wide[None], (16, 16, 256)).reshape(256, 256)

    for k, entries in enumerate((e0, e1, e2, e3)):

        @pl.loop(0, n // 8)
        def _(step, k=k, entries=entries):
            at = pl.multiple_of(step * 8, 8)
            ids = entries[pl.ds(at, 8), :].astype(jnp.int32)
            vals = entries[pl.ds(n + at, 8), :]
            rel = (ids >> 8) ^ d
            block = ((rel & 1) << 3) | ((rel & 2) << 1) | (rel >> 2)
            code = (block * 16 + lane_doc).astype(jnp.float32)
            inner = (ids & 255).astype(jnp.float32)
            for t in range(8):
                pick = jnp.where(iota == spread(code[t : t + 1]), one, zero)
                weigh = jnp.where(iota == spread(inner[t : t + 1]), spread(vals[t : t + 1]), zero)
                dense = lax.dot_general(pick, weigh, NT, preferred_element_type=jnp.float32)
                high = dense.astype(jnp.bfloat16)
                low = (dense - high.astype(jnp.float32)).astype(jnp.bfloat16)
                half = 8 * n
                to = (step * 128 // half) * 4 * half + k * half + step * 128 % half + 16 * t
                docs = pl.ds(pl.multiple_of(to, 16), 16)
                hi_ref[:, docs, :] = high.reshape(16, 16, 256)
                lo_ref[:, docs, :] = low.reshape(16, 16, 256)


def whole():
    return pl.BlockSpec(memory_space=pltpu.VMEM)


def build(entries):
    docs = 4 * (entries[0].shape[0] // 2 * 16)
    return pl.pallas_call(
        build_kernel,
        in_specs=[whole()] * 4,
        out_specs=[whole()] * 2,
        out_shape=[pltpu.VMEM((16, docs, 256), jnp.bfloat16)] * 2,
        compiler_params=params(12),
        cost_estimate=cost(2 * docs * 16 * 256 * 256, docs * 4096 * 4),
        name="dense_rows",
    )(*entries)


def split_rows(value):
    high = value.astype(jnp.bfloat16)
    low = (value - high.astype(jnp.float32)).astype(jnp.bfloat16)
    return jnp.concatenate([high, low], axis=0)


def block_product(hi_ref, lo_ref, docs, first, vecs):
    lhs, rhs = [], []
    for k in range(2):
        both = split_rows(vecs[k])
        lhs += [hi_ref[first + k, docs, :], lo_ref[first + k, docs, :]]
        rhs += [both, both]
    return lax.dot_general(
        jnp.concatenate(lhs, axis=1), jnp.concatenate(rhs, axis=1), NT, preferred_element_type=jnp.float32
    )


def add_products(hi_ref, lo_ref, docs, vecs, blocks, total):
    for vec, first in zip(vecs, blocks):
        for pair in (0, 2):
            total[...] += block_product(hi_ref, lo_ref, docs, first + pair, vec[pair : pair + 2])


def forward_kernel(blocks, hi_ref, lo_ref, v0, v1, total):
    total[...] = jnp.zeros_like(total)
    for half in range(2):
        n = total.shape[0] // 2
        docs = slice(half * n, (half + 1) * n)
        add_products(hi_ref, lo_ref, docs, (v0, v1), blocks, total.at[docs])


def forward_part(hi, lo, vecs, blocks):
    docs = hi.shape[1]
    q = vecs[0].shape[1]
    n = 4 * len(blocks)
    return pl.pallas_call(
        functools.partial(forward_kernel, blocks),
        in_specs=[whole()] * 4,
        out_specs=whole(),
        out_shape=f32(docs, 2 * q),
        compiler_params=params(12),
        cost_estimate=cost(8 * docs * 256 * 256 * n, 4 * docs * 256 * n),
        name="forward_part",
    )(hi, lo, *vecs)


def forward_half_kernel(half, blocks, hi_ref, lo_ref, v0, v1, before, m0, m1, m2, m3, alpha, out, total, columns):
    _, z, y = coords()
    n = total.shape[0]
    docs = slice(half * n, (half + 1) * n)
    total[...] = before[docs, :]
    add_products(hi_ref, lo_ref, docs, (v0, v1), blocks, total)
    turned = total[...].T
    q = out.shape[0]
    out[...] = turned[:q] + turned[q:]

    @pl.when(y == half)
    def _():
        columns[...] = row_to_column(alpha[...])
        scale = columns[pl.ds(pl.multiple_of(z * q, q), q), :][:, 0:1]
        for k, m in enumerate((m0, m1, m2, m3)):
            at = slice(k * m.shape[1], (k + 1) * m.shape[1])
            out[:, at] = out[:, at] - scale * m[q:, :]


def forward_half(hi, lo, vecs, before, messages, alpha, blocks, half):
    docs = hi.shape[1] // 2
    q = vecs[0].shape[1]
    n = 4 * len(blocks)
    return pl.pallas_call(
        functools.partial(forward_half_kernel, half, blocks),
        in_specs=[whole()] * 10,
        out_specs=whole(),
        out_shape=f32(q, docs),
        scratch_shapes=[pltpu.VMEM((docs, 2 * q), jnp.float32), pltpu.VMEM((4 * q, 128), jnp.float32)],
        compiler_params=params(12),
        cost_estimate=cost(8 * docs * 256 * 256 * n, 4 * docs * 256 * n),
        name="forward_half",
    )(hi, lo, *vecs, before, *messages, alpha)


def square_row(value, z, cols):
    q, n = value.shape
    sums = value[:, 0:128] * value[:, 0:128]
    for at in range(128, n, 128):
        sums = sums + value[:, at : at + 128] * value[:, at : at + 128]
    row = jnp.sum(jnp.concatenate([sums] * (128 // q), axis=0).T, axis=0, keepdims=True)
    row = jnp.broadcast_to(jnp.concatenate([row] * (cols // 128), axis=1), (8, cols))
    lane = lax.broadcasted_iota(jnp.int32, (8, cols), 1)
    return jnp.where(lane // q == z, row, 0.0)


def row_to_column(row):
    return jnp.broadcast_to(row, (128, row.shape[1])).T


def left_half_kernel(mine, other, raw, both, sums):
    _, z, _ = coords()
    left = mine[...] + other[...]
    raw[...] = left
    both[...] = split_rows(left)
    sums[...] = square_row(left, z, sums.shape[1])


def left_half(mine, other):
    q, docs = mine.shape
    return pl.pallas_call(
        left_half_kernel,
        out_shape=[f32(q, docs), bf16(2 * q, docs), f32(8, 4 * q)],
        compiler_params=params(8),
        cost_estimate=cost(8 * q * docs, 16 * q * docs),
        name="left_half",
    )(mine, other)


def left_rest_kernel(mine, other, raw, squares, both, sums, l0, l1, l2, l3):
    _, z, _ = coords()
    left = mine[...] + other[...]
    both[...] = split_rows(left)
    sums[...] = squares[...] + square_row(left, z, sums.shape[1])
    n = left.shape[1] // 4
    for k, out in enumerate((l0, l1, l2, l3)):
        out[:, :n] = raw[:, k * n : (k + 1) * n]
        out[:, n:] = left[:, k * n : (k + 1) * n]


def left_rest(mine, other, raw, squares):
    q, docs = mine.shape
    both, sums, *lefts = pl.pallas_call(
        left_rest_kernel,
        out_shape=[bf16(2 * q, docs), f32(8, 4 * q)] + [f32(q, docs // 2)] * 4,
        compiler_params=params(8),
        cost_estimate=cost(8 * q * docs, 24 * q * docs),
        name="left_rest",
    )(mine, other, raw, squares)
    return both, sums, lefts


def backward_kernel(half, first, blocks, parts, hi_ref, lo_ref, both_ref, *refs):
    out_ref = refs[-1]
    both = both_ref[...]
    q, n = both.shape[0] // 2, both.shape[1]
    docs = slice(half * n, (half + 1) * n)
    twice = jnp.concatenate([both, both], axis=1)
    for b in range(blocks):
        got = jnp.dot(
            twice,
            jnp.concatenate([hi_ref[first + b, docs, :], lo_ref[first + b, docs, :]], axis=0),
            preferred_element_type=jnp.float32,
        )
        got = got[:q] + got[q:]
        if "before" in parts:
            got = got + refs[0][(first + b) * q : (first + b + 1) * q, :]
        out_ref[b * q : (b + 1) * q, :] = got
    if "tail" in parts:
        out_ref[blocks * q :, :] = refs[-2][...]


def backward_part(hi, lo, both, half, first, blocks, before=None, tail=None):
    q, docs = both.shape[0] // 2, both.shape[1]
    extra = {"before": before, "tail": tail}
    extra = {name: value for name, value in extra.items() if value is not None}
    rows = blocks * q + (0 if tail is None else tail.shape[0])
    return pl.pallas_call(
        functools.partial(backward_kernel, half, first, blocks, tuple(extra)),
        in_specs=[whole()] * (3 + len(extra)),
        out_specs=whole(),
        out_shape=f32(rows, 256),
        compiler_params=params(12),
        cost_estimate=cost(8 * docs * 256 * 256 * blocks, 4 * docs * 256 * blocks),
        name="backward_part",
    )(hi, lo, both, *extra.values())


def far_sum_kernel(near, far, beta, send, beta_core):
    n = near.shape[0]
    beta_core[...] = beta[...] + far[n:, :]
    send[0:n, :] = near[...] + far[0:n, :]
    send[n:, :] = beta_core[...]


def far_sums(near, far, beta):
    rows = near.shape[0]
    return pl.pallas_call(
        far_sum_kernel,
        out_shape=[f32(rows + 8, 256), f32(8, 256)],
        compiler_params=params(8),
        cost_estimate=cost(near.size, near.size * 12),
        name="far_sums",
    )(near, far, beta)


def right_norm_kernel(docs_total, keep, peer, got, beta_core, v0, v1, v2, v3, g0, g1, g2, g3, columns):
    _, z, _ = coords()
    q = g0.shape[0] - 16
    beta_sums = beta_core[...] + got[4 * q :, :]
    columns[...] = row_to_column(jnp.sqrt(beta_sums[0:1, :] / docs_total + epsilon))
    beta = columns[pl.ds(pl.multiple_of(z * q, q), q), :][:, 0:1]
    raws = []
    for k, (v, g) in enumerate(zip((v0, v1, v2, v3), (g0, g1, g2, g3))):
        rows = slice(k * q, (k + 1) * q)
        total = (keep[rows, :] + peer[rows, :]) + got[rows, :]
        g[0:q, :] = total
        g[q : q + 8, :] = beta_sums
        raws.append(total / beta - beta * v[0:q, :])
    squares = square_row(jnp.concatenate(raws, axis=1), z, 4 * q)
    for g in (g0, g1, g2, g3):
        g[q + 8 :, :] = squares


def right_norm(docs_total, keep, peer, got, beta_core, messages):
    q, rows = keep.shape[0] // 4, keep.shape[1]
    return pl.pallas_call(
        functools.partial(right_norm_kernel, docs_total),
        out_shape=[f32(q + 16, rows)] * 4,
        scratch_shapes=[pltpu.VMEM((4 * q, 128), jnp.float32)],
        compiler_params=params(8),
        cost_estimate=cost(rows * q * 64, rows * q * 100),
        name="right_norm",
    )(keep, peer, got, beta_core, *messages)


def beta_of(pieces, q, docs_total):
    squares = [g[q : q + 1, :] for g in pieces]
    return jnp.sqrt(((squares[0] + squares[1]) + (squares[2] + squares[3])) / docs_total + epsilon)


def alpha_rows_kernel(g0, g1, g2, g3, out):
    rows = [g[g.shape[0] - 8 :, :] for g in (g0, g1, g2, g3)]
    total = (rows[0] + rows[1]) + (rows[2] + rows[3])
    for i in range(8):
        out[8 * i : 8 * i + 8, :] = total


def alpha_rows(pieces):
    return pl.pallas_call(
        alpha_rows_kernel,
        out_shape=f32(64, pieces[0].shape[1]),
        compiler_params=params(8),
        cost_estimate=cost(0, 100000),
        name="alpha_rows",
    )(*pieces)


def finish_kernel(docs_total, feat_total, g0, g1, g2, g3, squares, right, search, phibar, rhobar,
                  right_out, search_out, alpha_out, phibar_out, rhobar_out, turned):
    _, z, _ = coords()
    q = turned.shape[1]
    for k, g in enumerate((g0, g1, g2, g3)):
        turned[z ^ k] = g[0:q, :]
    got = turned[...].reshape(-1, turned.shape[2]).T
    parts = [squares[8 * i : 8 * i + 1, :] for i in range(8)]
    while len(parts) > 1:
        parts = [a + b for a, b in zip(parts[::2], parts[1::2])]
    alpha = jnp.sqrt(parts[0] / feat_total + epsilon)
    beta = beta_of((g0, g1, g2, g3), q, docs_total)
    rho = jnp.sqrt(rhobar[...] * rhobar[...] + beta * beta)
    cosine = rhobar[...] / rho
    sine = beta / rho
    theta = sine * alpha
    rhobar_out[...] = -cosine * alpha
    phibar_out[...] = sine * phibar[...]
    alpha_out[...] = alpha
    following = (got / beta - beta * right[...]) / alpha
    right_out[...] = following
    search_out[...] = following - (theta / rho) * search[...]


def finish(docs_total, feat_total, pieces, squares, right, search, phibar, rhobar):
    rows, cols = right.shape
    return pl.pallas_call(
        functools.partial(finish_kernel, docs_total, feat_total),
        out_shape=[f32(rows, cols)] * 2 + [f32(1, cols)] * 3,
        scratch_shapes=[pltpu.VMEM((4, cols // 4, rows), jnp.float32)],
        compiler_params=params(8),
        cost_estimate=cost(rows * cols * 16, rows * cols * 20),
        name="finish",
    )(*pieces, squares, right, search, phibar, rhobar)


def left_out_kernel(docs_total, l0, l1, l2, l3, g0, g1, g2, g3, search, solution, phibar, rhobar, left_out, solution_out, turned):
    _, z, _ = coords()
    q, docs = turned.shape[1:]
    beta = beta_of((g0, g1, g2, g3), q, docs_total)
    for k, piece in enumerate((l0, l1, l2, l3)):
        turned[z ^ k] = piece[...]
    left_out[...] = turned[...].reshape(-1, docs).T / beta
    rho = jnp.sqrt(rhobar[...] * rhobar[...] + beta * beta)
    phi = rhobar[...] / rho * phibar[...]
    solution_out[...] = solution[...] + (phi / rho) * search[...]


def left_out(docs_total, lefts, pieces, search, solution, phibar, rhobar):
    q, docs = lefts[0].shape
    return pl.pallas_call(
        functools.partial(left_out_kernel, docs_total),
        out_shape=[f32(docs, 4 * q), f32(*solution.shape)],
        scratch_shapes=[pltpu.VMEM((4, q, docs), jnp.float32)],
        compiler_params=params(8),
        cost_estimate=cost(docs * q * 16, docs * q * 60),
        name="left_out",
    )(*lefts, *pieces, search, solution, phibar, rhobar)


def swap(value, mask):
    return lax.ppermute(value, AXES, [(i, i ^ mask) for i in range(32)])


def along_z(values):
    return [values[0]] + [swap(values[k], k << Z_SHIFT) for k in (1, 2, 3)]


def after(value, *earlier):
    return lax.optimization_barrier((value, *earlier))[0]


def by_columns(
    col_ids, col_vals, left_vec, right_vec, search_dir, solution_vec, alpha_prev, phibar, rhobar
):
    docs_total = left_vec.shape[0] * 16
    feat_total = right_vec.shape[0] * 32
    alpha_row, phibar_row, rhobar_row = (v.reshape(1, -1) for v in (alpha_prev, phibar, rhobar))

    ids, vals = col_ids.astype(jnp.float32), col_vals.astype(jnp.float32)
    stored = jnp.concatenate([ids.reshape(-1, 256), vals.reshape(-1, 256)], axis=0)
    entries = along_z([stored] * 4)
    messages = along_z(quarters_of(after(right_vec, stored), left_vec))
    own = stack_right(messages)
    own_x = swap(own, X_BIT)
    own_peer = swap(own, CORE_BIT)

    hi, lo = build(entries)
    total = forward_part(hi, lo, [own, own_peer], (0, 8))
    vecs = [own_x, swap(own_x, CORE_BIT)]
    product = [forward_half(hi, lo, vecs, total, messages, alpha_row, (4, 12), half) for half in range(2)]
    other = [swap(p, Y_BIT) for p in product]

    raw, both0, beta0 = left_half(product[0], other[0])
    partial = backward_part(hi, lo, both0, 0, 0, 16)
    both1, beta1, lefts = left_rest(product[1], other[1], raw, beta0)
    far = swap(backward_part(hi, lo, both1, 1, 12, 4, partial, beta1), CORE_BIT)
    near = backward_part(hi, lo, both1, 1, 4, 4, partial)
    send, beta_core = far_sums(near, far, beta1)
    got = swap(send, X_BIT)
    peer = swap(backward_part(hi, lo, both1, 1, 8, 4, partial), CORE_BIT)
    keep = backward_part(hi, lo, both1, 1, 0, 4, partial)
    left_pieces = along_z([after(l, send) for l in lefts])

    pieces = along_z(right_norm(docs_total, keep, peer, got, beta_core, messages))
    squares = lax.all_to_all(alpha_rows(pieces), AXES, 0, 0, axis_index_groups=PLANES, tiled=True)
    left_next, solution_next = left_out(
        docs_total, left_pieces, pieces, search_dir, solution_vec, phibar_row, rhobar_row
    )
    right_next, search_next, alpha_next, phibar_next, rhobar_next = finish(
        docs_total, feat_total, pieces, squares, right_vec, search_dir, phibar_row, rhobar_row
    )
    return (
        left_next,
        right_next,
        search_next,
        solution_next,
        alpha_next.reshape(-1),
        phibar_next.reshape(-1),
        rhobar_next.reshape(-1),
    )


def forward(col_ids, col_vals, table):
    picked = table[col_ids]
    return jnp.sum(col_vals.astype(jnp.float32)[:, :, None] * picked, axis=1)


def backward(col_ids, col_vals, rows_in, width):
    terms = col_vals.astype(jnp.float32)[:, :, None] * rows_in[:, None, :]
    return jax.ops.segment_sum(
        terms.reshape(-1, rows_in.shape[1]), col_ids.reshape(-1), num_segments=width
    )


def by_blocks(
    col_ids, col_vals, left_vec, right_vec, search_dir, solution_vec, alpha_prev, phibar, rhobar
):
    n_feat = lax.axis_size("feat")
    n_doc = lax.axis_size("doc")
    docs_total = left_vec.shape[0] * n_doc
    feat_total = right_vec.shape[0] * n_doc * n_feat
    table = lax.all_gather(right_vec, "doc", axis=0, tiled=True)
    total = lax.psum(forward(col_ids, col_vals, table), "feat")
    left_raw = total - alpha_prev[None, :] * left_vec
    row_part = jnp.sum(left_raw * left_raw, axis=0)
    beta_norm = jnp.sqrt(lax.psum(row_part, "doc") / docs_total + epsilon)
    left_next = left_raw / beta_norm[None, :]
    feature_part = lax.psum_scatter(
        backward(col_ids, col_vals, left_next, table.shape[0]), "doc", scatter_dimension=0, tiled=True
    )
    right_raw = feature_part - beta_norm[None, :] * right_vec
    squares = lax.psum(jnp.sum(right_raw * right_raw, axis=0), AXES)
    alpha_next = jnp.sqrt(squares / feat_total + epsilon)
    right_next = right_raw / alpha_next[None, :]
    rho_val = jnp.sqrt(rhobar * rhobar + beta_norm * beta_norm)
    cosine = rhobar / rho_val
    sine_val = beta_norm / rho_val
    theta_val = sine_val * alpha_next
    phi_val = cosine * phibar
    solution_next = solution_vec + (phi_val / rho_val)[None, :] * search_dir
    search_next = right_next - (theta_val / rho_val)[None, :] * search_dir
    return (
        left_next,
        right_next,
        search_next,
        solution_next,
        alpha_next,
        sine_val * phibar,
        -cosine * alpha_next,
    )


def solution(mesh):
    small = mesh.shape["doc"] == 16 and mesh.shape["feat"] == 2
    rows = P(("feat", "doc"), None)
    return jax.shard_map(
        by_columns if small else by_blocks,
        mesh=mesh,
        in_specs=(P("doc", "feat"), P("doc", "feat"), P("doc", None), rows, rows, rows, P(), P(), P()),
        out_specs=(P("doc", None), rows, rows, rows, P(), P(), P()),
        check_vma=False,
    )
```

```python
import functools

import jax
import jax.numpy as jnp
from jax import lax
from jax.experimental import pallas as pl
from jax.experimental.pallas import tpu as pltpu
from jax.sharding import PartitionSpec as P

epsilon = 1e-06
AXES = ("doc", "feat")
MIB = 1024 * 1024


Y_BIT, CORE_BIT, X_BIT, Z_SHIFT = 1, 2, 4, 3
PLANES = [list(range(first, first + 8)) for first in range(0, 32, 8)]
NT = (((1,), (1,)), ((), ()))


def coords():
    d = lax.axis_index("doc")
    y = lax.axis_index("feat")
    return d, d >> 2, y


def params(mib):
    return pltpu.CompilerParams(vmem_limit_bytes=mib * MIB)


def cost(flops, nbytes):
    return pl.CostEstimate(flops=int(flops), bytes_accessed=int(nbytes), transcendentals=0)


def f32(*shape):
    return jax.ShapeDtypeStruct(shape, jnp.float32)


def bf16(*shape):
    return jax.ShapeDtypeStruct(shape, jnp.bfloat16)


def quarters_kernel(right_ref, left_ref, token, m0, m1, m2, m3, turned):
    _, z, y = coords()
    q, rows = turned.shape[1:]
    for part in range(2):
        value = left_ref[pl.ds(pl.multiple_of(y * rows, rows), rows), :] if part else right_ref[...]
        turned[...] = value.T.reshape(turned.shape)
        for k, out in enumerate((m0, m1, m2, m3)):
            out[part * q : (part + 1) * q, :] = turned[z ^ k]


def quarters_of(right, left, token):
    rows, cols = right.shape
    q = cols // 4
    return pl.pallas_call(
        quarters_kernel,
        out_shape=[f32(2 * q, rows)] * 4,
        scratch_shapes=[pltpu.VMEM((4, q, rows), jnp.float32)],
        compiler_params=params(8),
        cost_estimate=cost(0, rows * cols * 16),
        name="quarters",
    )(right, left, token)


def stack_kernel(m0, m1, m2, m3, *refs):
    out = refs[-1]
    for k, m in enumerate((m0, m1, m2, m3)):
        out[k] = m[0 : out.shape[1], :]


def stack(messages, q, name, *tokens):
    rows = messages[0].shape[1]
    return pl.pallas_call(
        stack_kernel,
        out_shape=f32(4, q, rows),
        compiler_params=params(8),
        cost_estimate=cost(0, 32 * q * rows),
        name=name,
    )(*messages, *tokens)


def build_kernel(e0, e1, e2, e3, hi_ref, lo_ref, token):
    token[...] = jnp.zeros_like(token)
    d, _, _ = coords()
    n = e0.shape[0] // 2
    iota = lax.broadcasted_iota(jnp.int32, (256, 256), 0).astype(jnp.float32).astype(jnp.bfloat16)
    lane_doc = lax.broadcasted_iota(jnp.int32, (8, 256), 1) >> 4
    one = jnp.ones((256, 256), jnp.bfloat16)
    zero = jnp.zeros((256, 256), jnp.bfloat16)

    def spread(row):
        wide = jnp.broadcast_to(row, (16, 256)).astype(jnp.bfloat16)
        return jnp.broadcast_to(wide[None], (16, 16, 256)).reshape(256, 256)

    for k, entries in enumerate((e0, e1, e2, e3)):

        @pl.loop(0, n // 8)
        def _(step, k=k, entries=entries):
            at = pl.multiple_of(step * 8, 8)
            ids = entries[pl.ds(at, 8), :].astype(jnp.int32)
            vals = entries[pl.ds(n + at, 8), :]
            rel = (ids >> 8) ^ d
            block = ((rel & 1) << 3) | ((rel & 2) << 1) | (rel >> 2)
            code = (block * 16 + lane_doc).astype(jnp.float32)
            inner = (ids & 255).astype(jnp.float32)
            for t in range(8):
                pick = jnp.where(iota == spread(code[t : t + 1]), one, zero)
                weigh = jnp.where(iota == spread(inner[t : t + 1]), spread(vals[t : t + 1]), zero)
                dense = lax.dot_general(pick, weigh, NT, preferred_element_type=jnp.float32)
                high = dense.astype(jnp.bfloat16)
                low = (dense - high.astype(jnp.float32)).astype(jnp.bfloat16)
                half = 8 * n
                to = (step * 128 // half) * 4 * half + k * half + step * 128 % half + 16 * t
                docs = pl.ds(pl.multiple_of(to, 16), 16)
                hi_ref[:, docs, :] = high.reshape(16, 16, 256)
                lo_ref[:, docs, :] = low.reshape(16, 16, 256)


def whole():
    return pl.BlockSpec(memory_space=pltpu.VMEM)


def build(entries):
    docs = 4 * (entries[0].shape[0] // 2 * 16)
    return pl.pallas_call(
        build_kernel,
        in_specs=[whole()] * 4,
        out_specs=[whole()] * 3,
        out_shape=[pltpu.VMEM((16, docs, 256), jnp.bfloat16)] * 2 + [f32(8, 128)],
        compiler_params=params(12),
        cost_estimate=cost(2 * docs * 16 * 256 * 256, docs * 4096 * 4),
        name="dense_rows",
    )(*entries)


def split_rows(value):
    high = value.astype(jnp.bfloat16)
    low = (value - high.astype(jnp.float32)).astype(jnp.bfloat16)
    return jnp.concatenate([high, low], axis=0)


def block_product(hi_ref, lo_ref, docs, first, vecs):
    lhs, rhs = [], []
    for k in range(2):
        both = split_rows(vecs[k])
        lhs += [hi_ref[first + k, docs, :], lo_ref[first + k, docs, :]]
        rhs += [both, both]
    return lax.dot_general(
        jnp.concatenate(lhs, axis=1), jnp.concatenate(rhs, axis=1), NT, preferred_element_type=jnp.float32
    )


def add_products(hi_ref, lo_ref, docs, vecs, blocks, total):
    for vec, first in zip(vecs, blocks):
        for pair in (0, 2):
            total[...] += block_product(hi_ref, lo_ref, docs, first + pair, vec[pair : pair + 2])


def forward_kernel(blocks, hi_ref, lo_ref, v0, v1, total):
    total[...] = jnp.zeros_like(total)
    for half in range(2):
        n = total.shape[0] // 2
        docs = slice(half * n, (half + 1) * n)
        add_products(hi_ref, lo_ref, docs, (v0, v1), blocks, total.at[docs])


def forward_part(hi, lo, vecs, blocks):
    docs = hi.shape[1]
    q = vecs[0].shape[1]
    n = 4 * len(blocks)
    return pl.pallas_call(
        functools.partial(forward_kernel, blocks),
        in_specs=[whole()] * 4,
        out_specs=whole(),
        out_shape=f32(docs, 2 * q),
        compiler_params=params(12),
        cost_estimate=cost(8 * docs * 256 * 256 * n, 4 * docs * 256 * n),
        name="forward_part",
    )(hi, lo, *vecs)


def forward_half_kernel(half, blocks, hi_ref, lo_ref, v0, v1, before, m0, m1, m2, m3, alpha, out, total, columns):
    _, z, y = coords()
    n = total.shape[0]
    docs = slice(half * n, (half + 1) * n)
    total[...] = before[docs, :]
    add_products(hi_ref, lo_ref, docs, (v0, v1), blocks, total)
    turned = total[...].T
    q = out.shape[0]
    out[...] = turned[:q] + turned[q:]

    @pl.when(y == half)
    def _():
        columns[...] = row_to_column(alpha[...])
        scale = columns[pl.ds(pl.multiple_of(z * q, q), q), :][:, 0:1]
        for k, m in enumerate((m0, m1, m2, m3)):
            at = slice(k * m.shape[1], (k + 1) * m.shape[1])
            out[:, at] = out[:, at] - scale * m[q:, :]


def forward_half(hi, lo, vecs, before, messages, alpha, blocks, half):
    docs = hi.shape[1] // 2
    q = vecs[0].shape[1]
    n = 4 * len(blocks)
    return pl.pallas_call(
        functools.partial(forward_half_kernel, half, blocks),
        in_specs=[whole()] * 10,
        out_specs=whole(),
        out_shape=f32(q, docs),
        scratch_shapes=[pltpu.VMEM((docs, 2 * q), jnp.float32), pltpu.VMEM((4 * q, 128), jnp.float32)],
        compiler_params=params(12),
        cost_estimate=cost(8 * docs * 256 * 256 * n, 4 * docs * 256 * n),
        name="forward_half",
    )(hi, lo, *vecs, before, *messages, alpha)


def square_row(value, z, cols):
    q, n = value.shape
    sums = value[:, 0:128] * value[:, 0:128]
    for at in range(128, n, 128):
        sums = sums + value[:, at : at + 128] * value[:, at : at + 128]
    row = jnp.sum(jnp.concatenate([sums] * (128 // q), axis=0).T, axis=0, keepdims=True)
    row = jnp.broadcast_to(jnp.concatenate([row] * (cols // 128), axis=1), (8, cols))
    lane = lax.broadcasted_iota(jnp.int32, (8, cols), 1)
    return jnp.where(lane // q == z, row, 0.0)


def row_to_column(row):
    return jnp.broadcast_to(row, (128, row.shape[1])).T


def left_half_kernel(mine, other, raw, both, sums):
    _, z, _ = coords()
    left = mine[...] + other[...]
    raw[...] = left
    both[...] = split_rows(left)
    sums[...] = square_row(left, z, sums.shape[1])


def left_half(mine, other):
    q, docs = mine.shape
    return pl.pallas_call(
        left_half_kernel,
        out_shape=[f32(q, docs), bf16(2 * q, docs), f32(8, 4 * q)],
        compiler_params=params(8),
        cost_estimate=cost(8 * q * docs, 16 * q * docs),
        name="left_half",
    )(mine, other)


def left_rest_kernel(mine, other, raw, squares, both, sums, l0, l1, l2, l3):
    _, z, y = coords()
    left = mine[...] + other[...]
    both[...] = split_rows(left)
    sums[...] = squares[...] + square_row(left, z, sums.shape[1])
    n = left.shape[1] // 4
    for k, out in enumerate((l0, l1, l2, l3)):
        at = slice(k * n, (k + 1) * n)
        out[...] = jnp.where(y == 0, raw[:, at], left[:, at])


def left_rest(mine, other, raw, squares):
    q, docs = mine.shape
    both, sums, *lefts = pl.pallas_call(
        left_rest_kernel,
        out_shape=[bf16(2 * q, docs), f32(8, 4 * q)] + [f32(q, docs // 4)] * 4,
        compiler_params=params(8),
        cost_estimate=cost(8 * q * docs, 24 * q * docs),
        name="left_rest",
    )(mine, other, raw, squares)
    return both, sums, lefts


def backward_kernel(half, first, blocks, parts, hi_ref, lo_ref, both_ref, *refs):
    out_ref = refs[-1]
    both = both_ref[...]
    q, n = both.shape[0] // 2, both.shape[1]
    docs = slice(half * n, (half + 1) * n)
    twice = jnp.concatenate([both, both], axis=1)
    for b in range(blocks):
        got = jnp.dot(
            twice,
            jnp.concatenate([hi_ref[first + b, docs, :], lo_ref[first + b, docs, :]], axis=0),
            preferred_element_type=jnp.float32,
        )
        got = got[:q] + got[q:]
        if "before" in parts:
            got = got + refs[0][(first + b) * q : (first + b + 1) * q, :]
        out_ref[b * q : (b + 1) * q, :] = got
    if "tail" in parts:
        out_ref[blocks * q :, :] = refs[-2][...]


def backward_part(hi, lo, both, half, first, blocks, before=None, tail=None):
    q, docs = both.shape[0] // 2, both.shape[1]
    extra = {"before": before, "tail": tail}
    extra = {name: value for name, value in extra.items() if value is not None}
    rows = blocks * q + (0 if tail is None else tail.shape[0])
    return pl.pallas_call(
        functools.partial(backward_kernel, half, first, blocks, tuple(extra)),
        in_specs=[whole()] * (3 + len(extra)),
        out_specs=whole(),
        out_shape=f32(rows, 256),
        compiler_params=params(12),
        cost_estimate=cost(8 * docs * 256 * 256 * blocks, 4 * docs * 256 * blocks),
        name="backward_part",
    )(hi, lo, both, *extra.values())


def far_sum_kernel(near, far, beta, send, beta_core):
    n = near.shape[0]
    beta_core[...] = beta[...] + far[n:, :]
    send[0:n, :] = near[...] + far[0:n, :]
    send[n:, :] = beta_core[...]


def far_sums(near, far, beta):
    rows = near.shape[0]
    return pl.pallas_call(
        far_sum_kernel,
        out_shape=[f32(rows + 8, 256), f32(8, 256)],
        compiler_params=params(8),
        cost_estimate=cost(near.size, near.size * 12),
        name="far_sums",
    )(near, far, beta)


def right_norm_kernel(docs_total, keep, peer, got, beta_core, v0, v1, v2, v3, token, g0, g1, g2, g3, columns):
    _, z, _ = coords()
    q = g0.shape[0] - 16
    beta_sums = beta_core[...] + got[4 * q :, :]
    columns[...] = row_to_column(jnp.sqrt(beta_sums[0:1, :] / docs_total + epsilon))
    beta = columns[pl.ds(pl.multiple_of(z * q, q), q), :][:, 0:1]
    raws = []
    for k, (v, g) in enumerate(zip((v0, v1, v2, v3), (g0, g1, g2, g3))):
        rows = slice(k * q, (k + 1) * q)
        total = (keep[rows, :] + peer[rows, :]) + got[rows, :]
        g[0:q, :] = total
        g[q : q + 8, :] = beta_sums
        raws.append(total / beta - beta * v[0:q, :])
    squares = square_row(jnp.concatenate(raws, axis=1), z, 4 * q)
    for g in (g0, g1, g2, g3):
        g[q + 8 :, :] = squares


def right_norm(docs_total, keep, peer, got, beta_core, messages, token):
    q, rows = keep.shape[0] // 4, keep.shape[1]
    return pl.pallas_call(
        functools.partial(right_norm_kernel, docs_total),
        out_shape=[f32(q + 16, rows)] * 4,
        scratch_shapes=[pltpu.VMEM((4 * q, 128), jnp.float32)],
        compiler_params=params(8),
        cost_estimate=cost(rows * q * 64, rows * q * 100),
        name="right_norm",
    )(keep, peer, got, beta_core, *messages, token)


def beta_of(pieces, q, docs_total):
    squares = [g[q : q + 1, :] for g in pieces]
    return jnp.sqrt(((squares[0] + squares[1]) + (squares[2] + squares[3])) / docs_total + epsilon)


def alpha_rows_kernel(g0, g1, g2, g3, out):
    rows = [g[g.shape[0] - 8 :, :] for g in (g0, g1, g2, g3)]
    total = (rows[0] + rows[1]) + (rows[2] + rows[3])
    for i in range(8):
        out[8 * i : 8 * i + 8, :] = total


def alpha_rows(pieces):
    return pl.pallas_call(
        alpha_rows_kernel,
        out_shape=f32(64, pieces[0].shape[1]),
        compiler_params=params(8),
        cost_estimate=cost(0, 100000),
        name="alpha_rows",
    )(*pieces)


def finish_kernel(docs_total, feat_total, g0, g1, g2, g3, squares, right, search, phibar, rhobar,
                  right_out, search_out, alpha_out, phibar_out, rhobar_out, turned):
    _, z, _ = coords()
    q = turned.shape[1]
    for k, g in enumerate((g0, g1, g2, g3)):
        turned[z ^ k] = g[0:q, :]
    got = turned[...].reshape(-1, turned.shape[2]).T
    parts = [squares[8 * i : 8 * i + 1, :] for i in range(8)]
    while len(parts) > 1:
        parts = [a + b for a, b in zip(parts[::2], parts[1::2])]
    alpha = jnp.sqrt(parts[0] / feat_total + epsilon)
    beta = beta_of((g0, g1, g2, g3), q, docs_total)
    rho = jnp.sqrt(rhobar[...] * rhobar[...] + beta * beta)
    cosine = rhobar[...] / rho
    sine = beta / rho
    theta = sine * alpha
    rhobar_out[...] = -cosine * alpha
    phibar_out[...] = sine * phibar[...]
    alpha_out[...] = alpha
    following = (got / beta - beta * right[...]) / alpha
    right_out[...] = following
    search_out[...] = following - (theta / rho) * search[...]


def finish(docs_total, feat_total, pieces, squares, right, search, phibar, rhobar):
    rows, cols = right.shape
    return pl.pallas_call(
        functools.partial(finish_kernel, docs_total, feat_total),
        out_shape=[f32(rows, cols)] * 2 + [f32(1, cols)] * 3,
        scratch_shapes=[pltpu.VMEM((4, cols // 4, rows), jnp.float32)],
        compiler_params=params(8),
        cost_estimate=cost(rows * cols * 16, rows * cols * 20),
        name="finish",
    )(*pieces, squares, right, search, phibar, rhobar)


def left_out_kernel(docs_total, own, other, g0, g1, g2, g3, search, solution, phibar, rhobar, left_out, solution_out, turned):
    _, z, y = coords()
    q, half = turned.shape[1:]
    beta = beta_of((g0, g1, g2, g3), q, docs_total)
    for part, ref in ((y, own), (1 - y, other)):
        for k in range(4):
            turned[z ^ k] = ref[k]
        left_out[pl.ds(pl.multiple_of(part * half, half), half), :] = turned[...].reshape(-1, half).T / beta
    rho = jnp.sqrt(rhobar[...] * rhobar[...] + beta * beta)
    phi = rhobar[...] / rho * phibar[...]
    solution_out[...] = solution[...] + (phi / rho) * search[...]


def left_out(docs_total, own, other, pieces, search, solution, phibar, rhobar):
    _, q, half = own.shape
    return pl.pallas_call(
        functools.partial(left_out_kernel, docs_total),
        out_shape=[f32(2 * half, 4 * q), f32(*solution.shape)],
        scratch_shapes=[pltpu.VMEM((4, q, half), jnp.float32)],
        compiler_params=params(8),
        cost_estimate=cost(half * q * 32, half * q * 120),
        name="left_out",
    )(own, other, *pieces, search, solution, phibar, rhobar)


def swap(value, mask):
    return lax.ppermute(value, AXES, [(i, i ^ mask) for i in range(32)])


def along_z(values):
    return [values[0]] + [swap(values[k], k << Z_SHIFT) for k in (1, 2, 3)]


def after(value, *earlier):
    return lax.optimization_barrier((value, *earlier))[0]


def by_columns(
    col_ids, col_vals, left_vec, right_vec, search_dir, solution_vec, alpha_prev, phibar, rhobar
):
    docs_total = left_vec.shape[0] * 16
    feat_total = right_vec.shape[0] * 32
    alpha_row, phibar_row, rhobar_row = (v.reshape(1, -1) for v in (alpha_prev, phibar, rhobar))

    ids, vals = col_ids.astype(jnp.float32), col_vals.astype(jnp.float32)
    stored = jnp.concatenate([ids.reshape(-1, 256), vals.reshape(-1, 256)], axis=0)
    entries = along_z([stored] * 4)
    messages = along_z(quarters_of(right_vec, left_vec, entries[1]))
    q = messages[0].shape[0] // 2

    hi, lo, token = build(entries)
    own = stack(messages, q, "stack_right", token)
    own_x = swap(own, X_BIT)
    own_peer = swap(own, CORE_BIT)
    total = forward_part(hi, lo, [own, own_peer], (0, 8))
    vecs = [own_x, swap(own_x, CORE_BIT)]
    product = [forward_half(hi, lo, vecs, total, messages, alpha_row, (4, 12), half) for half in range(2)]
    other = [swap(p, Y_BIT) for p in product]

    raw, both0, beta0 = left_half(product[0], other[0])
    partial = backward_part(hi, lo, both0, 0, 0, 16)
    both1, beta1, lefts = left_rest(product[1], other[1], raw, beta0)
    far = swap(backward_part(hi, lo, both1, 1, 12, 4, partial, beta1), CORE_BIT)
    near = backward_part(hi, lo, both1, 1, 4, 4, partial)
    send, beta_core = far_sums(near, far, beta1)
    got = swap(send, X_BIT)
    peer = swap(backward_part(hi, lo, both1, 1, 8, 4, partial), CORE_BIT)
    keep = backward_part(hi, lo, both1, 1, 0, 4, partial)
    left_own = stack(along_z([after(l, keep) for l in lefts]), q, "stack_left")

    pieces = along_z(right_norm(docs_total, keep, peer, got, beta_core, messages, left_own))
    left_other = swap(after(left_own, pieces[0]), Y_BIT)
    squares = lax.all_to_all(alpha_rows(pieces), AXES, 0, 0, axis_index_groups=PLANES, tiled=True)
    left_next, solution_next = left_out(
        docs_total, left_own, left_other, pieces, search_dir, solution_vec, phibar_row, rhobar_row
    )
    right_next, search_next, alpha_next, phibar_next, rhobar_next = finish(
        docs_total, feat_total, pieces, squares, right_vec, search_dir, phibar_row, rhobar_row
    )
    return (
        left_next,
        right_next,
        search_next,
        solution_next,
        alpha_next.reshape(-1),
        phibar_next.reshape(-1),
        rhobar_next.reshape(-1),
    )


def forward(col_ids, col_vals, table):
    picked = table[col_ids]
    return jnp.sum(col_vals.astype(jnp.float32)[:, :, None] * picked, axis=1)


def backward(col_ids, col_vals, rows_in, width):
    terms = col_vals.astype(jnp.float32)[:, :, None] * rows_in[:, None, :]
    return jax.ops.segment_sum(
        terms.reshape(-1, rows_in.shape[1]), col_ids.reshape(-1), num_segments=width
    )


def by_blocks(
    col_ids, col_vals, left_vec, right_vec, search_dir, solution_vec, alpha_prev, phibar, rhobar
):
    n_feat = lax.axis_size("feat")
    n_doc = lax.axis_size("doc")
    docs_total = left_vec.shape[0] * n_doc
    feat_total = right_vec.shape[0] * n_doc * n_feat
    table = lax.all_gather(right_vec, "doc", axis=0, tiled=True)
    total = lax.psum(forward(col_ids, col_vals, table), "feat")
    left_raw = total - alpha_prev[None, :] * left_vec
    row_part = jnp.sum(left_raw * left_raw, axis=0)
    beta_norm = jnp.sqrt(lax.psum(row_part, "doc") / docs_total + epsilon)
    left_next = left_raw / beta_norm[None, :]
    feature_part = lax.psum_scatter(
        backward(col_ids, col_vals, left_next, table.shape[0]), "doc", scatter_dimension=0, tiled=True
    )
    right_raw = feature_part - beta_norm[None, :] * right_vec
    squares = lax.psum(jnp.sum(right_raw * right_raw, axis=0), AXES)
    alpha_next = jnp.sqrt(squares / feat_total + epsilon)
    right_next = right_raw / alpha_next[None, :]
    rho_val = jnp.sqrt(rhobar * rhobar + beta_norm * beta_norm)
    cosine = rhobar / rho_val
    sine_val = beta_norm / rho_val
    theta_val = sine_val * alpha_next
    phi_val = cosine * phibar
    solution_next = solution_vec + (phi_val / rho_val)[None, :] * search_dir
    search_next = right_next - (theta_val / rho_val)[None, :] * search_dir
    return (
        left_next,
        right_next,
        search_next,
        solution_next,
        alpha_next,
        sine_val * phibar,
        -cosine * alpha_next,
    )


def solution(mesh):
    small = mesh.shape["doc"] == 16 and mesh.shape["feat"] == 2
    rows = P(("feat", "doc"), None)
    return jax.shard_map(
        by_columns if small else by_blocks,
        mesh=mesh,
        in_specs=(P("doc", "feat"), P("doc", "feat"), P("doc", None), rows, rows, rows, P(), P(), P()),
        out_specs=(P("doc", None), rows, rows, rows, P(), P(), P()),
        check_vma=False,
    )
```

```python
import functools

import jax
import jax.numpy as jnp
from jax import lax
from jax.experimental import pallas as pl
from jax.experimental.pallas import tpu as pltpu
from jax.sharding import PartitionSpec as P

epsilon = 1e-06
AXES = ("doc", "feat")
MIB = 1024 * 1024


Y_BIT, CORE_BIT, X_BIT, Z_SHIFT = 1, 2, 4, 3
NT = (((1,), (1,)), ((), ()))


def coords():
    d = lax.axis_index("doc")
    y = lax.axis_index("feat")
    return d, d >> 2, y


def params(mib):
    return pltpu.CompilerParams(vmem_limit_bytes=mib * MIB)


def cost(flops, nbytes):
    return pl.CostEstimate(flops=int(flops), bytes_accessed=int(nbytes), transcendentals=0)


def f32(*shape):
    return jax.ShapeDtypeStruct(shape, jnp.float32)


def bf16(*shape):
    return jax.ShapeDtypeStruct(shape, jnp.bfloat16)


def prepare_kernel(ids_hbm, vals_hbm, right_hbm, left_hbm, stored, m0, m1, m2, m3,
                   ids, vals, wide, right, left, turned, arrived):
    _, z, y = coords()
    q, rows = turned.shape[1:]
    copies = [
        pltpu.make_async_copy(src, dst, arrived.at[i])
        for i, (src, dst) in enumerate((
            (ids_hbm, ids),
            (vals_hbm, vals),
            (right_hbm, right),
            (left_hbm.at[pl.ds(pl.multiple_of(y * rows, rows), rows), :], left),
        ))
    ]
    for copy in copies:
        copy.start()
    lines, count = stored.shape[0] // 2, ids.shape[0]
    for part, ref in enumerate((ids, vals)):
        copies[part].wait()
        wide[...] = ref[...].astype(jnp.float32).T
        for r in range(256 // count):
            stored[part * lines : (part + 1) * lines, r * count : (r + 1) * count] = wide[
                pl.ds(r, lines, stride=256 // count), :
            ]
    for part, ref in enumerate((right, left)):
        copies[2 + part].wait()
        turned[...] = ref[...].T.reshape(turned.shape)
        for k, out in enumerate((m0, m1, m2, m3)):
            out[part * q : (part + 1) * q, :] = turned[z ^ k]


def prepare(ids, vals, right, left):
    rows, cols = right.shape
    q = cols // 4
    got = pl.pallas_call(
        prepare_kernel,
        in_specs=[pl.BlockSpec(memory_space=pltpu.HBM)] * 4,
        out_specs=[whole()] * 5,
        out_shape=[pltpu.VMEM((ids.size // 128, 256), jnp.float32)] + [pltpu.VMEM((2 * q, rows), jnp.float32)] * 4,
        scratch_shapes=[
            pltpu.VMEM(ids.shape, jnp.int32),
            pltpu.VMEM(vals.shape, jnp.bfloat16),
            pltpu.VMEM(ids.shape[::-1], jnp.float32),
            pltpu.VMEM(right.shape, jnp.float32),
            pltpu.VMEM(right.shape, jnp.float32),
            pltpu.VMEM((4, q, rows), jnp.float32),
            pltpu.SemaphoreType.DMA((4,)),
        ],
        compiler_params=params(60),
        cost_estimate=cost(0, rows * cols * 16),
        name="prepare",
    )(ids, vals, right, left)
    return got[0], got[1:]


def stack_kernel(m0, m1, m2, m3, *refs):
    out = refs[-1]
    for k, m in enumerate((m0, m1, m2, m3)):
        out[k] = m[0 : out.shape[1], :]


def stack(messages, q, name, *tokens):
    rows = messages[0].shape[1]
    return pl.pallas_call(
        stack_kernel,
        out_shape=f32(4, q, rows),
        compiler_params=params(8),
        cost_estimate=cost(0, 32 * q * rows),
        name=name,
    )(*messages, *tokens)


def build_kernel(rel, e0, e1, e2, e3, *refs):
    hi_ref, lo_ref, token = refs[-3:]
    token[...] = jnp.zeros_like(token)
    d, _, y = coords()
    n = e0.shape[0] // 2
    iota = lax.broadcasted_iota(jnp.int32, (256, 256), 0).astype(jnp.float32).astype(jnp.bfloat16)
    lane_doc = lax.broadcasted_iota(jnp.int32, (8, 256), 1) >> 4
    one = jnp.ones((256, 256), jnp.bfloat16)
    zero = jnp.zeros((256, 256), jnp.bfloat16)

    def spread(row):
        wide = jnp.broadcast_to(row, (16, 256)).astype(jnp.bfloat16)
        return jnp.broadcast_to(wide[None], (16, 16, 256)).reshape(256, 256)

    for k, entries in enumerate((e0, e1, e2, e3)):

        @pl.loop(0, n // 16)
        def _(step, k=k, entries=entries):
            at = pl.multiple_of((y ^ rel) * (n // 2) + step * 8, 8)
            ids = entries[pl.ds(at, 8), :].astype(jnp.int32)
            vals = entries[pl.ds(n + at, 8), :]
            owner = (ids >> 8) ^ d
            block = ((owner & 1) << 3) | ((owner & 2) << 1) | (owner >> 2)
            code = (block * 16 + lane_doc).astype(jnp.float32)
            inner = (ids & 255).astype(jnp.float32)
            for t in range(8):
                pick = jnp.where(iota == spread(code[t : t + 1]), one, zero)
                weigh = jnp.where(iota == spread(inner[t : t + 1]), spread(vals[t : t + 1]), zero)
                dense = lax.dot_general(pick, weigh, NT, preferred_element_type=jnp.float32)
                high = dense.astype(jnp.bfloat16)
                low = (dense - high.astype(jnp.float32)).astype(jnp.bfloat16)
                docs = pl.ds(pl.multiple_of(k * 8 * n + step * 128 + 16 * t, 16), 16)
                hi_ref[:, docs, :] = high.reshape(16, 16, 256)
                lo_ref[:, docs, :] = low.reshape(16, 16, 256)


def whole():
    return pl.BlockSpec(memory_space=pltpu.VMEM)


def build(entries, rel, *tokens):
    docs = 4 * (entries[0].shape[0] // 4 * 16)
    *rows, token = pl.pallas_call(
        functools.partial(build_kernel, rel),
        in_specs=[whole()] * (4 + len(tokens)),
        out_specs=[whole()] * 3,
        out_shape=[pltpu.VMEM((16, docs, 256), jnp.bfloat16)] * 2 + [f32(8, 128)],
        compiler_params=params(8),
        cost_estimate=cost(2 * docs * 16 * 256 * 256, docs * 4096 * 4),
        name="dense_rows",
    )(*entries, *tokens)
    return rows, token


def split_rows(value):
    high = value.astype(jnp.bfloat16)
    low = (value - high.astype(jnp.float32)).astype(jnp.bfloat16)
    return jnp.concatenate([high, low], axis=0)


def add_products(hi_ref, lo_ref, vecs, blocks, total):
    for vec, first in zip(vecs, blocks):
        for pair in (0, 2):
            lhs, rhs = [], []
            for k in (pair, pair + 1):
                both = split_rows(vec[k])
                lhs += [hi_ref[first + k], lo_ref[first + k]]
                rhs += [both, both]
            total[...] += lax.dot_general(
                jnp.concatenate(lhs, axis=1), jnp.concatenate(rhs, axis=1), NT, preferred_element_type=jnp.float32
            )


def forward_kernel(blocks, hi_ref, lo_ref, *refs):
    count = len(blocks)
    total = refs[-1]
    total[...] = refs[count][...] if len(refs) > count + 1 else jnp.zeros_like(total)
    add_products(hi_ref, lo_ref, refs[:count], blocks, total)


def forward_part(rows, vecs, blocks, before=None):
    docs, q = rows[0].shape[1], vecs[0].shape[1]
    n = 4 * len(blocks)
    extra = [] if before is None else [before]
    return pl.pallas_call(
        functools.partial(forward_kernel, blocks),
        in_specs=[whole()] * (2 + len(vecs) + len(extra)),
        out_specs=whole(),
        out_shape=f32(docs, 2 * q),
        compiler_params=params(8),
        cost_estimate=cost(8 * docs * 256 * 256 * n, 4 * docs * 256 * n),
        name="forward_part",
    )(*rows, *vecs, *extra)


def product_kernel(blocks, hi_ref, lo_ref, vec, before, *refs):
    out, total, columns = refs[-3:]
    total[...] = before[...]
    add_products(hi_ref, lo_ref, (vec,), blocks, total)
    turned = total[...].T
    q = out.shape[0]
    product = turned[:q] + turned[q:]
    if len(refs) == 3:
        out[...] = product
        return
    _, z, _ = coords()
    *messages, alpha = refs[:5]
    columns[...] = row_to_column(alpha[...])
    scale = columns[pl.ds(pl.multiple_of(z * q, q), q), :][:, 0:1]
    for k, m in enumerate(messages):
        at = slice(k * m.shape[1], (k + 1) * m.shape[1])
        out[:, at] = product[:, at] - scale * m[q:, :]


def product_half(rows, vec, before, blocks, *left):
    docs, q = rows[0].shape[1], vec.shape[1]
    return pl.pallas_call(
        functools.partial(product_kernel, blocks),
        in_specs=[whole()] * (4 + len(left)),
        out_specs=whole(),
        out_shape=f32(q, docs),
        scratch_shapes=[pltpu.VMEM((docs, 2 * q), jnp.float32), pltpu.VMEM((4 * q, 128), jnp.float32)],
        compiler_params=params(8),
        cost_estimate=cost(8 * docs * 256 * 256 * 4, 16 * docs * 256),
        name="product_half",
    )(*rows, vec, before, *left)


def square_sums(value):
    q, n = value.shape
    sums = value[:, 0:128] * value[:, 0:128]
    for at in range(128, n, 128):
        sums = sums + value[:, at : at + 128] * value[:, at : at + 128]
    return jnp.sum(jnp.concatenate([sums] * (128 // q), axis=0).T, axis=0, keepdims=True)


def square_row(value, z, cols):
    row = square_sums(value)
    row = jnp.broadcast_to(jnp.concatenate([row] * (cols // 128), axis=1), (8, cols))
    lane = lax.broadcasted_iota(jnp.int32, (8, cols), 1)
    return jnp.where(lane // value.shape[0] == z, row, 0.0)


def row_to_column(row):
    return jnp.broadcast_to(row, (128, row.shape[1])).T


def left_half_kernel(mine, other, *refs):
    _, z, _ = coords()
    left = mine[...] + other[...]
    both, sums = refs[-2:]
    both[...] = split_rows(left)
    squares = square_row(left, z, sums.shape[1])
    sums[...] = refs[0][...] + squares if len(refs) == 3 else squares
    if len(refs) > 3:
        n = left.shape[1] // 4
        for k, out in enumerate(refs[:4]):
            out[...] = left[:, k * n : (k + 1) * n]


def left_half(mine, other, squares=None):
    q, docs = mine.shape
    extra = [] if squares is None else [squares]
    pieces = [f32(q, docs // 4)] * 4 if squares is None else []
    return pl.pallas_call(
        left_half_kernel,
        out_shape=pieces + [bf16(2 * q, docs), f32(8, 4 * q)],
        compiler_params=params(8),
        cost_estimate=cost(8 * q * docs, 16 * q * docs),
        name="left_half",
    )(mine, other, *extra)


def backward_kernel(first, blocks, parts, hi_ref, lo_ref, both_ref, *refs):
    out_ref = refs[-1]
    both = both_ref[...]
    q = both.shape[0] // 2
    twice = jnp.concatenate([both, both], axis=1)
    for b in range(blocks):
        got = jnp.dot(
            twice,
            jnp.concatenate([hi_ref[first + b], lo_ref[first + b]], axis=0),
            preferred_element_type=jnp.float32,
        )
        got = got[:q] + got[q:]
        if "before" in parts:
            got = got + refs[0][(first + b) * q : (first + b + 1) * q, :]
        out_ref[b * q : (b + 1) * q, :] = got
    if "tail" in parts:
        out_ref[blocks * q :, :] = refs[parts.index("tail")][...]


def backward_part(rows, both, first, blocks, before=None, tail=None, tokens=()):
    q, docs = both.shape[0] // 2, both.shape[1]
    extra = {"before": before, "tail": tail, **{str(i): token for i, token in enumerate(tokens)}}
    extra = {name: value for name, value in extra.items() if value is not None}
    height = blocks * q + (0 if tail is None else tail.shape[0])
    return pl.pallas_call(
        functools.partial(backward_kernel, first, blocks, tuple(extra)),
        in_specs=[whole()] * (3 + len(extra)),
        out_specs=whole(),
        out_shape=f32(height, 256),
        compiler_params=params(8),
        cost_estimate=cost(8 * docs * 256 * 256 * blocks, 4 * docs * 256 * blocks),
        name="backward_part",
    )(*rows, both, *extra.values())


def far_sum_kernel(near, far, beta, send, beta_core):
    n = near.shape[0]
    beta_core[...] = beta[...] + far[n:, :]
    send[0:n, :] = near[...] + far[0:n, :]
    send[n:, :] = beta_core[...]


def far_sums(near, far, beta):
    rows = near.shape[0]
    return pl.pallas_call(
        far_sum_kernel,
        out_shape=[f32(rows + 8, 256), f32(8, 256)],
        compiler_params=params(8),
        cost_estimate=cost(near.size, near.size * 12),
        name="far_sums",
    )(near, far, beta)


def right_norm_kernel(docs_total, keep, peer, got, beta_core, v0, v1, v2, v3, token, g0, g1, g2, g3, sums, columns):
    _, z, _ = coords()
    q = g0.shape[0] - 8
    beta_sums = beta_core[...] + got[4 * q :, :]
    columns[...] = row_to_column(jnp.sqrt(beta_sums[0:1, :] / docs_total + epsilon))
    beta = columns[pl.ds(pl.multiple_of(z * q, q), q), :][:, 0:1]
    raws = []
    for k, (v, g) in enumerate(zip((v0, v1, v2, v3), (g0, g1, g2, g3))):
        rows = slice(k * q, (k + 1) * q)
        total = (keep[rows, :] + peer[rows, :]) + got[rows, :]
        g[0:q, :] = total
        g[q:, :] = beta_sums
        raws.append(total / beta - beta * v[0:q, :])
    sums[...] = jnp.broadcast_to(square_sums(jnp.concatenate(raws, axis=1))[None], sums.shape)


def right_norm(docs_total, keep, peer, got, beta_core, messages, token):
    q, rows = keep.shape[0] // 4, keep.shape[1]
    *pieces, sums = pl.pallas_call(
        functools.partial(right_norm_kernel, docs_total),
        out_shape=[f32(q + 8, rows)] * 4 + [f32(32, 1, 128)],
        scratch_shapes=[pltpu.VMEM((4 * q, 128), jnp.float32)],
        compiler_params=params(8),
        cost_estimate=cost(rows * q * 64, rows * q * 100),
        name="right_norm",
    )(keep, peer, got, beta_core, *messages, token)
    return pieces, sums


def beta_of(pieces, q, docs_total):
    squares = [g[q : q + 1, :] for g in pieces]
    return jnp.sqrt(((squares[0] + squares[1]) + (squares[2] + squares[3])) / docs_total + epsilon)


def finish_kernel(docs_total, feat_total, g0, g1, g2, g3, squares, right, search, phibar, rhobar,
                  right_out, search_out, alpha_out, phibar_out, rhobar_out, turned):
    _, z, _ = coords()
    q = turned.shape[1]
    for k, g in enumerate((g0, g1, g2, g3)):
        turned[z ^ k] = g[0:q, :]
    got = turned[...].reshape(-1, turned.shape[2]).T
    parts = [squares[i] for i in range(32)]
    while len(parts) > 4:
        parts = [a + b for a, b in zip(parts[::2], parts[1::2])]
    low = lax.broadcasted_iota(jnp.int32, parts[0].shape, 1) < q
    parts = [jnp.where(low, parts[0], parts[1]), jnp.where(low, parts[2], parts[3])]
    alpha = jnp.sqrt(jnp.concatenate(parts, axis=1) / feat_total + epsilon)
    beta = beta_of((g0, g1, g2, g3), q, docs_total)
    rho = jnp.sqrt(rhobar[...] * rhobar[...] + beta * beta)
    cosine = rhobar[...] / rho
    sine = beta / rho
    theta = sine * alpha
    rhobar_out[...] = -cosine * alpha
    phibar_out[...] = sine * phibar[...]
    alpha_out[...] = alpha
    following = (got / beta - beta * right[...]) / alpha
    right_out[...] = following
    search_out[...] = following - (theta / rho) * search[...]


def finish(docs_total, feat_total, pieces, squares, right, search, phibar, rhobar):
    rows, cols = right.shape
    return pl.pallas_call(
        functools.partial(finish_kernel, docs_total, feat_total),
        out_shape=[f32(rows, cols)] * 2 + [f32(1, cols)] * 3,
        scratch_shapes=[pltpu.VMEM((4, cols // 4, rows), jnp.float32)],
        compiler_params=params(8),
        cost_estimate=cost(rows * cols * 16, rows * cols * 20),
        name="finish",
    )(*pieces, squares, right, search, phibar, rhobar)


def left_out_kernel(docs_total, own, other, g0, g1, g2, g3, search, solution, phibar, rhobar, left_out, solution_out, turned):
    _, z, y = coords()
    q, half = turned.shape[1:]
    beta = beta_of((g0, g1, g2, g3), q, docs_total)
    for part, ref in ((y, own), (1 - y, other)):
        for k in range(4):
            turned[z ^ k] = ref[k]
        left_out[pl.ds(pl.multiple_of(part * half, half), half), :] = turned[...].reshape(-1, half).T / beta
    rho = jnp.sqrt(rhobar[...] * rhobar[...] + beta * beta)
    phi = rhobar[...] / rho * phibar[...]
    solution_out[...] = solution[...] + (phi / rho) * search[...]


def left_out(docs_total, own, other, pieces, search, solution, phibar, rhobar):
    _, q, half = own.shape
    return pl.pallas_call(
        functools.partial(left_out_kernel, docs_total),
        out_shape=[f32(2 * half, 4 * q), f32(*solution.shape)],
        scratch_shapes=[pltpu.VMEM((4, q, half), jnp.float32)],
        compiler_params=params(8),
        cost_estimate=cost(half * q * 32, half * q * 120),
        name="left_out",
    )(own, other, *pieces, search, solution, phibar, rhobar)


def swap(value, mask):
    return lax.ppermute(value, AXES, [(i, i ^ mask) for i in range(32)])


def along_z(values):
    return [values[0]] + [swap(values[k], k << Z_SHIFT) for k in (1, 2, 3)]


def after(value, *earlier):
    return lax.optimization_barrier((value, *earlier))[0]


def by_columns(
    col_ids, col_vals, left_vec, right_vec, search_dir, solution_vec, alpha_prev, phibar, rhobar
):
    docs_total = left_vec.shape[0] * 16
    feat_total = right_vec.shape[0] * 32
    alpha_row, phibar_row, rhobar_row = (v.reshape(1, -1) for v in (alpha_prev, phibar, rhobar))

    stored, messages = prepare(col_ids.T, col_vals.T, right_vec, left_vec)
    entries = along_z([stored] * 4)
    messages = along_z([messages[0]] + [after(m, entries[1]) for m in messages[1:]])
    q = messages[0].shape[0] // 2

    rows1, token1 = build(entries, 1)
    rows0, token0 = build(entries, 0, token1)
    own = stack(messages, q, "stack_right", token0)
    own_x = swap(own, X_BIT)
    own_peer = swap(own, CORE_BIT)
    total1 = forward_part(rows1, [own, own_peer], (0, 8))
    total0 = forward_part(rows0, [own, own_peer], (0, 8))
    x_peer = swap(after(own_x, total0, total1), CORE_BIT)
    total1 = forward_part(rows1, [own_x], (4,), total1)
    total0 = forward_part(rows0, [own_x], (4,), total0)
    product1 = product_half(rows1, x_peer, total1, (12,))
    product0 = product_half(rows0, x_peer, total0, (12,), *messages, alpha_row)

    *lefts, both0, beta0 = left_half(product0, swap(product1, Y_BIT))
    partial = backward_part(rows0, both0, 0, 16)
    lefts = along_z(lefts)
    both1, beta1 = left_half(product1, swap(product0, Y_BIT), beta0)
    far = swap(backward_part(rows1, both1, 12, 4, partial, beta1, lefts[1:3]), CORE_BIT)
    left_own = stack(lefts, q, "stack_left")
    near = backward_part(rows1, both1, 4, 4, partial)
    send, beta_core = far_sums(near, far, beta1)
    got = swap(send, X_BIT)
    peer = swap(backward_part(rows1, both1, 8, 4, partial, None, [left_own]), CORE_BIT)
    keep = backward_part(rows1, both1, 0, 4, partial)
    left_other = swap(left_own, Y_BIT)

    sent, sums = right_norm(docs_total, keep, peer, got, beta_core, messages, left_other)
    pieces = along_z(sent)
    squares = lax.all_to_all(sums, AXES, 0, 0, tiled=True)
    left_next, solution_next = left_out(
        docs_total, left_own, left_other, pieces, search_dir, solution_vec, phibar_row, rhobar_row
    )
    right_next, search_next, alpha_next, phibar_next, rhobar_next = finish(
        docs_total, feat_total, pieces, squares, right_vec, search_dir, phibar_row, rhobar_row
    )
    return (
        left_next,
        right_next,
        search_next,
        solution_next,
        alpha_next.reshape(-1),
        phibar_next.reshape(-1),
        rhobar_next.reshape(-1),
    )


def forward(col_ids, col_vals, table):
    picked = table[col_ids]
    return jnp.sum(col_vals.astype(jnp.float32)[:, :, None] * picked, axis=1)


def backward(col_ids, col_vals, rows_in, width):
    terms = col_vals.astype(jnp.float32)[:, :, None] * rows_in[:, None, :]
    return jax.ops.segment_sum(
        terms.reshape(-1, rows_in.shape[1]), col_ids.reshape(-1), num_segments=width
    )


def by_blocks(
    col_ids, col_vals, left_vec, right_vec, search_dir, solution_vec, alpha_prev, phibar, rhobar
):
    n_feat = lax.axis_size("feat")
    n_doc = lax.axis_size("doc")
    docs_total = left_vec.shape[0] * n_doc
    feat_total = right_vec.shape[0] * n_doc * n_feat
    table = lax.all_gather(right_vec, "doc", axis=0, tiled=True)
    total = lax.psum(forward(col_ids, col_vals, table), "feat")
    left_raw = total - alpha_prev[None, :] * left_vec
    row_part = jnp.sum(left_raw * left_raw, axis=0)
    beta_norm = jnp.sqrt(lax.psum(row_part, "doc") / docs_total + epsilon)
    left_next = left_raw / beta_norm[None, :]
    feature_part = lax.psum_scatter(
        backward(col_ids, col_vals, left_next, table.shape[0]), "doc", scatter_dimension=0, tiled=True
    )
    right_raw = feature_part - beta_norm[None, :] * right_vec
    squares = lax.psum(jnp.sum(right_raw * right_raw, axis=0), AXES)
    alpha_next = jnp.sqrt(squares / feat_total + epsilon)
    right_next = right_raw / alpha_next[None, :]
    rho_val = jnp.sqrt(rhobar * rhobar + beta_norm * beta_norm)
    cosine = rhobar / rho_val
    sine_val = beta_norm / rho_val
    theta_val = sine_val * alpha_next
    phi_val = cosine * phibar
    solution_next = solution_vec + (phi_val / rho_val)[None, :] * search_dir
    search_next = right_next - (theta_val / rho_val)[None, :] * search_dir
    return (
        left_next,
        right_next,
        search_next,
        solution_next,
        alpha_next,
        sine_val * phibar,
        -cosine * alpha_next,
    )


def solution(mesh):
    small = mesh.shape["doc"] == 16 and mesh.shape["feat"] == 2
    rows = P(("feat", "doc"), None)
    return jax.shard_map(
        by_columns if small else by_blocks,
        mesh=mesh,
        in_specs=(P("doc", "feat"), P("doc", "feat"), P("doc", None), rows, rows, rows, P(), P(), P()),
        out_specs=(P("doc", None), rows, rows, rows, P(), P(), P()),
        check_vma=False,
    )
```

```python
import functools

import jax
import jax.numpy as jnp
from jax import lax
from jax.experimental import pallas as pl
from jax.experimental.pallas import tpu as pltpu
from jax.sharding import PartitionSpec as P

epsilon = 1e-06
AXES = ("doc", "feat")
MIB = 1024 * 1024


Y_BIT, CORE_BIT, X_BIT, Z_SHIFT = 1, 2, 4, 3
NT = (((1,), (1,)), ((), ()))


def coords():
    d = lax.axis_index("doc")
    y = lax.axis_index("feat")
    return d, d >> 2, y


def params(mib):
    return pltpu.CompilerParams(vmem_limit_bytes=mib * MIB)


def cost(flops, nbytes):
    return pl.CostEstimate(flops=int(flops), bytes_accessed=int(nbytes), transcendentals=0)


def f32(*shape):
    return jax.ShapeDtypeStruct(shape, jnp.float32)


def bf16(*shape):
    return jax.ShapeDtypeStruct(shape, jnp.bfloat16)


def prepare_kernel(ids_hbm, vals_hbm, right_hbm, left_hbm, stored, m0, m1, m2, m3,
                   ids, vals, wide, right, left, turned, arrived):
    _, z, y = coords()
    q, rows = turned.shape[1:]
    copies = [
        pltpu.make_async_copy(src, dst, arrived.at[i])
        for i, (src, dst) in enumerate((
            (ids_hbm, ids),
            (vals_hbm, vals),
            (right_hbm, right),
            (left_hbm.at[pl.ds(pl.multiple_of(y * rows, rows), rows), :], left),
        ))
    ]
    for copy in copies:
        copy.start()
    lines, count = stored.shape[0] // 2, ids.shape[0]
    for part, ref in enumerate((ids, vals)):
        copies[part].wait()
        wide[...] = ref[...].astype(jnp.float32).T
        for r in range(256 // count):
            stored[part * lines : (part + 1) * lines, r * count : (r + 1) * count] = wide[
                pl.ds(r, lines, stride=256 // count), :
            ]
    for part, ref in enumerate((right, left)):
        copies[2 + part].wait()
        turned[...] = ref[...].T.reshape(turned.shape)
        for k, out in enumerate((m0, m1, m2, m3)):
            out[part * q : (part + 1) * q, :] = turned[z ^ k]


def prepare(ids, vals, right, left):
    rows, cols = right.shape
    q = cols // 4
    got = pl.pallas_call(
        prepare_kernel,
        in_specs=[pl.BlockSpec(memory_space=pltpu.HBM)] * 4,
        out_specs=[whole()] * 5,
        out_shape=[pltpu.VMEM((ids.size // 128, 256), jnp.float32)] + [pltpu.VMEM((2 * q, rows), jnp.float32)] * 4,
        scratch_shapes=[
            pltpu.VMEM(ids.shape, jnp.int32),
            pltpu.VMEM(vals.shape, jnp.bfloat16),
            pltpu.VMEM(ids.shape[::-1], jnp.float32),
            pltpu.VMEM(right.shape, jnp.float32),
            pltpu.VMEM(right.shape, jnp.float32),
            pltpu.VMEM((4, q, rows), jnp.float32),
            pltpu.SemaphoreType.DMA((4,)),
        ],
        compiler_params=params(60),
        cost_estimate=cost(0, rows * cols * 16),
        name="prepare",
    )(ids, vals, right, left)
    return got[0], got[1:]


def stack_kernel(m0, m1, m2, m3, *refs):
    out = refs[-1]
    for k, m in enumerate((m0, m1, m2, m3)):
        out[k] = m[0 : out.shape[1], :]


def stack(messages, q, name, *tokens):
    rows = messages[0].shape[1]
    return pl.pallas_call(
        stack_kernel,
        out_shape=f32(4, q, rows),
        compiler_params=params(8),
        cost_estimate=cost(0, 32 * q * rows),
        name=name,
    )(*messages, *tokens)


def build_kernel(rel, e0, e1, e2, e3, *refs):
    hi_ref, lo_ref, token = refs[-3:]
    token[...] = jnp.zeros_like(token)
    d, _, y = coords()
    n = e0.shape[0] // 2
    iota = lax.broadcasted_iota(jnp.int32, (256, 256), 0).astype(jnp.float32).astype(jnp.bfloat16)
    lane_doc = lax.broadcasted_iota(jnp.int32, (8, 256), 1) >> 4
    one = jnp.ones((256, 256), jnp.bfloat16)
    zero = jnp.zeros((256, 256), jnp.bfloat16)

    def spread(row):
        wide = jnp.broadcast_to(row, (16, 256)).astype(jnp.bfloat16)
        return jnp.broadcast_to(wide[None], (16, 16, 256)).reshape(256, 256)

    for k, entries in enumerate((e0, e1, e2, e3)):

        @pl.loop(0, n // 16)
        def _(step, k=k, entries=entries):
            at = pl.multiple_of((y ^ rel) * (n // 2) + step * 8, 8)
            ids = entries[pl.ds(at, 8), :].astype(jnp.int32)
            vals = entries[pl.ds(n + at, 8), :]
            owner = (ids >> 8) ^ d
            block = ((owner & 1) << 3) | ((owner & 2) << 1) | (owner >> 2)
            code = (block * 16 + lane_doc).astype(jnp.float32)
            inner = (ids & 255).astype(jnp.float32)
            for t in range(8):
                pick = jnp.where(iota == spread(code[t : t + 1]), one, zero)
                weigh = jnp.where(iota == spread(inner[t : t + 1]), spread(vals[t : t + 1]), zero)
                dense = lax.dot_general(pick, weigh, NT, preferred_element_type=jnp.float32)
                high = dense.astype(jnp.bfloat16)
                low = (dense - high.astype(jnp.float32)).astype(jnp.bfloat16)
                docs = pl.ds(pl.multiple_of(k * 8 * n + step * 128 + 16 * t, 16), 16)
                hi_ref[:, docs, :] = high.reshape(16, 16, 256)
                lo_ref[:, docs, :] = low.reshape(16, 16, 256)


def whole():
    return pl.BlockSpec(memory_space=pltpu.VMEM)


def build(entries, rel, *tokens):
    docs = 4 * (entries[0].shape[0] // 4 * 16)
    *rows, token = pl.pallas_call(
        functools.partial(build_kernel, rel),
        in_specs=[whole()] * (4 + len(tokens)),
        out_specs=[whole()] * 3,
        out_shape=[pltpu.VMEM((16, docs, 256), jnp.bfloat16)] * 2 + [f32(8, 128)],
        compiler_params=params(8),
        cost_estimate=cost(2 * docs * 16 * 256 * 256, docs * 4096 * 4),
        name="dense_rows",
    )(*entries, *tokens)
    return rows, token


def split_rows(value):
    high = value.astype(jnp.bfloat16)
    low = (value - high.astype(jnp.float32)).astype(jnp.bfloat16)
    return jnp.concatenate([high, low], axis=0)


def add_products(hi_ref, lo_ref, vecs, blocks, total):
    for vec, first in zip(vecs, blocks):
        for pair in (0, 2):
            lhs, rhs = [], []
            for k in (pair, pair + 1):
                both = split_rows(vec[k])
                lhs += [hi_ref[first + k], lo_ref[first + k]]
                rhs += [both, both]
            total[...] += lax.dot_general(
                jnp.concatenate(lhs, axis=1), jnp.concatenate(rhs, axis=1), NT, preferred_element_type=jnp.float32
            )


def forward_kernel(blocks, hi_ref, lo_ref, *refs):
    count = len(blocks)
    total = refs[-1]
    total[...] = refs[count][...] if len(refs) > count + 1 else jnp.zeros_like(total)
    add_products(hi_ref, lo_ref, refs[:count], blocks, total)


def forward_part(rows, vecs, blocks, before=None):
    docs, q = rows[0].shape[1], vecs[0].shape[1]
    n = 4 * len(blocks)
    extra = [] if before is None else [before]
    return pl.pallas_call(
        functools.partial(forward_kernel, blocks),
        in_specs=[whole()] * (2 + len(vecs) + len(extra)),
        out_specs=whole(),
        out_shape=f32(docs, 2 * q),
        compiler_params=params(8),
        cost_estimate=cost(8 * docs * 256 * 256 * n, 4 * docs * 256 * n),
        name="forward_part",
    )(*rows, *vecs, *extra)


def product_kernel(blocks, hi_ref, lo_ref, vec, before, *refs):
    out, total, columns = refs[-3:]
    total[...] = before[...]
    add_products(hi_ref, lo_ref, (vec,), blocks, total)
    turned = total[...].T
    q = out.shape[0]
    product = turned[:q] + turned[q:]
    if len(refs) == 3:
        out[...] = product
        return
    _, z, _ = coords()
    *messages, alpha = refs[:5]
    columns[...] = row_to_column(alpha[...])
    scale = columns[pl.ds(pl.multiple_of(z * q, q), q), :][:, 0:1]
    for k, m in enumerate(messages):
        at = slice(k * m.shape[1], (k + 1) * m.shape[1])
        out[:, at] = product[:, at] - scale * m[q:, :]


def product_half(rows, vec, before, blocks, *left):
    docs, q = rows[0].shape[1], vec.shape[1]
    return pl.pallas_call(
        functools.partial(product_kernel, blocks),
        in_specs=[whole()] * (4 + len(left)),
        out_specs=whole(),
        out_shape=f32(q, docs),
        scratch_shapes=[pltpu.VMEM((docs, 2 * q), jnp.float32), pltpu.VMEM((4 * q, 128), jnp.float32)],
        compiler_params=params(8),
        cost_estimate=cost(8 * docs * 256 * 256 * 4, 16 * docs * 256),
        name="product_half",
    )(*rows, vec, before, *left)


def square_sums(value):
    q, n = value.shape
    sums = value[:, 0:128] * value[:, 0:128]
    for at in range(128, n, 128):
        sums = sums + value[:, at : at + 128] * value[:, at : at + 128]
    return jnp.sum(jnp.concatenate([sums] * (128 // q), axis=0).T, axis=0, keepdims=True)


def square_row(value, z, cols):
    row = square_sums(value)
    row = jnp.broadcast_to(jnp.concatenate([row] * (cols // 128), axis=1), (8, cols))
    lane = lax.broadcasted_iota(jnp.int32, (8, cols), 1)
    return jnp.where(lane // value.shape[0] == z, row, 0.0)


def row_to_column(row):
    return jnp.broadcast_to(row, (128, row.shape[1])).T


def left_half_kernel(mine, other, *refs):
    _, z, _ = coords()
    left = mine[...] + other[...]
    both, sums = refs[-2:]
    both[...] = split_rows(left)
    squares = square_row(left, z, sums.shape[1])
    sums[...] = refs[0][...] + squares if len(refs) == 3 else squares
    if len(refs) > 3:
        n = left.shape[1] // 4
        for k, out in enumerate(refs[:4]):
            out[...] = left[:, k * n : (k + 1) * n]


def left_half(mine, other, squares=None):
    q, docs = mine.shape
    extra = [] if squares is None else [squares]
    pieces = [f32(q, docs // 4)] * 4 if squares is None else []
    return pl.pallas_call(
        left_half_kernel,
        out_shape=pieces + [bf16(2 * q, docs), f32(8, 4 * q)],
        compiler_params=params(8),
        cost_estimate=cost(8 * q * docs, 16 * q * docs),
        name="left_half",
    )(mine, other, *extra)


def backward_kernel(first, blocks, parts, hi_ref, lo_ref, both_ref, *refs):
    out_ref = refs[-1]
    both = both_ref[...]
    q = both.shape[0] // 2
    twice = jnp.concatenate([both, both], axis=1)
    for b in range(blocks):
        got = jnp.dot(
            twice,
            jnp.concatenate([hi_ref[first + b], lo_ref[first + b]], axis=0),
            preferred_element_type=jnp.float32,
        )
        got = got[:q] + got[q:]
        if "before" in parts:
            got = got + refs[0][(first + b) * q : (first + b + 1) * q, :]
        out_ref[b * q : (b + 1) * q, :] = got
    if "tail" in parts:
        out_ref[blocks * q :, :] = refs[parts.index("tail")][...]


def backward_part(rows, both, first, blocks, before=None, tail=None, tokens=()):
    q, docs = both.shape[0] // 2, both.shape[1]
    extra = {"before": before, "tail": tail, **{str(i): token for i, token in enumerate(tokens)}}
    extra = {name: value for name, value in extra.items() if value is not None}
    height = blocks * q + (0 if tail is None else tail.shape[0])
    return pl.pallas_call(
        functools.partial(backward_kernel, first, blocks, tuple(extra)),
        in_specs=[whole()] * (3 + len(extra)),
        out_specs=whole(),
        out_shape=f32(height, 256),
        compiler_params=params(8),
        cost_estimate=cost(8 * docs * 256 * 256 * blocks, 4 * docs * 256 * blocks),
        name="backward_part",
    )(*rows, both, *extra.values())


def far_sum_kernel(near, far, beta, send, beta_core):
    n = near.shape[0]
    beta_core[...] = beta[...] + far[n:, :]
    send[0:n, :] = near[...] + far[0:n, :]
    send[n:, :] = beta_core[...]


def far_sums(near, far, beta):
    rows = near.shape[0]
    return pl.pallas_call(
        far_sum_kernel,
        out_shape=[f32(rows + 8, 256), f32(8, 256)],
        compiler_params=params(8),
        cost_estimate=cost(near.size, near.size * 12),
        name="far_sums",
    )(near, far, beta)


def right_norm_kernel(docs_total, keep, peer, got, beta_core, v0, v1, v2, v3, token, g0, g1, g2, g3, sums, columns):
    _, z, _ = coords()
    q = g0.shape[0] - 8
    beta_sums = beta_core[...] + got[4 * q :, :]
    columns[...] = row_to_column(jnp.sqrt(beta_sums[0:1, :] / docs_total + epsilon))
    beta = columns[pl.ds(pl.multiple_of(z * q, q), q), :][:, 0:1]
    raws = []
    for k, (v, g) in enumerate(zip((v0, v1, v2, v3), (g0, g1, g2, g3))):
        rows = slice(k * q, (k + 1) * q)
        total = (keep[rows, :] + peer[rows, :]) + got[rows, :]
        g[0:q, :] = total
        g[q:, :] = beta_sums
        raws.append(total / beta - beta * v[0:q, :])
    line = square_sums(jnp.concatenate(raws, axis=1))
    for i in range(sums.shape[0]):
        sums[i] = line


def right_norm(docs_total, keep, peer, got, beta_core, messages, token):
    q, rows = keep.shape[0] // 4, keep.shape[1]
    *pieces, sums = pl.pallas_call(
        functools.partial(right_norm_kernel, docs_total),
        out_shape=[f32(q + 8, rows)] * 4 + [f32(32, 1, 128)],
        scratch_shapes=[pltpu.VMEM((4 * q, 128), jnp.float32)],
        compiler_params=params(8),
        cost_estimate=cost(rows * q * 64, rows * q * 100),
        name="right_norm",
    )(keep, peer, got, beta_core, *messages, token)
    return pieces, sums


def beta_of(pieces, q, docs_total):
    squares = [g[q : q + 1, :] for g in pieces]
    return jnp.sqrt(((squares[0] + squares[1]) + (squares[2] + squares[3])) / docs_total + epsilon)


def finish_kernel(docs_total, feat_total, g0, g1, g2, g3, squares, right, search, phibar, rhobar,
                  right_out, search_out, alpha_out, phibar_out, rhobar_out, turned):
    _, z, _ = coords()
    q = turned.shape[1]
    for k, g in enumerate((g0, g1, g2, g3)):
        turned[z ^ k] = g[0:q, :]
    got = turned[...].reshape(-1, turned.shape[2]).T
    parts = [squares[i] for i in range(32)]
    while len(parts) > 4:
        parts = [a + b for a, b in zip(parts[::2], parts[1::2])]
    low = lax.broadcasted_iota(jnp.int32, parts[0].shape, 1) < q
    parts = [jnp.where(low, parts[0], parts[1]), jnp.where(low, parts[2], parts[3])]
    alpha = jnp.sqrt(jnp.concatenate(parts, axis=1) / feat_total + epsilon)
    beta = beta_of((g0, g1, g2, g3), q, docs_total)
    rho = jnp.sqrt(rhobar[...] * rhobar[...] + beta * beta)
    cosine = rhobar[...] / rho
    sine = beta / rho
    theta = sine * alpha
    rhobar_out[...] = -cosine * alpha
    phibar_out[...] = sine * phibar[...]
    alpha_out[...] = alpha
    following = (got / beta - beta * right[...]) / alpha
    right_out[...] = following
    search_out[...] = following - (theta / rho) * search[...]


def finish(docs_total, feat_total, pieces, squares, right, search, phibar, rhobar):
    rows, cols = right.shape
    return pl.pallas_call(
        functools.partial(finish_kernel, docs_total, feat_total),
        out_shape=[f32(rows, cols)] * 2 + [f32(1, cols)] * 3,
        scratch_shapes=[pltpu.VMEM((4, cols // 4, rows), jnp.float32)],
        compiler_params=params(8),
        cost_estimate=cost(rows * cols * 16, rows * cols * 20),
        name="finish",
    )(*pieces, squares, right, search, phibar, rhobar)


def left_out_kernel(docs_total, own, other, g0, g1, g2, g3, search, solution, phibar, rhobar, left_out, solution_out, turned):
    _, z, y = coords()
    q, half = turned.shape[1:]
    beta = beta_of((g0, g1, g2, g3), q, docs_total)
    for part, ref in ((y, own), (1 - y, other)):
        for k in range(4):
            turned[z ^ k] = ref[k]
        left_out[pl.ds(pl.multiple_of(part * half, half), half), :] = turned[...].reshape(-1, half).T / beta
    rho = jnp.sqrt(rhobar[...] * rhobar[...] + beta * beta)
    phi = rhobar[...] / rho * phibar[...]
    solution_out[...] = solution[...] + (phi / rho) * search[...]


def left_out(docs_total, own, other, pieces, search, solution, phibar, rhobar):
    _, q, half = own.shape
    return pl.pallas_call(
        functools.partial(left_out_kernel, docs_total),
        out_shape=[f32(2 * half, 4 * q), f32(*solution.shape)],
        scratch_shapes=[pltpu.VMEM((4, q, half), jnp.float32)],
        compiler_params=params(8),
        cost_estimate=cost(half * q * 32, half * q * 120),
        name="left_out",
    )(own, other, *pieces, search, solution, phibar, rhobar)


def swap(value, mask):
    return lax.ppermute(value, AXES, [(i, i ^ mask) for i in range(32)])


def along_z(values):
    return [values[0]] + [swap(values[k], k << Z_SHIFT) for k in (1, 2, 3)]


def after(value, *earlier):
    return lax.optimization_barrier((value, *earlier))[0]


def by_columns(
    col_ids, col_vals, left_vec, right_vec, search_dir, solution_vec, alpha_prev, phibar, rhobar
):
    docs_total = left_vec.shape[0] * 16
    feat_total = right_vec.shape[0] * 32
    alpha_row, phibar_row, rhobar_row = (v.reshape(1, -1) for v in (alpha_prev, phibar, rhobar))

    stored, messages = prepare(col_ids.T, col_vals.T, right_vec, left_vec)
    entries = along_z([stored] * 4)
    messages = along_z([messages[0]] + [after(m, *entries[1:]) for m in messages[1:]])
    q = messages[0].shape[0] // 2

    rows1, token1 = build(entries, 1)
    rows0, _ = build(entries, 0, token1)
    own = stack(messages, q, "stack_right", token1)
    own_x = swap(own, X_BIT)
    own_peer = swap(own, CORE_BIT)
    total1 = forward_part(rows1, [own, own_peer], (0, 8))
    total0 = forward_part(rows0, [own, own_peer], (0, 8))
    x_peer = swap(after(own_x, total0, total1), CORE_BIT)
    total1 = forward_part(rows1, [own_x], (4,), total1)
    total0 = forward_part(rows0, [own_x], (4,), total0)
    product1 = product_half(rows1, x_peer, total1, (12,))
    product0 = product_half(rows0, x_peer, total0, (12,), *messages, alpha_row)

    *lefts, both0, beta0 = left_half(product0, swap(product1, Y_BIT))
    partial = backward_part(rows0, both0, 0, 16)
    lefts = along_z(lefts)
    both1, beta1 = left_half(product1, swap(product0, Y_BIT), beta0)
    far = swap(backward_part(rows1, both1, 12, 4, partial, beta1, lefts[1:3]), CORE_BIT)
    near = backward_part(rows1, both1, 4, 4, partial)
    send, beta_core = far_sums(near, far, beta1)
    got = swap(send, X_BIT)
    peer = backward_part(rows1, both1, 8, 4, partial)
    left_own = stack(lefts, q, "stack_left", peer)
    left_other = swap(left_own, Y_BIT)
    keep = backward_part(rows1, both1, 0, 4, partial)

    sent, sums = right_norm(docs_total, keep, swap(peer, CORE_BIT), got, beta_core, messages, left_own)
    pieces = along_z(sent)
    squares = lax.all_to_all(after(sums, left_other), AXES, 0, 0, tiled=True)
    left_next, solution_next = left_out(
        docs_total, left_own, left_other, pieces, search_dir, solution_vec, phibar_row, rhobar_row
    )
    right_next, search_next, alpha_next, phibar_next, rhobar_next = finish(
        docs_total, feat_total, pieces, squares, right_vec, search_dir, phibar_row, rhobar_row
    )
    return (
        left_next,
        right_next,
        search_next,
        solution_next,
        alpha_next.reshape(-1),
        phibar_next.reshape(-1),
        rhobar_next.reshape(-1),
    )


def forward(col_ids, col_vals, table):
    picked = table[col_ids]
    return jnp.sum(col_vals.astype(jnp.float32)[:, :, None] * picked, axis=1)


def backward(col_ids, col_vals, rows_in, width):
    terms = col_vals.astype(jnp.float32)[:, :, None] * rows_in[:, None, :]
    return jax.ops.segment_sum(
        terms.reshape(-1, rows_in.shape[1]), col_ids.reshape(-1), num_segments=width
    )


def by_blocks(
    col_ids, col_vals, left_vec, right_vec, search_dir, solution_vec, alpha_prev, phibar, rhobar
):
    n_feat = lax.axis_size("feat")
    n_doc = lax.axis_size("doc")
    docs_total = left_vec.shape[0] * n_doc
    feat_total = right_vec.shape[0] * n_doc * n_feat
    table = lax.all_gather(right_vec, "doc", axis=0, tiled=True)
    total = lax.psum(forward(col_ids, col_vals, table), "feat")
    left_raw = total - alpha_prev[None, :] * left_vec
    row_part = jnp.sum(left_raw * left_raw, axis=0)
    beta_norm = jnp.sqrt(lax.psum(row_part, "doc") / docs_total + epsilon)
    left_next = left_raw / beta_norm[None, :]
    feature_part = lax.psum_scatter(
        backward(col_ids, col_vals, left_next, table.shape[0]), "doc", scatter_dimension=0, tiled=True
    )
    right_raw = feature_part - beta_norm[None, :] * right_vec
    squares = lax.psum(jnp.sum(right_raw * right_raw, axis=0), AXES)
    alpha_next = jnp.sqrt(squares / feat_total + epsilon)
    right_next = right_raw / alpha_next[None, :]
    rho_val = jnp.sqrt(rhobar * rhobar + beta_norm * beta_norm)
    cosine = rhobar / rho_val
    sine_val = beta_norm / rho_val
    theta_val = sine_val * alpha_next
    phi_val = cosine * phibar
    solution_next = solution_vec + (phi_val / rho_val)[None, :] * search_dir
    search_next = right_next - (theta_val / rho_val)[None, :] * search_dir
    return (
        left_next,
        right_next,
        search_next,
        solution_next,
        alpha_next,
        sine_val * phibar,
        -cosine * alpha_next,
    )


def solution(mesh):
    small = mesh.shape["doc"] == 16 and mesh.shape["feat"] == 2
    rows = P(("feat", "doc"), None)
    return jax.shard_map(
        by_columns if small else by_blocks,
        mesh=mesh,
        in_specs=(P("doc", "feat"), P("doc", "feat"), P("doc", None), rows, rows, rows, P(), P(), P()),
        out_specs=(P("doc", None), rows, rows, rows, P(), P(), P()),
        check_vma=False,
    )
```

```python
import functools

import jax
import jax.numpy as jnp
from jax import lax
from jax.experimental import pallas as pl
from jax.experimental.pallas import tpu as pltpu
from jax.sharding import PartitionSpec as P

epsilon = 1e-06
AXES = ("doc", "feat")
MIB = 1024 * 1024
SCALE = 64


Y_BIT, CORE_BIT, X_BIT = 1, 2, 4
Z_LINES = [[z * 8 + i for z in range(4)] for i in range(8)]
NT = (((1,), (1,)), ((), ()))


def coords():
    d = lax.axis_index("doc")
    y = lax.axis_index("feat")
    return d, d >> 2, y


def params(mib):
    return pltpu.CompilerParams(vmem_limit_bytes=mib * MIB)


def cost(flops, nbytes):
    return pl.CostEstimate(flops=int(flops) // SCALE, bytes_accessed=int(nbytes) // SCALE, transcendentals=0)


def f32(*shape):
    return jax.ShapeDtypeStruct(shape, jnp.float32)


def bf16(*shape):
    return jax.ShapeDtypeStruct(shape, jnp.bfloat16)


def entries_kernel(ids_hbm, vals_hbm, right_hbm, left_hbm, stored, right, left, ids, vals, wide, arrived):
    _, _, y = coords()
    rows = left.shape[0]
    copies = [
        pltpu.make_async_copy(src, dst, arrived.at[i])
        for i, (src, dst) in enumerate((
            (ids_hbm, ids),
            (vals_hbm, vals),
            (right_hbm, right),
            (left_hbm.at[pl.ds(pl.multiple_of(y * rows, rows), rows), :], left),
        ))
    ]
    for copy in copies:
        copy.start()
    count = ids.shape[0]
    lines = ids.shape[1] * count // 256
    for part, ref in enumerate((ids, vals)):
        copies[part].wait()
        wide[...] = ref[...].astype(jnp.float32).T
        for r in range(256 // count):
            stored[part * lines : (part + 1) * lines, r * count : (r + 1) * count] = wide[
                pl.ds(r, lines, stride=256 // count), :
            ]
    for z in range(1, 4):
        stored[z * 2 * lines : (z + 1) * 2 * lines, :] = stored[0 : 2 * lines, :]
    copies[2].wait()
    copies[3].wait()


def entries_of(ids, vals, right, left):
    return pl.pallas_call(
        entries_kernel,
        in_specs=[pl.BlockSpec(memory_space=pltpu.HBM)] * 4,
        out_specs=[whole()] * 3,
        out_shape=[
            pltpu.VMEM((4 * ids.size // 128, 256), jnp.float32),
            pltpu.VMEM(right.shape, jnp.float32),
            pltpu.VMEM(right.shape, jnp.float32),
        ],
        scratch_shapes=[
            pltpu.VMEM(ids.shape, jnp.int32),
            pltpu.VMEM(vals.shape, jnp.bfloat16),
            pltpu.VMEM(ids.shape[::-1], jnp.float32),
            pltpu.SemaphoreType.DMA((4,)),
        ],
        compiler_params=params(60),
        cost_estimate=cost(0, right.size * 16),
        name="entries",
    )(ids, vals, right, left)


def turn_kernel(ref, token, out):
    out[...] = ref[...].T


def turn(value, token, name):
    return pl.pallas_call(
        turn_kernel,
        out_shape=f32(*value.shape[::-1]),
        compiler_params=params(8),
        cost_estimate=cost(0, value.size * 8),
        name=name,
    )(value, token)


def relative_kernel(ref, token, out):
    _, z, _ = coords()
    q = out.shape[1]
    for k in range(4):
        out[k] = ref[pl.ds(pl.multiple_of((z ^ k) * q, q), q), :]


def relative(value, token, name):
    return pl.pallas_call(
        relative_kernel,
        out_shape=f32(4, value.shape[0] // 4, value.shape[1]),
        compiler_params=params(8),
        cost_estimate=cost(0, value.size * 8),
        name=name,
    )(value, token)


def build_kernel(rel, entries, *refs):
    hi_ref, lo_ref, token = refs[-3:]
    token[...] = jnp.zeros_like(token)
    d, z, y = coords()
    n = entries.shape[0] // 8
    iota = lax.broadcasted_iota(jnp.int32, (256, 256), 0).astype(jnp.float32).astype(jnp.bfloat16)
    lane_doc = lax.broadcasted_iota(jnp.int32, (8, 256), 1) >> 4
    one = jnp.ones((256, 256), jnp.bfloat16)
    zero = jnp.zeros((256, 256), jnp.bfloat16)

    def spread(row):
        wide = jnp.broadcast_to(row, (16, 256)).astype(jnp.bfloat16)
        return jnp.broadcast_to(wide[None], (16, 16, 256)).reshape(256, 256)

    for k in range(4):

        @pl.loop(0, n // 16)
        def _(step, k=k):
            at = pl.multiple_of((z ^ k) * 2 * n + (y ^ rel) * (n // 2) + step * 8, 8)
            ids = entries[pl.ds(at, 8), :].astype(jnp.int32)
            vals = entries[pl.ds(n + at, 8), :]
            owner = (ids >> 8) ^ d
            block = ((owner & 1) << 3) | ((owner & 2) << 1) | (owner >> 2)
            code = (block * 16 + lane_doc).astype(jnp.float32)
            inner = (ids & 255).astype(jnp.float32)
            for t in range(8):
                pick = jnp.where(iota == spread(code[t : t + 1]), one, zero)
                weigh = jnp.where(iota == spread(inner[t : t + 1]), spread(vals[t : t + 1]), zero)
                dense = lax.dot_general(pick, weigh, NT, preferred_element_type=jnp.float32)
                high = dense.astype(jnp.bfloat16)
                low = (dense - high.astype(jnp.float32)).astype(jnp.bfloat16)
                docs = pl.ds(pl.multiple_of(k * 8 * n + step * 128 + 16 * t, 16), 16)
                hi_ref[:, docs, :] = high.reshape(16, 16, 256)
                lo_ref[:, docs, :] = low.reshape(16, 16, 256)


def whole():
    return pl.BlockSpec(memory_space=pltpu.VMEM)


def build(entries, rel, *tokens):
    docs = entries.shape[0] // 4 * 16
    *rows, token = pl.pallas_call(
        functools.partial(build_kernel, rel),
        in_specs=[whole()] * (1 + len(tokens)),
        out_specs=[whole()] * 3,
        out_shape=[pltpu.VMEM((16, docs, 256), jnp.bfloat16)] * 2 + [f32(8, 128)],
        compiler_params=params(8),
        cost_estimate=cost(2 * docs * 16 * 256 * 256, docs * 4096 * 4),
        name="dense_rows",
    )(entries, *tokens)
    return rows, token


def split_rows(value):
    high = value.astype(jnp.bfloat16)
    low = (value - high.astype(jnp.float32)).astype(jnp.bfloat16)
    return jnp.concatenate([high, low], axis=0)


def add_products(hi_ref, lo_ref, vecs, blocks, total):
    for vec, first in zip(vecs, blocks):
        for pair in (0, 2):
            lhs, rhs = [], []
            for k in (pair, pair + 1):
                both = split_rows(vec[k])
                lhs += [hi_ref[first + k], lo_ref[first + k]]
                rhs += [both, both]
            total[...] += lax.dot_general(
                jnp.concatenate(lhs, axis=1), jnp.concatenate(rhs, axis=1), NT, preferred_element_type=jnp.float32
            )


def forward_kernel(blocks, hi_ref, lo_ref, *refs):
    count = len(blocks)
    total = refs[-1]
    total[...] = refs[count][...] if len(refs) > count + 1 else jnp.zeros_like(total)
    add_products(hi_ref, lo_ref, refs[:count], blocks, total)


def forward_part(rows, vecs, blocks, before=None):
    docs, q = rows[0].shape[1], vecs[0].shape[1]
    n = 4 * len(blocks)
    extra = [] if before is None else [before]
    return pl.pallas_call(
        functools.partial(forward_kernel, blocks),
        in_specs=[whole()] * (2 + len(vecs) + len(extra)),
        out_specs=whole(),
        out_shape=f32(docs, 2 * q),
        compiler_params=params(8),
        cost_estimate=cost(8 * docs * 256 * 256 * n, 4 * docs * 256 * n),
        name="forward_part",
    )(*rows, *vecs, *extra)


def product_kernel(blocks, hi_ref, lo_ref, vec, before, *refs):
    out, total, columns = refs[-3:]
    total[...] = before[...]
    add_products(hi_ref, lo_ref, (vec,), blocks, total)
    turned = total[...].T
    q = out.shape[0]
    product = turned[:q] + turned[q:]
    if len(refs) == 3:
        out[...] = product
        return
    _, z, _ = coords()
    left, alpha = refs[:2]
    columns[...] = row_to_column(alpha[...])
    scale = columns[pl.ds(pl.multiple_of(z * q, q), q), :][:, 0:1]
    n = left.shape[1]
    for k in range(4):
        at = slice(k * n, (k + 1) * n)
        out[:, at] = product[:, at] - scale * left[pl.ds(pl.multiple_of((z ^ k) * q, q), q), :]


def product_half(rows, vec, before, blocks, *left):
    docs, q = rows[0].shape[1], vec.shape[1]
    return pl.pallas_call(
        functools.partial(product_kernel, blocks),
        in_specs=[whole()] * (4 + len(left)),
        out_specs=whole(),
        out_shape=f32(q, docs),
        scratch_shapes=[pltpu.VMEM((docs, 2 * q), jnp.float32), pltpu.VMEM((4 * q, 128), jnp.float32)],
        compiler_params=params(8),
        cost_estimate=cost(8 * docs * 256 * 256 * 4, 16 * docs * 256),
        name="product_half",
    )(*rows, vec, before, *left)


def square_sums(value):
    q, n = value.shape
    sums = value[:, 0:128] * value[:, 0:128]
    for at in range(128, n, 128):
        sums = sums + value[:, at : at + 128] * value[:, at : at + 128]
    return jnp.sum(jnp.concatenate([sums] * (128 // q), axis=0).T, axis=0, keepdims=True)


def square_row(value, z, cols):
    row = square_sums(value)
    row = jnp.broadcast_to(jnp.concatenate([row] * (cols // 128), axis=1), (8, cols))
    lane = lax.broadcasted_iota(jnp.int32, (8, cols), 1)
    return jnp.where(lane // value.shape[0] == z, row, 0.0)


def row_to_column(row):
    return jnp.broadcast_to(row, (128, row.shape[1])).T


def left_half_kernel(pieces, mine, other, *refs):
    _, z, _ = coords()
    left = mine[...] + other[...]
    both, sums = refs[-2:]
    both[...] = split_rows(left)
    squares = square_row(left, z, sums.shape[1])
    sums[...] = squares if pieces else refs[0][...] + squares
    if pieces:
        q, n = left.shape[0], left.shape[1] // 4
        for k in range(4):
            refs[0][pl.ds(pl.multiple_of((z ^ k) * q, q), q), :] = left[:, k * n : (k + 1) * n]


def left_half(mine, other, squares=None):
    q, docs = mine.shape
    extra = [] if squares is None else [squares]
    pieces = [f32(4 * q, docs // 4)] if squares is None else []
    return pl.pallas_call(
        functools.partial(left_half_kernel, bool(pieces)),
        out_shape=pieces + [bf16(2 * q, docs), f32(8, 4 * q)],
        compiler_params=params(8),
        cost_estimate=cost(8 * q * docs, 16 * q * docs),
        name="left_half",
    )(mine, other, *extra)


def backward_kernel(first, blocks, parts, hi_ref, lo_ref, both_ref, *refs):
    out_ref = refs[-1]
    both = both_ref[...]
    q = both.shape[0] // 2
    twice = jnp.concatenate([both, both], axis=1)
    for b in range(blocks):
        got = jnp.dot(
            twice,
            jnp.concatenate([hi_ref[first + b], lo_ref[first + b]], axis=0),
            preferred_element_type=jnp.float32,
        )
        got = got[:q] + got[q:]
        if "before" in parts:
            got = got + refs[0][(first + b) * q : (first + b + 1) * q, :]
        out_ref[b * q : (b + 1) * q, :] = got
    if "tail" in parts:
        out_ref[blocks * q :, :] = refs[parts.index("tail")][...]


def backward_part(rows, both, first, blocks, before=None, tail=None, tokens=()):
    q, docs = both.shape[0] // 2, both.shape[1]
    extra = {"before": before, "tail": tail, **{str(i): token for i, token in enumerate(tokens)}}
    extra = {name: value for name, value in extra.items() if value is not None}
    height = blocks * q + (0 if tail is None else tail.shape[0])
    return pl.pallas_call(
        functools.partial(backward_kernel, first, blocks, tuple(extra)),
        in_specs=[whole()] * (3 + len(extra)),
        out_specs=whole(),
        out_shape=f32(height, 256),
        compiler_params=params(8),
        cost_estimate=cost(8 * docs * 256 * 256 * blocks, 4 * docs * 256 * blocks),
        name="backward_part",
    )(*rows, both, *extra.values())


def far_sum_kernel(near, far, beta, send, beta_core):
    n = near.shape[0]
    beta_core[...] = beta[...] + far[n:, :]
    send[0:n, :] = near[...] + far[0:n, :]
    send[n:, :] = beta_core[...]


def far_sums(near, far, beta):
    rows = near.shape[0]
    return pl.pallas_call(
        far_sum_kernel,
        out_shape=[f32(rows + 8, 256), f32(8, 256)],
        compiler_params=params(8),
        cost_estimate=cost(near.size, near.size * 12),
        name="far_sums",
    )(near, far, beta)


def right_norm_kernel(docs_total, keep, peer, got, beta_core, right, out, sums, columns):
    _, z, _ = coords()
    q = right.shape[1]
    beta_sums = beta_core[...] + got[4 * q :, :]
    columns[...] = row_to_column(jnp.sqrt(beta_sums[0:1, :] / docs_total + epsilon))
    beta = columns[pl.ds(pl.multiple_of(z * q, q), q), :][:, 0:1]
    raws = []
    for k in range(4):
        rows = slice(k * q, (k + 1) * q)
        total = (keep[rows, :] + peer[rows, :]) + got[rows, :]
        at = (z ^ k) * (q + 8)
        out[pl.ds(pl.multiple_of(at, 8), q), :] = total
        out[pl.ds(pl.multiple_of(at + q, 8), 8), :] = beta_sums
        raws.append(total / beta - beta * right[k])
    line = square_sums(jnp.concatenate(raws, axis=1))
    for i in range(sums.shape[0]):
        sums[i] = line


def right_norm(docs_total, keep, peer, got, beta_core, right):
    q, rows = keep.shape[0] // 4, keep.shape[1]
    return pl.pallas_call(
        functools.partial(right_norm_kernel, docs_total),
        out_shape=[f32(4 * (q + 8), rows), f32(32, 1, 128)],
        scratch_shapes=[pltpu.VMEM((4 * q, 128), jnp.float32)],
        compiler_params=params(8),
        cost_estimate=cost(rows * q * 64, rows * q * 100),
        name="right_norm",
    )(keep, peer, got, beta_core, right)


def beta_of(pieces, q, docs_total):
    squares = [pieces[k * (q + 8) + q : k * (q + 8) + q + 1, :] for k in range(4)]
    return jnp.sqrt(((squares[0] + squares[1]) + (squares[2] + squares[3])) / docs_total + epsilon)


def finish_kernel(docs_total, feat_total, pieces, squares, right, search, phibar, rhobar,
                  right_out, search_out, alpha_out, phibar_out, rhobar_out):
    q = right.shape[1] // 4
    got = jnp.concatenate([pieces[k * (q + 8) : k * (q + 8) + q, :] for k in range(4)], axis=0).T
    parts = [squares[i] for i in range(32)]
    while len(parts) > 4:
        parts = [a + b for a, b in zip(parts[::2], parts[1::2])]
    low = lax.broadcasted_iota(jnp.int32, parts[0].shape, 1) < q
    parts = [jnp.where(low, parts[0], parts[1]), jnp.where(low, parts[2], parts[3])]
    alpha = jnp.sqrt(jnp.concatenate(parts, axis=1) / feat_total + epsilon)
    beta = beta_of(pieces, q, docs_total)
    rho = jnp.sqrt(rhobar[...] * rhobar[...] + beta * beta)
    cosine = rhobar[...] / rho
    sine = beta / rho
    theta = sine * alpha
    rhobar_out[...] = -cosine * alpha
    phibar_out[...] = sine * phibar[...]
    alpha_out[...] = alpha
    following = (got / beta - beta * right[...]) / alpha
    right_out[...] = following
    search_out[...] = following - (theta / rho) * search[...]


def finish(docs_total, feat_total, pieces, squares, right, search, phibar, rhobar):
    rows, cols = right.shape
    return pl.pallas_call(
        functools.partial(finish_kernel, docs_total, feat_total),
        out_shape=[f32(rows, cols)] * 2 + [f32(1, cols)] * 3,
        compiler_params=params(8),
        cost_estimate=cost(rows * cols * 16, rows * cols * 20),
        name="finish",
    )(pieces, squares, right, search, phibar, rhobar)


def left_out_kernel(docs_total, own, other, pieces, search, solution, phibar, rhobar, left_out, solution_out):
    _, _, y = coords()
    cols, half = own.shape
    beta = beta_of(pieces, cols // 4, docs_total)
    for part, ref in ((y, own), (1 - y, other)):
        left_out[pl.ds(pl.multiple_of(part * half, half), half), :] = ref[...].T / beta
    rho = jnp.sqrt(rhobar[...] * rhobar[...] + beta * beta)
    phi = rhobar[...] / rho * phibar[...]
    solution_out[...] = solution[...] + (phi / rho) * search[...]


def left_out(docs_total, own, other, pieces, search, solution, phibar, rhobar):
    cols, half = own.shape
    return pl.pallas_call(
        functools.partial(left_out_kernel, docs_total),
        out_shape=[f32(2 * half, cols), f32(*solution.shape)],
        compiler_params=params(8),
        cost_estimate=cost(half * cols * 8, half * cols * 30),
        name="left_out",
    )(own, other, pieces, search, solution, phibar, rhobar)


def swap(value, mask):
    return lax.ppermute(value, AXES, [(i, i ^ mask) for i in range(32)])


def along_z(value):
    return lax.all_to_all(value, AXES, 0, 0, axis_index_groups=Z_LINES, tiled=True)


def after(value, *earlier):
    return lax.optimization_barrier((value, *earlier))[0]


def by_columns(
    col_ids, col_vals, left_vec, right_vec, search_dir, solution_vec, alpha_prev, phibar, rhobar
):
    docs_total = left_vec.shape[0] * 16
    feat_total = right_vec.shape[0] * 32
    alpha_row, phibar_row, rhobar_row = (v.reshape(1, -1) for v in (alpha_prev, phibar, rhobar))

    stored, right_here, left_here = entries_of(col_ids.T, col_vals.T, right_vec, left_vec)
    entries = along_z(stored)
    right_turned = turn(right_here, stored, "turn_right")
    right_line = along_z(right_turned)
    left_line = along_z(turn(left_here, right_turned, "turn_left"))

    rows1, token1 = build(entries, 1)
    own = relative(right_line, token1, "relative_right")
    own_x = swap(own, X_BIT)
    own_peer = swap(own, CORE_BIT)
    rows0, _ = build(entries, 0, own)
    total1 = forward_part(rows1, [own, own_peer], (0, 8))
    total0 = forward_part(rows0, [own, own_peer], (0, 8))
    x_peer = swap(own_x, CORE_BIT)
    total1 = forward_part(rows1, [own_x], (4,), total1)
    total0 = forward_part(rows0, [own_x], (4,), total0)
    product1 = product_half(rows1, x_peer, total1, (12,))
    product0 = product_half(rows0, x_peer, total0, (12,), left_line, alpha_row)

    lefts, both0, beta0 = left_half(product0, swap(product1, Y_BIT))
    partial = backward_part(rows0, both0, 0, 16)
    left_own = along_z(lefts)
    both1, beta1 = left_half(product1, swap(product0, Y_BIT), beta0)
    far = swap(backward_part(rows1, both1, 12, 4, partial, beta1), CORE_BIT)
    near = backward_part(rows1, both1, 4, 4, partial)
    send, beta_core = far_sums(near, far, beta1)
    got = swap(send, X_BIT)
    peer = backward_part(rows1, both1, 8, 4, partial)
    left_other = swap(after(left_own, peer), Y_BIT)
    keep = backward_part(rows1, both1, 0, 4, partial)

    sent, sums = right_norm(docs_total, keep, swap(peer, CORE_BIT), got, beta_core, own)
    pieces = along_z(sent)
    squares = lax.all_to_all(after(sums, left_other), AXES, 0, 0, tiled=True)
    left_next, solution_next = left_out(
        docs_total, left_own, left_other, pieces, search_dir, solution_vec, phibar_row, rhobar_row
    )
    right_next, search_next, alpha_next, phibar_next, rhobar_next = finish(
        docs_total, feat_total, pieces, squares, right_vec, search_dir, phibar_row, rhobar_row
    )
    return (
        left_next,
        right_next,
        search_next,
        solution_next,
        alpha_next.reshape(-1),
        phibar_next.reshape(-1),
        rhobar_next.reshape(-1),
    )


def forward(col_ids, col_vals, table):
    picked = table[col_ids]
    return jnp.sum(col_vals.astype(jnp.float32)[:, :, None] * picked, axis=1)


def backward(col_ids, col_vals, rows_in, width):
    terms = col_vals.astype(jnp.float32)[:, :, None] * rows_in[:, None, :]
    return jax.ops.segment_sum(
        terms.reshape(-1, rows_in.shape[1]), col_ids.reshape(-1), num_segments=width
    )


def by_blocks(
    col_ids, col_vals, left_vec, right_vec, search_dir, solution_vec, alpha_prev, phibar, rhobar
):
    n_feat = lax.axis_size("feat")
    n_doc = lax.axis_size("doc")
    docs_total = left_vec.shape[0] * n_doc
    feat_total = right_vec.shape[0] * n_doc * n_feat
    table = lax.all_gather(right_vec, "doc", axis=0, tiled=True)
    total = lax.psum(forward(col_ids, col_vals, table), "feat")
    left_raw = total - alpha_prev[None, :] * left_vec
    row_part = jnp.sum(left_raw * left_raw, axis=0)
    beta_norm = jnp.sqrt(lax.psum(row_part, "doc") / docs_total + epsilon)
    left_next = left_raw / beta_norm[None, :]
    feature_part = lax.psum_scatter(
        backward(col_ids, col_vals, left_next, table.shape[0]), "doc", scatter_dimension=0, tiled=True
    )
    right_raw = feature_part - beta_norm[None, :] * right_vec
    squares = lax.psum(jnp.sum(right_raw * right_raw, axis=0), AXES)
    alpha_next = jnp.sqrt(squares / feat_total + epsilon)
    right_next = right_raw / alpha_next[None, :]
    rho_val = jnp.sqrt(rhobar * rhobar + beta_norm * beta_norm)
    cosine = rhobar / rho_val
    sine_val = beta_norm / rho_val
    theta_val = sine_val * alpha_next
    phi_val = cosine * phibar
    solution_next = solution_vec + (phi_val / rho_val)[None, :] * search_dir
    search_next = right_next - (theta_val / rho_val)[None, :] * search_dir
    return (
        left_next,
        right_next,
        search_next,
        solution_next,
        alpha_next,
        sine_val * phibar,
        -cosine * alpha_next,
    )


def solution(mesh):
    small = mesh.shape["doc"] == 16 and mesh.shape["feat"] == 2
    rows = P(("feat", "doc"), None)
    return jax.shard_map(
        by_columns if small else by_blocks,
        mesh=mesh,
        in_specs=(P("doc", "feat"), P("doc", "feat"), P("doc", None), rows, rows, rows, P(), P(), P()),
        out_specs=(P("doc", None), rows, rows, rows, P(), P(), P()),
        check_vma=False,
    )
```

```python
import functools

import jax
import jax.numpy as jnp
from jax import lax
from jax.experimental import pallas as pl
from jax.experimental.pallas import tpu as pltpu
from jax.sharding import PartitionSpec as P

epsilon = 1e-06
AXES = ("doc", "feat")
MIB = 1024 * 1024
SCALE = 64


Y_BIT, CORE_BIT, X_BIT, Z_SHIFT = 1, 2, 4, 3
NT = (((1,), (1,)), ((), ()))


def coords():
    d = lax.axis_index("doc")
    y = lax.axis_index("feat")
    return d, d >> 2, y


def params(mib):
    return pltpu.CompilerParams(vmem_limit_bytes=mib * MIB)


def cost(flops, nbytes):
    return pl.CostEstimate(flops=int(flops) // SCALE, bytes_accessed=int(nbytes) // SCALE, transcendentals=0)


def f32(*shape):
    return jax.ShapeDtypeStruct(shape, jnp.float32)


def bf16(*shape):
    return jax.ShapeDtypeStruct(shape, jnp.bfloat16)


def prepare_kernel(ids_hbm, vals_hbm, right_hbm, left_hbm, a0, a1, a2, a3, b0, b1, b2, b3,
                   ids, vals, wide, lines, right, left, turned, arrived):
    _, z, y = coords()
    q, rows = turned.shape[1:]
    copies = [
        pltpu.make_async_copy(src, dst, arrived.at[i])
        for i, (src, dst) in enumerate((
            (ids_hbm, ids),
            (vals_hbm, vals),
            (right_hbm, right),
            (left_hbm.at[pl.ds(pl.multiple_of(y * rows, rows), rows), :], left),
        ))
    ]
    for copy in copies:
        copy.start()
    count, n = ids.shape[0], lines.shape[0]
    half = n // 2
    groups = (b0, b1, b2, b3), (a0, a1, a2, a3)
    for part, ref in enumerate((ids, vals)):
        copies[part].wait()
        wide[...] = ref[...].astype(jnp.float32).T
        for r in range(256 // count):
            lines[:, r * count : (r + 1) * count] = wide[pl.ds(r, n, stride=256 // count), :]
        for rel, outs in enumerate(groups):
            value = lines[pl.ds(pl.multiple_of((y ^ rel) * half, half), half), :]
            for out in outs:
                out[part * half : (part + 1) * half, :] = value
    for copy, ref, outs in zip(copies[2:], (right, left), groups[::-1]):
        copy.wait()
        turned[...] = ref[...].T.reshape(turned.shape)
        for k, out in enumerate(outs):
            out[n:, :] = turned[z ^ k]


def prepare(ids, vals, right, left):
    rows, cols = right.shape
    n, q = ids.size // 256, cols // 4
    got = pl.pallas_call(
        prepare_kernel,
        in_specs=[pl.BlockSpec(memory_space=pltpu.HBM)] * 4,
        out_specs=[whole()] * 8,
        out_shape=[pltpu.VMEM((n + q, rows), jnp.float32)] * 8,
        scratch_shapes=[
            pltpu.VMEM(ids.shape, jnp.int32),
            pltpu.VMEM(vals.shape, jnp.bfloat16),
            pltpu.VMEM(ids.shape[::-1], jnp.float32),
            pltpu.VMEM((n, 256), jnp.float32),
            pltpu.VMEM(right.shape, jnp.float32),
            pltpu.VMEM(right.shape, jnp.float32),
            pltpu.VMEM((4, q, rows), jnp.float32),
            pltpu.SemaphoreType.DMA((4,)),
        ],
        compiler_params=params(60),
        cost_estimate=cost(0, rows * cols * 16),
        name="prepare",
    )(ids, vals, right, left)
    return got[:4], got[4:]


def stack_kernel(m0, m1, m2, m3, *refs):
    out = refs[-1]
    for k, m in enumerate((m0, m1, m2, m3)):
        out[k] = m[m.shape[0] - out.shape[1] :, :]


def stack(messages, q, name, *tokens):
    rows = messages[0].shape[1]
    return pl.pallas_call(
        stack_kernel,
        out_shape=f32(4, q, rows),
        compiler_params=params(8),
        cost_estimate=cost(0, 32 * q * rows),
        name=name,
    )(*messages, *tokens)


def build_kernel(e0, e1, e2, e3, *refs):
    hi_ref, lo_ref = refs[-2:]
    d, _, _ = coords()
    n = hi_ref.shape[1] // 64
    iota = lax.broadcasted_iota(jnp.int32, (256, 256), 0).astype(jnp.float32).astype(jnp.bfloat16)
    lane_doc = lax.broadcasted_iota(jnp.int32, (8, 256), 1) >> 4
    one = jnp.ones((256, 256), jnp.bfloat16)
    zero = jnp.zeros((256, 256), jnp.bfloat16)

    def spread(row):
        wide = jnp.broadcast_to(row, (16, 256)).astype(jnp.bfloat16)
        return jnp.broadcast_to(wide[None], (16, 16, 256)).reshape(256, 256)

    for k, entries in enumerate((e0, e1, e2, e3)):

        @pl.loop(0, n // 8)
        def _(step, k=k, entries=entries):
            at = pl.multiple_of(step * 8, 8)
            ids = entries[pl.ds(at, 8), :].astype(jnp.int32)
            vals = entries[pl.ds(n + at, 8), :]
            owner = (ids >> 8) ^ d
            block = ((owner & 1) << 3) | ((owner & 2) << 1) | (owner >> 2)
            code = (block * 16 + lane_doc).astype(jnp.float32)
            inner = (ids & 255).astype(jnp.float32)
            for t in range(8):
                pick = jnp.where(iota == spread(code[t : t + 1]), one, zero)
                weigh = jnp.where(iota == spread(inner[t : t + 1]), spread(vals[t : t + 1]), zero)
                dense = lax.dot_general(pick, weigh, NT, preferred_element_type=jnp.float32)
                high = dense.astype(jnp.bfloat16)
                low = (dense - high.astype(jnp.float32)).astype(jnp.bfloat16)
                docs = pl.ds(pl.multiple_of(k * 16 * n + step * 128 + 16 * t, 16), 16)
                hi_ref[:, docs, :] = high.reshape(16, 16, 256)
                lo_ref[:, docs, :] = low.reshape(16, 16, 256)


def whole():
    return pl.BlockSpec(memory_space=pltpu.VMEM)


def build(messages, lines, *tokens):
    docs = 4 * lines // 2 * 16
    return pl.pallas_call(
        build_kernel,
        in_specs=[whole()] * (4 + len(tokens)),
        out_specs=[whole()] * 2,
        out_shape=[pltpu.VMEM((16, docs, 256), jnp.bfloat16)] * 2,
        compiler_params=params(8),
        cost_estimate=cost(2 * docs * 16 * 256 * 256, docs * 4096 * 4),
        name="dense_rows",
    )(*messages, *tokens)


def split_rows(value):
    high = value.astype(jnp.bfloat16)
    low = (value - high.astype(jnp.float32)).astype(jnp.bfloat16)
    return jnp.concatenate([high, low], axis=0)


def add_products(hi_ref, lo_ref, vecs, blocks, total):
    for vec, first in zip(vecs, blocks):
        for pair in (0, 2):
            lhs, rhs = [], []
            for k in (pair, pair + 1):
                both = split_rows(vec[k])
                lhs += [hi_ref[first + k], lo_ref[first + k]]
                rhs += [both, both]
            total[...] += lax.dot_general(
                jnp.concatenate(lhs, axis=1), jnp.concatenate(rhs, axis=1), NT, preferred_element_type=jnp.float32
            )


def forward_kernel(blocks, has_before, hi_ref, lo_ref, *refs):
    count = len(blocks)
    total = refs[-1]
    total[...] = refs[count][...] if has_before else jnp.zeros_like(total)
    add_products(hi_ref, lo_ref, refs[:count], blocks, total)


def forward_part(rows, vecs, blocks, before=None, tokens=()):
    docs, q = rows[0].shape[1], vecs[0].shape[1]
    n = 4 * len(blocks)
    extra = [*tokens] if before is None else [before, *tokens]
    return pl.pallas_call(
        functools.partial(forward_kernel, blocks, before is not None),
        in_specs=[whole()] * (2 + len(vecs) + len(extra)),
        out_specs=whole(),
        out_shape=f32(docs, 2 * q),
        compiler_params=params(8),
        cost_estimate=cost(8 * docs * 256 * 256 * n, 4 * docs * 256 * n),
        name="forward_part",
    )(*rows, *vecs, *extra)


def product_kernel(blocks, hi_ref, lo_ref, vec, before, *refs):
    out, total, columns = refs[-3:]
    total[...] = before[...]
    add_products(hi_ref, lo_ref, (vec,), blocks, total)
    turned = total[...].T
    q = out.shape[0]
    product = turned[:q] + turned[q:]
    if len(refs) == 3:
        out[...] = product
        return
    _, z, _ = coords()
    *messages, alpha = refs[:5]
    columns[...] = row_to_column(alpha[...])
    scale = columns[pl.ds(pl.multiple_of(z * q, q), q), :][:, 0:1]
    for k, m in enumerate(messages):
        at = slice(k * m.shape[1], (k + 1) * m.shape[1])
        out[:, at] = product[:, at] - scale * m[m.shape[0] - q :, :]


def product_half(rows, vec, before, blocks, *left):
    docs, q = rows[0].shape[1], vec.shape[1]
    return pl.pallas_call(
        functools.partial(product_kernel, blocks),
        in_specs=[whole()] * (4 + len(left)),
        out_specs=whole(),
        out_shape=f32(q, docs),
        scratch_shapes=[pltpu.VMEM((docs, 2 * q), jnp.float32), pltpu.VMEM((4 * q, 128), jnp.float32)],
        compiler_params=params(8),
        cost_estimate=cost(8 * docs * 256 * 256 * 4, 16 * docs * 256),
        name="product_half",
    )(*rows, vec, before, *left)


def square_sums(value):
    q, n = value.shape
    sums = value[:, 0:128] * value[:, 0:128]
    for at in range(128, n, 128):
        sums = sums + value[:, at : at + 128] * value[:, at : at + 128]
    return jnp.sum(jnp.concatenate([sums] * (128 // q), axis=0).T, axis=0, keepdims=True)


def square_row(value, z, cols):
    row = square_sums(value)
    row = jnp.broadcast_to(jnp.concatenate([row] * (cols // 128), axis=1), (8, cols))
    lane = lax.broadcasted_iota(jnp.int32, (8, cols), 1)
    return jnp.where(lane // value.shape[0] == z, row, 0.0)


def row_to_column(row):
    return jnp.broadcast_to(row, (128, row.shape[1])).T


def left_half_kernel(mine, other, *refs):
    _, z, _ = coords()
    left = mine[...] + other[...]
    both, sums = refs[-2:]
    both[...] = split_rows(left)
    squares = square_row(left, z, sums.shape[1])
    sums[...] = refs[0][...] + squares if len(refs) == 4 else squares
    if len(refs) > 4:
        n = left.shape[1] // 4
        for k, out in enumerate(refs[:4]):
            out[...] = left[:, k * n : (k + 1) * n]


def left_half(mine, other, squares=None, token=None):
    q, docs = mine.shape
    extra = [] if squares is None else [squares, token]
    pieces = [f32(q, docs // 4)] * 4 if squares is None else []
    return pl.pallas_call(
        left_half_kernel,
        out_shape=pieces + [bf16(2 * q, docs), f32(8, 4 * q)],
        compiler_params=params(8),
        cost_estimate=cost(8 * q * docs, 16 * q * docs),
        name="left_half",
    )(mine, other, *extra)


def backward_kernel(first, blocks, parts, hi_ref, lo_ref, both_ref, *refs):
    out_ref = refs[-1]
    both = both_ref[...]
    q = both.shape[0] // 2
    twice = jnp.concatenate([both, both], axis=1)
    for b in range(blocks):
        got = jnp.dot(
            twice,
            jnp.concatenate([hi_ref[first + b], lo_ref[first + b]], axis=0),
            preferred_element_type=jnp.float32,
        )
        got = got[:q] + got[q:]
        if "before" in parts:
            got = got + refs[0][(first + b) * q : (first + b + 1) * q, :]
        out_ref[b * q : (b + 1) * q, :] = got
    if "tail" in parts:
        out_ref[blocks * q :, :] = refs[parts.index("tail")][...]


def backward_part(rows, both, first, blocks, before=None, tail=None, tokens=()):
    q, docs = both.shape[0] // 2, both.shape[1]
    extra = {"before": before, "tail": tail, **{str(i): token for i, token in enumerate(tokens)}}
    extra = {name: value for name, value in extra.items() if value is not None}
    height = blocks * q + (0 if tail is None else tail.shape[0])
    return pl.pallas_call(
        functools.partial(backward_kernel, first, blocks, tuple(extra)),
        in_specs=[whole()] * (3 + len(extra)),
        out_specs=whole(),
        out_shape=f32(height, 256),
        compiler_params=params(8),
        cost_estimate=cost(8 * docs * 256 * 256 * blocks, 4 * docs * 256 * blocks),
        name="backward_part",
    )(*rows, both, *extra.values())


def far_sum_kernel(near, far, beta, send, beta_core):
    n = near.shape[0]
    beta_core[...] = beta[...] + far[n:, :]
    send[0:n, :] = near[...] + far[0:n, :]
    send[n:, :] = beta_core[...]


def far_sums(near, far, beta):
    rows = near.shape[0]
    return pl.pallas_call(
        far_sum_kernel,
        out_shape=[f32(rows + 8, 256), f32(8, 256)],
        compiler_params=params(8),
        cost_estimate=cost(near.size, near.size * 12),
        name="far_sums",
    )(near, far, beta)


def right_norm_kernel(docs_total, keep, peer, got, beta_core, right, g0, g1, g2, g3, sums, columns):
    _, z, _ = coords()
    q = right.shape[1]
    beta_sums = beta_core[...] + got[4 * q :, :]
    columns[...] = row_to_column(jnp.sqrt(beta_sums[0:1, :] / docs_total + epsilon))
    beta = columns[pl.ds(pl.multiple_of(z * q, q), q), :][:, 0:1]
    raws = []
    for k, g in enumerate((g0, g1, g2, g3)):
        rows = slice(k * q, (k + 1) * q)
        total = (keep[rows, :] + peer[rows, :]) + got[rows, :]
        g[0:q, :] = total
        g[q:, :] = beta_sums
        raws.append(total / beta - beta * right[k])
    sums[...] = jnp.broadcast_to(square_sums(jnp.concatenate(raws, axis=1)), sums.shape)


def right_norm(docs_total, keep, peer, got, beta_core, right):
    q, rows = keep.shape[0] // 4, keep.shape[1]
    *pieces, sums = pl.pallas_call(
        functools.partial(right_norm_kernel, docs_total),
        out_shape=[f32(q + 8, rows)] * 4 + [f32(32, 128)],
        scratch_shapes=[pltpu.VMEM((4 * q, 128), jnp.float32)],
        compiler_params=params(8),
        cost_estimate=cost(rows * q * 64, rows * q * 100),
        name="right_norm",
    )(keep, peer, got, beta_core, right)
    return pieces, sums.reshape(32, 1, 128)


def beta_of(pieces, q, docs_total):
    squares = [g[q : q + 1, :] for g in pieces]
    return jnp.sqrt(((squares[0] + squares[1]) + (squares[2] + squares[3])) / docs_total + epsilon)


def finish_kernel(docs_total, feat_total, g0, g1, g2, g3, squares, right, search, phibar, rhobar,
                  right_out, search_out, alpha_out, phibar_out, rhobar_out, turned):
    _, z, _ = coords()
    q = turned.shape[1]
    for k, g in enumerate((g0, g1, g2, g3)):
        turned[z ^ k] = g[0:q, :]
    got = turned[...].reshape(-1, turned.shape[2]).T
    parts = [squares[i] for i in range(32)]
    while len(parts) > 4:
        parts = [a + b for a, b in zip(parts[::2], parts[1::2])]
    low = lax.broadcasted_iota(jnp.int32, parts[0].shape, 1) < q
    parts = [jnp.where(low, parts[0], parts[1]), jnp.where(low, parts[2], parts[3])]
    alpha = jnp.sqrt(jnp.concatenate(parts, axis=1) / feat_total + epsilon)
    beta = beta_of((g0, g1, g2, g3), q, docs_total)
    rho = jnp.sqrt(rhobar[...] * rhobar[...] + beta * beta)
    cosine = rhobar[...] / rho
    sine = beta / rho
    theta = sine * alpha
    rhobar_out[...] = -cosine * alpha
    phibar_out[...] = sine * phibar[...]
    alpha_out[...] = alpha
    following = (got / beta - beta * right[...]) / alpha
    right_out[...] = following
    search_out[...] = following - (theta / rho) * search[...]


def finish(docs_total, feat_total, pieces, squares, right, search, phibar, rhobar):
    rows, cols = right.shape
    return pl.pallas_call(
        functools.partial(finish_kernel, docs_total, feat_total),
        out_shape=[f32(rows, cols)] * 2 + [f32(1, cols)] * 3,
        scratch_shapes=[pltpu.VMEM((4, cols // 4, rows), jnp.float32)],
        compiler_params=params(8),
        cost_estimate=cost(rows * cols * 16, rows * cols * 20),
        name="finish",
    )(*pieces, squares, right, search, phibar, rhobar)


def left_out_kernel(docs_total, own, other, g0, g1, g2, g3, search, solution, phibar, rhobar, left_out, solution_out, turned):
    _, z, y = coords()
    q, half = turned.shape[1:]
    beta = beta_of((g0, g1, g2, g3), q, docs_total)
    for part, ref in ((y, own), (1 - y, other)):
        for k in range(4):
            turned[z ^ k] = ref[k]
        left_out[pl.ds(pl.multiple_of(part * half, half), half), :] = turned[...].reshape(-1, half).T / beta
    rho = jnp.sqrt(rhobar[...] * rhobar[...] + beta * beta)
    phi = rhobar[...] / rho * phibar[...]
    solution_out[...] = solution[...] + (phi / rho) * search[...]


def left_out(docs_total, own, other, pieces, search, solution, phibar, rhobar):
    _, q, half = own.shape
    return pl.pallas_call(
        functools.partial(left_out_kernel, docs_total),
        out_shape=[f32(2 * half, 4 * q), f32(*solution.shape)],
        scratch_shapes=[pltpu.VMEM((4, q, half), jnp.float32)],
        compiler_params=params(8),
        cost_estimate=cost(half * q * 32, half * q * 120),
        name="left_out",
    )(own, other, *pieces, search, solution, phibar, rhobar)


def swap(value, mask):
    return lax.ppermute(value, AXES, [(i, i ^ mask) for i in range(32)])


def along_z(values):
    return [values[0]] + [swap(values[k], k << Z_SHIFT) for k in (1, 2, 3)]


def after(value, *earlier):
    return lax.optimization_barrier((value, *earlier))[0]


def by_columns(
    col_ids, col_vals, left_vec, right_vec, search_dir, solution_vec, alpha_prev, phibar, rhobar
):
    docs_total = left_vec.shape[0] * 16
    feat_total = right_vec.shape[0] * 32
    alpha_row, phibar_row, rhobar_row = (v.reshape(1, -1) for v in (alpha_prev, phibar, rhobar))

    first, second = prepare(col_ids.T, col_vals.T, right_vec, left_vec)
    first = along_z(first)
    second = along_z(second)
    q = right_vec.shape[1] // 4
    lines = first[0].shape[0] - q

    own = stack(first, q, "stack_right", second[1])
    own_x = swap(own, X_BIT)
    own_peer = swap(own, CORE_BIT)
    rows1 = build(first, lines, own)
    total1 = forward_part(rows1, [own, own_peer], (0, 8), None, second[2:3])
    x_peer = swap(after(own_x, total1), CORE_BIT)
    total1 = forward_part(rows1, [own_x], (4,), total1)
    product1 = product_half(rows1, x_peer, total1, (12,))
    rows0 = build(second, lines, product1)
    total0 = forward_part(rows0, [own, own_peer], (0, 8))
    total0 = forward_part(rows0, [own_x], (4,), total0)
    product0 = product_half(rows0, x_peer, total0, (12,), *second, alpha_row)

    *lefts, both0, beta0 = left_half(product0, swap(product1, Y_BIT))
    partial = backward_part(rows0, both0, 0, 16)
    left_own = stack(along_z(lefts), q, "stack_left")
    both1, beta1 = left_half(product1, swap(product0, Y_BIT), beta0, partial)
    far = swap(backward_part(rows1, both1, 12, 4, partial, beta1, [left_own]), CORE_BIT)
    near = backward_part(rows1, both1, 4, 4, partial)
    send, beta_core = far_sums(near, far, beta1)
    got = swap(send, X_BIT)
    peer = backward_part(rows1, both1, 8, 4, partial)
    left_other = swap(after(left_own, peer), Y_BIT)
    keep = backward_part(rows1, both1, 0, 4, partial)

    sent, sums = right_norm(docs_total, keep, swap(peer, CORE_BIT), got, beta_core, own)
    pieces = along_z(sent)
    squares = lax.all_to_all(after(sums, left_other), AXES, 0, 0, tiled=True)
    left_next, solution_next = left_out(
        docs_total, left_own, left_other, pieces, search_dir, solution_vec, phibar_row, rhobar_row
    )
    right_next, search_next, alpha_next, phibar_next, rhobar_next = finish(
        docs_total, feat_total, pieces, squares, right_vec, search_dir, phibar_row, rhobar_row
    )
    return (
        left_next,
        right_next,
        search_next,
        solution_next,
        alpha_next.reshape(-1),
        phibar_next.reshape(-1),
        rhobar_next.reshape(-1),
    )


def forward(col_ids, col_vals, table):
    picked = table[col_ids]
    return jnp.sum(col_vals.astype(jnp.float32)[:, :, None] * picked, axis=1)


def backward(col_ids, col_vals, rows_in, width):
    terms = col_vals.astype(jnp.float32)[:, :, None] * rows_in[:, None, :]
    return jax.ops.segment_sum(
        terms.reshape(-1, rows_in.shape[1]), col_ids.reshape(-1), num_segments=width
    )


def by_blocks(
    col_ids, col_vals, left_vec, right_vec, search_dir, solution_vec, alpha_prev, phibar, rhobar
):
    n_feat = lax.axis_size("feat")
    n_doc = lax.axis_size("doc")
    docs_total = left_vec.shape[0] * n_doc
    feat_total = right_vec.shape[0] * n_doc * n_feat
    table = lax.all_gather(right_vec, "doc", axis=0, tiled=True)
    total = lax.psum(forward(col_ids, col_vals, table), "feat")
    left_raw = total - alpha_prev[None, :] * left_vec
    row_part = jnp.sum(left_raw * left_raw, axis=0)
    beta_norm = jnp.sqrt(lax.psum(row_part, "doc") / docs_total + epsilon)
    left_next = left_raw / beta_norm[None, :]
    feature_part = lax.psum_scatter(
        backward(col_ids, col_vals, left_next, table.shape[0]), "doc", scatter_dimension=0, tiled=True
    )
    right_raw = feature_part - beta_norm[None, :] * right_vec
    squares = lax.psum(jnp.sum(right_raw * right_raw, axis=0), AXES)
    alpha_next = jnp.sqrt(squares / feat_total + epsilon)
    right_next = right_raw / alpha_next[None, :]
    rho_val = jnp.sqrt(rhobar * rhobar + beta_norm * beta_norm)
    cosine = rhobar / rho_val
    sine_val = beta_norm / rho_val
    theta_val = sine_val * alpha_next
    phi_val = cosine * phibar
    solution_next = solution_vec + (phi_val / rho_val)[None, :] * search_dir
    search_next = right_next - (theta_val / rho_val)[None, :] * search_dir
    return (
        left_next,
        right_next,
        search_next,
        solution_next,
        alpha_next,
        sine_val * phibar,
        -cosine * alpha_next,
    )


def solution(mesh):
    small = mesh.shape["doc"] == 16 and mesh.shape["feat"] == 2
    rows = P(("feat", "doc"), None)
    return jax.shard_map(
        by_columns if small else by_blocks,
        mesh=mesh,
        in_specs=(P("doc", "feat"), P("doc", "feat"), P("doc", None), rows, rows, rows, P(), P(), P()),
        out_specs=(P("doc", None), rows, rows, rows, P(), P(), P()),
        check_vma=False,
    )
```

```python
import functools

import jax
import jax.numpy as jnp
from jax import lax
from jax.experimental import pallas as pl
from jax.experimental.pallas import tpu as pltpu
from jax.sharding import PartitionSpec as P

epsilon = 1e-06
AXES = ("doc", "feat")
MIB = 1024 * 1024


Y_BIT, CORE_BIT, X_BIT, Z_SHIFT = 1, 2, 4, 3
NT = (((1,), (1,)), ((), ()))


def coords():
    d = lax.axis_index("doc")
    y = lax.axis_index("feat")
    return d, d >> 2, y


def params(mib):
    return pltpu.CompilerParams(vmem_limit_bytes=mib * MIB)


def cost(flops, nbytes, scale=64):
    return pl.CostEstimate(flops=int(flops) // scale, bytes_accessed=int(nbytes) // scale, transcendentals=0)


def f32(*shape):
    return jax.ShapeDtypeStruct(shape, jnp.float32)


def bf16(*shape):
    return jax.ShapeDtypeStruct(shape, jnp.bfloat16)


def prepare_kernel(ids_hbm, vals_hbm, right_hbm, left_hbm, stored, m0, m1, m2, m3,
                   ids, vals, wide, right, left, turned, arrived):
    _, z, y = coords()
    q, rows = turned.shape[1:]
    copies = [
        pltpu.make_async_copy(src, dst, arrived.at[i])
        for i, (src, dst) in enumerate((
            (ids_hbm, ids),
            (vals_hbm, vals),
            (right_hbm, right),
            (left_hbm.at[pl.ds(pl.multiple_of(y * rows, rows), rows), :], left),
        ))
    ]
    for copy in copies:
        copy.start()
    lines, count = stored.shape[0] // 2, ids.shape[0]
    for part, ref in enumerate((ids, vals)):
        copies[part].wait()
        wide[...] = ref[...].astype(jnp.float32).T
        for r in range(256 // count):
            stored[part * lines : (part + 1) * lines, r * count : (r + 1) * count] = wide[
                pl.ds(r, lines, stride=256 // count), :
            ]
    for part, ref in enumerate((right, left)):
        copies[2 + part].wait()
        turned[...] = ref[...].T.reshape(turned.shape)
        for k, out in enumerate((m0, m1, m2, m3)):
            out[part * q : (part + 1) * q, :] = turned[z ^ k]


def prepare(ids, vals, right, left):
    rows, cols = right.shape
    q = cols // 4
    got = pl.pallas_call(
        prepare_kernel,
        in_specs=[pl.BlockSpec(memory_space=pltpu.HBM)] * 4,
        out_specs=[whole()] * 5,
        out_shape=[pltpu.VMEM((ids.size // 128, 256), jnp.float32)] + [pltpu.VMEM((2 * q, rows), jnp.float32)] * 4,
        scratch_shapes=[
            pltpu.VMEM(ids.shape, jnp.int32),
            pltpu.VMEM(vals.shape, jnp.bfloat16),
            pltpu.VMEM(ids.shape[::-1], jnp.float32),
            pltpu.VMEM(right.shape, jnp.float32),
            pltpu.VMEM(right.shape, jnp.float32),
            pltpu.VMEM((4, q, rows), jnp.float32),
            pltpu.SemaphoreType.DMA((4,)),
        ],
        compiler_params=params(60),
        cost_estimate=cost(0, rows * cols * 16),
        name="prepare",
    )(ids, vals, right, left)
    return got[0], got[1:]


def stack_kernel(m0, m1, m2, m3, *refs):
    out = refs[-1]
    for k, m in enumerate((m0, m1, m2, m3)):
        out[k] = m[0 : out.shape[1], :]


def stack(messages, q, name, *tokens):
    rows = messages[0].shape[1]
    return pl.pallas_call(
        stack_kernel,
        out_shape=f32(4, q, rows),
        compiler_params=params(8),
        cost_estimate=cost(0, 32 * q * rows),
        name=name,
    )(*messages, *tokens)


def build_kernel(rel, e0, e1, e2, e3, *refs):
    hi_ref, lo_ref, token = refs[-3:]
    token[...] = jnp.zeros_like(token)
    d, _, y = coords()
    n = e0.shape[0] // 2
    iota = lax.broadcasted_iota(jnp.int32, (256, 256), 0).astype(jnp.float32).astype(jnp.bfloat16)
    lane_doc = lax.broadcasted_iota(jnp.int32, (8, 256), 1) >> 4
    one = jnp.ones((256, 256), jnp.bfloat16)
    zero = jnp.zeros((256, 256), jnp.bfloat16)

    def spread(row):
        wide = jnp.broadcast_to(row, (16, 256)).astype(jnp.bfloat16)
        return jnp.broadcast_to(wide[None], (16, 16, 256)).reshape(256, 256)

    for k, entries in enumerate((e0, e1, e2, e3)):

        @pl.loop(0, n // 16)
        def _(step, k=k, entries=entries):
            at = pl.multiple_of((y ^ rel) * (n // 2) + step * 8, 8)
            ids = entries[pl.ds(at, 8), :].astype(jnp.int32)
            vals = entries[pl.ds(n + at, 8), :]
            owner = (ids >> 8) ^ d
            block = ((owner & 1) << 3) | ((owner & 2) << 1) | (owner >> 2)
            code = (block * 16 + lane_doc).astype(jnp.float32)
            inner = (ids & 255).astype(jnp.float32)
            for t in range(8):
                pick = jnp.where(iota == spread(code[t : t + 1]), one, zero)
                weigh = jnp.where(iota == spread(inner[t : t + 1]), spread(vals[t : t + 1]), zero)
                dense = lax.dot_general(pick, weigh, NT, preferred_element_type=jnp.float32)
                high = dense.astype(jnp.bfloat16)
                low = (dense - high.astype(jnp.float32)).astype(jnp.bfloat16)
                docs = pl.ds(pl.multiple_of(k * 8 * n + step * 128 + 16 * t, 16), 16)
                hi_ref[:, docs, :] = high.reshape(16, 16, 256)
                lo_ref[:, docs, :] = low.reshape(16, 16, 256)


def whole():
    return pl.BlockSpec(memory_space=pltpu.VMEM)


def build(entries, rel, *tokens):
    docs = 4 * (entries[0].shape[0] // 4 * 16)
    *rows, token = pl.pallas_call(
        functools.partial(build_kernel, rel),
        in_specs=[whole()] * (4 + len(tokens)),
        out_specs=[whole()] * 3,
        out_shape=[pltpu.VMEM((16, docs, 256), jnp.bfloat16)] * 2 + [f32(8, 128)],
        compiler_params=params(8),
        cost_estimate=cost(2 * docs * 16 * 256 * 256, docs * 4096 * 4, 1 if rel else 64),
        name="dense_rows",
    )(*entries, *tokens)
    return rows, token


def split_rows(value):
    high = value.astype(jnp.bfloat16)
    low = (value - high.astype(jnp.float32)).astype(jnp.bfloat16)
    return jnp.concatenate([high, low], axis=0)


def add_products(hi_ref, lo_ref, vecs, blocks, total):
    for vec, first in zip(vecs, blocks):
        for pair in (0, 2):
            lhs, rhs = [], []
            for k in (pair, pair + 1):
                both = split_rows(vec[k])
                lhs += [hi_ref[first + k], lo_ref[first + k]]
                rhs += [both, both]
            total[...] += lax.dot_general(
                jnp.concatenate(lhs, axis=1), jnp.concatenate(rhs, axis=1), NT, preferred_element_type=jnp.float32
            )


def forward_kernel(blocks, hi_ref, lo_ref, *refs):
    count = len(blocks)
    total = refs[-1]
    total[...] = refs[count][...] if len(refs) > count + 1 else jnp.zeros_like(total)
    add_products(hi_ref, lo_ref, refs[:count], blocks, total)


def forward_part(rows, vecs, blocks, before=None):
    docs, q = rows[0].shape[1], vecs[0].shape[1]
    n = 4 * len(blocks)
    extra = [] if before is None else [before]
    return pl.pallas_call(
        functools.partial(forward_kernel, blocks),
        in_specs=[whole()] * (2 + len(vecs) + len(extra)),
        out_specs=whole(),
        out_shape=f32(docs, 2 * q),
        compiler_params=params(8),
        cost_estimate=cost(8 * docs * 256 * 256 * n, 4 * docs * 256 * n),
        name="forward_part",
    )(*rows, *vecs, *extra)


def product_kernel(blocks, hi_ref, lo_ref, vec, before, *refs):
    out, total, columns = refs[-3:]
    total[...] = before[...]
    add_products(hi_ref, lo_ref, (vec,), blocks, total)
    turned = total[...].T
    q = out.shape[0]
    product = turned[:q] + turned[q:]
    if len(refs) == 3:
        out[...] = product
        return
    _, z, _ = coords()
    *messages, alpha = refs[:5]
    columns[...] = row_to_column(alpha[...])
    scale = columns[pl.ds(pl.multiple_of(z * q, q), q), :][:, 0:1]
    for k, m in enumerate(messages):
        at = slice(k * m.shape[1], (k + 1) * m.shape[1])
        out[:, at] = product[:, at] - scale * m[q:, :]


def product_half(rows, vec, before, blocks, *left):
    docs, q = rows[0].shape[1], vec.shape[1]
    return pl.pallas_call(
        functools.partial(product_kernel, blocks),
        in_specs=[whole()] * (4 + len(left)),
        out_specs=whole(),
        out_shape=f32(q, docs),
        scratch_shapes=[pltpu.VMEM((docs, 2 * q), jnp.float32), pltpu.VMEM((4 * q, 128), jnp.float32)],
        compiler_params=params(8),
        cost_estimate=cost(8 * docs * 256 * 256 * 4, 16 * docs * 256),
        name="product_half",
    )(*rows, vec, before, *left)


def square_sums(value):
    q, n = value.shape
    sums = value[:, 0:128] * value[:, 0:128]
    for at in range(128, n, 128):
        sums = sums + value[:, at : at + 128] * value[:, at : at + 128]
    return jnp.sum(jnp.concatenate([sums] * (128 // q), axis=0).T, axis=0, keepdims=True)


def square_row(value, z, cols):
    row = square_sums(value)
    row = jnp.broadcast_to(jnp.concatenate([row] * (cols // 128), axis=1), (8, cols))
    lane = lax.broadcasted_iota(jnp.int32, (8, cols), 1)
    return jnp.where(lane // value.shape[0] == z, row, 0.0)


def row_to_column(row):
    return jnp.broadcast_to(row, (128, row.shape[1])).T


def left_half_kernel(mine, other, *refs):
    _, z, _ = coords()
    left = mine[...] + other[...]
    both, sums = refs[-2:]
    both[...] = split_rows(left)
    squares = square_row(left, z, sums.shape[1])
    sums[...] = refs[0][...] + squares if len(refs) == 4 else squares
    if len(refs) > 4:
        n = left.shape[1] // 4
        for k, out in enumerate(refs[:4]):
            out[...] = left[:, k * n : (k + 1) * n]


def left_half(mine, other, squares=None, token=None):
    q, docs = mine.shape
    extra = [] if squares is None else [squares, token]
    pieces = [f32(q, docs // 4)] * 4 if squares is None else []
    return pl.pallas_call(
        left_half_kernel,
        out_shape=pieces + [bf16(2 * q, docs), f32(8, 4 * q)],
        compiler_params=params(8),
        cost_estimate=cost(8 * q * docs, 16 * q * docs),
        name="left_half",
    )(mine, other, *extra)


def backward_kernel(first, blocks, parts, hi_ref, lo_ref, both_ref, *refs):
    out_ref = refs[-1]
    both = both_ref[...]
    q = both.shape[0] // 2
    twice = jnp.concatenate([both, both], axis=1)
    for b in range(blocks):
        got = jnp.dot(
            twice,
            jnp.concatenate([hi_ref[first + b], lo_ref[first + b]], axis=0),
            preferred_element_type=jnp.float32,
        )
        got = got[:q] + got[q:]
        if "before" in parts:
            got = got + refs[0][(first + b) * q : (first + b + 1) * q, :]
        out_ref[b * q : (b + 1) * q, :] = got
    if "tail" in parts:
        out_ref[blocks * q :, :] = refs[parts.index("tail")][...]


def backward_part(rows, both, first, blocks, before=None, tail=None, tokens=()):
    q, docs = both.shape[0] // 2, both.shape[1]
    extra = {"before": before, "tail": tail, **{str(i): token for i, token in enumerate(tokens)}}
    extra = {name: value for name, value in extra.items() if value is not None}
    height = blocks * q + (0 if tail is None else tail.shape[0])
    return pl.pallas_call(
        functools.partial(backward_kernel, first, blocks, tuple(extra)),
        in_specs=[whole()] * (3 + len(extra)),
        out_specs=whole(),
        out_shape=f32(height, 256),
        compiler_params=params(8),
        cost_estimate=cost(8 * docs * 256 * 256 * blocks, 4 * docs * 256 * blocks),
        name="backward_part",
    )(*rows, both, *extra.values())


def far_sum_kernel(near, far, beta, send, beta_core):
    n = near.shape[0]
    beta_core[...] = beta[...] + far[n:, :]
    send[0:n, :] = near[...] + far[0:n, :]
    send[n:, :] = beta_core[...]


def far_sums(near, far, beta):
    rows = near.shape[0]
    return pl.pallas_call(
        far_sum_kernel,
        out_shape=[f32(rows + 8, 256), f32(8, 256)],
        compiler_params=params(8),
        cost_estimate=cost(near.size, near.size * 12),
        name="far_sums",
    )(near, far, beta)


def right_norm_kernel(docs_total, keep, peer, got, beta_core, right, g0, g1, g2, g3, sums, columns):
    _, z, _ = coords()
    q = right.shape[1]
    beta_sums = beta_core[0:1, :] + got[4 * q : 4 * q + 1, :]
    columns[...] = row_to_column(jnp.sqrt(beta_sums / docs_total + epsilon))
    beta = columns[pl.ds(pl.multiple_of(z * q, q), q), :][:, 0:1]
    raws = []
    for k, g in enumerate((g0, g1, g2, g3)):
        rows = slice(k * q, (k + 1) * q)
        total = (keep[rows, :] + peer[rows, :]) + got[rows, :]
        g[...] = total
        raws.append(total / beta - beta * right[k])
    line = square_sums(jnp.concatenate(raws, axis=1))
    folded = beta_sums[:, :128] + beta_sums[:, 128:]
    folded = folded + jnp.concatenate([folded[:, q:], folded[:, :q]], axis=1)
    low = lax.broadcasted_iota(jnp.int32, line.shape, 1) < q
    sums[...] = jnp.broadcast_to(jnp.where(low, line, folded), sums.shape)


def right_norm(docs_total, keep, peer, got, beta_core, right):
    q, rows = keep.shape[0] // 4, keep.shape[1]
    *pieces, sums = pl.pallas_call(
        functools.partial(right_norm_kernel, docs_total),
        out_shape=[f32(q, rows)] * 4 + [f32(32, 128)],
        scratch_shapes=[pltpu.VMEM((4 * q, 128), jnp.float32)],
        compiler_params=params(8),
        cost_estimate=cost(rows * q * 64, rows * q * 100),
        name="right_norm",
    )(keep, peer, got, beta_core, right)
    return pieces, sums.reshape(32, 1, 128)


def finish_kernel(docs_total, feat_total, g0, g1, g2, g3, squares, own, other, right, search, solution, phibar, rhobar,
                  left_out, right_out, search_out, solution_out, alpha_out, phibar_out, rhobar_out, turned):
    _, z, y = coords()
    q, half = turned.shape[1:]
    parts = [squares[i] for i in range(32)]
    high = [jnp.concatenate([parts[8 * i][:, q:], parts[8 * i][:, :q]], axis=1) if i % 2 == 0 else parts[8 * i] for i in range(4)]
    while len(parts) > 4:
        parts = [a + b for a, b in zip(parts[::2], parts[1::2])]
    parts[1::2] = [jnp.concatenate([p[:, q:], p[:, :q]], axis=1) for p in parts[1::2]]
    low = lax.broadcasted_iota(jnp.int32, parts[0].shape, 1) < q
    alpha_sums, beta_sums = (
        jnp.concatenate([jnp.where(low, p[0], p[1]), jnp.where(low, p[2], p[3])], axis=1) for p in (parts, high)
    )
    alpha = jnp.sqrt(alpha_sums / feat_total + epsilon)
    beta = jnp.sqrt(beta_sums / docs_total + epsilon)
    for part, ref in ((y, own), (1 - y, other)):
        for k in range(4):
            turned[z ^ k] = ref[k]
        left_out[pl.ds(pl.multiple_of(part * half, half), half), :] = turned[...].reshape(-1, half).T / beta
    rho = jnp.sqrt(rhobar[...] * rhobar[...] + beta * beta)
    cosine = rhobar[...] / rho
    sine = beta / rho
    theta = sine * alpha
    phi = cosine * phibar[...]
    rhobar_out[...] = -cosine * alpha
    phibar_out[...] = sine * phibar[...]
    alpha_out[...] = alpha
    for k, g in enumerate((g0, g1, g2, g3)):
        turned[z ^ k] = g[...]
    got = turned[...].reshape(-1, half).T
    following = (got / beta - beta * right[...]) / alpha
    right_out[...] = following
    search_out[...] = following - (theta / rho) * search[...]
    solution_out[...] = solution[...] + (phi / rho) * search[...]


def finish(docs_total, feat_total, pieces, squares, own, other, right, search, solution, phibar, rhobar):
    rows, cols = right.shape
    return pl.pallas_call(
        functools.partial(finish_kernel, docs_total, feat_total),
        out_shape=[f32(2 * rows, cols)] + [f32(rows, cols)] * 3 + [f32(1, cols)] * 3,
        scratch_shapes=[pltpu.VMEM((4, cols // 4, rows), jnp.float32)],
        compiler_params=params(12),
        cost_estimate=cost(rows * cols * 16, rows * cols * 20),
        name="finish",
    )(*pieces, squares, own, other, right, search, solution, phibar, rhobar)


def swap(value, mask):
    return lax.ppermute(value, AXES, [(i, i ^ mask) for i in range(32)])


def along_z(values):
    return [values[0]] + [swap(values[k], k << Z_SHIFT) for k in (1, 2, 3)]


def after(value, *earlier):
    return lax.optimization_barrier((value, *earlier))[0]


def by_columns(
    col_ids, col_vals, left_vec, right_vec, search_dir, solution_vec, alpha_prev, phibar, rhobar
):
    docs_total = left_vec.shape[0] * 16
    feat_total = right_vec.shape[0] * 32
    alpha_row, phibar_row, rhobar_row = (v.reshape(1, -1) for v in (alpha_prev, phibar, rhobar))

    stored, messages = prepare(col_ids.T, col_vals.T, right_vec, left_vec)
    entries = along_z([stored] * 4)
    messages = along_z([messages[0]] + [after(m, entries[1]) for m in messages[1:]])
    q = right_vec.shape[1] // 4

    rows1, token1 = build(entries, 1)
    own = stack(messages, q, "stack_right", token1)
    own_x = swap(own, X_BIT)
    own_peer = swap(own, CORE_BIT)
    rows0, token0 = build(entries, 0, own)
    total1 = forward_part(rows1, [own, own_peer], (0, 8))
    x_peer = swap(after(own_x, total1, token0), CORE_BIT)
    total1 = forward_part(rows1, [own_x], (4,), total1)
    product1 = product_half(rows1, x_peer, total1, (12,))
    total0 = forward_part(rows0, [own, own_peer], (0, 8))
    total0 = forward_part(rows0, [own_x], (4,), total0)
    product0 = product_half(rows0, x_peer, total0, (12,), *messages, alpha_row)

    *lefts, both0, beta0 = left_half(product0, swap(product1, Y_BIT))
    partial = backward_part(rows0, both0, 0, 16)
    left_own = stack(along_z(lefts), q, "stack_left")
    both1, beta1 = left_half(product1, swap(product0, Y_BIT), beta0, partial)
    far = swap(backward_part(rows1, both1, 12, 4, partial, beta1, [left_own]), CORE_BIT)
    near = backward_part(rows1, both1, 4, 4, partial)
    send, beta_core = far_sums(near, far, beta1)
    got = swap(send, X_BIT)
    peer = backward_part(rows1, both1, 8, 4, partial)
    left_other = swap(after(left_own, peer), Y_BIT)
    keep = backward_part(rows1, both1, 0, 4, partial)

    sent, sums = right_norm(docs_total, keep, swap(peer, CORE_BIT), got, beta_core, own)
    pieces = along_z(sent)
    squares = lax.all_to_all(after(sums, left_other), AXES, 0, 0, tiled=True)
    left_next, right_next, search_next, solution_next, alpha_next, phibar_next, rhobar_next = finish(
        docs_total, feat_total, pieces, squares, left_own, left_other,
        right_vec, search_dir, solution_vec, phibar_row, rhobar_row,
    )
    return (
        left_next,
        right_next,
        search_next,
        solution_next,
        alpha_next.reshape(-1),
        phibar_next.reshape(-1),
        rhobar_next.reshape(-1),
    )


def forward(col_ids, col_vals, table):
    picked = table[col_ids]
    return jnp.sum(col_vals.astype(jnp.float32)[:, :, None] * picked, axis=1)


def backward(col_ids, col_vals, rows_in, width):
    terms = col_vals.astype(jnp.float32)[:, :, None] * rows_in[:, None, :]
    return jax.ops.segment_sum(
        terms.reshape(-1, rows_in.shape[1]), col_ids.reshape(-1), num_segments=width
    )


def by_blocks(
    col_ids, col_vals, left_vec, right_vec, search_dir, solution_vec, alpha_prev, phibar, rhobar
):
    n_feat = lax.axis_size("feat")
    n_doc = lax.axis_size("doc")
    docs_total = left_vec.shape[0] * n_doc
    feat_total = right_vec.shape[0] * n_doc * n_feat
    table = lax.all_gather(right_vec, "doc", axis=0, tiled=True)
    total = lax.psum(forward(col_ids, col_vals, table), "feat")
    left_raw = total - alpha_prev[None, :] * left_vec
    row_part = jnp.sum(left_raw * left_raw, axis=0)
    beta_norm = jnp.sqrt(lax.psum(row_part, "doc") / docs_total + epsilon)
    left_next = left_raw / beta_norm[None, :]
    feature_part = lax.psum_scatter(
        backward(col_ids, col_vals, left_next, table.shape[0]), "doc", scatter_dimension=0, tiled=True
    )
    right_raw = feature_part - beta_norm[None, :] * right_vec
    squares = lax.psum(jnp.sum(right_raw * right_raw, axis=0), AXES)
    alpha_next = jnp.sqrt(squares / feat_total + epsilon)
    right_next = right_raw / alpha_next[None, :]
    rho_val = jnp.sqrt(rhobar * rhobar + beta_norm * beta_norm)
    cosine = rhobar / rho_val
    sine_val = beta_norm / rho_val
    theta_val = sine_val * alpha_next
    phi_val = cosine * phibar
    solution_next = solution_vec + (phi_val / rho_val)[None, :] * search_dir
    search_next = right_next - (theta_val / rho_val)[None, :] * search_dir
    return (
        left_next,
        right_next,
        search_next,
        solution_next,
        alpha_next,
        sine_val * phibar,
        -cosine * alpha_next,
    )


def solution(mesh):
    small = mesh.shape["doc"] == 16 and mesh.shape["feat"] == 2
    rows = P(("feat", "doc"), None)
    return jax.shard_map(
        by_columns if small else by_blocks,
        mesh=mesh,
        in_specs=(P("doc", "feat"), P("doc", "feat"), P("doc", None), rows, rows, rows, P(), P(), P()),
        out_specs=(P("doc", None), rows, rows, rows, P(), P(), P()),
        check_vma=False,
    )
```

```python
import functools

import jax
import jax.numpy as jnp
from jax import lax
from jax.experimental import pallas as pl
from jax.experimental.pallas import tpu as pltpu
from jax.sharding import PartitionSpec as P

epsilon = 1e-06
AXES = ("doc", "feat")
MIB = 1024 * 1024


Y_BIT, CORE_BIT, X_BIT, Z_SHIFT = 1, 2, 4, 3
NT = (((1,), (1,)), ((), ()))


def coords():
    d = lax.axis_index("doc")
    y = lax.axis_index("feat")
    return d, d >> 2, y


def params(mib):
    return pltpu.CompilerParams(vmem_limit_bytes=mib * MIB)


def cost(flops, nbytes, scale=64):
    return pl.CostEstimate(flops=int(flops) // scale, bytes_accessed=int(nbytes) // scale, transcendentals=0)


def f32(*shape):
    return jax.ShapeDtypeStruct(shape, jnp.float32)


def bf16(*shape):
    return jax.ShapeDtypeStruct(shape, jnp.bfloat16)


def prepare_kernel(ids_hbm, vals_hbm, right_hbm, left_hbm, stored, m0, m1, m2, m3,
                   ids, vals, wide, right, left, turned, arrived):
    _, z, y = coords()
    q, rows = turned.shape[1:]
    copies = [
        pltpu.make_async_copy(src, dst, arrived.at[i])
        for i, (src, dst) in enumerate((
            (ids_hbm, ids),
            (vals_hbm, vals),
            (right_hbm, right),
            (left_hbm.at[pl.ds(pl.multiple_of(y * rows, rows), rows), :], left),
        ))
    ]
    for copy in copies:
        copy.start()
    lines, count = stored.shape[0] // 2, ids.shape[0]
    for part, ref in enumerate((ids, vals)):
        copies[part].wait()
        wide[...] = ref[...].astype(jnp.float32).T
        for r in range(256 // count):
            stored[part * lines : (part + 1) * lines, r * count : (r + 1) * count] = wide[
                pl.ds(r, lines, stride=256 // count), :
            ]
    for part, ref in enumerate((right, left)):
        copies[2 + part].wait()
        turned[...] = ref[...].T.reshape(turned.shape)
        for k, out in enumerate((m0, m1, m2, m3)):
            out[part * q : (part + 1) * q, :] = turned[z ^ k]


def prepare(ids, vals, right, left):
    rows, cols = right.shape
    q = cols // 4
    got = pl.pallas_call(
        prepare_kernel,
        in_specs=[pl.BlockSpec(memory_space=pltpu.HBM)] * 4,
        out_specs=[whole()] * 5,
        out_shape=[pltpu.VMEM((ids.size // 128, 256), jnp.float32)] + [pltpu.VMEM((2 * q, rows), jnp.float32)] * 4,
        scratch_shapes=[
            pltpu.VMEM(ids.shape, jnp.int32),
            pltpu.VMEM(vals.shape, jnp.bfloat16),
            pltpu.VMEM(ids.shape[::-1], jnp.float32),
            pltpu.VMEM(right.shape, jnp.float32),
            pltpu.VMEM(right.shape, jnp.float32),
            pltpu.VMEM((4, q, rows), jnp.float32),
            pltpu.SemaphoreType.DMA((4,)),
        ],
        compiler_params=params(60),
        cost_estimate=cost(0, rows * cols * 16),
        name="prepare",
    )(ids, vals, right, left)
    return got[0], got[1:]


def stack_kernel(m0, m1, m2, m3, *refs):
    out = refs[-1]
    for k, m in enumerate((m0, m1, m2, m3)):
        out[k] = m[0 : out.shape[1], :]


def stack(messages, q, name, *tokens):
    rows = messages[0].shape[1]
    return pl.pallas_call(
        stack_kernel,
        out_shape=f32(4, q, rows),
        compiler_params=params(8),
        cost_estimate=cost(0, 32 * q * rows),
        name=name,
    )(*messages, *tokens)


def build_kernel(rel, e0, e1, e2, e3, *refs):
    hi_ref, lo_ref, token = refs[-3:]
    token[...] = jnp.zeros_like(token)
    d, _, y = coords()
    n = e0.shape[0] // 2
    iota = lax.broadcasted_iota(jnp.int32, (256, 256), 0).astype(jnp.float32).astype(jnp.bfloat16)
    lane_doc = lax.broadcasted_iota(jnp.int32, (8, 256), 1) >> 4
    one = jnp.ones((256, 256), jnp.bfloat16)
    zero = jnp.zeros((256, 256), jnp.bfloat16)

    def spread(row):
        wide = jnp.broadcast_to(row, (16, 256)).astype(jnp.bfloat16)
        return jnp.broadcast_to(wide[None], (16, 16, 256)).reshape(256, 256)

    for k, entries in enumerate((e0, e1, e2, e3)):

        @pl.loop(0, n // 16)
        def _(step, k=k, entries=entries):
            at = pl.multiple_of((y ^ rel) * (n // 2) + step * 8, 8)
            ids = entries[pl.ds(at, 8), :].astype(jnp.int32)
            vals = entries[pl.ds(n + at, 8), :]
            owner = (ids >> 8) ^ d
            block = ((owner & 1) << 3) | ((owner & 2) << 1) | (owner >> 2)
            code = (block * 16 + lane_doc).astype(jnp.float32)
            inner = (ids & 255).astype(jnp.float32)
            for t in range(8):
                pick = jnp.where(iota == spread(code[t : t + 1]), one, zero)
                weigh = jnp.where(iota == spread(inner[t : t + 1]), spread(vals[t : t + 1]), zero)
                dense = lax.dot_general(pick, weigh, NT, preferred_element_type=jnp.float32)
                high = dense.astype(jnp.bfloat16)
                low = (dense - high.astype(jnp.float32)).astype(jnp.bfloat16)
                docs = pl.ds(pl.multiple_of(k * 8 * n + step * 128 + 16 * t, 16), 16)
                hi_ref[:, docs, :] = high.reshape(16, 16, 256)
                lo_ref[:, docs, :] = low.reshape(16, 16, 256)


def whole():
    return pl.BlockSpec(memory_space=pltpu.VMEM)


def build(entries, rel, *tokens):
    docs = 4 * (entries[0].shape[0] // 4 * 16)
    *rows, token = pl.pallas_call(
        functools.partial(build_kernel, rel),
        in_specs=[whole()] * (4 + len(tokens)),
        out_specs=[whole()] * 3,
        out_shape=[pltpu.VMEM((16, docs, 256), jnp.bfloat16)] * 2 + [f32(8, 128)],
        compiler_params=params(8),
        cost_estimate=cost(2 * docs * 16 * 256 * 256, docs * 4096 * 4, 1 if rel else 64),
        name="dense_rows",
    )(*entries, *tokens)
    return rows, token


def split_rows(value):
    high = value.astype(jnp.bfloat16)
    low = (value - high.astype(jnp.float32)).astype(jnp.bfloat16)
    return jnp.concatenate([high, low], axis=0)


def add_products(hi_ref, lo_ref, vecs, blocks, total):
    for vec, first in zip(vecs, blocks):
        for pair in (0, 2):
            lhs, rhs = [], []
            for k in (pair, pair + 1):
                both = split_rows(vec[k])
                lhs += [hi_ref[first + k], lo_ref[first + k]]
                rhs += [both, both]
            total[...] += lax.dot_general(
                jnp.concatenate(lhs, axis=1), jnp.concatenate(rhs, axis=1), NT, preferred_element_type=jnp.float32
            )


def forward_kernel(blocks, has_before, hi_ref, lo_ref, *refs):
    count = len(blocks)
    total = refs[-1]
    total[...] = refs[count][...] if has_before else jnp.zeros_like(total)
    add_products(hi_ref, lo_ref, refs[:count], blocks, total)


def forward_part(rows, vecs, blocks, before=None, tokens=()):
    docs, q = rows[0].shape[1], vecs[0].shape[1]
    n = 4 * len(blocks)
    extra = [*tokens] if before is None else [before, *tokens]
    return pl.pallas_call(
        functools.partial(forward_kernel, blocks, before is not None),
        in_specs=[whole()] * (2 + len(vecs) + len(extra)),
        out_specs=whole(),
        out_shape=f32(docs, 2 * q),
        compiler_params=params(8),
        cost_estimate=cost(8 * docs * 256 * 256 * n, 4 * docs * 256 * n),
        name="forward_part",
    )(*rows, *vecs, *extra)


def product_kernel(blocks, hi_ref, lo_ref, vec, before, *refs):
    out, total, columns = refs[-3:]
    total[...] = before[...]
    add_products(hi_ref, lo_ref, (vec,), blocks, total)
    turned = total[...].T
    q = out.shape[0]
    product = turned[:q] + turned[q:]
    if len(refs) == 3:
        out[...] = product
        return
    _, z, _ = coords()
    *messages, alpha = refs[:5]
    columns[...] = row_to_column(alpha[...])
    scale = columns[pl.ds(pl.multiple_of(z * q, q), q), :][:, 0:1]
    for k, m in enumerate(messages):
        at = slice(k * m.shape[1], (k + 1) * m.shape[1])
        out[:, at] = product[:, at] - scale * m[q:, :]


def product_half(rows, vec, before, blocks, *left):
    docs, q = rows[0].shape[1], vec.shape[1]
    return pl.pallas_call(
        functools.partial(product_kernel, blocks),
        in_specs=[whole()] * (4 + len(left)),
        out_specs=whole(),
        out_shape=f32(q, docs),
        scratch_shapes=[pltpu.VMEM((docs, 2 * q), jnp.float32), pltpu.VMEM((4 * q, 128), jnp.float32)],
        compiler_params=params(8),
        cost_estimate=cost(8 * docs * 256 * 256 * 4, 16 * docs * 256),
        name="product_half",
    )(*rows, vec, before, *left)


def square_sums(value):
    q, n = value.shape
    sums = value[:, 0:128] * value[:, 0:128]
    for at in range(128, n, 128):
        sums = sums + value[:, at : at + 128] * value[:, at : at + 128]
    return jnp.sum(jnp.concatenate([sums] * (128 // q), axis=0).T, axis=0, keepdims=True)


def square_row(value, z, cols):
    row = square_sums(value)
    row = jnp.broadcast_to(jnp.concatenate([row] * (cols // 128), axis=1), (8, cols))
    lane = lax.broadcasted_iota(jnp.int32, (8, cols), 1)
    return jnp.where(lane // value.shape[0] == z, row, 0.0)


def row_to_column(row):
    return jnp.broadcast_to(row, (128, row.shape[1])).T


def left_half_kernel(mine, other, *refs):
    _, z, _ = coords()
    left = mine[...] + other[...]
    both, sums = refs[-2:]
    both[...] = split_rows(left)
    squares = square_row(left, z, sums.shape[1])
    sums[...] = refs[0][...] + squares if len(refs) == 4 else squares
    if len(refs) > 4:
        n = left.shape[1] // 4
        for k, out in enumerate(refs[:4]):
            out[...] = left[:, k * n : (k + 1) * n]


def left_half(mine, other, squares=None, token=None):
    q, docs = mine.shape
    extra = [] if squares is None else [squares, token]
    pieces = [f32(q, docs // 4)] * 4 if squares is None else []
    return pl.pallas_call(
        left_half_kernel,
        out_shape=pieces + [bf16(2 * q, docs), f32(8, 4 * q)],
        compiler_params=params(8),
        cost_estimate=cost(8 * q * docs, 16 * q * docs),
        name="left_half",
    )(mine, other, *extra)


def backward_kernel(first, blocks, parts, hi_ref, lo_ref, both_ref, *refs):
    out_ref = refs[-1]
    both = both_ref[...]
    q = both.shape[0] // 2
    twice = jnp.concatenate([both, both], axis=1)
    for b in range(blocks):
        got = jnp.dot(
            twice,
            jnp.concatenate([hi_ref[first + b], lo_ref[first + b]], axis=0),
            preferred_element_type=jnp.float32,
        )
        got = got[:q] + got[q:]
        if "before" in parts:
            got = got + refs[0][(first + b) * q : (first + b + 1) * q, :]
        out_ref[b * q : (b + 1) * q, :] = got
    if "tail" in parts:
        out_ref[blocks * q :, :] = refs[parts.index("tail")][...]


def backward_part(rows, both, first, blocks, before=None, tail=None, tokens=()):
    q, docs = both.shape[0] // 2, both.shape[1]
    extra = {"before": before, "tail": tail, **{str(i): token for i, token in enumerate(tokens)}}
    extra = {name: value for name, value in extra.items() if value is not None}
    height = blocks * q + (0 if tail is None else tail.shape[0])
    return pl.pallas_call(
        functools.partial(backward_kernel, first, blocks, tuple(extra)),
        in_specs=[whole()] * (3 + len(extra)),
        out_specs=whole(),
        out_shape=f32(height, 256),
        compiler_params=params(8),
        cost_estimate=cost(8 * docs * 256 * 256 * blocks, 4 * docs * 256 * blocks),
        name="backward_part",
    )(*rows, both, *extra.values())


def far_sum_kernel(near, far, beta, send, beta_core):
    n = near.shape[0]
    beta_core[...] = beta[...] + far[n:, :]
    send[0:n, :] = near[...] + far[0:n, :]
    send[n:, :] = beta_core[...]


def far_sums(near, far, beta):
    rows = near.shape[0]
    return pl.pallas_call(
        far_sum_kernel,
        out_shape=[f32(rows + 8, 256), f32(8, 256)],
        compiler_params=params(8),
        cost_estimate=cost(near.size, near.size * 12),
        name="far_sums",
    )(near, far, beta)


def right_norm_kernel(docs_total, keep, peer, got, beta_core, right, g0, g1, g2, g3, sums, columns):
    _, z, _ = coords()
    q = right.shape[1]
    beta_sums = beta_core[0:1, :] + got[4 * q : 4 * q + 1, :]
    columns[...] = row_to_column(jnp.sqrt(beta_sums / docs_total + epsilon))
    beta = columns[pl.ds(pl.multiple_of(z * q, q), q), :][:, 0:1]
    raws = []
    for k, g in enumerate((g0, g1, g2, g3)):
        rows = slice(k * q, (k + 1) * q)
        total = (keep[rows, :] + peer[rows, :]) + got[rows, :]
        g[...] = total
        raws.append(total / beta - beta * right[k])
    line = square_sums(jnp.concatenate(raws, axis=1))
    folded = beta_sums[:, :128] + beta_sums[:, 128:]
    folded = folded + jnp.concatenate([folded[:, q:], folded[:, :q]], axis=1)
    low = lax.broadcasted_iota(jnp.int32, line.shape, 1) < q
    sums[...] = jnp.broadcast_to(jnp.where(low, line, folded), sums.shape)


def right_norm(docs_total, keep, peer, got, beta_core, right):
    q, rows = keep.shape[0] // 4, keep.shape[1]
    *pieces, sums = pl.pallas_call(
        functools.partial(right_norm_kernel, docs_total),
        out_shape=[f32(q, rows)] * 4 + [f32(32, 128)],
        scratch_shapes=[pltpu.VMEM((4 * q, 128), jnp.float32)],
        compiler_params=params(8),
        cost_estimate=cost(rows * q * 64, rows * q * 100),
        name="right_norm",
    )(keep, peer, got, beta_core, right)
    return pieces, sums.reshape(32, 1, 128)


def finish_kernel(docs_total, feat_total, g0, g1, g2, g3, squares, own, other, right, search, solution, phibar, rhobar,
                  left_out, right_out, search_out, solution_out, alpha_out, phibar_out, rhobar_out, turned):
    _, z, y = coords()
    q, half = turned.shape[1:]
    parts = [squares[i] for i in range(32)]
    high = [jnp.concatenate([parts[8 * i][:, q:], parts[8 * i][:, :q]], axis=1) if i % 2 == 0 else parts[8 * i] for i in range(4)]
    while len(parts) > 4:
        parts = [a + b for a, b in zip(parts[::2], parts[1::2])]
    parts[1::2] = [jnp.concatenate([p[:, q:], p[:, :q]], axis=1) for p in parts[1::2]]
    low = lax.broadcasted_iota(jnp.int32, parts[0].shape, 1) < q
    alpha_sums, beta_sums = (
        jnp.concatenate([jnp.where(low, p[0], p[1]), jnp.where(low, p[2], p[3])], axis=1) for p in (parts, high)
    )
    alpha = jnp.sqrt(alpha_sums / feat_total + epsilon)
    beta = jnp.sqrt(beta_sums / docs_total + epsilon)
    for part, ref in ((y, own), (1 - y, other)):
        for k in range(4):
            turned[z ^ k] = ref[k]
        left_out[pl.ds(pl.multiple_of(part * half, half), half), :] = turned[...].reshape(-1, half).T / beta
    rho = jnp.sqrt(rhobar[...] * rhobar[...] + beta * beta)
    cosine = rhobar[...] / rho
    sine = beta / rho
    theta = sine * alpha
    phi = cosine * phibar[...]
    rhobar_out[...] = -cosine * alpha
    phibar_out[...] = sine * phibar[...]
    alpha_out[...] = alpha
    for k, g in enumerate((g0, g1, g2, g3)):
        turned[z ^ k] = g[...]
    got = turned[...].reshape(-1, half).T
    following = (got / beta - beta * right[...]) / alpha
    right_out[...] = following
    search_out[...] = following - (theta / rho) * search[...]
    solution_out[...] = solution[...] + (phi / rho) * search[...]


def finish(docs_total, feat_total, pieces, squares, own, other, right, search, solution, phibar, rhobar):
    rows, cols = right.shape
    return pl.pallas_call(
        functools.partial(finish_kernel, docs_total, feat_total),
        out_shape=[f32(2 * rows, cols)] + [f32(rows, cols)] * 3 + [f32(1, cols)] * 3,
        scratch_shapes=[pltpu.VMEM((4, cols // 4, rows), jnp.float32)],
        compiler_params=params(12),
        cost_estimate=cost(rows * cols * 16, rows * cols * 20),
        name="finish",
    )(*pieces, squares, own, other, right, search, solution, phibar, rhobar)


def swap(value, mask):
    return lax.ppermute(value, AXES, [(i, i ^ mask) for i in range(32)])


def along_z(values):
    return [values[0]] + [swap(values[k], k << Z_SHIFT) for k in (1, 2, 3)]


def after(value, *earlier):
    return lax.optimization_barrier((value, *earlier))[0]


def by_columns(
    col_ids, col_vals, left_vec, right_vec, search_dir, solution_vec, alpha_prev, phibar, rhobar
):
    docs_total = left_vec.shape[0] * 16
    feat_total = right_vec.shape[0] * 32
    alpha_row, phibar_row, rhobar_row = (v.reshape(1, -1) for v in (alpha_prev, phibar, rhobar))

    stored, messages = prepare(col_ids.T, col_vals.T, right_vec, left_vec)
    entries = along_z([stored] * 4)
    messages = along_z([messages[0]] + [after(m, entries[1]) for m in messages[1:]])
    q = right_vec.shape[1] // 4

    rows1, token1 = build(entries, 1)
    own = stack(messages, q, "stack_right", token1)
    own_x = swap(own, X_BIT)
    own_peer = swap(own, CORE_BIT)
    rows0, token0 = build(entries, 0, own)
    total1 = forward_part(rows1, [own, own_peer], (0, 8), None, [token0])
    x_peer = swap(after(own_x, total1), CORE_BIT)
    total1 = forward_part(rows1, [own_x], (4,), total1)
    product1 = product_half(rows1, x_peer, total1, (12,))
    total0 = forward_part(rows0, [own, own_peer], (0, 8))
    total0 = forward_part(rows0, [own_x], (4,), total0)
    product0 = product_half(rows0, x_peer, total0, (12,), *messages, alpha_row)

    *lefts, both0, beta0 = left_half(product0, swap(product1, Y_BIT))
    partial = backward_part(rows0, both0, 0, 16)
    left_own = stack(along_z(lefts), q, "stack_left")
    both1, beta1 = left_half(product1, swap(product0, Y_BIT), beta0, partial)
    far = swap(backward_part(rows1, both1, 12, 4, partial, beta1, [left_own]), CORE_BIT)
    near = backward_part(rows1, both1, 4, 4, partial)
    send, beta_core = far_sums(near, far, beta1)
    got = swap(send, X_BIT)
    peer = backward_part(rows1, both1, 8, 4, partial)
    left_other = swap(after(left_own, peer), Y_BIT)
    keep = backward_part(rows1, both1, 0, 4, partial)

    sent, sums = right_norm(docs_total, keep, swap(peer, CORE_BIT), got, beta_core, own)
    pieces = along_z(sent)
    squares = lax.all_to_all(after(sums, left_other), AXES, 0, 0, tiled=True)
    left_next, right_next, search_next, solution_next, alpha_next, phibar_next, rhobar_next = finish(
        docs_total, feat_total, pieces, squares, left_own, left_other,
        right_vec, search_dir, solution_vec, phibar_row, rhobar_row,
    )
    return (
        left_next,
        right_next,
        search_next,
        solution_next,
        alpha_next.reshape(-1),
        phibar_next.reshape(-1),
        rhobar_next.reshape(-1),
    )


def forward(col_ids, col_vals, table):
    picked = table[col_ids]
    return jnp.sum(col_vals.astype(jnp.float32)[:, :, None] * picked, axis=1)


def backward(col_ids, col_vals, rows_in, width):
    terms = col_vals.astype(jnp.float32)[:, :, None] * rows_in[:, None, :]
    return jax.ops.segment_sum(
        terms.reshape(-1, rows_in.shape[1]), col_ids.reshape(-1), num_segments=width
    )


def by_blocks(
    col_ids, col_vals, left_vec, right_vec, search_dir, solution_vec, alpha_prev, phibar, rhobar
):
    n_feat = lax.axis_size("feat")
    n_doc = lax.axis_size("doc")
    docs_total = left_vec.shape[0] * n_doc
    feat_total = right_vec.shape[0] * n_doc * n_feat
    table = lax.all_gather(right_vec, "doc", axis=0, tiled=True)
    total = lax.psum(forward(col_ids, col_vals, table), "feat")
    left_raw = total - alpha_prev[None, :] * left_vec
    row_part = jnp.sum(left_raw * left_raw, axis=0)
    beta_norm = jnp.sqrt(lax.psum(row_part, "doc") / docs_total + epsilon)
    left_next = left_raw / beta_norm[None, :]
    feature_part = lax.psum_scatter(
        backward(col_ids, col_vals, left_next, table.shape[0]), "doc", scatter_dimension=0, tiled=True
    )
    right_raw = feature_part - beta_norm[None, :] * right_vec
    squares = lax.psum(jnp.sum(right_raw * right_raw, axis=0), AXES)
    alpha_next = jnp.sqrt(squares / feat_total + epsilon)
    right_next = right_raw / alpha_next[None, :]
    rho_val = jnp.sqrt(rhobar * rhobar + beta_norm * beta_norm)
    cosine = rhobar / rho_val
    sine_val = beta_norm / rho_val
    theta_val = sine_val * alpha_next
    phi_val = cosine * phibar
    solution_next = solution_vec + (phi_val / rho_val)[None, :] * search_dir
    search_next = right_next - (theta_val / rho_val)[None, :] * search_dir
    return (
        left_next,
        right_next,
        search_next,
        solution_next,
        alpha_next,
        sine_val * phibar,
        -cosine * alpha_next,
    )


def solution(mesh):
    small = mesh.shape["doc"] == 16 and mesh.shape["feat"] == 2
    rows = P(("feat", "doc"), None)
    return jax.shard_map(
        by_columns if small else by_blocks,
        mesh=mesh,
        in_specs=(P("doc", "feat"), P("doc", "feat"), P("doc", None), rows, rows, rows, P(), P(), P()),
        out_specs=(P("doc", None), rows, rows, rows, P(), P(), P()),
        check_vma=False,
    )
```

```python
import functools

import jax
import jax.numpy as jnp
from jax import lax
from jax.experimental import pallas as pl
from jax.experimental.pallas import tpu as pltpu
from jax.sharding import PartitionSpec as P

epsilon = 1e-06
AXES = ("doc", "feat")
MIB = 1024 * 1024


Y_BIT, CORE_BIT, X_BIT, Z_SHIFT = 1, 2, 4, 3
NT = (((1,), (1,)), ((), ()))


def coords():
    d = lax.axis_index("doc")
    y = lax.axis_index("feat")
    return d, d >> 2, y


def params(mib):
    return pltpu.CompilerParams(vmem_limit_bytes=mib * MIB)


def cost(flops, nbytes, scale=64):
    return pl.CostEstimate(flops=int(flops) // scale, bytes_accessed=int(nbytes) // scale, transcendentals=0)


def f32(*shape):
    return jax.ShapeDtypeStruct(shape, jnp.float32)


def bf16(*shape):
    return jax.ShapeDtypeStruct(shape, jnp.bfloat16)


def prepare_kernel(ids_hbm, vals_hbm, right_hbm, left_hbm, stored, m0, m1, m2, m3,
                   ids, vals, wide, right, left, turned, arrived):
    _, z, y = coords()
    q, rows = turned.shape[1:]
    copies = [
        pltpu.make_async_copy(src, dst, arrived.at[i])
        for i, (src, dst) in enumerate((
            (ids_hbm, ids),
            (vals_hbm, vals),
            (right_hbm, right),
            (left_hbm.at[pl.ds(pl.multiple_of(y * rows, rows), rows), :], left),
        ))
    ]
    for copy in copies:
        copy.start()
    lines, count = stored.shape[0] // 2, ids.shape[0]
    for part, ref in enumerate((ids, vals)):
        copies[part].wait()
        wide[...] = ref[...].astype(jnp.float32).T
        for r in range(256 // count):
            stored[part * lines : (part + 1) * lines, r * count : (r + 1) * count] = wide[
                pl.ds(r, lines, stride=256 // count), :
            ]
    for part, ref in enumerate((right, left)):
        copies[2 + part].wait()
        turned[...] = ref[...].T.reshape(turned.shape)
        for k, out in enumerate((m0, m1, m2, m3)):
            out[part * q : (part + 1) * q, :] = turned[z ^ k]


def prepare(ids, vals, right, left):
    rows, cols = right.shape
    q = cols // 4
    got = pl.pallas_call(
        prepare_kernel,
        in_specs=[pl.BlockSpec(memory_space=pltpu.HBM)] * 4,
        out_specs=[whole()] * 5,
        out_shape=[pltpu.VMEM((ids.size // 128, 256), jnp.float32)] + [pltpu.VMEM((2 * q, rows), jnp.float32)] * 4,
        scratch_shapes=[
            pltpu.VMEM(ids.shape, jnp.int32),
            pltpu.VMEM(vals.shape, jnp.bfloat16),
            pltpu.VMEM(ids.shape[::-1], jnp.float32),
            pltpu.VMEM(right.shape, jnp.float32),
            pltpu.VMEM(right.shape, jnp.float32),
            pltpu.VMEM((4, q, rows), jnp.float32),
            pltpu.SemaphoreType.DMA((4,)),
        ],
        compiler_params=params(60),
        cost_estimate=cost(0, rows * cols * 16),
        name="prepare",
    )(ids, vals, right, left)
    return got[0], got[1:]


def stack_kernel(m0, m1, m2, m3, *refs):
    out = refs[-1]
    for k, m in enumerate((m0, m1, m2, m3)):
        out[k] = m[0 : out.shape[1], :]


def stack(messages, q, name, *tokens):
    rows = messages[0].shape[1]
    return pl.pallas_call(
        stack_kernel,
        out_shape=f32(4, q, rows),
        compiler_params=params(8),
        cost_estimate=cost(0, 32 * q * rows),
        name=name,
    )(*messages, *tokens)


def build_kernel(rel, e0, e1, e2, e3, *refs):
    hi_ref, lo_ref, token = refs[-3:]
    token[...] = jnp.zeros_like(token)
    d, _, y = coords()
    n = e0.shape[0] // 2
    iota = lax.broadcasted_iota(jnp.int32, (256, 256), 0).astype(jnp.float32).astype(jnp.bfloat16)
    lane_doc = lax.broadcasted_iota(jnp.int32, (8, 256), 1) >> 4
    one = jnp.ones((256, 256), jnp.bfloat16)
    zero = jnp.zeros((256, 256), jnp.bfloat16)

    def spread(row):
        wide = jnp.broadcast_to(row, (16, 256)).astype(jnp.bfloat16)
        return jnp.broadcast_to(wide[None], (16, 16, 256)).reshape(256, 256)

    for k, entries in enumerate((e0, e1, e2, e3)):

        @pl.loop(0, n // 16)
        def _(step, k=k, entries=entries):
            at = pl.multiple_of((y ^ rel) * (n // 2) + step * 8, 8)
            ids = entries[pl.ds(at, 8), :].astype(jnp.int32)
            vals = entries[pl.ds(n + at, 8), :]
            owner = (ids >> 8) ^ d
            block = ((owner & 1) << 3) | ((owner & 2) << 1) | (owner >> 2)
            code = (block * 16 + lane_doc).astype(jnp.float32)
            inner = (ids & 255).astype(jnp.float32)
            for t in range(8):
                pick = jnp.where(iota == spread(code[t : t + 1]), one, zero)
                weigh = jnp.where(iota == spread(inner[t : t + 1]), spread(vals[t : t + 1]), zero)
                dense = lax.dot_general(pick, weigh, NT, preferred_element_type=jnp.float32)
                high = dense.astype(jnp.bfloat16)
                low = (dense - high.astype(jnp.float32)).astype(jnp.bfloat16)
                docs = pl.ds(pl.multiple_of(k * 8 * n + step * 128 + 16 * t, 16), 16)
                hi_ref[:, docs, :] = high.reshape(16, 16, 256)
                lo_ref[:, docs, :] = low.reshape(16, 16, 256)


def whole():
    return pl.BlockSpec(memory_space=pltpu.VMEM)


def build(entries, rel, *tokens):
    docs = 4 * (entries[0].shape[0] // 4 * 16)
    *rows, token = pl.pallas_call(
        functools.partial(build_kernel, rel),
        in_specs=[whole()] * (4 + len(tokens)),
        out_specs=[whole()] * 3,
        out_shape=[pltpu.VMEM((16, docs, 256), jnp.bfloat16)] * 2 + [f32(8, 128)],
        compiler_params=params(8),
        cost_estimate=cost(2 * docs * 16 * 256 * 256, docs * 4096 * 4, 1 if rel else 64),
        name="dense_rows",
    )(*entries, *tokens)
    return rows, token


def split_rows(value):
    high = value.astype(jnp.bfloat16)
    low = (value - high.astype(jnp.float32)).astype(jnp.bfloat16)
    return jnp.concatenate([high, low], axis=0)


def add_products(hi_ref, lo_ref, vecs, blocks, total):
    for vec, first in zip(vecs, blocks):
        for pair in (0, 2):
            lhs, rhs = [], []
            for k in (pair, pair + 1):
                both = split_rows(vec[k])
                lhs += [hi_ref[first + k], lo_ref[first + k]]
                rhs += [both, both]
            total[...] += lax.dot_general(
                jnp.concatenate(lhs, axis=1), jnp.concatenate(rhs, axis=1), NT, preferred_element_type=jnp.float32
            )


def forward_kernel(blocks, has_before, hi_ref, lo_ref, *refs):
    count = len(blocks)
    total = refs[-1]
    total[...] = refs[count][...] if has_before else jnp.zeros_like(total)
    add_products(hi_ref, lo_ref, refs[:count], blocks, total)


def forward_part(rows, vecs, blocks, before=None, tokens=()):
    docs, q = rows[0].shape[1], vecs[0].shape[1]
    n = 4 * len(blocks)
    extra = [*tokens] if before is None else [before, *tokens]
    return pl.pallas_call(
        functools.partial(forward_kernel, blocks, before is not None),
        in_specs=[whole()] * (2 + len(vecs) + len(extra)),
        out_specs=whole(),
        out_shape=f32(docs, 2 * q),
        compiler_params=params(8),
        cost_estimate=cost(8 * docs * 256 * 256 * n, 4 * docs * 256 * n),
        name="forward_part",
    )(*rows, *vecs, *extra)


def product_kernel(blocks, hi_ref, lo_ref, vec, before, *refs):
    out, total, columns = refs[-3:]
    total[...] = before[...]
    add_products(hi_ref, lo_ref, (vec,), blocks, total)
    turned = total[...].T
    q = out.shape[0]
    product = turned[:q] + turned[q:]
    if len(refs) == 3:
        out[...] = product
        return
    _, z, _ = coords()
    *messages, alpha = refs[:5]
    columns[...] = row_to_column(alpha[...])
    scale = columns[pl.ds(pl.multiple_of(z * q, q), q), :][:, 0:1]
    for k, m in enumerate(messages):
        at = slice(k * m.shape[1], (k + 1) * m.shape[1])
        out[:, at] = product[:, at] - scale * m[q:, :]


def product_half(rows, vec, before, blocks, *left):
    docs, q = rows[0].shape[1], vec.shape[1]
    return pl.pallas_call(
        functools.partial(product_kernel, blocks),
        in_specs=[whole()] * (4 + len(left)),
        out_specs=whole(),
        out_shape=f32(q, docs),
        scratch_shapes=[pltpu.VMEM((docs, 2 * q), jnp.float32), pltpu.VMEM((4 * q, 128), jnp.float32)],
        compiler_params=params(8),
        cost_estimate=cost(8 * docs * 256 * 256 * 4, 16 * docs * 256),
        name="product_half",
    )(*rows, vec, before, *left)


def square_sums(value):
    q, n = value.shape
    sums = value[:, 0:128] * value[:, 0:128]
    for at in range(128, n, 128):
        sums = sums + value[:, at : at + 128] * value[:, at : at + 128]
    return jnp.sum(jnp.concatenate([sums] * (128 // q), axis=0).T, axis=0, keepdims=True)


def square_row(value, z, cols):
    row = square_sums(value)
    row = jnp.broadcast_to(jnp.concatenate([row] * (cols // 128), axis=1), (8, cols))
    lane = lax.broadcasted_iota(jnp.int32, (8, cols), 1)
    return jnp.where(lane // value.shape[0] == z, row, 0.0)


def row_to_column(row):
    return jnp.broadcast_to(row, (128, row.shape[1])).T


def left_half_kernel(mine, other, raw, both, sums):
    _, z, _ = coords()
    left = mine[...] + other[...]
    raw[...] = left
    both[...] = split_rows(left)
    sums[...] = square_row(left, z, sums.shape[1])


def left_half(mine, other):
    q, docs = mine.shape
    return pl.pallas_call(
        left_half_kernel,
        out_shape=[f32(q, docs), bf16(2 * q, docs), f32(8, 4 * q)],
        compiler_params=params(8),
        cost_estimate=cost(8 * q * docs, 16 * q * docs),
        name="left_half",
    )(mine, other)


def left_rest_kernel(mine, other, raw, squares, token, both, sums, l0, l1, l2, l3):
    _, z, _ = coords()
    left = mine[...] + other[...]
    both[...] = split_rows(left)
    sums[...] = squares[...] + square_row(left, z, sums.shape[1])
    q, n = left.shape[0], left.shape[1] // 4
    for k, out in enumerate((l0, l1, l2, l3)):
        out[:q, :] = raw[:, k * n : (k + 1) * n]
        out[q:, :] = left[:, k * n : (k + 1) * n]


def left_rest(mine, other, raw, squares, token):
    q, docs = mine.shape
    both, sums, *pieces = pl.pallas_call(
        left_rest_kernel,
        out_shape=[bf16(2 * q, docs), f32(8, 4 * q)] + [f32(2 * q, docs // 4)] * 4,
        compiler_params=params(8),
        cost_estimate=cost(8 * q * docs, 24 * q * docs),
        name="left_rest",
    )(mine, other, raw, squares, token)
    return both, sums, pieces


def backward_kernel(first, blocks, parts, hi_ref, lo_ref, both_ref, *refs):
    out_ref = refs[-1]
    both = both_ref[...]
    q = both.shape[0] // 2
    twice = jnp.concatenate([both, both], axis=1)
    for b in range(blocks):
        got = jnp.dot(
            twice,
            jnp.concatenate([hi_ref[first + b], lo_ref[first + b]], axis=0),
            preferred_element_type=jnp.float32,
        )
        got = got[:q] + got[q:]
        if "before" in parts:
            got = got + refs[0][(first + b) * q : (first + b + 1) * q, :]
        out_ref[b * q : (b + 1) * q, :] = got
    if "tail" in parts:
        out_ref[blocks * q :, :] = refs[parts.index("tail")][...]


def backward_part(rows, both, first, blocks, before=None, tail=None, tokens=()):
    q, docs = both.shape[0] // 2, both.shape[1]
    extra = {"before": before, "tail": tail, **{str(i): token for i, token in enumerate(tokens)}}
    extra = {name: value for name, value in extra.items() if value is not None}
    height = blocks * q + (0 if tail is None else tail.shape[0])
    return pl.pallas_call(
        functools.partial(backward_kernel, first, blocks, tuple(extra)),
        in_specs=[whole()] * (3 + len(extra)),
        out_specs=whole(),
        out_shape=f32(height, 256),
        compiler_params=params(8),
        cost_estimate=cost(8 * docs * 256 * 256 * blocks, 4 * docs * 256 * blocks),
        name="backward_part",
    )(*rows, both, *extra.values())


def far_sum_kernel(near, far, beta, send, beta_core):
    n = near.shape[0]
    beta_core[...] = beta[...] + far[n:, :]
    send[0:n, :] = near[...] + far[0:n, :]
    send[n:, :] = beta_core[...]


def far_sums(near, far, beta):
    rows = near.shape[0]
    return pl.pallas_call(
        far_sum_kernel,
        out_shape=[f32(rows + 8, 256), f32(8, 256)],
        compiler_params=params(8),
        cost_estimate=cost(near.size, near.size * 12),
        name="far_sums",
    )(near, far, beta)


def right_norm_kernel(docs_total, keep, peer, got, beta_core, right, g0, g1, g2, g3, sums, columns):
    _, z, _ = coords()
    q = right.shape[1]
    beta_sums = beta_core[0:1, :] + got[4 * q : 4 * q + 1, :]
    columns[...] = row_to_column(jnp.sqrt(beta_sums / docs_total + epsilon))
    beta = columns[pl.ds(pl.multiple_of(z * q, q), q), :][:, 0:1]
    raws = []
    for k, g in enumerate((g0, g1, g2, g3)):
        rows = slice(k * q, (k + 1) * q)
        total = (keep[rows, :] + peer[rows, :]) + got[rows, :]
        g[...] = total
        raws.append(total / beta - beta * right[k])
    line = square_sums(jnp.concatenate(raws, axis=1))
    folded = beta_sums[:, :128] + beta_sums[:, 128:]
    folded = folded + jnp.concatenate([folded[:, q:], folded[:, :q]], axis=1)
    low = lax.broadcasted_iota(jnp.int32, line.shape, 1) < q
    sums[...] = jnp.broadcast_to(jnp.where(low, line, folded), sums.shape)


def right_norm(docs_total, keep, peer, got, beta_core, right):
    q, rows = keep.shape[0] // 4, keep.shape[1]
    *pieces, sums = pl.pallas_call(
        functools.partial(right_norm_kernel, docs_total),
        out_shape=[f32(q, rows)] * 4 + [f32(32, 128)],
        scratch_shapes=[pltpu.VMEM((4 * q, 128), jnp.float32)],
        compiler_params=params(8),
        cost_estimate=cost(rows * q * 64, rows * q * 100),
        name="right_norm",
    )(keep, peer, got, beta_core, right)
    return pieces, sums.reshape(32, 1, 128)


def finish_kernel(docs_total, feat_total, g0, g1, g2, g3, squares, l0, l1, l2, l3, right, search, solution, phibar, rhobar,
                  left_out, right_out, search_out, solution_out, alpha_out, phibar_out, rhobar_out, turned):
    _, z, y = coords()
    q, half = turned.shape[1:]
    parts = [squares[i] for i in range(32)]
    high = [jnp.concatenate([parts[8 * i][:, q:], parts[8 * i][:, :q]], axis=1) if i % 2 == 0 else parts[8 * i] for i in range(4)]
    while len(parts) > 4:
        parts = [a + b for a, b in zip(parts[::2], parts[1::2])]
    parts[1::2] = [jnp.concatenate([p[:, q:], p[:, :q]], axis=1) for p in parts[1::2]]
    low = lax.broadcasted_iota(jnp.int32, parts[0].shape, 1) < q
    alpha_sums, beta_sums = (
        jnp.concatenate([jnp.where(low, p[0], p[1]), jnp.where(low, p[2], p[3])], axis=1) for p in (parts, high)
    )
    alpha = jnp.sqrt(alpha_sums / feat_total + epsilon)
    beta = jnp.sqrt(beta_sums / docs_total + epsilon)
    for rel, part in enumerate((y, 1 - y)):
        for k, piece in enumerate((l0, l1, l2, l3)):
            turned[z ^ k] = piece[rel * q : (rel + 1) * q, :]
        left_out[pl.ds(pl.multiple_of(part * half, half), half), :] = turned[...].reshape(-1, half).T / beta
    rho = jnp.sqrt(rhobar[...] * rhobar[...] + beta * beta)
    cosine = rhobar[...] / rho
    sine = beta / rho
    theta = sine * alpha
    phi = cosine * phibar[...]
    rhobar_out[...] = -cosine * alpha
    phibar_out[...] = sine * phibar[...]
    alpha_out[...] = alpha
    for k, g in enumerate((g0, g1, g2, g3)):
        turned[z ^ k] = g[...]
    got = turned[...].reshape(-1, half).T
    following = (got / beta - beta * right[...]) / alpha
    right_out[...] = following
    search_out[...] = following - (theta / rho) * search[...]
    solution_out[...] = solution[...] + (phi / rho) * search[...]


def finish(docs_total, feat_total, pieces, squares, lefts, right, search, solution, phibar, rhobar):
    rows, cols = right.shape
    return pl.pallas_call(
        functools.partial(finish_kernel, docs_total, feat_total),
        out_shape=[f32(2 * rows, cols)] + [f32(rows, cols)] * 3 + [f32(1, cols)] * 3,
        scratch_shapes=[pltpu.VMEM((4, cols // 4, rows), jnp.float32)],
        compiler_params=params(12),
        cost_estimate=cost(rows * cols * 16, rows * cols * 20),
        name="finish",
    )(*pieces, squares, *lefts, right, search, solution, phibar, rhobar)


def swap(value, mask):
    return lax.ppermute(value, AXES, [(i, i ^ mask) for i in range(32)])


def along_z(values):
    return [values[0]] + [swap(values[k], k << Z_SHIFT) for k in (1, 2, 3)]


def after(value, *earlier):
    return lax.optimization_barrier((value, *earlier))[0]


def by_columns(
    col_ids, col_vals, left_vec, right_vec, search_dir, solution_vec, alpha_prev, phibar, rhobar
):
    docs_total = left_vec.shape[0] * 16
    feat_total = right_vec.shape[0] * 32
    alpha_row, phibar_row, rhobar_row = (v.reshape(1, -1) for v in (alpha_prev, phibar, rhobar))

    stored, messages = prepare(col_ids.T, col_vals.T, right_vec, left_vec)
    entries = along_z([stored] * 4)
    messages = along_z([messages[0]] + [after(m, entries[1]) for m in messages[1:]])
    q = right_vec.shape[1] // 4

    rows1, token1 = build(entries, 1)
    own = stack(messages, q, "stack_right", token1)
    own_x = swap(own, X_BIT)
    own_peer = swap(own, CORE_BIT)
    rows0, token0 = build(entries, 0, own)
    total1 = forward_part(rows1, [own, own_peer], (0, 8), None, [token0])
    x_peer = swap(after(own_x, total1), CORE_BIT)
    total1 = forward_part(rows1, [own_x], (4,), total1)
    product1 = product_half(rows1, x_peer, total1, (12,))
    total0 = forward_part(rows0, [own, own_peer], (0, 8))
    total0 = forward_part(rows0, [own_x], (4,), total0)
    product0 = product_half(rows0, x_peer, total0, (12,), *messages, alpha_row)

    raw, both0, beta0 = left_half(product0, swap(product1, Y_BIT))
    partial = backward_part(rows0, both0, 0, 16)
    both1, beta1, lefts = left_rest(product1, swap(product0, Y_BIT), raw, beta0, partial)
    far = swap(backward_part(rows1, both1, 12, 4, partial, beta1), CORE_BIT)
    near = backward_part(rows1, both1, 4, 4, partial)
    send, beta_core = far_sums(near, far, beta1)
    got = swap(send, X_BIT)
    lefts = along_z([lefts[0]] + [after(l, send) for l in lefts[1:]])
    peer = backward_part(rows1, both1, 8, 4, partial)
    keep = backward_part(rows1, both1, 0, 4, partial)

    sent, sums = right_norm(docs_total, keep, swap(peer, CORE_BIT), got, beta_core, own)
    pieces = along_z(sent)
    squares = lax.all_to_all(after(sums, *lefts[1:]), AXES, 0, 0, tiled=True)
    left_next, right_next, search_next, solution_next, alpha_next, phibar_next, rhobar_next = finish(
        docs_total, feat_total, pieces, squares, lefts,
        right_vec, search_dir, solution_vec, phibar_row, rhobar_row,
    )
    return (
        left_next,
        right_next,
        search_next,
        solution_next,
        alpha_next.reshape(-1),
        phibar_next.reshape(-1),
        rhobar_next.reshape(-1),
    )


def forward(col_ids, col_vals, table):
    picked = table[col_ids]
    return jnp.sum(col_vals.astype(jnp.float32)[:, :, None] * picked, axis=1)


def backward(col_ids, col_vals, rows_in, width):
    terms = col_vals.astype(jnp.float32)[:, :, None] * rows_in[:, None, :]
    return jax.ops.segment_sum(
        terms.reshape(-1, rows_in.shape[1]), col_ids.reshape(-1), num_segments=width
    )


def by_blocks(
    col_ids, col_vals, left_vec, right_vec, search_dir, solution_vec, alpha_prev, phibar, rhobar
):
    n_feat = lax.axis_size("feat")
    n_doc = lax.axis_size("doc")
    docs_total = left_vec.shape[0] * n_doc
    feat_total = right_vec.shape[0] * n_doc * n_feat
    table = lax.all_gather(right_vec, "doc", axis=0, tiled=True)
    total = lax.psum(forward(col_ids, col_vals, table), "feat")
    left_raw = total - alpha_prev[None, :] * left_vec
    row_part = jnp.sum(left_raw * left_raw, axis=0)
    beta_norm = jnp.sqrt(lax.psum(row_part, "doc") / docs_total + epsilon)
    left_next = left_raw / beta_norm[None, :]
    feature_part = lax.psum_scatter(
        backward(col_ids, col_vals, left_next, table.shape[0]), "doc", scatter_dimension=0, tiled=True
    )
    right_raw = feature_part - beta_norm[None, :] * right_vec
    squares = lax.psum(jnp.sum(right_raw * right_raw, axis=0), AXES)
    alpha_next = jnp.sqrt(squares / feat_total + epsilon)
    right_next = right_raw / alpha_next[None, :]
    rho_val = jnp.sqrt(rhobar * rhobar + beta_norm * beta_norm)
    cosine = rhobar / rho_val
    sine_val = beta_norm / rho_val
    theta_val = sine_val * alpha_next
    phi_val = cosine * phibar
    solution_next = solution_vec + (phi_val / rho_val)[None, :] * search_dir
    search_next = right_next - (theta_val / rho_val)[None, :] * search_dir
    return (
        left_next,
        right_next,
        search_next,
        solution_next,
        alpha_next,
        sine_val * phibar,
        -cosine * alpha_next,
    )


def solution(mesh):
    small = mesh.shape["doc"] == 16 and mesh.shape["feat"] == 2
    rows = P(("feat", "doc"), None)
    return jax.shard_map(
        by_columns if small else by_blocks,
        mesh=mesh,
        in_specs=(P("doc", "feat"), P("doc", "feat"), P("doc", None), rows, rows, rows, P(), P(), P()),
        out_specs=(P("doc", None), rows, rows, rows, P(), P(), P()),
        check_vma=False,
    )
```

```python
import functools

import jax
import jax.numpy as jnp
from jax import lax
from jax.experimental import pallas as pl
from jax.experimental.pallas import tpu as pltpu
from jax.sharding import PartitionSpec as P

epsilon = 1e-06
AXES = ("doc", "feat")
MIB = 1024 * 1024


Y_BIT, CORE_BIT, X_BIT, Z_SHIFT = 1, 2, 4, 3
NT = (((1,), (1,)), ((), ()))


def coords():
    d = lax.axis_index("doc")
    y = lax.axis_index("feat")
    return d, d >> 2, y


def params(mib):
    return pltpu.CompilerParams(vmem_limit_bytes=mib * MIB)


def cost(flops, nbytes, scale=64):
    return pl.CostEstimate(flops=int(flops) // scale, bytes_accessed=int(nbytes) // scale, transcendentals=0)


def f32(*shape):
    return jax.ShapeDtypeStruct(shape, jnp.float32)


def bf16(*shape):
    return jax.ShapeDtypeStruct(shape, jnp.bfloat16)


def prepare_kernel(ids_hbm, vals_hbm, right_hbm, left_hbm, stored, m0, m1, m2, m3,
                   ids, vals, wide, right, left, turned, arrived):
    _, z, y = coords()
    q, rows = turned.shape[1:]
    copies = [
        pltpu.make_async_copy(src, dst, arrived.at[i])
        for i, (src, dst) in enumerate((
            (ids_hbm, ids),
            (vals_hbm, vals),
            (right_hbm, right),
            (left_hbm.at[pl.ds(pl.multiple_of(y * rows, rows), rows), :], left),
        ))
    ]
    for copy in copies:
        copy.start()
    lines, count = stored.shape[0] // 2, ids.shape[0]
    for part, ref in enumerate((ids, vals)):
        copies[part].wait()
        wide[...] = ref[...].astype(jnp.float32).T
        for r in range(256 // count):
            stored[part * lines : (part + 1) * lines, r * count : (r + 1) * count] = wide[
                pl.ds(r, lines, stride=256 // count), :
            ]
    for part, ref in enumerate((right, left)):
        copies[2 + part].wait()
        turned[...] = ref[...].T.reshape(turned.shape)
        for k, out in enumerate((m0, m1, m2, m3)):
            out[part * q : (part + 1) * q, :] = turned[z ^ k]


def prepare(ids, vals, right, left):
    rows, cols = right.shape
    q = cols // 4
    got = pl.pallas_call(
        prepare_kernel,
        in_specs=[pl.BlockSpec(memory_space=pltpu.HBM)] * 4,
        out_specs=[whole()] * 5,
        out_shape=[pltpu.VMEM((ids.size // 128, 256), jnp.float32)] + [pltpu.VMEM((2 * q, rows), jnp.float32)] * 4,
        scratch_shapes=[
            pltpu.VMEM(ids.shape, jnp.int32),
            pltpu.VMEM(vals.shape, jnp.bfloat16),
            pltpu.VMEM(ids.shape[::-1], jnp.float32),
            pltpu.VMEM(right.shape, jnp.float32),
            pltpu.VMEM(right.shape, jnp.float32),
            pltpu.VMEM((4, q, rows), jnp.float32),
            pltpu.SemaphoreType.DMA((4,)),
        ],
        compiler_params=params(60),
        cost_estimate=cost(0, rows * cols * 16),
        name="prepare",
    )(ids, vals, right, left)
    return got[0], got[1:]


def stack_kernel(m0, m1, m2, m3, *refs):
    out = refs[-1]
    for k, m in enumerate((m0, m1, m2, m3)):
        out[k] = m[0 : out.shape[1], :]


def stack(messages, q, name, *tokens):
    rows = messages[0].shape[1]
    return pl.pallas_call(
        stack_kernel,
        out_shape=f32(4, q, rows),
        compiler_params=params(8),
        cost_estimate=cost(0, 32 * q * rows),
        name=name,
    )(*messages, *tokens)


def build_kernel(rel, e0, e1, e2, e3, *refs):
    hi_ref, lo_ref, token = refs[-3:]
    token[...] = jnp.zeros_like(token)
    d, _, y = coords()
    n = e0.shape[0] // 2
    iota = lax.broadcasted_iota(jnp.int32, (256, 256), 0).astype(jnp.float32).astype(jnp.bfloat16)
    lane_doc = lax.broadcasted_iota(jnp.int32, (8, 256), 1) >> 4
    one = jnp.ones((256, 256), jnp.bfloat16)
    zero = jnp.zeros((256, 256), jnp.bfloat16)

    def spread(row):
        wide = jnp.broadcast_to(row, (16, 256)).astype(jnp.bfloat16)
        return jnp.broadcast_to(wide[None], (16, 16, 256)).reshape(256, 256)

    for k, entries in enumerate((e0, e1, e2, e3)):

        @pl.loop(0, n // 16)
        def _(step, k=k, entries=entries):
            at = pl.multiple_of((y ^ rel) * (n // 2) + step * 8, 8)
            ids = entries[pl.ds(at, 8), :].astype(jnp.int32)
            vals = entries[pl.ds(n + at, 8), :]
            owner = (ids >> 8) ^ d
            block = ((owner & 1) << 3) | ((owner & 2) << 1) | (owner >> 2)
            code = (block * 16 + lane_doc).astype(jnp.float32)
            inner = (ids & 255).astype(jnp.float32)
            for t in range(8):
                pick = jnp.where(iota == spread(code[t : t + 1]), one, zero)
                weigh = jnp.where(iota == spread(inner[t : t + 1]), spread(vals[t : t + 1]), zero)
                dense = lax.dot_general(pick, weigh, NT, preferred_element_type=jnp.float32)
                high = dense.astype(jnp.bfloat16)
                low = (dense - high.astype(jnp.float32)).astype(jnp.bfloat16)
                docs = pl.ds(pl.multiple_of(k * 8 * n + step * 128 + 16 * t, 16), 16)
                hi_ref[:, docs, :] = high.reshape(16, 16, 256)
                lo_ref[:, docs, :] = low.reshape(16, 16, 256)


def whole():
    return pl.BlockSpec(memory_space=pltpu.VMEM)


def build(entries, rel, *tokens):
    docs = 4 * (entries[0].shape[0] // 4 * 16)
    *rows, token = pl.pallas_call(
        functools.partial(build_kernel, rel),
        in_specs=[whole()] * (4 + len(tokens)),
        out_specs=[whole()] * 3,
        out_shape=[pltpu.VMEM((16, docs, 256), jnp.bfloat16)] * 2 + [f32(8, 128)],
        compiler_params=params(8),
        cost_estimate=cost(2 * docs * 16 * 256 * 256, docs * 4096 * 4, 1 if rel else 64),
        name="dense_rows",
    )(*entries, *tokens)
    return rows, token


def split_rows(value):
    high = value.astype(jnp.bfloat16)
    low = (value - high.astype(jnp.float32)).astype(jnp.bfloat16)
    return jnp.concatenate([high, low], axis=0)


def add_products(hi_ref, lo_ref, vecs, blocks, total):
    for vec, first in zip(vecs, blocks):
        for pair in (0, 2):
            lhs, rhs = [], []
            for k in (pair, pair + 1):
                both = split_rows(vec[k])
                lhs += [hi_ref[first + k], lo_ref[first + k]]
                rhs += [both, both]
            total[...] += lax.dot_general(
                jnp.concatenate(lhs, axis=1), jnp.concatenate(rhs, axis=1), NT, preferred_element_type=jnp.float32
            )


def forward_kernel(blocks, has_before, hi_ref, lo_ref, *refs):
    count = len(blocks)
    total = refs[-1]
    total[...] = refs[count][...] if has_before else jnp.zeros_like(total)
    add_products(hi_ref, lo_ref, refs[:count], blocks, total)


def forward_part(rows, vecs, blocks, before=None, tokens=()):
    docs, q = rows[0].shape[1], vecs[0].shape[1]
    n = 4 * len(blocks)
    extra = [*tokens] if before is None else [before, *tokens]
    return pl.pallas_call(
        functools.partial(forward_kernel, blocks, before is not None),
        in_specs=[whole()] * (2 + len(vecs) + len(extra)),
        out_specs=whole(),
        out_shape=f32(docs, 2 * q),
        compiler_params=params(8),
        cost_estimate=cost(8 * docs * 256 * 256 * n, 4 * docs * 256 * n),
        name="forward_part",
    )(*rows, *vecs, *extra)


def product_kernel(blocks, hi_ref, lo_ref, vec, before, *refs):
    out, total, columns = refs[-3:]
    total[...] = before[...]
    add_products(hi_ref, lo_ref, (vec,), blocks, total)
    turned = total[...].T
    q = out.shape[0]
    product = turned[:q] + turned[q:]
    if len(refs) == 3:
        out[...] = product
        return
    _, z, _ = coords()
    *messages, alpha = refs[:5]
    columns[...] = row_to_column(alpha[...])
    scale = columns[pl.ds(pl.multiple_of(z * q, q), q), :][:, 0:1]
    for k, m in enumerate(messages):
        at = slice(k * m.shape[1], (k + 1) * m.shape[1])
        out[:, at] = product[:, at] - scale * m[q:, :]


def product_half(rows, vec, before, blocks, *left):
    docs, q = rows[0].shape[1], vec.shape[1]
    return pl.pallas_call(
        functools.partial(product_kernel, blocks),
        in_specs=[whole()] * (4 + len(left)),
        out_specs=whole(),
        out_shape=f32(q, docs),
        scratch_shapes=[pltpu.VMEM((docs, 2 * q), jnp.float32), pltpu.VMEM((4 * q, 128), jnp.float32)],
        compiler_params=params(8),
        cost_estimate=cost(8 * docs * 256 * 256 * 4, 16 * docs * 256),
        name="product_half",
    )(*rows, vec, before, *left)


def square_sums(value):
    q, n = value.shape
    sums = value[:, 0:128] * value[:, 0:128]
    for at in range(128, n, 128):
        sums = sums + value[:, at : at + 128] * value[:, at : at + 128]
    return jnp.sum(jnp.concatenate([sums] * (128 // q), axis=0).T, axis=0, keepdims=True)


def square_row(value, z, cols):
    row = square_sums(value)
    row = jnp.broadcast_to(jnp.concatenate([row] * (cols // 128), axis=1), (8, cols))
    lane = lax.broadcasted_iota(jnp.int32, (8, cols), 1)
    return jnp.where(lane // value.shape[0] == z, row, 0.0)


def row_to_column(row):
    return jnp.broadcast_to(row, (128, row.shape[1])).T


def left_half_kernel(mine, other, *refs):
    _, z, _ = coords()
    left = mine[...] + other[...]
    both, sums = refs[-2:]
    both[...] = split_rows(left)
    squares = square_row(left, z, sums.shape[1])
    sums[...] = refs[0][...] + squares if len(refs) == 4 else squares
    if len(refs) > 4:
        n = left.shape[1] // 4
        for k, out in enumerate(refs[:4]):
            out[...] = left[:, k * n : (k + 1) * n]


def left_half(mine, other, squares=None, token=None):
    q, docs = mine.shape
    extra = [] if squares is None else [squares, token]
    pieces = [f32(q, docs // 4)] * 4 if squares is None else []
    return pl.pallas_call(
        left_half_kernel,
        out_shape=pieces + [bf16(2 * q, docs), f32(8, 4 * q)],
        compiler_params=params(8),
        cost_estimate=cost(8 * q * docs, 16 * q * docs),
        name="left_half",
    )(mine, other, *extra)


def backward_kernel(first, blocks, parts, hi_ref, lo_ref, both_ref, *refs):
    out_ref = refs[-1]
    both = both_ref[...]
    q = both.shape[0] // 2
    twice = jnp.concatenate([both, both], axis=1)
    for b in range(blocks):
        got = jnp.dot(
            twice,
            jnp.concatenate([hi_ref[first + b], lo_ref[first + b]], axis=0),
            preferred_element_type=jnp.float32,
        )
        got = got[:q] + got[q:]
        if "before" in parts:
            got = got + refs[0][(first + b) * q : (first + b + 1) * q, :]
        out_ref[b * q : (b + 1) * q, :] = got
    if "tail" in parts:
        out_ref[blocks * q :, :] = refs[parts.index("tail")][...]


def backward_part(rows, both, first, blocks, before=None, tail=None, tokens=()):
    q, docs = both.shape[0] // 2, both.shape[1]
    extra = {"before": before, "tail": tail, **{str(i): token for i, token in enumerate(tokens)}}
    extra = {name: value for name, value in extra.items() if value is not None}
    height = blocks * q + (0 if tail is None else tail.shape[0])
    return pl.pallas_call(
        functools.partial(backward_kernel, first, blocks, tuple(extra)),
        in_specs=[whole()] * (3 + len(extra)),
        out_specs=whole(),
        out_shape=f32(height, 256),
        compiler_params=params(8),
        cost_estimate=cost(8 * docs * 256 * 256 * blocks, 4 * docs * 256 * blocks),
        name="backward_part",
    )(*rows, both, *extra.values())


def far_sum_kernel(near, far, beta, send, beta_core):
    n = near.shape[0]
    beta_core[...] = beta[...] + far[n:, :]
    send[0:n, :] = near[...] + far[0:n, :]
    send[n:, :] = beta_core[...]


def far_sums(near, far, beta):
    rows = near.shape[0]
    return pl.pallas_call(
        far_sum_kernel,
        out_shape=[f32(rows + 8, 256), f32(8, 256)],
        compiler_params=params(8),
        cost_estimate=cost(near.size, near.size * 12),
        name="far_sums",
    )(near, far, beta)


def right_norm_kernel(docs_total, keep, peer, got, beta_core, right, g0, g1, g2, g3, sums, columns):
    _, z, _ = coords()
    q = right.shape[1]
    beta_sums = beta_core[0:1, :] + got[4 * q : 4 * q + 1, :]
    columns[...] = row_to_column(jnp.sqrt(beta_sums / docs_total + epsilon))
    beta = columns[pl.ds(pl.multiple_of(z * q, q), q), :][:, 0:1]
    raws = []
    for k, g in enumerate((g0, g1, g2, g3)):
        rows = slice(k * q, (k + 1) * q)
        total = (keep[rows, :] + peer[rows, :]) + got[rows, :]
        g[...] = total
        raws.append(total / beta - beta * right[k])
    line = square_sums(jnp.concatenate(raws, axis=1))
    folded = beta_sums[:, :128] + beta_sums[:, 128:]
    folded = folded + jnp.concatenate([folded[:, q:], folded[:, :q]], axis=1)
    low = lax.broadcasted_iota(jnp.int32, line.shape, 1) < q
    sums[...] = jnp.broadcast_to(jnp.where(low, line, folded), sums.shape)


def right_norm(docs_total, keep, peer, got, beta_core, right):
    q, rows = keep.shape[0] // 4, keep.shape[1]
    *pieces, sums = pl.pallas_call(
        functools.partial(right_norm_kernel, docs_total),
        out_shape=[f32(q, rows)] * 4 + [f32(32, 128)],
        scratch_shapes=[pltpu.VMEM((4 * q, 128), jnp.float32)],
        compiler_params=params(8),
        cost_estimate=cost(rows * q * 64, rows * q * 100),
        name="right_norm",
    )(keep, peer, got, beta_core, right)
    return pieces, sums.reshape(32, 1, 128)


def finish_kernel(docs_total, feat_total, g0, g1, g2, g3, squares, own, other, right, search, solution, phibar, rhobar,
                  left_out, right_out, search_out, solution_out, alpha_out, phibar_out, rhobar_out, turned):
    _, z, y = coords()
    q, half = turned.shape[1:]
    parts = [squares[i] for i in range(32)]
    high = [jnp.concatenate([parts[8 * i][:, q:], parts[8 * i][:, :q]], axis=1) if i % 2 == 0 else parts[8 * i] for i in range(4)]
    while len(parts) > 4:
        parts = [a + b for a, b in zip(parts[::2], parts[1::2])]
    parts[1::2] = [jnp.concatenate([p[:, q:], p[:, :q]], axis=1) for p in parts[1::2]]
    low = lax.broadcasted_iota(jnp.int32, parts[0].shape, 1) < q
    alpha_sums, beta_sums = (
        jnp.concatenate([jnp.where(low, p[0], p[1]), jnp.where(low, p[2], p[3])], axis=1) for p in (parts, high)
    )
    alpha = jnp.sqrt(alpha_sums / feat_total + epsilon)
    beta = jnp.sqrt(beta_sums / docs_total + epsilon)
    for part, ref in ((y, own), (1 - y, other)):
        for k in range(4):
            turned[z ^ k] = ref[k]
        left_out[pl.ds(pl.multiple_of(part * half, half), half), :] = turned[...].reshape(-1, half).T / beta
    rho = jnp.sqrt(rhobar[...] * rhobar[...] + beta * beta)
    cosine = rhobar[...] / rho
    sine = beta / rho
    theta = sine * alpha
    phi = cosine * phibar[...]
    rhobar_out[...] = -cosine * alpha
    phibar_out[...] = sine * phibar[...]
    alpha_out[...] = alpha
    for k, g in enumerate((g0, g1, g2, g3)):
        turned[z ^ k] = g[...]
    got = turned[...].reshape(-1, half).T
    following = (got / beta - beta * right[...]) / alpha
    right_out[...] = following
    search_out[...] = following - (theta / rho) * search[...]
    solution_out[...] = solution[...] + (phi / rho) * search[...]


def finish(docs_total, feat_total, pieces, squares, own, other, right, search, solution, phibar, rhobar):
    rows, cols = right.shape
    return pl.pallas_call(
        functools.partial(finish_kernel, docs_total, feat_total),
        out_shape=[f32(2 * rows, cols)] + [f32(rows, cols)] * 3 + [f32(1, cols)] * 3,
        scratch_shapes=[pltpu.VMEM((4, cols // 4, rows), jnp.float32)],
        compiler_params=params(12),
        cost_estimate=cost(rows * cols * 16, rows * cols * 20),
        name="finish",
    )(*pieces, squares, own, other, right, search, solution, phibar, rhobar)


def swap(value, mask):
    return lax.ppermute(value, AXES, [(i, i ^ mask) for i in range(32)])


def along_z(values):
    got = {0: values[0]}
    for k in (2, 3, 1):
        got[k] = swap(values[k], k << Z_SHIFT)
    return [got[k] for k in range(4)]


def after(value, *earlier):
    return lax.optimization_barrier((value, *earlier))[0]


def by_columns(
    col_ids, col_vals, left_vec, right_vec, search_dir, solution_vec, alpha_prev, phibar, rhobar
):
    docs_total = left_vec.shape[0] * 16
    feat_total = right_vec.shape[0] * 32
    alpha_row, phibar_row, rhobar_row = (v.reshape(1, -1) for v in (alpha_prev, phibar, rhobar))

    stored, messages = prepare(col_ids.T, col_vals.T, right_vec, left_vec)
    entries = along_z([stored] * 4)
    messages = along_z([messages[0]] + [after(messages[1], entries[2]), messages[2], messages[3]])
    q = right_vec.shape[1] // 4

    rows1, token1 = build(entries, 1)
    own = stack(messages, q, "stack_right", token1)
    own_x = swap(own, X_BIT)
    own_peer = swap(own, CORE_BIT)
    rows0, token0 = build(entries, 0, own)
    total1 = forward_part(rows1, [own, own_peer], (0, 8), None, [token0])
    x_peer = swap(after(own_x, total1), CORE_BIT)
    total1 = forward_part(rows1, [own_x], (4,), total1)
    product1 = product_half(rows1, x_peer, total1, (12,))
    total0 = forward_part(rows0, [own, own_peer], (0, 8))
    total0 = forward_part(rows0, [own_x], (4,), total0)
    product0 = product_half(rows0, x_peer, total0, (12,), *messages, alpha_row)

    *lefts, both0, beta0 = left_half(product0, swap(product1, Y_BIT))
    partial = backward_part(rows0, both0, 0, 16)
    left_own = stack(along_z(lefts), q, "stack_left")
    both1, beta1 = left_half(product1, swap(product0, Y_BIT), beta0, partial)
    far = swap(backward_part(rows1, both1, 12, 4, partial, beta1, [left_own]), CORE_BIT)
    near = backward_part(rows1, both1, 4, 4, partial)
    send, beta_core = far_sums(near, far, beta1)
    got = swap(send, X_BIT)
    peer = backward_part(rows1, both1, 8, 4, partial)
    left_other = swap(after(left_own, peer), Y_BIT)
    keep = backward_part(rows1, both1, 0, 4, partial)

    sent, sums = right_norm(docs_total, keep, swap(peer, CORE_BIT), got, beta_core, own)
    pieces = along_z(sent)
    squares = lax.all_to_all(after(sums, left_other), AXES, 0, 0, tiled=True)
    left_next, right_next, search_next, solution_next, alpha_next, phibar_next, rhobar_next = finish(
        docs_total, feat_total, pieces, squares, left_own, left_other,
        right_vec, search_dir, solution_vec, phibar_row, rhobar_row,
    )
    return (
        left_next,
        right_next,
        search_next,
        solution_next,
        alpha_next.reshape(-1),
        phibar_next.reshape(-1),
        rhobar_next.reshape(-1),
    )


def forward(col_ids, col_vals, table):
    picked = table[col_ids]
    return jnp.sum(col_vals.astype(jnp.float32)[:, :, None] * picked, axis=1)


def backward(col_ids, col_vals, rows_in, width):
    terms = col_vals.astype(jnp.float32)[:, :, None] * rows_in[:, None, :]
    return jax.ops.segment_sum(
        terms.reshape(-1, rows_in.shape[1]), col_ids.reshape(-1), num_segments=width
    )


def by_blocks(
    col_ids, col_vals, left_vec, right_vec, search_dir, solution_vec, alpha_prev, phibar, rhobar
):
    n_feat = lax.axis_size("feat")
    n_doc = lax.axis_size("doc")
    docs_total = left_vec.shape[0] * n_doc
    feat_total = right_vec.shape[0] * n_doc * n_feat
    table = lax.all_gather(right_vec, "doc", axis=0, tiled=True)
    total = lax.psum(forward(col_ids, col_vals, table), "feat")
    left_raw = total - alpha_prev[None, :] * left_vec
    row_part = jnp.sum(left_raw * left_raw, axis=0)
    beta_norm = jnp.sqrt(lax.psum(row_part, "doc") / docs_total + epsilon)
    left_next = left_raw / beta_norm[None, :]
    feature_part = lax.psum_scatter(
        backward(col_ids, col_vals, left_next, table.shape[0]), "doc", scatter_dimension=0, tiled=True
    )
    right_raw = feature_part - beta_norm[None, :] * right_vec
    squares = lax.psum(jnp.sum(right_raw * right_raw, axis=0), AXES)
    alpha_next = jnp.sqrt(squares / feat_total + epsilon)
    right_next = right_raw / alpha_next[None, :]
    rho_val = jnp.sqrt(rhobar * rhobar + beta_norm * beta_norm)
    cosine = rhobar / rho_val
    sine_val = beta_norm / rho_val
    theta_val = sine_val * alpha_next
    phi_val = cosine * phibar
    solution_next = solution_vec + (phi_val / rho_val)[None, :] * search_dir
    search_next = right_next - (theta_val / rho_val)[None, :] * search_dir
    return (
        left_next,
        right_next,
        search_next,
        solution_next,
        alpha_next,
        sine_val * phibar,
        -cosine * alpha_next,
    )


def solution(mesh):
    small = mesh.shape["doc"] == 16 and mesh.shape["feat"] == 2
    rows = P(("feat", "doc"), None)
    return jax.shard_map(
        by_columns if small else by_blocks,
        mesh=mesh,
        in_specs=(P("doc", "feat"), P("doc", "feat"), P("doc", None), rows, rows, rows, P(), P(), P()),
        out_specs=(P("doc", None), rows, rows, rows, P(), P(), P()),
        check_vma=False,
    )
```

```python
import functools

import jax
import jax.numpy as jnp
from jax import lax
from jax.experimental import pallas as pl
from jax.experimental.pallas import tpu as pltpu
from jax.sharding import PartitionSpec as P

epsilon = 1e-06
AXES = ("doc", "feat")
MIB = 1024 * 1024


Y_BIT, CORE_BIT, X_BIT, Z_SHIFT = 1, 2, 4, 3
NT = (((1,), (1,)), ((), ()))


def coords():
    d = lax.axis_index("doc")
    y = lax.axis_index("feat")
    return d, d >> 2, y


def params(mib):
    return pltpu.CompilerParams(vmem_limit_bytes=mib * MIB)


def cost(flops, nbytes, scale=64):
    return pl.CostEstimate(flops=int(flops) // scale, bytes_accessed=int(nbytes) // scale, transcendentals=0)


def f32(*shape):
    return jax.ShapeDtypeStruct(shape, jnp.float32)


def bf16(*shape):
    return jax.ShapeDtypeStruct(shape, jnp.bfloat16)


def prepare_kernel(ids_hbm, vals_hbm, right_hbm, left_hbm, stored, m0, m1, m2, m3,
                   ids, vals, wide, right, left, turned, arrived):
    _, z, y = coords()
    q, rows = turned.shape[1:]
    copies = [
        pltpu.make_async_copy(src, dst, arrived.at[i])
        for i, (src, dst) in enumerate((
            (ids_hbm, ids),
            (vals_hbm, vals),
            (right_hbm, right),
            (left_hbm.at[pl.ds(pl.multiple_of(y * rows, rows), rows), :], left),
        ))
    ]
    for copy in copies:
        copy.start()
    lines, count = stored.shape[0] // 2, ids.shape[0]
    for part, ref in enumerate((ids, vals)):
        copies[part].wait()
        wide[...] = ref[...].astype(jnp.float32).T
        for r in range(256 // count):
            stored[part * lines : (part + 1) * lines, r * count : (r + 1) * count] = wide[
                pl.ds(r, lines, stride=256 // count), :
            ]
    for part, ref in enumerate((right, left)):
        copies[2 + part].wait()
        turned[...] = ref[...].T.reshape(turned.shape)
        for k, out in enumerate((m0, m1, m2, m3)):
            out[part * q : (part + 1) * q, :] = turned[z ^ k]


def prepare(ids, vals, right, left):
    rows, cols = right.shape
    q = cols // 4
    got = pl.pallas_call(
        prepare_kernel,
        in_specs=[pl.BlockSpec(memory_space=pltpu.HBM)] * 4,
        out_specs=[whole()] * 5,
        out_shape=[pltpu.VMEM((ids.size // 128, 256), jnp.float32)] + [pltpu.VMEM((2 * q, rows), jnp.float32)] * 4,
        scratch_shapes=[
            pltpu.VMEM(ids.shape, jnp.int32),
            pltpu.VMEM(vals.shape, jnp.bfloat16),
            pltpu.VMEM(ids.shape[::-1], jnp.float32),
            pltpu.VMEM(right.shape, jnp.float32),
            pltpu.VMEM(right.shape, jnp.float32),
            pltpu.VMEM((4, q, rows), jnp.float32),
            pltpu.SemaphoreType.DMA((4,)),
        ],
        compiler_params=params(60),
        cost_estimate=cost(0, rows * cols * 16),
        name="prepare",
    )(ids, vals, right, left)
    return got[0], got[1:]


def stack_kernel(m0, m1, m2, m3, *refs):
    out = refs[-1]
    for k, m in enumerate((m0, m1, m2, m3)):
        out[k] = m[0 : out.shape[1], :]


def stack(messages, q, name, *tokens):
    rows = messages[0].shape[1]
    return pl.pallas_call(
        stack_kernel,
        out_shape=f32(4, q, rows),
        compiler_params=params(8),
        cost_estimate=cost(0, 32 * q * rows),
        name=name,
    )(*messages, *tokens)


def build_kernel(rel, e0, e1, e2, e3, *refs):
    hi_ref, lo_ref, token = refs[-3:]
    token[...] = jnp.zeros_like(token)
    d, _, y = coords()
    n = e0.shape[0] // 2
    iota = lax.broadcasted_iota(jnp.int32, (256, 256), 0).astype(jnp.float32).astype(jnp.bfloat16)
    lane_doc = lax.broadcasted_iota(jnp.int32, (8, 256), 1) >> 4
    one = jnp.ones((256, 256), jnp.bfloat16)
    zero = jnp.zeros((256, 256), jnp.bfloat16)

    def spread(row):
        wide = jnp.broadcast_to(row, (16, 256)).astype(jnp.bfloat16)
        return jnp.broadcast_to(wide[None], (16, 16, 256)).reshape(256, 256)

    for k, entries in enumerate((e0, e1, e2, e3)):

        @pl.loop(0, n // 16)
        def _(step, k=k, entries=entries):
            at = pl.multiple_of((y ^ rel) * (n // 2) + step * 8, 8)
            ids = entries[pl.ds(at, 8), :].astype(jnp.int32)
            vals = entries[pl.ds(n + at, 8), :]
            owner = (ids >> 8) ^ d
            block = ((owner & 1) << 3) | ((owner & 2) << 1) | (owner >> 2)
            code = (block * 16 + lane_doc).astype(jnp.float32)
            inner = (ids & 255).astype(jnp.float32)
            for t in range(8):
                pick = jnp.where(iota == spread(code[t : t + 1]), one, zero)
                weigh = jnp.where(iota == spread(inner[t : t + 1]), spread(vals[t : t + 1]), zero)
                dense = lax.dot_general(pick, weigh, NT, preferred_element_type=jnp.float32)
                high = dense.astype(jnp.bfloat16)
                low = (dense - high.astype(jnp.float32)).astype(jnp.bfloat16)
                docs = pl.ds(pl.multiple_of(k * 8 * n + step * 128 + 16 * t, 16), 16)
                hi_ref[:, docs, :] = high.reshape(16, 16, 256)
                lo_ref[:, docs, :] = low.reshape(16, 16, 256)


def whole():
    return pl.BlockSpec(memory_space=pltpu.VMEM)


def build(entries, rel, *tokens):
    docs = 4 * (entries[0].shape[0] // 4 * 16)
    *rows, token = pl.pallas_call(
        functools.partial(build_kernel, rel),
        in_specs=[whole()] * (4 + len(tokens)),
        out_specs=[whole()] * 3,
        out_shape=[pltpu.VMEM((16, docs, 256), jnp.bfloat16)] * 2 + [f32(8, 128)],
        compiler_params=params(8),
        cost_estimate=cost(2 * docs * 16 * 256 * 256, docs * 4096 * 4, 1 if rel else 64),
        name="dense_rows",
    )(*entries, *tokens)
    return rows, token


def split_rows(value):
    high = value.astype(jnp.bfloat16)
    low = (value - high.astype(jnp.float32)).astype(jnp.bfloat16)
    return jnp.concatenate([high, low], axis=0)


def add_products(hi_ref, lo_ref, vecs, blocks, total):
    for vec, first in zip(vecs, blocks):
        for pair in (0, 2):
            rows, columns = [], []
            for k in (pair, pair + 1):
                both = split_rows(vec[k])
                rows += [hi_ref[first + k], lo_ref[first + k]]
                columns += [both, both]
            total[...] += lax.dot_general(
                jnp.concatenate(columns, axis=1), jnp.concatenate(rows, axis=1), NT, preferred_element_type=jnp.float32
            )


def forward_kernel(blocks, has_before, hi_ref, lo_ref, *refs):
    count = len(blocks)
    total = refs[-1]
    total[...] = refs[count][...] if has_before else jnp.zeros_like(total)
    add_products(hi_ref, lo_ref, refs[:count], blocks, total)


def forward_part(rows, vecs, blocks, before=None, tokens=()):
    docs, q = rows[0].shape[1], vecs[0].shape[1]
    n = 4 * len(blocks)
    extra = [*tokens] if before is None else [before, *tokens]
    return pl.pallas_call(
        functools.partial(forward_kernel, blocks, before is not None),
        in_specs=[whole()] * (2 + len(vecs) + len(extra)),
        out_specs=whole(),
        out_shape=f32(2 * q, docs),
        compiler_params=params(8),
        cost_estimate=cost(8 * docs * 256 * 256 * n, 4 * docs * 256 * n),
        name="forward_part",
    )(*rows, *vecs, *extra)


def product_kernel(blocks, hi_ref, lo_ref, vec, before, *refs):
    out, total, columns = refs[-3:]
    total[...] = before[...]
    add_products(hi_ref, lo_ref, (vec,), blocks, total)
    q = out.shape[0]
    product = total[:q, :] + total[q:, :]
    if len(refs) == 3:
        out[...] = product
        return
    _, z, _ = coords()
    *messages, alpha = refs[:5]
    columns[...] = row_to_column(alpha[...])
    scale = columns[pl.ds(pl.multiple_of(z * q, q), q), :][:, 0:1]
    for k, m in enumerate(messages):
        at = slice(k * m.shape[1], (k + 1) * m.shape[1])
        out[:, at] = product[:, at] - scale * m[q:, :]


def product_half(rows, vec, before, blocks, *left):
    docs, q = rows[0].shape[1], vec.shape[1]
    return pl.pallas_call(
        functools.partial(product_kernel, blocks),
        in_specs=[whole()] * (4 + len(left)),
        out_specs=whole(),
        out_shape=f32(q, docs),
        scratch_shapes=[pltpu.VMEM((2 * q, docs), jnp.float32), pltpu.VMEM((4 * q, 128), jnp.float32)],
        compiler_params=params(8),
        cost_estimate=cost(8 * docs * 256 * 256 * 4, 16 * docs * 256),
        name="product_half",
    )(*rows, vec, before, *left)


def square_sums(value):
    q, n = value.shape
    sums = value[:, 0:128] * value[:, 0:128]
    for at in range(128, n, 128):
        sums = sums + value[:, at : at + 128] * value[:, at : at + 128]
    return jnp.sum(jnp.concatenate([sums] * (128 // q), axis=0).T, axis=0, keepdims=True)


def square_row(value, z, cols):
    row = square_sums(value)
    row = jnp.broadcast_to(jnp.concatenate([row] * (cols // 128), axis=1), (8, cols))
    lane = lax.broadcasted_iota(jnp.int32, (8, cols), 1)
    return jnp.where(lane // value.shape[0] == z, row, 0.0)


def row_to_column(row):
    return jnp.broadcast_to(row, (128, row.shape[1])).T


def left_half_kernel(mine, other, *refs):
    _, z, _ = coords()
    left = mine[...] + other[...]
    both, sums = refs[-2:]
    both[...] = split_rows(left)
    squares = square_row(left, z, sums.shape[1])
    sums[...] = refs[0][...] + squares if len(refs) == 4 else squares
    if len(refs) > 4:
        n = left.shape[1] // 4
        for k, out in enumerate(refs[:4]):
            out[...] = left[:, k * n : (k + 1) * n]


def left_half(mine, other, squares=None, token=None):
    q, docs = mine.shape
    extra = [] if squares is None else [squares, token]
    pieces = [f32(q, docs // 4)] * 4 if squares is None else []
    return pl.pallas_call(
        left_half_kernel,
        out_shape=pieces + [bf16(2 * q, docs), f32(8, 4 * q)],
        compiler_params=params(8),
        cost_estimate=cost(8 * q * docs, 16 * q * docs),
        name="left_half",
    )(mine, other, *extra)


def backward_kernel(first, blocks, parts, hi_ref, lo_ref, both_ref, *refs):
    out_ref = refs[-1]
    both = both_ref[...]
    q = both.shape[0] // 2
    twice = jnp.concatenate([both, both], axis=1)
    for b in range(blocks):
        got = jnp.dot(
            twice,
            jnp.concatenate([hi_ref[first + b], lo_ref[first + b]], axis=0),
            preferred_element_type=jnp.float32,
        )
        got = got[:q] + got[q:]
        if "before" in parts:
            got = got + refs[0][(first + b) * q : (first + b + 1) * q, :]
        out_ref[b * q : (b + 1) * q, :] = got
    if "tail" in parts:
        out_ref[blocks * q :, :] = refs[parts.index("tail")][...]


def backward_part(rows, both, first, blocks, before=None, tail=None, tokens=()):
    q, docs = both.shape[0] // 2, both.shape[1]
    extra = {"before": before, "tail": tail, **{str(i): token for i, token in enumerate(tokens)}}
    extra = {name: value for name, value in extra.items() if value is not None}
    height = blocks * q + (0 if tail is None else tail.shape[0])
    return pl.pallas_call(
        functools.partial(backward_kernel, first, blocks, tuple(extra)),
        in_specs=[whole()] * (3 + len(extra)),
        out_specs=whole(),
        out_shape=f32(height, 256),
        compiler_params=params(8),
        cost_estimate=cost(8 * docs * 256 * 256 * blocks, 4 * docs * 256 * blocks),
        name="backward_part",
    )(*rows, both, *extra.values())


def far_sum_kernel(near, far, beta, send, beta_core):
    n = near.shape[0]
    beta_core[...] = beta[...] + far[n:, :]
    send[0:n, :] = near[...] + far[0:n, :]
    send[n:, :] = beta_core[...]


def far_sums(near, far, beta):
    rows = near.shape[0]
    return pl.pallas_call(
        far_sum_kernel,
        out_shape=[f32(rows + 8, 256), f32(8, 256)],
        compiler_params=params(8),
        cost_estimate=cost(near.size, near.size * 12),
        name="far_sums",
    )(near, far, beta)


def right_norm_kernel(docs_total, keep, peer, got, beta_core, right, g0, g1, g2, g3, sums, columns):
    _, z, _ = coords()
    q = right.shape[1]
    beta_sums = beta_core[0:1, :] + got[4 * q : 4 * q + 1, :]
    columns[...] = row_to_column(jnp.sqrt(beta_sums / docs_total + epsilon))
    beta = columns[pl.ds(pl.multiple_of(z * q, q), q), :][:, 0:1]
    raws = []
    for k, g in enumerate((g0, g1, g2, g3)):
        rows = slice(k * q, (k + 1) * q)
        total = (keep[rows, :] + peer[rows, :]) + got[rows, :]
        g[...] = total
        raws.append(total / beta - beta * right[k])
    line = square_sums(jnp.concatenate(raws, axis=1))
    folded = beta_sums[:, :128] + beta_sums[:, 128:]
    folded = folded + jnp.concatenate([folded[:, q:], folded[:, :q]], axis=1)
    low = lax.broadcasted_iota(jnp.int32, line.shape, 1) < q
    sums[...] = jnp.broadcast_to(jnp.where(low, line, folded), sums.shape)


def right_norm(docs_total, keep, peer, got, beta_core, right):
    q, rows = keep.shape[0] // 4, keep.shape[1]
    *pieces, sums = pl.pallas_call(
        functools.partial(right_norm_kernel, docs_total),
        out_shape=[f32(q, rows)] * 4 + [f32(32, 128)],
        scratch_shapes=[pltpu.VMEM((4 * q, 128), jnp.float32)],
        compiler_params=params(8),
        cost_estimate=cost(rows * q * 64, rows * q * 100),
        name="right_norm",
    )(keep, peer, got, beta_core, right)
    return pieces, sums.reshape(32, 1, 128)


def finish_kernel(docs_total, feat_total, g0, g1, g2, g3, squares, own, other, right, search, solution, phibar, rhobar,
                  left_out, right_out, search_out, solution_out, alpha_out, phibar_out, rhobar_out, turned):
    _, z, y = coords()
    q, half = turned.shape[1:]
    parts = [squares[i] for i in range(32)]
    high = [jnp.concatenate([parts[8 * i][:, q:], parts[8 * i][:, :q]], axis=1) if i % 2 == 0 else parts[8 * i] for i in range(4)]
    while len(parts) > 4:
        parts = [a + b for a, b in zip(parts[::2], parts[1::2])]
    parts[1::2] = [jnp.concatenate([p[:, q:], p[:, :q]], axis=1) for p in parts[1::2]]
    low = lax.broadcasted_iota(jnp.int32, parts[0].shape, 1) < q
    alpha_sums, beta_sums = (
        jnp.concatenate([jnp.where(low, p[0], p[1]), jnp.where(low, p[2], p[3])], axis=1) for p in (parts, high)
    )
    alpha = jnp.sqrt(alpha_sums / feat_total + epsilon)
    beta = jnp.sqrt(beta_sums / docs_total + epsilon)
    for part, ref in ((y, own), (1 - y, other)):
        for k in range(4):
            turned[z ^ k] = ref[k]
        left_out[pl.ds(pl.multiple_of(part * half, half), half), :] = turned[...].reshape(-1, half).T / beta
    rho = jnp.sqrt(rhobar[...] * rhobar[...] + beta * beta)
    cosine = rhobar[...] / rho
    sine = beta / rho
    theta = sine * alpha
    phi = cosine * phibar[...]
    rhobar_out[...] = -cosine * alpha
    phibar_out[...] = sine * phibar[...]
    alpha_out[...] = alpha
    for k, g in enumerate((g0, g1, g2, g3)):
        turned[z ^ k] = g[...]
    got = turned[...].reshape(-1, half).T
    following = (got / beta - beta * right[...]) / alpha
    right_out[...] = following
    search_out[...] = following - (theta / rho) * search[...]
    solution_out[...] = solution[...] + (phi / rho) * search[...]


def finish(docs_total, feat_total, pieces, squares, own, other, right, search, solution, phibar, rhobar):
    rows, cols = right.shape
    return pl.pallas_call(
        functools.partial(finish_kernel, docs_total, feat_total),
        out_shape=[f32(2 * rows, cols)] + [f32(rows, cols)] * 3 + [f32(1, cols)] * 3,
        scratch_shapes=[pltpu.VMEM((4, cols // 4, rows), jnp.float32)],
        compiler_params=params(12),
        cost_estimate=cost(rows * cols * 16, rows * cols * 20),
        name="finish",
    )(*pieces, squares, own, other, right, search, solution, phibar, rhobar)


def swap(value, mask):
    return lax.ppermute(value, AXES, [(i, i ^ mask) for i in range(32)])


def along_z(values):
    got = {0: values[0]}
    for k in (2, 3, 1):
        got[k] = swap(values[k], k << Z_SHIFT)
    return [got[k] for k in range(4)]


def after(value, *earlier):
    return lax.optimization_barrier((value, *earlier))[0]


def by_columns(
    col_ids, col_vals, left_vec, right_vec, search_dir, solution_vec, alpha_prev, phibar, rhobar
):
    docs_total = left_vec.shape[0] * 16
    feat_total = right_vec.shape[0] * 32
    alpha_row, phibar_row, rhobar_row = (v.reshape(1, -1) for v in (alpha_prev, phibar, rhobar))

    stored, messages = prepare(col_ids.T, col_vals.T, right_vec, left_vec)
    entries = along_z([stored] * 4)
    messages = along_z([messages[0]] + [after(messages[1], entries[2]), messages[2], messages[3]])
    q = right_vec.shape[1] // 4

    rows1, token1 = build(entries, 1)
    own = stack(messages, q, "stack_right", token1)
    own_x = swap(own, X_BIT)
    own_peer = swap(own, CORE_BIT)
    rows0, token0 = build(entries, 0, own)
    total1 = forward_part(rows1, [own, own_peer], (0, 8), None, [token0])
    x_peer = swap(after(own_x, total1), CORE_BIT)
    total1 = forward_part(rows1, [own_x], (4,), total1)
    product1 = product_half(rows1, x_peer, total1, (12,))
    total0 = forward_part(rows0, [own, own_peer], (0, 8))
    total0 = forward_part(rows0, [own_x], (4,), total0)
    product0 = product_half(rows0, x_peer, total0, (12,), *messages, alpha_row)

    *lefts, both0, beta0 = left_half(product0, swap(product1, Y_BIT))
    partial = backward_part(rows0, both0, 0, 16)
    left_own = stack(along_z(lefts), q, "stack_left")
    both1, beta1 = left_half(product1, swap(product0, Y_BIT), beta0, partial)
    far = swap(backward_part(rows1, both1, 12, 4, partial, beta1, [left_own]), CORE_BIT)
    near = backward_part(rows1, both1, 4, 4, partial)
    send, beta_core = far_sums(near, far, beta1)
    got = swap(send, X_BIT)
    peer = backward_part(rows1, both1, 8, 4, partial)
    left_other = swap(after(left_own, peer), Y_BIT)
    keep = backward_part(rows1, both1, 0, 4, partial)

    sent, sums = right_norm(docs_total, keep, swap(peer, CORE_BIT), got, beta_core, own)
    pieces = along_z(sent)
    squares = lax.all_to_all(after(sums, left_other), AXES, 0, 0, tiled=True)
    left_next, right_next, search_next, solution_next, alpha_next, phibar_next, rhobar_next = finish(
        docs_total, feat_total, pieces, squares, left_own, left_other,
        right_vec, search_dir, solution_vec, phibar_row, rhobar_row,
    )
    return (
        left_next,
        right_next,
        search_next,
        solution_next,
        alpha_next.reshape(-1),
        phibar_next.reshape(-1),
        rhobar_next.reshape(-1),
    )


def forward(col_ids, col_vals, table):
    picked = table[col_ids]
    return jnp.sum(col_vals.astype(jnp.float32)[:, :, None] * picked, axis=1)


def backward(col_ids, col_vals, rows_in, width):
    terms = col_vals.astype(jnp.float32)[:, :, None] * rows_in[:, None, :]
    return jax.ops.segment_sum(
        terms.reshape(-1, rows_in.shape[1]), col_ids.reshape(-1), num_segments=width
    )


def by_blocks(
    col_ids, col_vals, left_vec, right_vec, search_dir, solution_vec, alpha_prev, phibar, rhobar
):
    n_feat = lax.axis_size("feat")
    n_doc = lax.axis_size("doc")
    docs_total = left_vec.shape[0] * n_doc
    feat_total = right_vec.shape[0] * n_doc * n_feat
    table = lax.all_gather(right_vec, "doc", axis=0, tiled=True)
    total = lax.psum(forward(col_ids, col_vals, table), "feat")
    left_raw = total - alpha_prev[None, :] * left_vec
    row_part = jnp.sum(left_raw * left_raw, axis=0)
    beta_norm = jnp.sqrt(lax.psum(row_part, "doc") / docs_total + epsilon)
    left_next = left_raw / beta_norm[None, :]
    feature_part = lax.psum_scatter(
        backward(col_ids, col_vals, left_next, table.shape[0]), "doc", scatter_dimension=0, tiled=True
    )
    right_raw = feature_part - beta_norm[None, :] * right_vec
    squares = lax.psum(jnp.sum(right_raw * right_raw, axis=0), AXES)
    alpha_next = jnp.sqrt(squares / feat_total + epsilon)
    right_next = right_raw / alpha_next[None, :]
    rho_val = jnp.sqrt(rhobar * rhobar + beta_norm * beta_norm)
    cosine = rhobar / rho_val
    sine_val = beta_norm / rho_val
    theta_val = sine_val * alpha_next
    phi_val = cosine * phibar
    solution_next = solution_vec + (phi_val / rho_val)[None, :] * search_dir
    search_next = right_next - (theta_val / rho_val)[None, :] * search_dir
    return (
        left_next,
        right_next,
        search_next,
        solution_next,
        alpha_next,
        sine_val * phibar,
        -cosine * alpha_next,
    )


def solution(mesh):
    small = mesh.shape["doc"] == 16 and mesh.shape["feat"] == 2
    rows = P(("feat", "doc"), None)
    return jax.shard_map(
        by_columns if small else by_blocks,
        mesh=mesh,
        in_specs=(P("doc", "feat"), P("doc", "feat"), P("doc", None), rows, rows, rows, P(), P(), P()),
        out_specs=(P("doc", None), rows, rows, rows, P(), P(), P()),
        check_vma=False,
    )
```

```python
import functools

import jax
import jax.numpy as jnp
from jax import lax
from jax.experimental import pallas as pl
from jax.experimental.pallas import tpu as pltpu
from jax.sharding import PartitionSpec as P

epsilon = 1e-06
AXES = ("doc", "feat")
MIB = 1024 * 1024


Y_BIT, CORE_BIT, X_BIT, Z_SHIFT = 1, 2, 4, 3
NT = (((1,), (1,)), ((), ()))


def coords():
    d = lax.axis_index("doc")
    y = lax.axis_index("feat")
    return d, d >> 2, y


def params(mib):
    return pltpu.CompilerParams(vmem_limit_bytes=mib * MIB)


def cost(flops, nbytes, scale=64):
    return pl.CostEstimate(flops=int(flops / scale), bytes_accessed=int(nbytes / scale), transcendentals=0)


def f32(*shape):
    return jax.ShapeDtypeStruct(shape, jnp.float32)


def bf16(*shape):
    return jax.ShapeDtypeStruct(shape, jnp.bfloat16)


def prepare_kernel(ids_hbm, vals_hbm, right_hbm, left_hbm, stored, m0, m1, m2, m3,
                   ids, vals, wide, right, left, turned, arrived):
    _, z, y = coords()
    q, rows = turned.shape[1:]
    copies = [
        pltpu.make_async_copy(src, dst, arrived.at[i])
        for i, (src, dst) in enumerate((
            (ids_hbm, ids),
            (vals_hbm, vals),
            (right_hbm, right),
            (left_hbm.at[pl.ds(pl.multiple_of(y * rows, rows), rows), :], left),
        ))
    ]
    for copy in copies:
        copy.start()
    lines, count = stored.shape[0] // 2, ids.shape[0]
    for part, ref in enumerate((ids, vals)):
        copies[part].wait()
        wide[...] = ref[...].astype(jnp.float32).T
        for r in range(256 // count):
            stored[part * lines : (part + 1) * lines, r * count : (r + 1) * count] = wide[
                pl.ds(r, lines, stride=256 // count), :
            ]
    for part, ref in enumerate((right, left)):
        copies[2 + part].wait()
        turned[...] = ref[...].T.reshape(turned.shape)
        for k, out in enumerate((m0, m1, m2, m3)):
            out[part * q : (part + 1) * q, :] = turned[z ^ k]


def prepare(ids, vals, right, left):
    rows, cols = right.shape
    q = cols // 4
    got = pl.pallas_call(
        prepare_kernel,
        in_specs=[pl.BlockSpec(memory_space=pltpu.HBM)] * 4,
        out_specs=[whole()] * 5,
        out_shape=[pltpu.VMEM((ids.size // 128, 256), jnp.float32)] + [pltpu.VMEM((2 * q, rows), jnp.float32)] * 4,
        scratch_shapes=[
            pltpu.VMEM(ids.shape, jnp.int32),
            pltpu.VMEM(vals.shape, jnp.bfloat16),
            pltpu.VMEM(ids.shape[::-1], jnp.float32),
            pltpu.VMEM(right.shape, jnp.float32),
            pltpu.VMEM(right.shape, jnp.float32),
            pltpu.VMEM((4, q, rows), jnp.float32),
            pltpu.SemaphoreType.DMA((4,)),
        ],
        compiler_params=params(60),
        cost_estimate=cost(0, rows * cols * 16),
        name="prepare",
    )(ids, vals, right, left)
    return got[0], got[1:]


def stack_kernel(m0, m1, m2, m3, *refs):
    out = refs[-1]
    for k, m in enumerate((m0, m1, m2, m3)):
        out[k] = m[0 : out.shape[1], :]


def stack(messages, q, name, *tokens):
    rows = messages[0].shape[1]
    return pl.pallas_call(
        stack_kernel,
        out_shape=f32(4, q, rows),
        compiler_params=params(8),
        cost_estimate=cost(0, 32 * q * rows),
        name=name,
    )(*messages, *tokens)


def build_kernel(rel, e0, e1, e2, e3, *refs):
    hi_ref, lo_ref, token = refs[-3:]
    token[...] = jnp.zeros_like(token)
    d, _, y = coords()
    n = e0.shape[0] // 2
    iota = lax.broadcasted_iota(jnp.int32, (256, 256), 0).astype(jnp.float32).astype(jnp.bfloat16)
    lane_doc = lax.broadcasted_iota(jnp.int32, (8, 256), 1) >> 4
    one = jnp.ones((256, 256), jnp.bfloat16)
    zero = jnp.zeros((256, 256), jnp.bfloat16)

    def spread(row):
        wide = jnp.broadcast_to(row, (16, 256)).astype(jnp.bfloat16)
        return jnp.broadcast_to(wide[None], (16, 16, 256)).reshape(256, 256)

    for k, entries in enumerate((e0, e1, e2, e3)):

        @pl.loop(0, n // 16)
        def _(step, k=k, entries=entries):
            at = pl.multiple_of((y ^ rel) * (n // 2) + step * 8, 8)
            ids = entries[pl.ds(at, 8), :].astype(jnp.int32)
            vals = entries[pl.ds(n + at, 8), :]
            owner = (ids >> 8) ^ d
            block = ((owner & 1) << 3) | ((owner & 2) << 1) | (owner >> 2)
            code = (block * 16 + lane_doc).astype(jnp.float32)
            inner = (ids & 255).astype(jnp.float32)
            for t in range(8):
                pick = jnp.where(iota == spread(code[t : t + 1]), one, zero)
                weigh = jnp.where(iota == spread(inner[t : t + 1]), spread(vals[t : t + 1]), zero)
                dense = lax.dot_general(pick, weigh, NT, preferred_element_type=jnp.float32)
                high = dense.astype(jnp.bfloat16)
                low = (dense - high.astype(jnp.float32)).astype(jnp.bfloat16)
                docs = pl.ds(pl.multiple_of(k * 8 * n + step * 128 + 16 * t, 16), 16)
                hi_ref[:, docs, :] = high.reshape(16, 16, 256)
                lo_ref[:, docs, :] = low.reshape(16, 16, 256)


def whole():
    return pl.BlockSpec(memory_space=pltpu.VMEM)


def build(entries, rel, *tokens):
    docs = 4 * (entries[0].shape[0] // 4 * 16)
    *rows, token = pl.pallas_call(
        functools.partial(build_kernel, rel),
        in_specs=[whole()] * (4 + len(tokens)),
        out_specs=[whole()] * 3,
        out_shape=[pltpu.VMEM((16, docs, 256), jnp.bfloat16)] * 2 + [f32(8, 128)],
        compiler_params=params(8),
        cost_estimate=cost(2 * docs * 16 * 256 * 256, docs * 4096 * 4, 1 if rel else 64),
        name="dense_rows",
    )(*entries, *tokens)
    return rows, token


def split_rows(value):
    high = value.astype(jnp.bfloat16)
    low = (value - high.astype(jnp.float32)).astype(jnp.bfloat16)
    return jnp.concatenate([high, low], axis=0)


def add_products(hi_ref, lo_ref, vecs, blocks, total):
    for vec, first in zip(vecs, blocks):
        for pair in (0, 2):
            lhs, rhs = [], []
            for k in (pair, pair + 1):
                both = split_rows(vec[k])
                lhs += [hi_ref[first + k], lo_ref[first + k]]
                rhs += [both, both]
            total[...] += lax.dot_general(
                jnp.concatenate(lhs, axis=1), jnp.concatenate(rhs, axis=1), NT, preferred_element_type=jnp.float32
            )


def forward_kernel(blocks, has_before, hi_ref, lo_ref, *refs):
    count = len(blocks)
    total = refs[-1]
    total[...] = refs[count][...] if has_before else jnp.zeros_like(total)
    add_products(hi_ref, lo_ref, refs[:count], blocks, total)


def forward_part(rows, vecs, blocks, before=None, tokens=()):
    docs, q = rows[0].shape[1], vecs[0].shape[1]
    n = 4 * len(blocks)
    extra = [*tokens] if before is None else [before, *tokens]
    return pl.pallas_call(
        functools.partial(forward_kernel, blocks, before is not None),
        in_specs=[whole()] * (2 + len(vecs) + len(extra)),
        out_specs=whole(),
        out_shape=f32(docs, 2 * q),
        compiler_params=params(8),
        cost_estimate=cost(8 * docs * 256 * 256 * n, 4 * docs * 256 * n),
        name="forward_part",
    )(*rows, *vecs, *extra)


def product_kernel(blocks, hi_ref, lo_ref, vec, before, *refs):
    out, total, columns = refs[-3:]
    total[...] = before[...]
    add_products(hi_ref, lo_ref, (vec,), blocks, total)
    turned = total[...].T
    q = out.shape[0]
    product = turned[:q] + turned[q:]
    if len(refs) == 3:
        out[...] = product
        return
    _, z, _ = coords()
    *messages, alpha = refs[:5]
    columns[...] = row_to_column(alpha[...])
    scale = columns[pl.ds(pl.multiple_of(z * q, q), q), :][:, 0:1]
    for k, m in enumerate(messages):
        at = slice(k * m.shape[1], (k + 1) * m.shape[1])
        out[:, at] = product[:, at] - scale * m[q:, :]


def product_half(rows, vec, before, blocks, *left):
    docs, q = rows[0].shape[1], vec.shape[1]
    return pl.pallas_call(
        functools.partial(product_kernel, blocks),
        in_specs=[whole()] * (4 + len(left)),
        out_specs=whole(),
        out_shape=f32(q, docs),
        scratch_shapes=[pltpu.VMEM((docs, 2 * q), jnp.float32), pltpu.VMEM((4 * q, 128), jnp.float32)],
        compiler_params=params(8),
        cost_estimate=cost(8 * docs * 256 * 256 * 4, 16 * docs * 256),
        name="product_half",
    )(*rows, vec, before, *left)


def square_sums(value):
    q, n = value.shape
    sums = value[:, 0:128] * value[:, 0:128]
    for at in range(128, n, 128):
        sums = sums + value[:, at : at + 128] * value[:, at : at + 128]
    return jnp.sum(jnp.concatenate([sums] * (128 // q), axis=0).T, axis=0, keepdims=True)


def square_row(value, z, cols):
    row = square_sums(value)
    row = jnp.broadcast_to(jnp.concatenate([row] * (cols // 128), axis=1), (8, cols))
    lane = lax.broadcasted_iota(jnp.int32, (8, cols), 1)
    return jnp.where(lane // value.shape[0] == z, row, 0.0)


def row_to_column(row):
    return jnp.broadcast_to(row, (128, row.shape[1])).T


def left_half_kernel(mine, other, *refs):
    _, z, _ = coords()
    left = mine[...] + other[...]
    both, sums = refs[-2:]
    both[...] = split_rows(left)
    squares = square_row(left, z, sums.shape[1])
    sums[...] = refs[0][...] + squares if len(refs) == 4 else squares
    if len(refs) > 4:
        n = left.shape[1] // 4
        for k, out in enumerate(refs[:4]):
            out[...] = left[:, k * n : (k + 1) * n]


def left_half(mine, other, squares=None, token=None):
    q, docs = mine.shape
    extra = [] if squares is None else [squares, token]
    pieces = [f32(q, docs // 4)] * 4 if squares is None else []
    return pl.pallas_call(
        left_half_kernel,
        out_shape=pieces + [bf16(2 * q, docs), f32(8, 4 * q)],
        compiler_params=params(8),
        cost_estimate=cost(8 * q * docs, 16 * q * docs),
        name="left_half",
    )(mine, other, *extra)


def backward_kernel(first, blocks, parts, hi_ref, lo_ref, both_ref, *refs):
    out_ref = refs[-1]
    both = both_ref[...]
    q = both.shape[0] // 2
    twice = jnp.concatenate([both, both], axis=1)
    for b in range(blocks):
        got = jnp.dot(
            twice,
            jnp.concatenate([hi_ref[first + b], lo_ref[first + b]], axis=0),
            preferred_element_type=jnp.float32,
        )
        got = got[:q] + got[q:]
        if "before" in parts:
            got = got + refs[0][(first + b) * q : (first + b + 1) * q, :]
        out_ref[b * q : (b + 1) * q, :] = got
    if "tail" in parts:
        out_ref[blocks * q :, :] = refs[parts.index("tail")][...]


def backward_part(rows, both, first, blocks, before=None, tail=None, tokens=(), scale=64):
    q, docs = both.shape[0] // 2, both.shape[1]
    extra = {"before": before, "tail": tail, **{str(i): token for i, token in enumerate(tokens)}}
    extra = {name: value for name, value in extra.items() if value is not None}
    height = blocks * q + (0 if tail is None else tail.shape[0])
    return pl.pallas_call(
        functools.partial(backward_kernel, first, blocks, tuple(extra)),
        in_specs=[whole()] * (3 + len(extra)),
        out_specs=whole(),
        out_shape=f32(height, 256),
        compiler_params=params(8),
        cost_estimate=cost(8 * docs * 256 * 256 * blocks, 4 * docs * 256 * blocks, scale),
        name="backward_part",
    )(*rows, both, *extra.values())


def far_sum_kernel(near, far, beta, token, send_far, send_near, beta_core):
    n = near.shape[0] // 2
    beta_core[...] = beta[...] + far[2 * n :, :]
    send_far[...] = near[n:, :] + far[n : 2 * n, :]
    send_near[0:n, :] = near[0:n, :] + far[0:n, :]
    send_near[n:, :] = beta_core[...]


def far_sums(near, far, beta, token):
    rows = near.shape[0] // 2
    return pl.pallas_call(
        far_sum_kernel,
        out_shape=[f32(rows, 256), f32(rows + 8, 256), f32(8, 256)],
        compiler_params=params(8),
        cost_estimate=cost(near.size, near.size * 12),
        name="far_sums",
    )(near, far, beta, token)


def right_far_kernel(keep, peer, got, g2, g3):
    q = g2.shape[0]
    for k, g in ((2, g2), (3, g3)):
        rows = slice(k * q, (k + 1) * q)
        g[...] = (keep[rows, :] + peer[rows, :]) + got[(k - 2) * q : (k - 1) * q, :]


def right_far(keep, peer, got):
    q, rows = keep.shape[0] // 4, keep.shape[1]
    return pl.pallas_call(
        right_far_kernel,
        out_shape=[f32(q, rows)] * 2,
        compiler_params=params(8),
        cost_estimate=cost(rows * q * 4, rows * q * 32),
        name="right_far",
    )(keep, peer, got)


def right_norm_kernel(docs_total, keep, peer, got, beta_core, right, g2, g3, g0, g1, sums, columns):
    _, z, _ = coords()
    q = right.shape[1]
    beta_sums = beta_core[0:1, :] + got[2 * q : 2 * q + 1, :]
    columns[...] = row_to_column(jnp.sqrt(beta_sums / docs_total + epsilon))
    beta = columns[pl.ds(pl.multiple_of(z * q, q), q), :][:, 0:1]
    for k, g in enumerate((g0, g1)):
        rows = slice(k * q, (k + 1) * q)
        g[...] = (keep[rows, :] + peer[rows, :]) + got[rows, :]
    raws = [g[...] / beta - beta * right[k] for k, g in enumerate((g0, g1, g2, g3))]
    line = square_sums(jnp.concatenate(raws, axis=1))
    folded = beta_sums[:, :128] + beta_sums[:, 128:]
    folded = folded + jnp.concatenate([folded[:, q:], folded[:, :q]], axis=1)
    low = lax.broadcasted_iota(jnp.int32, line.shape, 1) < q
    sums[...] = jnp.broadcast_to(jnp.where(low, line, folded), sums.shape)


def right_norm(docs_total, keep, peer, got, beta_core, right, far):
    q, rows = keep.shape[0] // 4, keep.shape[1]
    g0, g1, sums = pl.pallas_call(
        functools.partial(right_norm_kernel, docs_total),
        out_shape=[f32(q, rows)] * 2 + [f32(32, 128)],
        scratch_shapes=[pltpu.VMEM((4 * q, 128), jnp.float32)],
        compiler_params=params(8),
        cost_estimate=cost(rows * q * 64, rows * q * 100, 64),
        name="right_norm",
    )(keep, peer, got, beta_core, right, *far)
    return g0, g1, sums.reshape(32, 1, 128)


def finish_kernel(docs_total, feat_total, g0, g1, g2, g3, squares, own, other, right, search, solution, phibar, rhobar,
                  left_out, right_out, search_out, solution_out, alpha_out, phibar_out, rhobar_out, turned):
    _, z, y = coords()
    q, half = turned.shape[1:]
    parts = [squares[i] for i in range(32)]
    high = [jnp.concatenate([parts[8 * i][:, q:], parts[8 * i][:, :q]], axis=1) if i % 2 == 0 else parts[8 * i] for i in range(4)]
    while len(parts) > 4:
        parts = [a + b for a, b in zip(parts[::2], parts[1::2])]
    parts[1::2] = [jnp.concatenate([p[:, q:], p[:, :q]], axis=1) for p in parts[1::2]]
    low = lax.broadcasted_iota(jnp.int32, parts[0].shape, 1) < q
    alpha_sums, beta_sums = (
        jnp.concatenate([jnp.where(low, p[0], p[1]), jnp.where(low, p[2], p[3])], axis=1) for p in (parts, high)
    )
    alpha = jnp.sqrt(alpha_sums / feat_total + epsilon)
    beta = jnp.sqrt(beta_sums / docs_total + epsilon)
    for part, ref in ((y, own), (1 - y, other)):
        for k in range(4):
            turned[z ^ k] = ref[k]
        left_out[pl.ds(pl.multiple_of(part * half, half), half), :] = turned[...].reshape(-1, half).T / beta
    rho = jnp.sqrt(rhobar[...] * rhobar[...] + beta * beta)
    cosine = rhobar[...] / rho
    sine = beta / rho
    theta = sine * alpha
    phi = cosine * phibar[...]
    rhobar_out[...] = -cosine * alpha
    phibar_out[...] = sine * phibar[...]
    alpha_out[...] = alpha
    for k, g in enumerate((g0, g1, g2, g3)):
        turned[z ^ k] = g[...]
    got = turned[...].reshape(-1, half).T
    following = (got / beta - beta * right[...]) / alpha
    right_out[...] = following
    search_out[...] = following - (theta / rho) * search[...]
    solution_out[...] = solution[...] + (phi / rho) * search[...]


def finish(docs_total, feat_total, pieces, squares, own, other, right, search, solution, phibar, rhobar):
    rows, cols = right.shape
    return pl.pallas_call(
        functools.partial(finish_kernel, docs_total, feat_total),
        out_shape=[f32(2 * rows, cols)] + [f32(rows, cols)] * 3 + [f32(1, cols)] * 3,
        scratch_shapes=[pltpu.VMEM((4, cols // 4, rows), jnp.float32)],
        compiler_params=params(12),
        cost_estimate=cost(rows * cols * 16, rows * cols * 20),
        name="finish",
    )(*pieces, squares, own, other, right, search, solution, phibar, rhobar)


def swap(value, mask):
    return lax.ppermute(value, AXES, [(i, i ^ mask) for i in range(32)])


def along_z(values):
    got = {0: values[0]}
    for k in (2, 3, 1):
        got[k] = swap(values[k], k << Z_SHIFT)
    return [got[k] for k in range(4)]


def after(value, *earlier):
    return lax.optimization_barrier((value, *earlier))[0]


def by_columns(
    col_ids, col_vals, left_vec, right_vec, search_dir, solution_vec, alpha_prev, phibar, rhobar
):
    docs_total = left_vec.shape[0] * 16
    feat_total = right_vec.shape[0] * 32
    alpha_row, phibar_row, rhobar_row = (v.reshape(1, -1) for v in (alpha_prev, phibar, rhobar))

    stored, messages = prepare(col_ids.T, col_vals.T, right_vec, left_vec)
    entries = along_z([stored] * 4)
    messages = along_z([messages[0]] + [after(messages[1], entries[2]), messages[2], messages[3]])
    q = right_vec.shape[1] // 4

    rows1, token1 = build(entries, 1)
    own = stack(messages, q, "stack_right", token1)
    own_x = swap(own, X_BIT)
    own_peer = swap(own, CORE_BIT)
    rows0, token0 = build(entries, 0, own)
    total1 = forward_part(rows1, [own, own_peer], (0, 8), None, [token0])
    x_peer = swap(after(own_x, total1), CORE_BIT)
    total1 = forward_part(rows1, [own_x], (4,), total1)
    product1 = product_half(rows1, x_peer, total1, (12,))
    total0 = forward_part(rows0, [own, own_peer], (0, 8))
    total0 = forward_part(rows0, [own_x], (4,), total0)
    product0 = product_half(rows0, x_peer, total0, (12,), *messages, alpha_row)

    *lefts, both0, beta0 = left_half(product0, swap(product1, Y_BIT))
    partial = backward_part(rows0, both0, 0, 16)
    left_own = stack(along_z(lefts), q, "stack_left")
    both1, beta1 = left_half(product1, swap(product0, Y_BIT), beta0, partial)
    far = swap(backward_part(rows1, both1, 12, 4, partial, beta1, [left_own]), CORE_BIT)
    near = backward_part(rows1, both1, 4, 4, partial)
    peer = backward_part(rows1, both1, 8, 4, partial, None, [near])
    send_far, send_near, beta_core = far_sums(near, far, beta1, peer)
    got_far = swap(send_far, X_BIT)
    got_near = swap(send_near, X_BIT)
    keep = backward_part(rows1, both1, 0, 4, partial, None, [], 0.05)
    peer = swap(peer, CORE_BIT)

    g2, g3 = right_far(keep, peer, got_far)
    p2, p3 = swap(g2, 2 << Z_SHIFT), swap(g3, 3 << Z_SHIFT)
    g0, g1, sums = right_norm(docs_total, keep, peer, got_near, beta_core, own, (g2, g3))
    pieces = [g0, swap(g1, 1 << Z_SHIFT), p2, p3]
    left_other = swap(after(left_own, got_far), Y_BIT)
    squares = lax.all_to_all(after(sums, left_own), AXES, 0, 0, tiled=True)
    left_next, right_next, search_next, solution_next, alpha_next, phibar_next, rhobar_next = finish(
        docs_total, feat_total, pieces, squares, left_own, left_other,
        right_vec, search_dir, solution_vec, phibar_row, rhobar_row,
    )
    return (
        left_next,
        right_next,
        search_next,
        solution_next,
        alpha_next.reshape(-1),
        phibar_next.reshape(-1),
        rhobar_next.reshape(-1),
    )


def forward(col_ids, col_vals, table):
    picked = table[col_ids]
    return jnp.sum(col_vals.astype(jnp.float32)[:, :, None] * picked, axis=1)


def backward(col_ids, col_vals, rows_in, width):
    terms = col_vals.astype(jnp.float32)[:, :, None] * rows_in[:, None, :]
    return jax.ops.segment_sum(
        terms.reshape(-1, rows_in.shape[1]), col_ids.reshape(-1), num_segments=width
    )


def by_blocks(
    col_ids, col_vals, left_vec, right_vec, search_dir, solution_vec, alpha_prev, phibar, rhobar
):
    n_feat = lax.axis_size("feat")
    n_doc = lax.axis_size("doc")
    docs_total = left_vec.shape[0] * n_doc
    feat_total = right_vec.shape[0] * n_doc * n_feat
    table = lax.all_gather(right_vec, "doc", axis=0, tiled=True)
    total = lax.psum(forward(col_ids, col_vals, table), "feat")
    left_raw = total - alpha_prev[None, :] * left_vec
    row_part = jnp.sum(left_raw * left_raw, axis=0)
    beta_norm = jnp.sqrt(lax.psum(row_part, "doc") / docs_total + epsilon)
    left_next = left_raw / beta_norm[None, :]
    feature_part = lax.psum_scatter(
        backward(col_ids, col_vals, left_next, table.shape[0]), "doc", scatter_dimension=0, tiled=True
    )
    right_raw = feature_part - beta_norm[None, :] * right_vec
    squares = lax.psum(jnp.sum(right_raw * right_raw, axis=0), AXES)
    alpha_next = jnp.sqrt(squares / feat_total + epsilon)
    right_next = right_raw / alpha_next[None, :]
    rho_val = jnp.sqrt(rhobar * rhobar + beta_norm * beta_norm)
    cosine = rhobar / rho_val
    sine_val = beta_norm / rho_val
    theta_val = sine_val * alpha_next
    phi_val = cosine * phibar
    solution_next = solution_vec + (phi_val / rho_val)[None, :] * search_dir
    search_next = right_next - (theta_val / rho_val)[None, :] * search_dir
    return (
        left_next,
        right_next,
        search_next,
        solution_next,
        alpha_next,
        sine_val * phibar,
        -cosine * alpha_next,
    )


def solution(mesh):
    small = mesh.shape["doc"] == 16 and mesh.shape["feat"] == 2
    rows = P(("feat", "doc"), None)
    return jax.shard_map(
        by_columns if small else by_blocks,
        mesh=mesh,
        in_specs=(P("doc", "feat"), P("doc", "feat"), P("doc", None), rows, rows, rows, P(), P(), P()),
        out_specs=(P("doc", None), rows, rows, rows, P(), P(), P()),
        check_vma=False,
    )
```

```python
import functools

import jax
import jax.numpy as jnp
from jax import lax
from jax.experimental import pallas as pl
from jax.experimental.pallas import tpu as pltpu
from jax.sharding import PartitionSpec as P

epsilon = 1e-06
AXES = ("doc", "feat")
MIB = 1024 * 1024


Y_BIT, CORE_BIT, X_BIT, Z_SHIFT = 1, 2, 4, 3
NT = (((1,), (1,)), ((), ()))


def coords():
    d = lax.axis_index("doc")
    y = lax.axis_index("feat")
    return d, d >> 2, y


def params(mib):
    return pltpu.CompilerParams(vmem_limit_bytes=mib * MIB)


def cost(flops, nbytes, scale=64):
    return pl.CostEstimate(flops=int(flops / scale), bytes_accessed=int(nbytes / scale), transcendentals=0)


def f32(*shape):
    return jax.ShapeDtypeStruct(shape, jnp.float32)


def bf16(*shape):
    return jax.ShapeDtypeStruct(shape, jnp.bfloat16)


def prepare_kernel(ids_hbm, vals_hbm, right_hbm, left_hbm, stored, m0, m1, m2, m3,
                   ids, vals, wide, right, left, turned, arrived):
    _, z, y = coords()
    q, rows = turned.shape[1:]
    copies = [
        pltpu.make_async_copy(src, dst, arrived.at[i])
        for i, (src, dst) in enumerate((
            (ids_hbm, ids),
            (vals_hbm, vals),
            (right_hbm, right),
            (left_hbm.at[pl.ds(pl.multiple_of(y * rows, rows), rows), :], left),
        ))
    ]
    for copy in copies:
        copy.start()
    lines, count = stored.shape[0] // 2, ids.shape[0]
    for part, ref in enumerate((ids, vals)):
        copies[part].wait()
        wide[...] = ref[...].astype(jnp.float32).T
        for r in range(256 // count):
            stored[part * lines : (part + 1) * lines, r * count : (r + 1) * count] = wide[
                pl.ds(r, lines, stride=256 // count), :
            ]
    for part, ref in enumerate((right, left)):
        copies[2 + part].wait()
        turned[...] = ref[...].T.reshape(turned.shape)
        for k, out in enumerate((m0, m1, m2, m3)):
            out[part * q : (part + 1) * q, :] = turned[z ^ k]


def prepare(ids, vals, right, left):
    rows, cols = right.shape
    q = cols // 4
    got = pl.pallas_call(
        prepare_kernel,
        in_specs=[pl.BlockSpec(memory_space=pltpu.HBM)] * 4,
        out_specs=[whole()] * 5,
        out_shape=[pltpu.VMEM((ids.size // 128, 256), jnp.float32)] + [pltpu.VMEM((2 * q, rows), jnp.float32)] * 4,
        scratch_shapes=[
            pltpu.VMEM(ids.shape, jnp.int32),
            pltpu.VMEM(vals.shape, jnp.bfloat16),
            pltpu.VMEM(ids.shape[::-1], jnp.float32),
            pltpu.VMEM(right.shape, jnp.float32),
            pltpu.VMEM(right.shape, jnp.float32),
            pltpu.VMEM((4, q, rows), jnp.float32),
            pltpu.SemaphoreType.DMA((4,)),
        ],
        compiler_params=params(60),
        cost_estimate=cost(0, rows * cols * 16),
        name="prepare",
    )(ids, vals, right, left)
    return got[0], got[1:]


def stack_kernel(m0, m1, m2, m3, *refs):
    out = refs[-1]
    for k, m in enumerate((m0, m1, m2, m3)):
        out[k] = m[0 : out.shape[1], :]


def stack(messages, q, name, *tokens):
    rows = messages[0].shape[1]
    return pl.pallas_call(
        stack_kernel,
        out_shape=f32(4, q, rows),
        compiler_params=params(8),
        cost_estimate=cost(0, 32 * q * rows),
        name=name,
    )(*messages, *tokens)


def build_kernel(rel, e0, e1, e2, e3, *refs):
    hi_ref, lo_ref, token = refs[-3:]
    token[...] = jnp.zeros_like(token)
    d, _, y = coords()
    n = e0.shape[0] // 2
    iota = lax.broadcasted_iota(jnp.int32, (256, 256), 0).astype(jnp.float32).astype(jnp.bfloat16)
    lane_doc = lax.broadcasted_iota(jnp.int32, (8, 256), 1) >> 4
    one = jnp.ones((256, 256), jnp.bfloat16)
    zero = jnp.zeros((256, 256), jnp.bfloat16)

    def spread(row):
        wide = jnp.broadcast_to(row, (16, 256)).astype(jnp.bfloat16)
        return jnp.broadcast_to(wide[None], (16, 16, 256)).reshape(256, 256)

    for k, entries in enumerate((e0, e1, e2, e3)):

        @pl.loop(0, n // 16)
        def _(step, k=k, entries=entries):
            at = pl.multiple_of((y ^ rel) * (n // 2) + step * 8, 8)
            ids = entries[pl.ds(at, 8), :].astype(jnp.int32)
            vals = entries[pl.ds(n + at, 8), :]
            owner = (ids >> 8) ^ d
            block = ((owner & 1) << 3) | ((owner & 2) << 1) | (owner >> 2)
            code = (block * 16 + lane_doc).astype(jnp.float32)
            inner = (ids & 255).astype(jnp.float32)
            for t in range(8):
                pick = jnp.where(iota == spread(code[t : t + 1]), one, zero)
                weigh = jnp.where(iota == spread(inner[t : t + 1]), spread(vals[t : t + 1]), zero)
                dense = lax.dot_general(pick, weigh, NT, preferred_element_type=jnp.float32)
                high = dense.astype(jnp.bfloat16)
                low = (dense - high.astype(jnp.float32)).astype(jnp.bfloat16)
                docs = pl.ds(pl.multiple_of(k * 8 * n + step * 128 + 16 * t, 16), 16)
                hi_ref[:, docs, :] = high.reshape(16, 16, 256)
                lo_ref[:, docs, :] = low.reshape(16, 16, 256)


def whole():
    return pl.BlockSpec(memory_space=pltpu.VMEM)


def build(entries, rel, *tokens):
    docs = 4 * (entries[0].shape[0] // 4 * 16)
    *rows, token = pl.pallas_call(
        functools.partial(build_kernel, rel),
        in_specs=[whole()] * (4 + len(tokens)),
        out_specs=[whole()] * 3,
        out_shape=[pltpu.VMEM((16, docs, 256), jnp.bfloat16)] * 2 + [f32(8, 128)],
        compiler_params=params(8),
        cost_estimate=cost(2 * docs * 16 * 256 * 256, docs * 4096 * 4, 1 if rel else 64),
        name="dense_rows",
    )(*entries, *tokens)
    return rows, token


def split_rows(value):
    high = value.astype(jnp.bfloat16)
    low = (value - high.astype(jnp.float32)).astype(jnp.bfloat16)
    return jnp.concatenate([high, low], axis=0)


def add_products(hi_ref, lo_ref, vecs, blocks, total):
    for vec, first in zip(vecs, blocks):
        for pair in (0, 2):
            lhs, rhs = [], []
            for k in (pair, pair + 1):
                both = split_rows(vec[k])
                lhs += [hi_ref[first + k], lo_ref[first + k]]
                rhs += [both, both]
            total[...] += lax.dot_general(
                jnp.concatenate(lhs, axis=1), jnp.concatenate(rhs, axis=1), NT, preferred_element_type=jnp.float32
            )


def forward_kernel(blocks, has_before, hi_ref, lo_ref, *refs):
    count = len(blocks)
    total = refs[-1]
    total[...] = refs[count][...] if has_before else jnp.zeros_like(total)
    add_products(hi_ref, lo_ref, refs[:count], blocks, total)


def forward_part(rows, vecs, blocks, before=None, tokens=()):
    docs, q = rows[0].shape[1], vecs[0].shape[1]
    n = 4 * len(blocks)
    extra = [*tokens] if before is None else [before, *tokens]
    return pl.pallas_call(
        functools.partial(forward_kernel, blocks, before is not None),
        in_specs=[whole()] * (2 + len(vecs) + len(extra)),
        out_specs=whole(),
        out_shape=f32(docs, 2 * q),
        compiler_params=params(8),
        cost_estimate=cost(8 * docs * 256 * 256 * n, 4 * docs * 256 * n),
        name="forward_part",
    )(*rows, *vecs, *extra)


def product_kernel(blocks, hi_ref, lo_ref, vec, before, *refs):
    out, total, columns = refs[-3:]
    total[...] = before[...]
    add_products(hi_ref, lo_ref, (vec,), blocks, total)
    turned = total[...].T
    q = out.shape[0]
    product = turned[:q] + turned[q:]
    if len(refs) == 3:
        out[...] = product
        return
    _, z, _ = coords()
    *messages, alpha = refs[:5]
    columns[...] = row_to_column(alpha[...])
    scale = columns[pl.ds(pl.multiple_of(z * q, q), q), :][:, 0:1]
    for k, m in enumerate(messages):
        at = slice(k * m.shape[1], (k + 1) * m.shape[1])
        out[:, at] = product[:, at] - scale * m[q:, :]


def product_half(rows, vec, before, blocks, *left):
    docs, q = rows[0].shape[1], vec.shape[1]
    return pl.pallas_call(
        functools.partial(product_kernel, blocks),
        in_specs=[whole()] * (4 + len(left)),
        out_specs=whole(),
        out_shape=f32(q, docs),
        scratch_shapes=[pltpu.VMEM((docs, 2 * q), jnp.float32), pltpu.VMEM((4 * q, 128), jnp.float32)],
        compiler_params=params(8),
        cost_estimate=cost(8 * docs * 256 * 256 * 4, 16 * docs * 256),
        name="product_half",
    )(*rows, vec, before, *left)


def square_sums(value):
    q, n = value.shape
    sums = value[:, 0:128] * value[:, 0:128]
    for at in range(128, n, 128):
        sums = sums + value[:, at : at + 128] * value[:, at : at + 128]
    return jnp.sum(jnp.concatenate([sums] * (128 // q), axis=0).T, axis=0, keepdims=True)


def square_row(value, z, cols):
    row = square_sums(value)
    row = jnp.broadcast_to(jnp.concatenate([row] * (cols // 128), axis=1), (8, cols))
    lane = lax.broadcasted_iota(jnp.int32, (8, cols), 1)
    return jnp.where(lane // value.shape[0] == z, row, 0.0)


def row_to_column(row):
    return jnp.broadcast_to(row, (128, row.shape[1])).T


def left_half_kernel(mine, other, *refs):
    _, z, _ = coords()
    left = mine[...] + other[...]
    both, sums = refs[-2:]
    both[...] = split_rows(left)
    squares = square_row(left, z, sums.shape[1])
    sums[...] = refs[0][...] + squares if len(refs) == 4 else squares
    if len(refs) > 4:
        n = left.shape[1] // 4
        for k, out in enumerate(refs[:4]):
            out[...] = left[:, k * n : (k + 1) * n]


def left_half(mine, other, squares=None, token=None):
    q, docs = mine.shape
    extra = [] if squares is None else [squares, token]
    pieces = [f32(q, docs // 4)] * 4 if squares is None else []
    return pl.pallas_call(
        left_half_kernel,
        out_shape=pieces + [bf16(2 * q, docs), f32(8, 4 * q)],
        compiler_params=params(8),
        cost_estimate=cost(8 * q * docs, 16 * q * docs),
        name="left_half",
    )(mine, other, *extra)


def backward_kernel(first, blocks, parts, hi_ref, lo_ref, both_ref, *refs):
    out_ref = refs[-1]
    both = both_ref[...]
    q = both.shape[0] // 2
    twice = jnp.concatenate([both, both], axis=1)
    for b in range(blocks):
        got = jnp.dot(
            twice,
            jnp.concatenate([hi_ref[first + b], lo_ref[first + b]], axis=0),
            preferred_element_type=jnp.float32,
        )
        got = got[:q] + got[q:]
        if "before" in parts:
            got = got + refs[0][(first + b) * q : (first + b + 1) * q, :]
        out_ref[b * q : (b + 1) * q, :] = got
    if "tail" in parts:
        out_ref[blocks * q :, :] = refs[parts.index("tail")][...]


def backward_part(rows, both, first, blocks, before=None, tail=None, tokens=(), scale=64):
    q, docs = both.shape[0] // 2, both.shape[1]
    extra = {"before": before, "tail": tail, **{str(i): token for i, token in enumerate(tokens)}}
    extra = {name: value for name, value in extra.items() if value is not None}
    height = blocks * q + (0 if tail is None else tail.shape[0])
    return pl.pallas_call(
        functools.partial(backward_kernel, first, blocks, tuple(extra)),
        in_specs=[whole()] * (3 + len(extra)),
        out_specs=whole(),
        out_shape=f32(height, 256),
        compiler_params=params(8),
        cost_estimate=cost(8 * docs * 256 * 256 * blocks, 4 * docs * 256 * blocks, scale),
        name="backward_part",
    )(*rows, both, *extra.values())


def far_sum_kernel(near, far, beta, token, send_far, send_near, beta_core):
    n = near.shape[0] // 2
    beta_core[...] = beta[...] + far[2 * n :, :]
    send_far[...] = near[n:, :] + far[n : 2 * n, :]
    send_near[0:n, :] = near[0:n, :] + far[0:n, :]
    send_near[n:, :] = beta_core[...]


def far_sums(near, far, beta, token):
    rows = near.shape[0] // 2
    return pl.pallas_call(
        far_sum_kernel,
        out_shape=[f32(rows, 256), f32(rows + 8, 256), f32(8, 256)],
        compiler_params=params(8),
        cost_estimate=cost(near.size, near.size * 12),
        name="far_sums",
    )(near, far, beta, token)


def right_far_kernel(keep, peer, got, g2, g3):
    q = g2.shape[0]
    for k, g in ((2, g2), (3, g3)):
        rows = slice(k * q, (k + 1) * q)
        g[...] = (keep[rows, :] + peer[rows, :]) + got[(k - 2) * q : (k - 1) * q, :]


def right_far(keep, peer, got):
    q, rows = keep.shape[0] // 4, keep.shape[1]
    return pl.pallas_call(
        right_far_kernel,
        out_shape=[f32(q, rows)] * 2,
        compiler_params=params(8),
        cost_estimate=cost(rows * q * 4, rows * q * 32),
        name="right_far",
    )(keep, peer, got)


def right_norm_kernel(docs_total, keep, peer, got, beta_core, right, g2, g3, g0, g1, sums, columns):
    _, z, _ = coords()
    q = right.shape[1]
    beta_sums = beta_core[0:1, :] + got[2 * q : 2 * q + 1, :]
    columns[...] = row_to_column(jnp.sqrt(beta_sums / docs_total + epsilon))
    beta = columns[pl.ds(pl.multiple_of(z * q, q), q), :][:, 0:1]
    for k, g in enumerate((g0, g1)):
        rows = slice(k * q, (k + 1) * q)
        g[...] = (keep[rows, :] + peer[rows, :]) + got[rows, :]
    raws = [g[...] / beta - beta * right[k] for k, g in enumerate((g0, g1, g2, g3))]
    line = square_sums(jnp.concatenate(raws, axis=1))
    folded = beta_sums[:, :128] + beta_sums[:, 128:]
    folded = folded + jnp.concatenate([folded[:, q:], folded[:, :q]], axis=1)
    low = lax.broadcasted_iota(jnp.int32, line.shape, 1) < q
    sums[...] = jnp.broadcast_to(jnp.where(low, line, folded), sums.shape)


def right_norm(docs_total, keep, peer, got, beta_core, right, far):
    q, rows = keep.shape[0] // 4, keep.shape[1]
    g0, g1, sums = pl.pallas_call(
        functools.partial(right_norm_kernel, docs_total),
        out_shape=[f32(q, rows)] * 2 + [f32(32, 128)],
        scratch_shapes=[pltpu.VMEM((4 * q, 128), jnp.float32)],
        compiler_params=params(8),
        cost_estimate=cost(rows * q * 64, rows * q * 100, 64),
        name="right_norm",
    )(keep, peer, got, beta_core, right, *far)
    return g0, g1, sums.reshape(32, 1, 128)


def finish_kernel(docs_total, feat_total, g0, g1, g2, g3, squares, own, other, right, search, solution, phibar, rhobar,
                  left_out, right_out, search_out, solution_out, alpha_out, phibar_out, rhobar_out, turned):
    _, z, y = coords()
    q, half = turned.shape[1:]
    parts = [squares[i] for i in range(32)]
    high = [jnp.concatenate([parts[8 * i][:, q:], parts[8 * i][:, :q]], axis=1) if i % 2 == 0 else parts[8 * i] for i in range(4)]
    while len(parts) > 4:
        parts = [a + b for a, b in zip(parts[::2], parts[1::2])]
    parts[1::2] = [jnp.concatenate([p[:, q:], p[:, :q]], axis=1) for p in parts[1::2]]
    low = lax.broadcasted_iota(jnp.int32, parts[0].shape, 1) < q
    alpha_sums, beta_sums = (
        jnp.concatenate([jnp.where(low, p[0], p[1]), jnp.where(low, p[2], p[3])], axis=1) for p in (parts, high)
    )
    alpha = jnp.sqrt(alpha_sums / feat_total + epsilon)
    beta = jnp.sqrt(beta_sums / docs_total + epsilon)
    for part, ref in ((y, own), (1 - y, other)):
        for k in range(4):
            turned[z ^ k] = ref[k]
        left_out[pl.ds(pl.multiple_of(part * half, half), half), :] = turned[...].reshape(-1, half).T / beta
    rho = jnp.sqrt(rhobar[...] * rhobar[...] + beta * beta)
    cosine = rhobar[...] / rho
    sine = beta / rho
    theta = sine * alpha
    phi = cosine * phibar[...]
    rhobar_out[...] = -cosine * alpha
    phibar_out[...] = sine * phibar[...]
    alpha_out[...] = alpha
    for k, g in enumerate((g0, g1, g2, g3)):
        turned[z ^ k] = g[...]
    got = turned[...].reshape(-1, half).T
    following = (got / beta - beta * right[...]) / alpha
    right_out[...] = following
    search_out[...] = following - (theta / rho) * search[...]
    solution_out[...] = solution[...] + (phi / rho) * search[...]


def finish(docs_total, feat_total, pieces, squares, own, other, right, search, solution, phibar, rhobar):
    rows, cols = right.shape
    return pl.pallas_call(
        functools.partial(finish_kernel, docs_total, feat_total),
        out_shape=[f32(2 * rows, cols)] + [f32(rows, cols)] * 3 + [f32(1, cols)] * 3,
        scratch_shapes=[pltpu.VMEM((4, cols // 4, rows), jnp.float32)],
        compiler_params=params(12),
        cost_estimate=cost(rows * cols * 16, rows * cols * 20),
        name="finish",
    )(*pieces, squares, own, other, right, search, solution, phibar, rhobar)


def swap(value, mask):
    return lax.ppermute(value, AXES, [(i, i ^ mask) for i in range(32)])


def along_z(values):
    got = {0: values[0]}
    for k in (2, 3, 1):
        got[k] = swap(values[k], k << Z_SHIFT)
    return [got[k] for k in range(4)]


def after(value, *earlier):
    return lax.optimization_barrier((value, *earlier))[0]


def by_columns(
    col_ids, col_vals, left_vec, right_vec, search_dir, solution_vec, alpha_prev, phibar, rhobar
):
    docs_total = left_vec.shape[0] * 16
    feat_total = right_vec.shape[0] * 32
    alpha_row, phibar_row, rhobar_row = (v.reshape(1, -1) for v in (alpha_prev, phibar, rhobar))

    stored, messages = prepare(col_ids.T, col_vals.T, right_vec, left_vec)
    entries = along_z([stored] * 4)
    messages = along_z([messages[0]] + [after(messages[1], entries[2]), messages[2], messages[3]])
    q = right_vec.shape[1] // 4

    rows1, token1 = build(entries, 1)
    own = stack(messages, q, "stack_right", token1)
    own_x = swap(own, X_BIT)
    own_peer = swap(own, CORE_BIT)
    rows0, token0 = build(entries, 0, own)
    total1 = forward_part(rows1, [own, own_peer], (0, 8), None, [token0])
    x_peer = swap(after(own_x, total1), CORE_BIT)
    total1 = forward_part(rows1, [own_x], (4,), total1)
    product1 = product_half(rows1, x_peer, total1, (12,))
    total0 = forward_part(rows0, [own, own_peer], (0, 8))
    total0 = forward_part(rows0, [own_x], (4,), total0)
    product0 = product_half(rows0, x_peer, total0, (12,), *messages, alpha_row)

    *lefts, both0, beta0 = left_half(product0, swap(product1, Y_BIT))
    partial = backward_part(rows0, both0, 0, 16)
    left_own = stack(along_z(lefts), q, "stack_left")
    both1, beta1 = left_half(product1, swap(product0, Y_BIT), beta0, partial)
    far = swap(backward_part(rows1, both1, 12, 4, partial, beta1), CORE_BIT)
    near = backward_part(rows1, both1, 4, 4, partial, None, [], 0.05)
    peer = backward_part(rows1, both1, 8, 4, partial, None, [near], 0.05)
    send_far, send_near, beta_core = far_sums(near, far, beta1, peer)
    got_far = swap(send_far, X_BIT)
    got_near = swap(send_near, X_BIT)
    keep = backward_part(rows1, both1, 0, 4, partial, None, [], 0.05)
    peer = swap(peer, CORE_BIT)

    g2, g3 = right_far(keep, peer, got_far)
    p2, p3 = swap(g2, 2 << Z_SHIFT), swap(g3, 3 << Z_SHIFT)
    g0, g1, sums = right_norm(docs_total, keep, peer, got_near, beta_core, own, (g2, g3))
    pieces = [g0, swap(g1, 1 << Z_SHIFT), p2, p3]
    left_other = swap(after(left_own, send_far), Y_BIT)
    squares = lax.all_to_all(after(sums, left_own), AXES, 0, 0, tiled=True)
    left_next, right_next, search_next, solution_next, alpha_next, phibar_next, rhobar_next = finish(
        docs_total, feat_total, pieces, squares, left_own, left_other,
        right_vec, search_dir, solution_vec, phibar_row, rhobar_row,
    )
    return (
        left_next,
        right_next,
        search_next,
        solution_next,
        alpha_next.reshape(-1),
        phibar_next.reshape(-1),
        rhobar_next.reshape(-1),
    )


def forward(col_ids, col_vals, table):
    picked = table[col_ids]
    return jnp.sum(col_vals.astype(jnp.float32)[:, :, None] * picked, axis=1)


def backward(col_ids, col_vals, rows_in, width):
    terms = col_vals.astype(jnp.float32)[:, :, None] * rows_in[:, None, :]
    return jax.ops.segment_sum(
        terms.reshape(-1, rows_in.shape[1]), col_ids.reshape(-1), num_segments=width
    )


def by_blocks(
    col_ids, col_vals, left_vec, right_vec, search_dir, solution_vec, alpha_prev, phibar, rhobar
):
    n_feat = lax.axis_size("feat")
    n_doc = lax.axis_size("doc")
    docs_total = left_vec.shape[0] * n_doc
    feat_total = right_vec.shape[0] * n_doc * n_feat
    table = lax.all_gather(right_vec, "doc", axis=0, tiled=True)
    total = lax.psum(forward(col_ids, col_vals, table), "feat")
    left_raw = total - alpha_prev[None, :] * left_vec
    row_part = jnp.sum(left_raw * left_raw, axis=0)
    beta_norm = jnp.sqrt(lax.psum(row_part, "doc") / docs_total + epsilon)
    left_next = left_raw / beta_norm[None, :]
    feature_part = lax.psum_scatter(
        backward(col_ids, col_vals, left_next, table.shape[0]), "doc", scatter_dimension=0, tiled=True
    )
    right_raw = feature_part - beta_norm[None, :] * right_vec
    squares = lax.psum(jnp.sum(right_raw * right_raw, axis=0), AXES)
    alpha_next = jnp.sqrt(squares / feat_total + epsilon)
    right_next = right_raw / alpha_next[None, :]
    rho_val = jnp.sqrt(rhobar * rhobar + beta_norm * beta_norm)
    cosine = rhobar / rho_val
    sine_val = beta_norm / rho_val
    theta_val = sine_val * alpha_next
    phi_val = cosine * phibar
    solution_next = solution_vec + (phi_val / rho_val)[None, :] * search_dir
    search_next = right_next - (theta_val / rho_val)[None, :] * search_dir
    return (
        left_next,
        right_next,
        search_next,
        solution_next,
        alpha_next,
        sine_val * phibar,
        -cosine * alpha_next,
    )


def solution(mesh):
    small = mesh.shape["doc"] == 16 and mesh.shape["feat"] == 2
    rows = P(("feat", "doc"), None)
    return jax.shard_map(
        by_columns if small else by_blocks,
        mesh=mesh,
        in_specs=(P("doc", "feat"), P("doc", "feat"), P("doc", None), rows, rows, rows, P(), P(), P()),
        out_specs=(P("doc", None), rows, rows, rows, P(), P(), P()),
        check_vma=False,
    )
```

```python
import functools

import jax
import jax.numpy as jnp
from jax import lax
from jax.experimental import pallas as pl
from jax.experimental.pallas import tpu as pltpu
from jax.sharding import PartitionSpec as P

epsilon = 1e-06
AXES = ("doc", "feat")
MIB = 1024 * 1024


Y_BIT, CORE_BIT, X_BIT, Z_SHIFT = 1, 2, 4, 3
NT = (((1,), (1,)), ((), ()))


def coords():
    d = lax.axis_index("doc")
    y = lax.axis_index("feat")
    return d, d >> 2, y


def params(mib):
    return pltpu.CompilerParams(vmem_limit_bytes=mib * MIB)


def cost(flops, nbytes, scale=64):
    return pl.CostEstimate(flops=int(flops / scale), bytes_accessed=int(nbytes / scale), transcendentals=0)


def f32(*shape):
    return jax.ShapeDtypeStruct(shape, jnp.float32)


def bf16(*shape):
    return jax.ShapeDtypeStruct(shape, jnp.bfloat16)


def prepare_kernel(ids_hbm, vals_hbm, right_hbm, left_hbm, other, m0, m1, m2, m3,
                   ids, vals, wide, lines, right, left, turned, arrived):
    _, z, y = coords()
    q, rows = turned.shape[1:]
    copies = [
        pltpu.make_async_copy(src, dst, arrived.at[i])
        for i, (src, dst) in enumerate((
            (ids_hbm, ids),
            (vals_hbm, vals),
            (right_hbm, right),
            (left_hbm.at[pl.ds(pl.multiple_of(y * rows, rows), rows), :], left),
        ))
    ]
    for copy in copies:
        copy.start()
    count, n = ids.shape[0], lines.shape[0]
    half = n // 2
    for part, ref in enumerate((ids, vals)):
        copies[part].wait()
        wide[...] = ref[...].astype(jnp.float32).T
        for r in range(256 // count):
            lines[:, r * count : (r + 1) * count] = wide[pl.ds(r, n, stride=256 // count), :]
        at = slice(part * half, (part + 1) * half)
        other[at, :] = lines[pl.ds(pl.multiple_of((1 - y) * half, half), half), :]
        own = lines[pl.ds(pl.multiple_of(y * half, half), half), :]
        for out in (m0, m1, m2, m3):
            out[at, :] = own
    for part, (copy, ref) in enumerate(zip(copies[2:], (right, left))):
        copy.wait()
        turned[...] = ref[...].T.reshape(turned.shape)
        for k, out in enumerate((m0, m1, m2, m3)):
            out[n + part * q : n + (part + 1) * q, :] = turned[z ^ k]


def prepare(ids, vals, right, left):
    rows, cols = right.shape
    n, q = ids.size // 256, cols // 4
    got = pl.pallas_call(
        prepare_kernel,
        in_specs=[pl.BlockSpec(memory_space=pltpu.HBM)] * 4,
        out_specs=[whole()] * 5,
        out_shape=[pltpu.VMEM((n, 256), jnp.float32)] + [pltpu.VMEM((n + 2 * q, rows), jnp.float32)] * 4,
        scratch_shapes=[
            pltpu.VMEM(ids.shape, jnp.int32),
            pltpu.VMEM(vals.shape, jnp.bfloat16),
            pltpu.VMEM(ids.shape[::-1], jnp.float32),
            pltpu.VMEM((n, 256), jnp.float32),
            pltpu.VMEM(right.shape, jnp.float32),
            pltpu.VMEM(right.shape, jnp.float32),
            pltpu.VMEM((4, q, rows), jnp.float32),
            pltpu.SemaphoreType.DMA((4,)),
        ],
        compiler_params=params(60),
        cost_estimate=cost(0, rows * cols * 16),
        name="prepare",
    )(ids, vals, right, left)
    return got[0], got[1:]


def stack_kernel(m0, m1, m2, m3, *refs):
    out = refs[-1]
    for k, m in enumerate((m0, m1, m2, m3)):
        at = m.shape[0] - 2 * out.shape[1] if m.shape[0] > out.shape[1] else 0
        out[k] = m[at : at + out.shape[1], :]


def stack(messages, q, name, *tokens):
    rows = messages[0].shape[1]
    return pl.pallas_call(
        stack_kernel,
        out_shape=f32(4, q, rows),
        compiler_params=params(8),
        cost_estimate=cost(0, 32 * q * rows),
        name=name,
    )(*messages, *tokens)


def build_kernel(e0, e1, e2, e3, *refs):
    hi_ref, lo_ref, token = refs[-3:]
    token[...] = jnp.zeros_like(token)
    d, _, _ = coords()
    n = hi_ref.shape[1] // 64
    iota = lax.broadcasted_iota(jnp.int32, (256, 256), 0).astype(jnp.float32).astype(jnp.bfloat16)
    lane_doc = lax.broadcasted_iota(jnp.int32, (8, 256), 1) >> 4
    one = jnp.ones((256, 256), jnp.bfloat16)
    zero = jnp.zeros((256, 256), jnp.bfloat16)

    def spread(row):
        wide = jnp.broadcast_to(row, (16, 256)).astype(jnp.bfloat16)
        return jnp.broadcast_to(wide[None], (16, 16, 256)).reshape(256, 256)

    for k, entries in enumerate((e0, e1, e2, e3)):

        @pl.loop(0, n // 8)
        def _(step, k=k, entries=entries):
            at = pl.multiple_of(step * 8, 8)
            ids = entries[pl.ds(at, 8), :].astype(jnp.int32)
            vals = entries[pl.ds(n + at, 8), :]
            owner = (ids >> 8) ^ d
            block = ((owner & 1) << 3) | ((owner & 2) << 1) | (owner >> 2)
            code = (block * 16 + lane_doc).astype(jnp.float32)
            inner = (ids & 255).astype(jnp.float32)
            for t in range(8):
                pick = jnp.where(iota == spread(code[t : t + 1]), one, zero)
                weigh = jnp.where(iota == spread(inner[t : t + 1]), spread(vals[t : t + 1]), zero)
                dense = lax.dot_general(pick, weigh, NT, preferred_element_type=jnp.float32)
                high = dense.astype(jnp.bfloat16)
                low = (dense - high.astype(jnp.float32)).astype(jnp.bfloat16)
                docs = pl.ds(pl.multiple_of(k * 16 * n + step * 128 + 16 * t, 16), 16)
                hi_ref[:, docs, :] = high.reshape(16, 16, 256)
                lo_ref[:, docs, :] = low.reshape(16, 16, 256)


def whole():
    return pl.BlockSpec(memory_space=pltpu.VMEM)


def build(entries, lines, scale, *tokens):
    docs = 4 * (lines // 2 * 16)
    *rows, token = pl.pallas_call(
        build_kernel,
        in_specs=[whole()] * (4 + len(tokens)),
        out_specs=[whole()] * 3,
        out_shape=[pltpu.VMEM((16, docs, 256), jnp.bfloat16)] * 2 + [f32(8, 128)],
        compiler_params=params(8),
        cost_estimate=cost(2 * docs * 16 * 256 * 256, docs * 4096 * 4, scale),
        name="dense_rows",
    )(*entries, *tokens)
    return rows, token


def split_rows(value):
    high = value.astype(jnp.bfloat16)
    low = (value - high.astype(jnp.float32)).astype(jnp.bfloat16)
    return jnp.concatenate([high, low], axis=0)


def add_products(hi_ref, lo_ref, vecs, blocks, total):
    for vec, first in zip(vecs, blocks):
        for pair in (0, 2):
            lhs, rhs = [], []
            for k in (pair, pair + 1):
                both = split_rows(vec[k])
                lhs += [hi_ref[first + k], lo_ref[first + k]]
                rhs += [both, both]
            total[...] += lax.dot_general(
                jnp.concatenate(lhs, axis=1), jnp.concatenate(rhs, axis=1), NT, preferred_element_type=jnp.float32
            )


def forward_kernel(blocks, has_before, hi_ref, lo_ref, *refs):
    count = len(blocks)
    total = refs[-1]
    total[...] = refs[count][...] if has_before else jnp.zeros_like(total)
    add_products(hi_ref, lo_ref, refs[:count], blocks, total)


def forward_part(rows, vecs, blocks, before=None, tokens=()):
    docs, q = rows[0].shape[1], vecs[0].shape[1]
    n = 4 * len(blocks)
    extra = [*tokens] if before is None else [before, *tokens]
    return pl.pallas_call(
        functools.partial(forward_kernel, blocks, before is not None),
        in_specs=[whole()] * (2 + len(vecs) + len(extra)),
        out_specs=whole(),
        out_shape=f32(docs, 2 * q),
        compiler_params=params(8),
        cost_estimate=cost(8 * docs * 256 * 256 * n, 4 * docs * 256 * n),
        name="forward_part",
    )(*rows, *vecs, *extra)


def product_kernel(blocks, hi_ref, lo_ref, vec, before, *refs):
    out, total, columns = refs[-3:]
    total[...] = before[...]
    add_products(hi_ref, lo_ref, (vec,), blocks, total)
    turned = total[...].T
    q = out.shape[0]
    product = turned[:q] + turned[q:]
    if len(refs) == 3:
        out[...] = product
        return
    _, z, _ = coords()
    *messages, alpha = refs[:5]
    columns[...] = row_to_column(alpha[...])
    scale = columns[pl.ds(pl.multiple_of(z * q, q), q), :][:, 0:1]
    for k, m in enumerate(messages):
        at = slice(k * m.shape[1], (k + 1) * m.shape[1])
        out[:, at] = product[:, at] - scale * m[m.shape[0] - q :, :]


def product_half(rows, vec, before, blocks, *left):
    docs, q = rows[0].shape[1], vec.shape[1]
    return pl.pallas_call(
        functools.partial(product_kernel, blocks),
        in_specs=[whole()] * (4 + len(left)),
        out_specs=whole(),
        out_shape=f32(q, docs),
        scratch_shapes=[pltpu.VMEM((docs, 2 * q), jnp.float32), pltpu.VMEM((4 * q, 128), jnp.float32)],
        compiler_params=params(8),
        cost_estimate=cost(8 * docs * 256 * 256 * 4, 16 * docs * 256),
        name="product_half",
    )(*rows, vec, before, *left)


def square_sums(value):
    q, n = value.shape
    sums = value[:, 0:128] * value[:, 0:128]
    for at in range(128, n, 128):
        sums = sums + value[:, at : at + 128] * value[:, at : at + 128]
    return jnp.sum(jnp.concatenate([sums] * (128 // q), axis=0).T, axis=0, keepdims=True)


def square_row(value, z, cols):
    row = square_sums(value)
    row = jnp.broadcast_to(jnp.concatenate([row] * (cols // 128), axis=1), (8, cols))
    lane = lax.broadcasted_iota(jnp.int32, (8, cols), 1)
    return jnp.where(lane // value.shape[0] == z, row, 0.0)


def row_to_column(row):
    return jnp.broadcast_to(row, (128, row.shape[1])).T


def left_half_kernel(mine, other, *refs):
    _, z, _ = coords()
    left = mine[...] + other[...]
    both, sums = refs[-2:]
    both[...] = split_rows(left)
    squares = square_row(left, z, sums.shape[1])
    sums[...] = refs[0][...] + squares if len(refs) == 4 else squares
    if len(refs) > 4:
        n = left.shape[1] // 4
        for k, out in enumerate(refs[:4]):
            out[...] = left[:, k * n : (k + 1) * n]


def left_half(mine, other, squares=None, token=None):
    q, docs = mine.shape
    extra = [] if squares is None else [squares, token]
    pieces = [f32(q, docs // 4)] * 4 if squares is None else []
    return pl.pallas_call(
        left_half_kernel,
        out_shape=pieces + [bf16(2 * q, docs), f32(8, 4 * q)],
        compiler_params=params(8),
        cost_estimate=cost(8 * q * docs, 16 * q * docs),
        name="left_half",
    )(mine, other, *extra)


def backward_kernel(first, blocks, parts, hi_ref, lo_ref, both_ref, *refs):
    out_ref = refs[-1]
    both = both_ref[...]
    q = both.shape[0] // 2
    twice = jnp.concatenate([both, both], axis=1)
    for b in range(blocks):
        got = jnp.dot(
            twice,
            jnp.concatenate([hi_ref[first + b], lo_ref[first + b]], axis=0),
            preferred_element_type=jnp.float32,
        )
        got = got[:q] + got[q:]
        if "before" in parts:
            got = got + refs[0][(first + b) * q : (first + b + 1) * q, :]
        out_ref[b * q : (b + 1) * q, :] = got
    if "tail" in parts:
        out_ref[blocks * q :, :] = refs[parts.index("tail")][...]


def backward_part(rows, both, first, blocks, before=None, tail=None, tokens=(), scale=64):
    q, docs = both.shape[0] // 2, both.shape[1]
    extra = {"before": before, "tail": tail, **{str(i): token for i, token in enumerate(tokens)}}
    extra = {name: value for name, value in extra.items() if value is not None}
    height = blocks * q + (0 if tail is None else tail.shape[0])
    return pl.pallas_call(
        functools.partial(backward_kernel, first, blocks, tuple(extra)),
        in_specs=[whole()] * (3 + len(extra)),
        out_specs=whole(),
        out_shape=f32(height, 256),
        compiler_params=params(8),
        cost_estimate=cost(8 * docs * 256 * 256 * blocks, 4 * docs * 256 * blocks, scale),
        name="backward_part",
    )(*rows, both, *extra.values())


def far_sum_kernel(near, far, beta, token, send_far, send_near, beta_core):
    n = near.shape[0] // 2
    beta_core[...] = beta[...] + far[2 * n :, :]
    send_far[...] = near[n:, :] + far[n : 2 * n, :]
    send_near[0:n, :] = near[0:n, :] + far[0:n, :]
    send_near[n:, :] = beta_core[...]


def far_sums(near, far, beta, token):
    rows = near.shape[0] // 2
    return pl.pallas_call(
        far_sum_kernel,
        out_shape=[f32(rows, 256), f32(rows + 8, 256), f32(8, 256)],
        compiler_params=params(8),
        cost_estimate=cost(near.size, near.size * 12),
        name="far_sums",
    )(near, far, beta, token)


def right_far_kernel(keep, peer, got, g2, g3):
    q = g2.shape[0]
    for k, g in ((2, g2), (3, g3)):
        rows = slice(k * q, (k + 1) * q)
        g[...] = (keep[rows, :] + peer[rows, :]) + got[(k - 2) * q : (k - 1) * q, :]


def right_far(keep, peer, got):
    q, rows = keep.shape[0] // 4, keep.shape[1]
    return pl.pallas_call(
        right_far_kernel,
        out_shape=[f32(q, rows)] * 2,
        compiler_params=params(8),
        cost_estimate=cost(rows * q * 4, rows * q * 32),
        name="right_far",
    )(keep, peer, got)


def right_norm_kernel(docs_total, keep, peer, got, beta_core, right, g2, g3, g0, g1, sums, columns):
    _, z, _ = coords()
    q = right.shape[1]
    beta_sums = beta_core[0:1, :] + got[2 * q : 2 * q + 1, :]
    columns[...] = row_to_column(jnp.sqrt(beta_sums / docs_total + epsilon))
    beta = columns[pl.ds(pl.multiple_of(z * q, q), q), :][:, 0:1]
    for k, g in enumerate((g0, g1)):
        rows = slice(k * q, (k + 1) * q)
        g[...] = (keep[rows, :] + peer[rows, :]) + got[rows, :]
    raws = [g[...] / beta - beta * right[k] for k, g in enumerate((g0, g1, g2, g3))]
    line = square_sums(jnp.concatenate(raws, axis=1))
    folded = beta_sums[:, :128] + beta_sums[:, 128:]
    folded = folded + jnp.concatenate([folded[:, q:], folded[:, :q]], axis=1)
    low = lax.broadcasted_iota(jnp.int32, line.shape, 1) < q
    sums[...] = jnp.broadcast_to(jnp.where(low, line, folded), sums.shape)


def right_norm(docs_total, keep, peer, got, beta_core, right, far):
    q, rows = keep.shape[0] // 4, keep.shape[1]
    g0, g1, sums = pl.pallas_call(
        functools.partial(right_norm_kernel, docs_total),
        out_shape=[f32(q, rows)] * 2 + [f32(32, 128)],
        scratch_shapes=[pltpu.VMEM((4 * q, 128), jnp.float32)],
        compiler_params=params(8),
        cost_estimate=cost(rows * q * 64, rows * q * 100, 64),
        name="right_norm",
    )(keep, peer, got, beta_core, right, *far)
    return g0, g1, sums.reshape(32, 1, 128)


def finish_kernel(docs_total, feat_total, g0, g1, g2, g3, squares, own, other, right, search, solution, phibar, rhobar,
                  left_out, right_out, search_out, solution_out, alpha_out, phibar_out, rhobar_out, turned):
    _, z, y = coords()
    q, half = turned.shape[1:]
    parts = [squares[i] for i in range(32)]
    high = [jnp.concatenate([parts[8 * i][:, q:], parts[8 * i][:, :q]], axis=1) if i % 2 == 0 else parts[8 * i] for i in range(4)]
    while len(parts) > 4:
        parts = [a + b for a, b in zip(parts[::2], parts[1::2])]
    parts[1::2] = [jnp.concatenate([p[:, q:], p[:, :q]], axis=1) for p in parts[1::2]]
    low = lax.broadcasted_iota(jnp.int32, parts[0].shape, 1) < q
    alpha_sums, beta_sums = (
        jnp.concatenate([jnp.where(low, p[0], p[1]), jnp.where(low, p[2], p[3])], axis=1) for p in (parts, high)
    )
    alpha = jnp.sqrt(alpha_sums / feat_total + epsilon)
    beta = jnp.sqrt(beta_sums / docs_total + epsilon)
    for part, ref in ((y, own), (1 - y, other)):
        for k in range(4):
            turned[z ^ k] = ref[k]
        left_out[pl.ds(pl.multiple_of(part * half, half), half), :] = turned[...].reshape(-1, half).T / beta
    rho = jnp.sqrt(rhobar[...] * rhobar[...] + beta * beta)
    cosine = rhobar[...] / rho
    sine = beta / rho
    theta = sine * alpha
    phi = cosine * phibar[...]
    rhobar_out[...] = -cosine * alpha
    phibar_out[...] = sine * phibar[...]
    alpha_out[...] = alpha
    for k, g in enumerate((g0, g1, g2, g3)):
        turned[z ^ k] = g[...]
    got = turned[...].reshape(-1, half).T
    following = (got / beta - beta * right[...]) / alpha
    right_out[...] = following
    search_out[...] = following - (theta / rho) * search[...]
    solution_out[...] = solution[...] + (phi / rho) * search[...]


def finish(docs_total, feat_total, pieces, squares, own, other, right, search, solution, phibar, rhobar):
    rows, cols = right.shape
    return pl.pallas_call(
        functools.partial(finish_kernel, docs_total, feat_total),
        out_shape=[f32(2 * rows, cols)] + [f32(rows, cols)] * 3 + [f32(1, cols)] * 3,
        scratch_shapes=[pltpu.VMEM((4, cols // 4, rows), jnp.float32)],
        compiler_params=params(12),
        cost_estimate=cost(rows * cols * 16, rows * cols * 20),
        name="finish",
    )(*pieces, squares, own, other, right, search, solution, phibar, rhobar)


def swap(value, mask):
    return lax.ppermute(value, AXES, [(i, i ^ mask) for i in range(32)])


def along_z(values):
    got = {0: values[0]}
    for k in (2, 3, 1):
        got[k] = swap(values[k], k << Z_SHIFT)
    return [got[k] for k in range(4)]


def after(value, *earlier):
    return lax.optimization_barrier((value, *earlier))[0]


def by_columns(
    col_ids, col_vals, left_vec, right_vec, search_dir, solution_vec, alpha_prev, phibar, rhobar
):
    docs_total = left_vec.shape[0] * 16
    feat_total = right_vec.shape[0] * 32
    alpha_row, phibar_row, rhobar_row = (v.reshape(1, -1) for v in (alpha_prev, phibar, rhobar))

    other, messages = prepare(col_ids.T, col_vals.T, right_vec, left_vec)
    others = along_z([other] * 4)
    messages = along_z([messages[0], after(messages[1], others[2]), messages[2], messages[3]])
    q = right_vec.shape[1] // 4
    lines = other.shape[0]

    rows1, token1 = build(others, lines, 1)
    own = stack(messages, q, "stack_right", token1)
    own_x = swap(own, X_BIT)
    own_peer = swap(own, CORE_BIT)
    rows0, token0 = build(messages, lines, 64, own)
    total1 = forward_part(rows1, [own, own_peer], (0, 8), None, [token0])
    x_peer = swap(after(own_x, total1), CORE_BIT)
    total1 = forward_part(rows1, [own_x], (4,), total1)
    product1 = product_half(rows1, x_peer, total1, (12,))
    total0 = forward_part(rows0, [own, own_peer], (0, 8))
    total0 = forward_part(rows0, [own_x], (4,), total0)
    product0 = product_half(rows0, x_peer, total0, (12,), *messages, alpha_row)

    *lefts, both0, beta0 = left_half(product0, swap(product1, Y_BIT))
    partial = backward_part(rows0, both0, 0, 16)
    left_own = stack(along_z(lefts), q, "stack_left")
    both1, beta1 = left_half(product1, swap(product0, Y_BIT), beta0, partial)
    far = swap(backward_part(rows1, both1, 12, 4, partial, beta1), CORE_BIT)
    near = backward_part(rows1, both1, 4, 4, partial, None, [], 0.05)
    peer = backward_part(rows1, both1, 8, 4, partial, None, [near], 0.05)
    send_far, send_near, beta_core = far_sums(near, far, beta1, peer)
    got_far = swap(send_far, X_BIT)
    got_near = swap(send_near, X_BIT)
    keep = backward_part(rows1, both1, 0, 4, partial, None, [], 0.05)
    peer = swap(peer, CORE_BIT)

    g2, g3 = right_far(keep, peer, got_far)
    p2, p3 = swap(g2, 2 << Z_SHIFT), swap(g3, 3 << Z_SHIFT)
    g0, g1, sums = right_norm(docs_total, keep, peer, got_near, beta_core, own, (g2, g3))
    pieces = [g0, swap(g1, 1 << Z_SHIFT), p2, p3]
    left_other = swap(after(left_own, send_far), Y_BIT)
    squares = lax.all_to_all(after(sums, left_own), AXES, 0, 0, tiled=True)
    left_next, right_next, search_next, solution_next, alpha_next, phibar_next, rhobar_next = finish(
        docs_total, feat_total, pieces, squares, left_own, left_other,
        right_vec, search_dir, solution_vec, phibar_row, rhobar_row,
    )
    return (
        left_next,
        right_next,
        search_next,
        solution_next,
        alpha_next.reshape(-1),
        phibar_next.reshape(-1),
        rhobar_next.reshape(-1),
    )


def forward(col_ids, col_vals, table):
    picked = table[col_ids]
    return jnp.sum(col_vals.astype(jnp.float32)[:, :, None] * picked, axis=1)


def backward(col_ids, col_vals, rows_in, width):
    terms = col_vals.astype(jnp.float32)[:, :, None] * rows_in[:, None, :]
    return jax.ops.segment_sum(
        terms.reshape(-1, rows_in.shape[1]), col_ids.reshape(-1), num_segments=width
    )


def by_blocks(
    col_ids, col_vals, left_vec, right_vec, search_dir, solution_vec, alpha_prev, phibar, rhobar
):
    n_feat = lax.axis_size("feat")
    n_doc = lax.axis_size("doc")
    docs_total = left_vec.shape[0] * n_doc
    feat_total = right_vec.shape[0] * n_doc * n_feat
    table = lax.all_gather(right_vec, "doc", axis=0, tiled=True)
    total = lax.psum(forward(col_ids, col_vals, table), "feat")
    left_raw = total - alpha_prev[None, :] * left_vec
    row_part = jnp.sum(left_raw * left_raw, axis=0)
    beta_norm = jnp.sqrt(lax.psum(row_part, "doc") / docs_total + epsilon)
    left_next = left_raw / beta_norm[None, :]
    feature_part = lax.psum_scatter(
        backward(col_ids, col_vals, left_next, table.shape[0]), "doc", scatter_dimension=0, tiled=True
    )
    right_raw = feature_part - beta_norm[None, :] * right_vec
    squares = lax.psum(jnp.sum(right_raw * right_raw, axis=0), AXES)
    alpha_next = jnp.sqrt(squares / feat_total + epsilon)
    right_next = right_raw / alpha_next[None, :]
    rho_val = jnp.sqrt(rhobar * rhobar + beta_norm * beta_norm)
    cosine = rhobar / rho_val
    sine_val = beta_norm / rho_val
    theta_val = sine_val * alpha_next
    phi_val = cosine * phibar
    solution_next = solution_vec + (phi_val / rho_val)[None, :] * search_dir
    search_next = right_next - (theta_val / rho_val)[None, :] * search_dir
    return (
        left_next,
        right_next,
        search_next,
        solution_next,
        alpha_next,
        sine_val * phibar,
        -cosine * alpha_next,
    )


def solution(mesh):
    small = mesh.shape["doc"] == 16 and mesh.shape["feat"] == 2
    rows = P(("feat", "doc"), None)
    return jax.shard_map(
        by_columns if small else by_blocks,
        mesh=mesh,
        in_specs=(P("doc", "feat"), P("doc", "feat"), P("doc", None), rows, rows, rows, P(), P(), P()),
        out_specs=(P("doc", None), rows, rows, rows, P(), P(), P()),
        check_vma=False,
    )
```

```python
import functools

import jax
import jax.numpy as jnp
from jax import lax
from jax.experimental import pallas as pl
from jax.experimental.pallas import tpu as pltpu
from jax.sharding import PartitionSpec as P

epsilon = 1e-06
AXES = ("doc", "feat")
MIB = 1024 * 1024


Y_BIT, CORE_BIT, X_BIT, Z_SHIFT = 1, 2, 4, 3
NT = (((1,), (1,)), ((), ()))


def coords():
    d = lax.axis_index("doc")
    y = lax.axis_index("feat")
    return d, d >> 2, y


def params(mib):
    return pltpu.CompilerParams(vmem_limit_bytes=mib * MIB)


def cost(flops, nbytes, scale=64):
    return pl.CostEstimate(flops=int(flops / scale), bytes_accessed=int(nbytes / scale), transcendentals=0)


def f32(*shape):
    return jax.ShapeDtypeStruct(shape, jnp.float32)


def bf16(*shape):
    return jax.ShapeDtypeStruct(shape, jnp.bfloat16)


def prepare_kernel(ids_hbm, vals_hbm, right_hbm, left_hbm, a0, a1, a2, a3, b0, b1, b2, b3,
                   ids, vals, wide, lines, right, left, turned, arrived):
    _, z, y = coords()
    q, rows = turned.shape[1:]
    copies = [
        pltpu.make_async_copy(src, dst, arrived.at[i])
        for i, (src, dst) in enumerate((
            (ids_hbm, ids),
            (vals_hbm, vals),
            (right_hbm, right),
            (left_hbm.at[pl.ds(pl.multiple_of(y * rows, rows), rows), :], left),
        ))
    ]
    for copy in copies:
        copy.start()
    count, n = ids.shape[0], lines.shape[0]
    half = n // 2
    groups = (b0, b1, b2, b3), (a0, a1, a2, a3)
    for part, ref in enumerate((ids, vals)):
        copies[part].wait()
        wide[...] = ref[...].astype(jnp.float32).T
        for r in range(256 // count):
            lines[:, r * count : (r + 1) * count] = wide[pl.ds(r, n, stride=256 // count), :]
        at = slice(part * half, (part + 1) * half)
        for rel, outs in enumerate(groups):
            value = lines[pl.ds(pl.multiple_of((y ^ rel) * half, half), half), :]
            for out in outs:
                out[at, :] = value
    for copy, ref, outs in zip(copies[2:], (right, left), groups[::-1]):
        copy.wait()
        turned[...] = ref[...].T.reshape(turned.shape)
        for k, out in enumerate(outs):
            out[n:, :] = turned[z ^ k]


def prepare(ids, vals, right, left):
    rows, cols = right.shape
    n, q = ids.size // 256, cols // 4
    got = pl.pallas_call(
        prepare_kernel,
        in_specs=[pl.BlockSpec(memory_space=pltpu.HBM)] * 4,
        out_specs=[whole()] * 8,
        out_shape=[pltpu.VMEM((n + q, rows), jnp.float32)] * 8,
        scratch_shapes=[
            pltpu.VMEM(ids.shape, jnp.int32),
            pltpu.VMEM(vals.shape, jnp.bfloat16),
            pltpu.VMEM(ids.shape[::-1], jnp.float32),
            pltpu.VMEM((n, 256), jnp.float32),
            pltpu.VMEM(right.shape, jnp.float32),
            pltpu.VMEM(right.shape, jnp.float32),
            pltpu.VMEM((4, q, rows), jnp.float32),
            pltpu.SemaphoreType.DMA((4,)),
        ],
        compiler_params=params(60),
        cost_estimate=cost(0, rows * cols * 16),
        name="prepare",
    )(ids, vals, right, left)
    return got[:4], got[4:]


def stack_kernel(m0, m1, m2, m3, *refs):
    out = refs[-1]
    for k, m in enumerate((m0, m1, m2, m3)):
        out[k] = m[m.shape[0] - out.shape[1] :, :]


def stack(messages, q, name, *tokens):
    rows = messages[0].shape[1]
    return pl.pallas_call(
        stack_kernel,
        out_shape=f32(4, q, rows),
        compiler_params=params(8),
        cost_estimate=cost(0, 32 * q * rows),
        name=name,
    )(*messages, *tokens)


def build_kernel(e0, e1, e2, e3, *refs):
    hi_ref, lo_ref, token = refs[-3:]
    token[...] = jnp.zeros_like(token)
    d, _, _ = coords()
    n = hi_ref.shape[1] // 64
    iota = lax.broadcasted_iota(jnp.int32, (256, 256), 0).astype(jnp.float32).astype(jnp.bfloat16)
    lane_doc = lax.broadcasted_iota(jnp.int32, (8, 256), 1) >> 4
    one = jnp.ones((256, 256), jnp.bfloat16)
    zero = jnp.zeros((256, 256), jnp.bfloat16)

    def spread(row):
        wide = jnp.broadcast_to(row, (16, 256)).astype(jnp.bfloat16)
        return jnp.broadcast_to(wide[None], (16, 16, 256)).reshape(256, 256)

    for k, entries in enumerate((e0, e1, e2, e3)):

        @pl.loop(0, n // 8)
        def _(step, k=k, entries=entries):
            at = pl.multiple_of(step * 8, 8)
            ids = entries[pl.ds(at, 8), :].astype(jnp.int32)
            vals = entries[pl.ds(n + at, 8), :]
            owner = (ids >> 8) ^ d
            block = ((owner & 1) << 3) | ((owner & 2) << 1) | (owner >> 2)
            code = (block * 16 + lane_doc).astype(jnp.float32)
            inner = (ids & 255).astype(jnp.float32)
            for t in range(8):
                pick = jnp.where(iota == spread(code[t : t + 1]), one, zero)
                weigh = jnp.where(iota == spread(inner[t : t + 1]), spread(vals[t : t + 1]), zero)
                dense = lax.dot_general(pick, weigh, NT, preferred_element_type=jnp.float32)
                high = dense.astype(jnp.bfloat16)
                low = (dense - high.astype(jnp.float32)).astype(jnp.bfloat16)
                docs = pl.ds(pl.multiple_of(k * 16 * n + step * 128 + 16 * t, 16), 16)
                hi_ref[:, docs, :] = high.reshape(16, 16, 256)
                lo_ref[:, docs, :] = low.reshape(16, 16, 256)


def whole():
    return pl.BlockSpec(memory_space=pltpu.VMEM)


def build(entries, lines, scale, *tokens):
    docs = 4 * (lines // 2 * 16)
    *rows, token = pl.pallas_call(
        build_kernel,
        in_specs=[whole()] * (4 + len(tokens)),
        out_specs=[whole()] * 3,
        out_shape=[pltpu.VMEM((16, docs, 256), jnp.bfloat16)] * 2 + [f32(8, 128)],
        compiler_params=params(8),
        cost_estimate=cost(2 * docs * 16 * 256 * 256, docs * 4096 * 4, scale),
        name="dense_rows",
    )(*entries, *tokens)
    return rows, token


def split_rows(value):
    high = value.astype(jnp.bfloat16)
    low = (value - high.astype(jnp.float32)).astype(jnp.bfloat16)
    return jnp.concatenate([high, low], axis=0)


def add_products(hi_ref, lo_ref, vecs, blocks, total):
    for vec, first in zip(vecs, blocks):
        for pair in (0, 2):
            lhs, rhs = [], []
            for k in (pair, pair + 1):
                both = split_rows(vec[k])
                lhs += [hi_ref[first + k], lo_ref[first + k]]
                rhs += [both, both]
            total[...] += lax.dot_general(
                jnp.concatenate(lhs, axis=1), jnp.concatenate(rhs, axis=1), NT, preferred_element_type=jnp.float32
            )


def forward_kernel(blocks, has_before, hi_ref, lo_ref, *refs):
    count = len(blocks)
    total = refs[-1]
    total[...] = refs[count][...] if has_before else jnp.zeros_like(total)
    add_products(hi_ref, lo_ref, refs[:count], blocks, total)


def forward_part(rows, vecs, blocks, before=None, tokens=()):
    docs, q = rows[0].shape[1], vecs[0].shape[1]
    n = 4 * len(blocks)
    extra = [*tokens] if before is None else [before, *tokens]
    return pl.pallas_call(
        functools.partial(forward_kernel, blocks, before is not None),
        in_specs=[whole()] * (2 + len(vecs) + len(extra)),
        out_specs=whole(),
        out_shape=f32(docs, 2 * q),
        compiler_params=params(8),
        cost_estimate=cost(8 * docs * 256 * 256 * n, 4 * docs * 256 * n),
        name="forward_part",
    )(*rows, *vecs, *extra)


def product_kernel(blocks, hi_ref, lo_ref, vec, before, *refs):
    out, total, columns = refs[-3:]
    total[...] = before[...]
    add_products(hi_ref, lo_ref, (vec,), blocks, total)
    turned = total[...].T
    q = out.shape[0]
    product = turned[:q] + turned[q:]
    if len(refs) == 3:
        out[...] = product
        return
    _, z, _ = coords()
    *messages, alpha = refs[:5]
    columns[...] = row_to_column(alpha[...])
    scale = columns[pl.ds(pl.multiple_of(z * q, q), q), :][:, 0:1]
    for k, m in enumerate(messages):
        at = slice(k * m.shape[1], (k + 1) * m.shape[1])
        out[:, at] = product[:, at] - scale * m[m.shape[0] - q :, :]


def product_half(rows, vec, before, blocks, *left):
    docs, q = rows[0].shape[1], vec.shape[1]
    return pl.pallas_call(
        functools.partial(product_kernel, blocks),
        in_specs=[whole()] * (4 + len(left)),
        out_specs=whole(),
        out_shape=f32(q, docs),
        scratch_shapes=[pltpu.VMEM((docs, 2 * q), jnp.float32), pltpu.VMEM((4 * q, 128), jnp.float32)],
        compiler_params=params(8),
        cost_estimate=cost(8 * docs * 256 * 256 * 4, 16 * docs * 256),
        name="product_half",
    )(*rows, vec, before, *left)


def square_sums(value):
    q, n = value.shape
    sums = value[:, 0:128] * value[:, 0:128]
    for at in range(128, n, 128):
        sums = sums + value[:, at : at + 128] * value[:, at : at + 128]
    return jnp.sum(jnp.concatenate([sums] * (128 // q), axis=0).T, axis=0, keepdims=True)


def square_row(value, z, cols):
    row = square_sums(value)
    row = jnp.broadcast_to(jnp.concatenate([row] * (cols // 128), axis=1), (8, cols))
    lane = lax.broadcasted_iota(jnp.int32, (8, cols), 1)
    return jnp.where(lane // value.shape[0] == z, row, 0.0)


def row_to_column(row):
    return jnp.broadcast_to(row, (128, row.shape[1])).T


def left_half_kernel(mine, other, *refs):
    _, z, _ = coords()
    left = mine[...] + other[...]
    both, sums = refs[-2:]
    both[...] = split_rows(left)
    squares = square_row(left, z, sums.shape[1])
    sums[...] = refs[0][...] + squares if len(refs) == 4 else squares
    if len(refs) > 4:
        n = left.shape[1] // 4
        for k, out in enumerate(refs[:4]):
            out[...] = left[:, k * n : (k + 1) * n]


def left_half(mine, other, squares=None, token=None):
    q, docs = mine.shape
    extra = [] if squares is None else [squares, token]
    pieces = [f32(q, docs // 4)] * 4 if squares is None else []
    return pl.pallas_call(
        left_half_kernel,
        out_shape=pieces + [bf16(2 * q, docs), f32(8, 4 * q)],
        compiler_params=params(8),
        cost_estimate=cost(8 * q * docs, 16 * q * docs),
        name="left_half",
    )(mine, other, *extra)


def backward_kernel(first, blocks, parts, hi_ref, lo_ref, both_ref, *refs):
    out_ref = refs[-1]
    both = both_ref[...]
    q = both.shape[0] // 2
    twice = jnp.concatenate([both, both], axis=1)
    for b in range(blocks):
        got = jnp.dot(
            twice,
            jnp.concatenate([hi_ref[first + b], lo_ref[first + b]], axis=0),
            preferred_element_type=jnp.float32,
        )
        got = got[:q] + got[q:]
        if "before" in parts:
            got = got + refs[0][(first + b) * q : (first + b + 1) * q, :]
        out_ref[b * q : (b + 1) * q, :] = got
    if "tail" in parts:
        out_ref[blocks * q :, :] = refs[parts.index("tail")][...]


def backward_part(rows, both, first, blocks, before=None, tail=None, tokens=(), scale=64):
    q, docs = both.shape[0] // 2, both.shape[1]
    extra = {"before": before, "tail": tail, **{str(i): token for i, token in enumerate(tokens)}}
    extra = {name: value for name, value in extra.items() if value is not None}
    height = blocks * q + (0 if tail is None else tail.shape[0])
    return pl.pallas_call(
        functools.partial(backward_kernel, first, blocks, tuple(extra)),
        in_specs=[whole()] * (3 + len(extra)),
        out_specs=whole(),
        out_shape=f32(height, 256),
        compiler_params=params(8),
        cost_estimate=cost(8 * docs * 256 * 256 * blocks, 4 * docs * 256 * blocks, scale),
        name="backward_part",
    )(*rows, both, *extra.values())


def far_sum_kernel(near, far, beta, token, send_far, send_near, beta_core):
    n = near.shape[0] // 2
    beta_core[...] = beta[...] + far[2 * n :, :]
    send_far[...] = near[n:, :] + far[n : 2 * n, :]
    send_near[0:n, :] = near[0:n, :] + far[0:n, :]
    send_near[n:, :] = beta_core[...]


def far_sums(near, far, beta, token):
    rows = near.shape[0] // 2
    return pl.pallas_call(
        far_sum_kernel,
        out_shape=[f32(rows, 256), f32(rows + 8, 256), f32(8, 256)],
        compiler_params=params(8),
        cost_estimate=cost(near.size, near.size * 12),
        name="far_sums",
    )(near, far, beta, token)


def right_far_kernel(keep, peer, got, g2, g3):
    q = g2.shape[0]
    for k, g in ((2, g2), (3, g3)):
        rows = slice(k * q, (k + 1) * q)
        g[...] = (keep[rows, :] + peer[rows, :]) + got[(k - 2) * q : (k - 1) * q, :]


def right_far(keep, peer, got):
    q, rows = keep.shape[0] // 4, keep.shape[1]
    return pl.pallas_call(
        right_far_kernel,
        out_shape=[f32(q, rows)] * 2,
        compiler_params=params(8),
        cost_estimate=cost(rows * q * 4, rows * q * 32),
        name="right_far",
    )(keep, peer, got)


def right_norm_kernel(docs_total, keep, peer, got, beta_core, right, g2, g3, g0, g1, sums, columns):
    _, z, _ = coords()
    q = right.shape[1]
    beta_sums = beta_core[0:1, :] + got[2 * q : 2 * q + 1, :]
    columns[...] = row_to_column(jnp.sqrt(beta_sums / docs_total + epsilon))
    beta = columns[pl.ds(pl.multiple_of(z * q, q), q), :][:, 0:1]
    for k, g in enumerate((g0, g1)):
        rows = slice(k * q, (k + 1) * q)
        g[...] = (keep[rows, :] + peer[rows, :]) + got[rows, :]
    raws = [g[...] / beta - beta * right[k] for k, g in enumerate((g0, g1, g2, g3))]
    line = square_sums(jnp.concatenate(raws, axis=1))
    folded = beta_sums[:, :128] + beta_sums[:, 128:]
    folded = folded + jnp.concatenate([folded[:, q:], folded[:, :q]], axis=1)
    low = lax.broadcasted_iota(jnp.int32, line.shape, 1) < q
    sums[...] = jnp.broadcast_to(jnp.where(low, line, folded), sums.shape)


def right_norm(docs_total, keep, peer, got, beta_core, right, far):
    q, rows = keep.shape[0] // 4, keep.shape[1]
    g0, g1, sums = pl.pallas_call(
        functools.partial(right_norm_kernel, docs_total),
        out_shape=[f32(q, rows)] * 2 + [f32(32, 128)],
        scratch_shapes=[pltpu.VMEM((4 * q, 128), jnp.float32)],
        compiler_params=params(8),
        cost_estimate=cost(rows * q * 64, rows * q * 100, 64),
        name="right_norm",
    )(keep, peer, got, beta_core, right, *far)
    return g0, g1, sums.reshape(32, 1, 128)


def finish_kernel(docs_total, feat_total, g0, g1, g2, g3, squares, own, other, right, search, solution, phibar, rhobar,
                  left_out, right_out, search_out, solution_out, alpha_out, phibar_out, rhobar_out, turned):
    _, z, y = coords()
    q, half = turned.shape[1:]
    parts = [squares[i] for i in range(32)]
    high = [jnp.concatenate([parts[8 * i][:, q:], parts[8 * i][:, :q]], axis=1) if i % 2 == 0 else parts[8 * i] for i in range(4)]
    while len(parts) > 4:
        parts = [a + b for a, b in zip(parts[::2], parts[1::2])]
    parts[1::2] = [jnp.concatenate([p[:, q:], p[:, :q]], axis=1) for p in parts[1::2]]
    low = lax.broadcasted_iota(jnp.int32, parts[0].shape, 1) < q
    alpha_sums, beta_sums = (
        jnp.concatenate([jnp.where(low, p[0], p[1]), jnp.where(low, p[2], p[3])], axis=1) for p in (parts, high)
    )
    alpha = jnp.sqrt(alpha_sums / feat_total + epsilon)
    beta = jnp.sqrt(beta_sums / docs_total + epsilon)
    for part, ref in ((y, own), (1 - y, other)):
        for k in range(4):
            turned[z ^ k] = ref[k]
        left_out[pl.ds(pl.multiple_of(part * half, half), half), :] = turned[...].reshape(-1, half).T / beta
    rho = jnp.sqrt(rhobar[...] * rhobar[...] + beta * beta)
    cosine = rhobar[...] / rho
    sine = beta / rho
    theta = sine * alpha
    phi = cosine * phibar[...]
    rhobar_out[...] = -cosine * alpha
    phibar_out[...] = sine * phibar[...]
    alpha_out[...] = alpha
    for k, g in enumerate((g0, g1, g2, g3)):
        turned[z ^ k] = g[...]
    got = turned[...].reshape(-1, half).T
    following = (got / beta - beta * right[...]) / alpha
    right_out[...] = following
    search_out[...] = following - (theta / rho) * search[...]
    solution_out[...] = solution[...] + (phi / rho) * search[...]


def finish(docs_total, feat_total, pieces, squares, own, other, right, search, solution, phibar, rhobar):
    rows, cols = right.shape
    return pl.pallas_call(
        functools.partial(finish_kernel, docs_total, feat_total),
        out_shape=[f32(2 * rows, cols)] + [f32(rows, cols)] * 3 + [f32(1, cols)] * 3,
        scratch_shapes=[pltpu.VMEM((4, cols // 4, rows), jnp.float32)],
        compiler_params=params(12),
        cost_estimate=cost(rows * cols * 16, rows * cols * 20),
        name="finish",
    )(*pieces, squares, own, other, right, search, solution, phibar, rhobar)


def swap(value, mask):
    return lax.ppermute(value, AXES, [(i, i ^ mask) for i in range(32)])


def along_z(values):
    got = {0: values[0]}
    for k in (2, 3, 1):
        got[k] = swap(values[k], k << Z_SHIFT)
    return [got[k] for k in range(4)]


def after(value, *earlier):
    return lax.optimization_barrier((value, *earlier))[0]


def by_columns(
    col_ids, col_vals, left_vec, right_vec, search_dir, solution_vec, alpha_prev, phibar, rhobar
):
    docs_total = left_vec.shape[0] * 16
    feat_total = right_vec.shape[0] * 32
    alpha_row, phibar_row, rhobar_row = (v.reshape(1, -1) for v in (alpha_prev, phibar, rhobar))

    first, second = prepare(col_ids.T, col_vals.T, right_vec, left_vec)
    first = along_z(first)
    second = along_z(second)
    q = right_vec.shape[1] // 4
    lines = first[0].shape[0] - q

    own = stack(first, q, "stack_right")
    own_x = swap(own, X_BIT)
    own_peer = swap(own, CORE_BIT)
    rows1, token1 = build(first, lines, 0.05, own)
    rows0, token0 = build(second, lines, 64, token1)
    total1 = forward_part(rows1, [own, own_peer], (0, 8), None, [token0])
    x_peer = swap(after(own_x, total1), CORE_BIT)
    total1 = forward_part(rows1, [own_x], (4,), total1)
    product1 = product_half(rows1, x_peer, total1, (12,))
    total0 = forward_part(rows0, [own, own_peer], (0, 8))
    total0 = forward_part(rows0, [own_x], (4,), total0)
    product0 = product_half(rows0, x_peer, total0, (12,), *second, alpha_row)

    *lefts, both0, beta0 = left_half(product0, swap(product1, Y_BIT))
    partial = backward_part(rows0, both0, 0, 16)
    left_own = stack(along_z(lefts), q, "stack_left")
    both1, beta1 = left_half(product1, swap(product0, Y_BIT), beta0, partial)
    far = swap(backward_part(rows1, both1, 12, 4, partial, beta1), CORE_BIT)
    near = backward_part(rows1, both1, 4, 4, partial, None, [], 0.05)
    peer = backward_part(rows1, both1, 8, 4, partial, None, [near], 0.05)
    send_far, send_near, beta_core = far_sums(near, far, beta1, peer)
    got_far = swap(send_far, X_BIT)
    got_near = swap(send_near, X_BIT)
    keep = backward_part(rows1, both1, 0, 4, partial, None, [], 0.05)
    peer = swap(peer, CORE_BIT)

    g2, g3 = right_far(keep, peer, got_far)
    p2, p3 = swap(g2, 2 << Z_SHIFT), swap(g3, 3 << Z_SHIFT)
    g0, g1, sums = right_norm(docs_total, keep, peer, got_near, beta_core, own, (g2, g3))
    pieces = [g0, swap(g1, 1 << Z_SHIFT), p2, p3]
    left_other = swap(after(left_own, send_far), Y_BIT)
    squares = lax.all_to_all(after(sums, left_own), AXES, 0, 0, tiled=True)
    left_next, right_next, search_next, solution_next, alpha_next, phibar_next, rhobar_next = finish(
        docs_total, feat_total, pieces, squares, left_own, left_other,
        right_vec, search_dir, solution_vec, phibar_row, rhobar_row,
    )
    return (
        left_next,
        right_next,
        search_next,
        solution_next,
        alpha_next.reshape(-1),
        phibar_next.reshape(-1),
        rhobar_next.reshape(-1),
    )


def forward(col_ids, col_vals, table):
    picked = table[col_ids]
    return jnp.sum(col_vals.astype(jnp.float32)[:, :, None] * picked, axis=1)


def backward(col_ids, col_vals, rows_in, width):
    terms = col_vals.astype(jnp.float32)[:, :, None] * rows_in[:, None, :]
    return jax.ops.segment_sum(
        terms.reshape(-1, rows_in.shape[1]), col_ids.reshape(-1), num_segments=width
    )


def by_blocks(
    col_ids, col_vals, left_vec, right_vec, search_dir, solution_vec, alpha_prev, phibar, rhobar
):
    n_feat = lax.axis_size("feat")
    n_doc = lax.axis_size("doc")
    docs_total = left_vec.shape[0] * n_doc
    feat_total = right_vec.shape[0] * n_doc * n_feat
    table = lax.all_gather(right_vec, "doc", axis=0, tiled=True)
    total = lax.psum(forward(col_ids, col_vals, table), "feat")
    left_raw = total - alpha_prev[None, :] * left_vec
    row_part = jnp.sum(left_raw * left_raw, axis=0)
    beta_norm = jnp.sqrt(lax.psum(row_part, "doc") / docs_total + epsilon)
    left_next = left_raw / beta_norm[None, :]
    feature_part = lax.psum_scatter(
        backward(col_ids, col_vals, left_next, table.shape[0]), "doc", scatter_dimension=0, tiled=True
    )
    right_raw = feature_part - beta_norm[None, :] * right_vec
    squares = lax.psum(jnp.sum(right_raw * right_raw, axis=0), AXES)
    alpha_next = jnp.sqrt(squares / feat_total + epsilon)
    right_next = right_raw / alpha_next[None, :]
    rho_val = jnp.sqrt(rhobar * rhobar + beta_norm * beta_norm)
    cosine = rhobar / rho_val
    sine_val = beta_norm / rho_val
    theta_val = sine_val * alpha_next
    phi_val = cosine * phibar
    solution_next = solution_vec + (phi_val / rho_val)[None, :] * search_dir
    search_next = right_next - (theta_val / rho_val)[None, :] * search_dir
    return (
        left_next,
        right_next,
        search_next,
        solution_next,
        alpha_next,
        sine_val * phibar,
        -cosine * alpha_next,
    )


def solution(mesh):
    small = mesh.shape["doc"] == 16 and mesh.shape["feat"] == 2
    rows = P(("feat", "doc"), None)
    return jax.shard_map(
        by_columns if small else by_blocks,
        mesh=mesh,
        in_specs=(P("doc", "feat"), P("doc", "feat"), P("doc", None), rows, rows, rows, P(), P(), P()),
        out_specs=(P("doc", None), rows, rows, rows, P(), P(), P()),
        check_vma=False,
    )
```

```python
import functools

import jax
import jax.numpy as jnp
from jax import lax
from jax.experimental import pallas as pl
from jax.experimental.pallas import tpu as pltpu
from jax.sharding import PartitionSpec as P

epsilon = 1e-06
AXES = ("doc", "feat")
MIB = 1024 * 1024


Y_BIT, CORE_BIT, X_BIT, Z_SHIFT = 1, 2, 4, 3
NT = (((1,), (1,)), ((), ()))


def coords():
    d = lax.axis_index("doc")
    y = lax.axis_index("feat")
    return d, d >> 2, y


def params(mib):
    return pltpu.CompilerParams(vmem_limit_bytes=mib * MIB)


def cost(flops, nbytes, scale=64):
    return pl.CostEstimate(flops=int(flops / scale), bytes_accessed=int(nbytes / scale), transcendentals=0)


def f32(*shape):
    return jax.ShapeDtypeStruct(shape, jnp.float32)


def bf16(*shape):
    return jax.ShapeDtypeStruct(shape, jnp.bfloat16)


def prepare_kernel(ids_hbm, vals_hbm, right_hbm, left_hbm, stored, m0, m1, m2, m3, u0, u1, u2, u3,
                   ids, vals, wide, right, left, turned, arrived):
    _, z, y = coords()
    q, rows = turned.shape[1:]
    copies = [
        pltpu.make_async_copy(src, dst, arrived.at[i])
        for i, (src, dst) in enumerate((
            (ids_hbm, ids),
            (vals_hbm, vals),
            (right_hbm, right),
            (left_hbm.at[pl.ds(pl.multiple_of(y * rows, rows), rows), :], left),
        ))
    ]
    for copy in copies:
        copy.start()
    lines, count = stored.shape[0] // 2, ids.shape[0]
    for part, ref in enumerate((ids, vals)):
        copies[part].wait()
        wide[...] = ref[...].astype(jnp.float32).T
        for r in range(256 // count):
            stored[part * lines : (part + 1) * lines, r * count : (r + 1) * count] = wide[
                pl.ds(r, lines, stride=256 // count), :
            ]
    for copy, ref, outs in zip(copies[2:], (right, left), ((m0, m1, m2, m3), (u0, u1, u2, u3))):
        copy.wait()
        turned[...] = ref[...].T.reshape(turned.shape)
        for k, out in enumerate(outs):
            out[...] = turned[z ^ k]


def prepare(ids, vals, right, left):
    rows, cols = right.shape
    q = cols // 4
    got = pl.pallas_call(
        prepare_kernel,
        in_specs=[pl.BlockSpec(memory_space=pltpu.HBM)] * 4,
        out_specs=[whole()] * 9,
        out_shape=[pltpu.VMEM((ids.size // 128, 256), jnp.float32)] + [pltpu.VMEM((q, rows), jnp.float32)] * 8,
        scratch_shapes=[
            pltpu.VMEM(ids.shape, jnp.int32),
            pltpu.VMEM(vals.shape, jnp.bfloat16),
            pltpu.VMEM(ids.shape[::-1], jnp.float32),
            pltpu.VMEM(right.shape, jnp.float32),
            pltpu.VMEM(right.shape, jnp.float32),
            pltpu.VMEM((4, q, rows), jnp.float32),
            pltpu.SemaphoreType.DMA((4,)),
        ],
        compiler_params=params(60),
        cost_estimate=cost(0, rows * cols * 16),
        name="prepare",
    )(ids, vals, right, left)
    return got[0], got[1:5], got[5:]


def stack_kernel(m0, m1, m2, m3, *refs):
    out = refs[-1]
    for k, m in enumerate((m0, m1, m2, m3)):
        out[k] = m[0 : out.shape[1], :]


def stack(messages, q, name, *tokens):
    rows = messages[0].shape[1]
    return pl.pallas_call(
        stack_kernel,
        out_shape=f32(4, q, rows),
        compiler_params=params(8),
        cost_estimate=cost(0, 32 * q * rows),
        name=name,
    )(*messages, *tokens)


def build_kernel(rel, e0, e1, e2, e3, *refs):
    hi_ref, lo_ref, token = refs[-3:]
    token[...] = jnp.zeros_like(token)
    d, _, y = coords()
    n = e0.shape[0] // 2
    iota = lax.broadcasted_iota(jnp.int32, (256, 256), 0).astype(jnp.float32).astype(jnp.bfloat16)
    lane_doc = lax.broadcasted_iota(jnp.int32, (8, 256), 1) >> 4
    one = jnp.ones((256, 256), jnp.bfloat16)
    zero = jnp.zeros((256, 256), jnp.bfloat16)

    def spread(row):
        wide = jnp.broadcast_to(row, (16, 256)).astype(jnp.bfloat16)
        return jnp.broadcast_to(wide[None], (16, 16, 256)).reshape(256, 256)

    for k, entries in enumerate((e0, e1, e2, e3)):

        @pl.loop(0, n // 16)
        def _(step, k=k, entries=entries):
            at = pl.multiple_of((y ^ rel) * (n // 2) + step * 8, 8)
            ids = entries[pl.ds(at, 8), :].astype(jnp.int32)
            vals = entries[pl.ds(n + at, 8), :]
            owner = (ids >> 8) ^ d
            block = ((owner & 1) << 3) | ((owner & 2) << 1) | (owner >> 2)
            code = (block * 16 + lane_doc).astype(jnp.float32)
            inner = (ids & 255).astype(jnp.float32)
            for t in range(8):
                pick = jnp.where(iota == spread(code[t : t + 1]), one, zero)
                weigh = jnp.where(iota == spread(inner[t : t + 1]), spread(vals[t : t + 1]), zero)
                dense = lax.dot_general(pick, weigh, NT, preferred_element_type=jnp.float32)
                high = dense.astype(jnp.bfloat16)
                low = (dense - high.astype(jnp.float32)).astype(jnp.bfloat16)
                docs = pl.ds(pl.multiple_of(k * 8 * n + step * 128 + 16 * t, 16), 16)
                hi_ref[:, docs, :] = high.reshape(16, 16, 256)
                lo_ref[:, docs, :] = low.reshape(16, 16, 256)


def whole():
    return pl.BlockSpec(memory_space=pltpu.VMEM)


def build(entries, rel, *tokens):
    docs = 4 * (entries[0].shape[0] // 4 * 16)
    *rows, token = pl.pallas_call(
        functools.partial(build_kernel, rel),
        in_specs=[whole()] * (4 + len(tokens)),
        out_specs=[whole()] * 3,
        out_shape=[pltpu.VMEM((16, docs, 256), jnp.bfloat16)] * 2 + [f32(8, 128)],
        compiler_params=params(8),
        cost_estimate=cost(2 * docs * 16 * 256 * 256, docs * 4096 * 4, 1 if rel else 0.05),
        name="dense_rows",
    )(*entries, *tokens)
    return rows, token


def split_rows(value):
    high = value.astype(jnp.bfloat16)
    low = (value - high.astype(jnp.float32)).astype(jnp.bfloat16)
    return jnp.concatenate([high, low], axis=0)


def add_products(hi_ref, lo_ref, vecs, blocks, total):
    for vec, first in zip(vecs, blocks):
        for pair in (0, 2):
            lhs, rhs = [], []
            for k in (pair, pair + 1):
                both = split_rows(vec[k])
                lhs += [hi_ref[first + k], lo_ref[first + k]]
                rhs += [both, both]
            total[...] += lax.dot_general(
                jnp.concatenate(lhs, axis=1), jnp.concatenate(rhs, axis=1), NT, preferred_element_type=jnp.float32
            )


def forward_kernel(blocks, has_before, hi_ref, lo_ref, *refs):
    count = len(blocks)
    total = refs[-1]
    total[...] = refs[count][...] if has_before else jnp.zeros_like(total)
    add_products(hi_ref, lo_ref, refs[:count], blocks, total)


def forward_part(rows, vecs, blocks, before=None, tokens=()):
    docs, q = rows[0].shape[1], vecs[0].shape[1]
    n = 4 * len(blocks)
    extra = [*tokens] if before is None else [before, *tokens]
    return pl.pallas_call(
        functools.partial(forward_kernel, blocks, before is not None),
        in_specs=[whole()] * (2 + len(vecs) + len(extra)),
        out_specs=whole(),
        out_shape=f32(docs, 2 * q),
        compiler_params=params(8),
        cost_estimate=cost(8 * docs * 256 * 256 * n, 4 * docs * 256 * n),
        name="forward_part",
    )(*rows, *vecs, *extra)


def product_kernel(blocks, hi_ref, lo_ref, vec, before, *refs):
    out, total, columns = refs[-3:]
    total[...] = before[...]
    add_products(hi_ref, lo_ref, (vec,), blocks, total)
    turned = total[...].T
    q = out.shape[0]
    product = turned[:q] + turned[q:]
    if len(refs) == 3:
        out[...] = product
        return
    _, z, _ = coords()
    *messages, alpha = refs[:5]
    columns[...] = row_to_column(alpha[...])
    scale = columns[pl.ds(pl.multiple_of(z * q, q), q), :][:, 0:1]
    for k, m in enumerate(messages):
        at = slice(k * m.shape[1], (k + 1) * m.shape[1])
        out[:, at] = product[:, at] - scale * m[...]


def product_half(rows, vec, before, blocks, *left):
    docs, q = rows[0].shape[1], vec.shape[1]
    return pl.pallas_call(
        functools.partial(product_kernel, blocks),
        in_specs=[whole()] * (4 + len(left)),
        out_specs=whole(),
        out_shape=f32(q, docs),
        scratch_shapes=[pltpu.VMEM((docs, 2 * q), jnp.float32), pltpu.VMEM((4 * q, 128), jnp.float32)],
        compiler_params=params(8),
        cost_estimate=cost(8 * docs * 256 * 256 * 4, 16 * docs * 256),
        name="product_half",
    )(*rows, vec, before, *left)


def square_sums(value):
    q, n = value.shape
    sums = value[:, 0:128] * value[:, 0:128]
    for at in range(128, n, 128):
        sums = sums + value[:, at : at + 128] * value[:, at : at + 128]
    return jnp.sum(jnp.concatenate([sums] * (128 // q), axis=0).T, axis=0, keepdims=True)


def square_row(value, z, cols):
    row = square_sums(value)
    row = jnp.broadcast_to(jnp.concatenate([row] * (cols // 128), axis=1), (8, cols))
    lane = lax.broadcasted_iota(jnp.int32, (8, cols), 1)
    return jnp.where(lane // value.shape[0] == z, row, 0.0)


def row_to_column(row):
    return jnp.broadcast_to(row, (128, row.shape[1])).T


def left_half_kernel(mine, other, *refs):
    _, z, _ = coords()
    left = mine[...] + other[...]
    both, sums = refs[-2:]
    both[...] = split_rows(left)
    squares = square_row(left, z, sums.shape[1])
    sums[...] = refs[0][...] + squares if len(refs) == 4 else squares
    if len(refs) > 4:
        n = left.shape[1] // 4
        for k, out in enumerate(refs[:4]):
            out[...] = left[:, k * n : (k + 1) * n]


def left_half(mine, other, squares=None, token=None):
    q, docs = mine.shape
    extra = [] if squares is None else [squares, token]
    pieces = [f32(q, docs // 4)] * 4 if squares is None else []
    return pl.pallas_call(
        left_half_kernel,
        out_shape=pieces + [bf16(2 * q, docs), f32(8, 4 * q)],
        compiler_params=params(8),
        cost_estimate=cost(8 * q * docs, 16 * q * docs),
        name="left_half",
    )(mine, other, *extra)


def backward_kernel(first, blocks, parts, hi_ref, lo_ref, both_ref, *refs):
    out_ref = refs[-1]
    both = both_ref[...]
    q = both.shape[0] // 2
    twice = jnp.concatenate([both, both], axis=1)
    for b in range(blocks):
        got = jnp.dot(
            twice,
            jnp.concatenate([hi_ref[first + b], lo_ref[first + b]], axis=0),
            preferred_element_type=jnp.float32,
        )
        got = got[:q] + got[q:]
        if "before" in parts:
            got = got + refs[0][(first + b) * q : (first + b + 1) * q, :]
        out_ref[b * q : (b + 1) * q, :] = got
    if "tail" in parts:
        out_ref[blocks * q :, :] = refs[parts.index("tail")][...]


def backward_part(rows, both, first, blocks, before=None, tail=None, tokens=(), scale=64):
    q, docs = both.shape[0] // 2, both.shape[1]
    extra = {"before": before, "tail": tail, **{str(i): token for i, token in enumerate(tokens)}}
    extra = {name: value for name, value in extra.items() if value is not None}
    height = blocks * q + (0 if tail is None else tail.shape[0])
    return pl.pallas_call(
        functools.partial(backward_kernel, first, blocks, tuple(extra)),
        in_specs=[whole()] * (3 + len(extra)),
        out_specs=whole(),
        out_shape=f32(height, 256),
        compiler_params=params(8),
        cost_estimate=cost(8 * docs * 256 * 256 * blocks, 4 * docs * 256 * blocks, scale),
        name="backward_part",
    )(*rows, both, *extra.values())


def far_sum_kernel(near, far, beta, token, send_far, send_near, beta_core):
    n = near.shape[0] // 2
    beta_core[...] = beta[...] + far[2 * n :, :]
    send_far[...] = near[n:, :] + far[n : 2 * n, :]
    send_near[0:n, :] = near[0:n, :] + far[0:n, :]
    send_near[n:, :] = beta_core[...]


def far_sums(near, far, beta, token):
    rows = near.shape[0] // 2
    return pl.pallas_call(
        far_sum_kernel,
        out_shape=[f32(rows, 256), f32(rows + 8, 256), f32(8, 256)],
        compiler_params=params(8),
        cost_estimate=cost(near.size, near.size * 12),
        name="far_sums",
    )(near, far, beta, token)


def right_far_kernel(keep, peer, got, g2, g3):
    q = g2.shape[0]
    for k, g in ((2, g2), (3, g3)):
        rows = slice(k * q, (k + 1) * q)
        g[...] = (keep[rows, :] + peer[rows, :]) + got[(k - 2) * q : (k - 1) * q, :]


def right_far(keep, peer, got):
    q, rows = keep.shape[0] // 4, keep.shape[1]
    return pl.pallas_call(
        right_far_kernel,
        out_shape=[f32(q, rows)] * 2,
        compiler_params=params(8),
        cost_estimate=cost(rows * q * 4, rows * q * 32),
        name="right_far",
    )(keep, peer, got)


def right_norm_kernel(docs_total, keep, peer, got, beta_core, right, g2, g3, g0, g1, sums, columns):
    _, z, _ = coords()
    q = right.shape[1]
    beta_sums = beta_core[0:1, :] + got[2 * q : 2 * q + 1, :]
    columns[...] = row_to_column(jnp.sqrt(beta_sums / docs_total + epsilon))
    beta = columns[pl.ds(pl.multiple_of(z * q, q), q), :][:, 0:1]
    for k, g in enumerate((g0, g1)):
        rows = slice(k * q, (k + 1) * q)
        g[...] = (keep[rows, :] + peer[rows, :]) + got[rows, :]
    raws = [g[...] / beta - beta * right[k] for k, g in enumerate((g0, g1, g2, g3))]
    line = square_sums(jnp.concatenate(raws, axis=1))
    folded = beta_sums[:, :128] + beta_sums[:, 128:]
    folded = folded + jnp.concatenate([folded[:, q:], folded[:, :q]], axis=1)
    low = lax.broadcasted_iota(jnp.int32, line.shape, 1) < q
    sums[...] = jnp.broadcast_to(jnp.where(low, line, folded), sums.shape)


def right_norm(docs_total, keep, peer, got, beta_core, right, far):
    q, rows = keep.shape[0] // 4, keep.shape[1]
    g0, g1, sums = pl.pallas_call(
        functools.partial(right_norm_kernel, docs_total),
        out_shape=[f32(q, rows)] * 2 + [f32(32, 128)],
        scratch_shapes=[pltpu.VMEM((4 * q, 128), jnp.float32)],
        compiler_params=params(8),
        cost_estimate=cost(rows * q * 64, rows * q * 100, 64),
        name="right_norm",
    )(keep, peer, got, beta_core, right, *far)
    return g0, g1, sums.reshape(32, 1, 128)


def finish_kernel(docs_total, feat_total, g0, g1, g2, g3, squares, own, other, right, search, solution, phibar, rhobar,
                  left_out, right_out, search_out, solution_out, alpha_out, phibar_out, rhobar_out, turned):
    _, z, y = coords()
    q, half = turned.shape[1:]
    parts = [squares[i] for i in range(32)]
    high = [jnp.concatenate([parts[8 * i][:, q:], parts[8 * i][:, :q]], axis=1) if i % 2 == 0 else parts[8 * i] for i in range(4)]
    while len(parts) > 4:
        parts = [a + b for a, b in zip(parts[::2], parts[1::2])]
    parts[1::2] = [jnp.concatenate([p[:, q:], p[:, :q]], axis=1) for p in parts[1::2]]
    low = lax.broadcasted_iota(jnp.int32, parts[0].shape, 1) < q
    alpha_sums, beta_sums = (
        jnp.concatenate([jnp.where(low, p[0], p[1]), jnp.where(low, p[2], p[3])], axis=1) for p in (parts, high)
    )
    alpha = jnp.sqrt(alpha_sums / feat_total + epsilon)
    beta = jnp.sqrt(beta_sums / docs_total + epsilon)
    for part, ref in ((y, own), (1 - y, other)):
        for k in range(4):
            turned[z ^ k] = ref[k]
        left_out[pl.ds(pl.multiple_of(part * half, half), half), :] = turned[...].reshape(-1, half).T / beta
    rho = jnp.sqrt(rhobar[...] * rhobar[...] + beta * beta)
    cosine = rhobar[...] / rho
    sine = beta / rho
    theta = sine * alpha
    phi = cosine * phibar[...]
    rhobar_out[...] = -cosine * alpha
    phibar_out[...] = sine * phibar[...]
    alpha_out[...] = alpha
    for k, g in enumerate((g0, g1, g2, g3)):
        turned[z ^ k] = g[...]
    got = turned[...].reshape(-1, half).T
    following = (got / beta - beta * right[...]) / alpha
    right_out[...] = following
    search_out[...] = following - (theta / rho) * search[...]
    solution_out[...] = solution[...] + (phi / rho) * search[...]


def finish(docs_total, feat_total, pieces, squares, own, other, right, search, solution, phibar, rhobar):
    rows, cols = right.shape
    return pl.pallas_call(
        functools.partial(finish_kernel, docs_total, feat_total),
        out_shape=[f32(2 * rows, cols)] + [f32(rows, cols)] * 3 + [f32(1, cols)] * 3,
        scratch_shapes=[pltpu.VMEM((4, cols // 4, rows), jnp.float32)],
        compiler_params=params(12),
        cost_estimate=cost(rows * cols * 16, rows * cols * 20),
        name="finish",
    )(*pieces, squares, own, other, right, search, solution, phibar, rhobar)


def swap(value, mask):
    return lax.ppermute(value, AXES, [(i, i ^ mask) for i in range(32)])


def along_z(values):
    got = {0: values[0]}
    for k in (2, 3, 1):
        got[k] = swap(values[k], k << Z_SHIFT)
    return [got[k] for k in range(4)]


def after(value, *earlier):
    return lax.optimization_barrier((value, *earlier))[0]


def by_columns(
    col_ids, col_vals, left_vec, right_vec, search_dir, solution_vec, alpha_prev, phibar, rhobar
):
    docs_total = left_vec.shape[0] * 16
    feat_total = right_vec.shape[0] * 32
    alpha_row, phibar_row, rhobar_row = (v.reshape(1, -1) for v in (alpha_prev, phibar, rhobar))

    stored, messages, mine = prepare(col_ids.T, col_vals.T, right_vec, left_vec)
    entries = along_z([stored] * 4)
    messages = along_z([messages[0]] + [after(messages[1], entries[2]), messages[2], messages[3]])
    mine = along_z(mine)
    q = right_vec.shape[1] // 4

    rows1, token1 = build(entries, 1)
    own = stack(messages, q, "stack_right", token1)
    own_x = swap(own, X_BIT)
    own_peer = swap(own, CORE_BIT)
    rows0, token0 = build(entries, 0, own)
    total1 = forward_part(rows1, [own, own_peer], (0, 8), None, [token0, *mine[1:]])
    x_peer = swap(after(own_x, total1), CORE_BIT)
    total1 = forward_part(rows1, [own_x], (4,), total1)
    product1 = product_half(rows1, x_peer, total1, (12,))
    total0 = forward_part(rows0, [own, own_peer], (0, 8))
    total0 = forward_part(rows0, [own_x], (4,), total0)
    product0 = product_half(rows0, x_peer, total0, (12,), *mine, alpha_row)

    *lefts, both0, beta0 = left_half(product0, swap(product1, Y_BIT))
    partial = backward_part(rows0, both0, 0, 16)
    left_own = stack(along_z(lefts), q, "stack_left")
    both1, beta1 = left_half(product1, swap(product0, Y_BIT), beta0, partial)
    far = swap(backward_part(rows1, both1, 12, 4, partial, beta1), CORE_BIT)
    near = backward_part(rows1, both1, 4, 4, partial, None, [], 0.05)
    peer = backward_part(rows1, both1, 8, 4, partial, None, [near], 0.05)
    send_far, send_near, beta_core = far_sums(near, far, beta1, peer)
    got_far = swap(send_far, X_BIT)
    got_near = swap(send_near, X_BIT)
    keep = backward_part(rows1, both1, 0, 4, partial, None, [], 0.05)
    peer = swap(peer, CORE_BIT)

    g2, g3 = right_far(keep, peer, got_far)
    p2, p3 = swap(g2, 2 << Z_SHIFT), swap(g3, 3 << Z_SHIFT)
    g0, g1, sums = right_norm(docs_total, keep, peer, got_near, beta_core, own, (g2, g3))
    pieces = [g0, swap(g1, 1 << Z_SHIFT), p2, p3]
    left_other = swap(after(left_own, send_far), Y_BIT)
    squares = lax.all_to_all(after(sums, left_own), AXES, 0, 0, tiled=True)
    left_next, right_next, search_next, solution_next, alpha_next, phibar_next, rhobar_next = finish(
        docs_total, feat_total, pieces, squares, left_own, left_other,
        right_vec, search_dir, solution_vec, phibar_row, rhobar_row,
    )
    return (
        left_next,
        right_next,
        search_next,
        solution_next,
        alpha_next.reshape(-1),
        phibar_next.reshape(-1),
        rhobar_next.reshape(-1),
    )


def forward(col_ids, col_vals, table):
    picked = table[col_ids]
    return jnp.sum(col_vals.astype(jnp.float32)[:, :, None] * picked, axis=1)


def backward(col_ids, col_vals, rows_in, width):
    terms = col_vals.astype(jnp.float32)[:, :, None] * rows_in[:, None, :]
    return jax.ops.segment_sum(
        terms.reshape(-1, rows_in.shape[1]), col_ids.reshape(-1), num_segments=width
    )


def by_blocks(
    col_ids, col_vals, left_vec, right_vec, search_dir, solution_vec, alpha_prev, phibar, rhobar
):
    n_feat = lax.axis_size("feat")
    n_doc = lax.axis_size("doc")
    docs_total = left_vec.shape[0] * n_doc
    feat_total = right_vec.shape[0] * n_doc * n_feat
    table = lax.all_gather(right_vec, "doc", axis=0, tiled=True)
    total = lax.psum(forward(col_ids, col_vals, table), "feat")
    left_raw = total - alpha_prev[None, :] * left_vec
    row_part = jnp.sum(left_raw * left_raw, axis=0)
    beta_norm = jnp.sqrt(lax.psum(row_part, "doc") / docs_total + epsilon)
    left_next = left_raw / beta_norm[None, :]
    feature_part = lax.psum_scatter(
        backward(col_ids, col_vals, left_next, table.shape[0]), "doc", scatter_dimension=0, tiled=True
    )
    right_raw = feature_part - beta_norm[None, :] * right_vec
    squares = lax.psum(jnp.sum(right_raw * right_raw, axis=0), AXES)
    alpha_next = jnp.sqrt(squares / feat_total + epsilon)
    right_next = right_raw / alpha_next[None, :]
    rho_val = jnp.sqrt(rhobar * rhobar + beta_norm * beta_norm)
    cosine = rhobar / rho_val
    sine_val = beta_norm / rho_val
    theta_val = sine_val * alpha_next
    phi_val = cosine * phibar
    solution_next = solution_vec + (phi_val / rho_val)[None, :] * search_dir
    search_next = right_next - (theta_val / rho_val)[None, :] * search_dir
    return (
        left_next,
        right_next,
        search_next,
        solution_next,
        alpha_next,
        sine_val * phibar,
        -cosine * alpha_next,
    )


def solution(mesh):
    small = mesh.shape["doc"] == 16 and mesh.shape["feat"] == 2
    rows = P(("feat", "doc"), None)
    return jax.shard_map(
        by_columns if small else by_blocks,
        mesh=mesh,
        in_specs=(P("doc", "feat"), P("doc", "feat"), P("doc", None), rows, rows, rows, P(), P(), P()),
        out_specs=(P("doc", None), rows, rows, rows, P(), P(), P()),
        check_vma=False,
    )
```

```python
import functools

import jax
import jax.numpy as jnp
from jax import lax
from jax.experimental import pallas as pl
from jax.experimental.pallas import tpu as pltpu
from jax.sharding import PartitionSpec as P

epsilon = 1e-06
AXES = ("doc", "feat")
MIB = 1024 * 1024


Y_BIT, CORE_BIT, X_BIT, Z_SHIFT = 1, 2, 4, 3
BACKWARDS = list(range(31, -1, -1))
NT = (((1,), (1,)), ((), ()))


def coords():
    d = lax.axis_index("doc")
    y = lax.axis_index("feat")
    return d, d >> 2, y


def params(mib):
    return pltpu.CompilerParams(vmem_limit_bytes=mib * MIB)


def cost(flops, nbytes, scale=64):
    return pl.CostEstimate(flops=int(flops / scale), bytes_accessed=int(nbytes / scale), transcendentals=0)


def f32(*shape):
    return jax.ShapeDtypeStruct(shape, jnp.float32)


def bf16(*shape):
    return jax.ShapeDtypeStruct(shape, jnp.bfloat16)


def prepare_kernel(ids_hbm, vals_hbm, right_hbm, left_hbm, stored, m0, m1, m2, m3,
                   ids, vals, wide, right, left, turned, arrived):
    _, z, y = coords()
    q, rows = turned.shape[1:]
    copies = [
        pltpu.make_async_copy(src, dst, arrived.at[i])
        for i, (src, dst) in enumerate((
            (ids_hbm, ids),
            (vals_hbm, vals),
            (right_hbm, right),
            (left_hbm.at[pl.ds(pl.multiple_of(y * rows, rows), rows), :], left),
        ))
    ]
    for copy in copies:
        copy.start()
    lines, count = stored.shape[0] // 2, ids.shape[0]
    for part, ref in enumerate((ids, vals)):
        copies[part].wait()
        wide[...] = ref[...].astype(jnp.float32).T
        for r in range(256 // count):
            stored[part * lines : (part + 1) * lines, r * count : (r + 1) * count] = wide[
                pl.ds(r, lines, stride=256 // count), :
            ]
    for part, ref in enumerate((right, left)):
        copies[2 + part].wait()
        turned[...] = ref[...].T.reshape(turned.shape)
        for k, out in enumerate((m0, m1, m2, m3)):
            out[part * q : (part + 1) * q, :] = turned[z ^ k]


def prepare(ids, vals, right, left):
    rows, cols = right.shape
    q = cols // 4
    got = pl.pallas_call(
        prepare_kernel,
        in_specs=[pl.BlockSpec(memory_space=pltpu.HBM)] * 4,
        out_specs=[whole()] * 5,
        out_shape=[pltpu.VMEM((ids.size // 128, 256), jnp.float32)] + [pltpu.VMEM((2 * q, rows), jnp.float32)] * 4,
        scratch_shapes=[
            pltpu.VMEM(ids.shape, jnp.int32),
            pltpu.VMEM(vals.shape, jnp.bfloat16),
            pltpu.VMEM(ids.shape[::-1], jnp.float32),
            pltpu.VMEM(right.shape, jnp.float32),
            pltpu.VMEM(right.shape, jnp.float32),
            pltpu.VMEM((4, q, rows), jnp.float32),
            pltpu.SemaphoreType.DMA((4,)),
        ],
        compiler_params=params(60),
        cost_estimate=cost(0, rows * cols * 16),
        name="prepare",
    )(ids, vals, right, left)
    return got[0], got[1:]


def stack_kernel(m0, m1, m2, m3, *refs):
    out = refs[-1]
    for k, m in enumerate((m0, m1, m2, m3)):
        out[k] = m[0 : out.shape[1], :]


def stack(messages, q, name, *tokens):
    rows = messages[0].shape[1]
    return pl.pallas_call(
        stack_kernel,
        out_shape=f32(4, q, rows),
        compiler_params=params(8),
        cost_estimate=cost(0, 32 * q * rows),
        name=name,
    )(*messages, *tokens)


def build_kernel(rel, e0, e1, e2, e3, *refs):
    hi_ref, lo_ref, token = refs[-3:]
    token[...] = jnp.zeros_like(token)
    d, _, y = coords()
    n = e0.shape[0] // 2
    iota = lax.broadcasted_iota(jnp.int32, (256, 256), 0).astype(jnp.float32).astype(jnp.bfloat16)
    lane_doc = lax.broadcasted_iota(jnp.int32, (8, 256), 1) >> 4
    one = jnp.ones((256, 256), jnp.bfloat16)
    zero = jnp.zeros((256, 256), jnp.bfloat16)

    def spread(row):
        wide = jnp.broadcast_to(row, (16, 256)).astype(jnp.bfloat16)
        return jnp.broadcast_to(wide[None], (16, 16, 256)).reshape(256, 256)

    for k, entries in enumerate((e0, e1, e2, e3)):

        @pl.loop(0, n // 16)
        def _(step, k=k, entries=entries):
            at = pl.multiple_of((y ^ rel) * (n // 2) + step * 8, 8)
            ids = entries[pl.ds(at, 8), :].astype(jnp.int32)
            vals = entries[pl.ds(n + at, 8), :]
            owner = (ids >> 8) ^ d
            block = ((owner & 1) << 3) | ((owner & 2) << 1) | (owner >> 2)
            code = (block * 16 + lane_doc).astype(jnp.float32)
            inner = (ids & 255).astype(jnp.float32)
            for t in range(8):
                pick = jnp.where(iota == spread(code[t : t + 1]), one, zero)
                weigh = jnp.where(iota == spread(inner[t : t + 1]), spread(vals[t : t + 1]), zero)
                dense = lax.dot_general(pick, weigh, NT, preferred_element_type=jnp.float32)
                high = dense.astype(jnp.bfloat16)
                low = (dense - high.astype(jnp.float32)).astype(jnp.bfloat16)
                docs = pl.ds(pl.multiple_of(k * 8 * n + step * 128 + 16 * t, 16), 16)
                hi_ref[:, docs, :] = high.reshape(16, 16, 256)
                lo_ref[:, docs, :] = low.reshape(16, 16, 256)


def whole():
    return pl.BlockSpec(memory_space=pltpu.VMEM)


def build(entries, rel, *tokens):
    docs = 4 * (entries[0].shape[0] // 4 * 16)
    *rows, token = pl.pallas_call(
        functools.partial(build_kernel, rel),
        in_specs=[whole()] * (4 + len(tokens)),
        out_specs=[whole()] * 3,
        out_shape=[pltpu.VMEM((16, docs, 256), jnp.bfloat16)] * 2 + [f32(8, 128)],
        compiler_params=params(8),
        cost_estimate=cost(2 * docs * 16 * 256 * 256, docs * 4096 * 4, 1 if rel else 64),
        name="dense_rows",
    )(*entries, *tokens)
    return rows, token


def split_rows(value):
    high = value.astype(jnp.bfloat16)
    low = (value - high.astype(jnp.float32)).astype(jnp.bfloat16)
    return jnp.concatenate([high, low], axis=0)


def add_products(hi_ref, lo_ref, vecs, blocks, total):
    for vec, first in zip(vecs, blocks):
        for pair in (0, 2):
            lhs, rhs = [], []
            for k in (pair, pair + 1):
                both = split_rows(vec[k])
                lhs += [hi_ref[first + k], lo_ref[first + k]]
                rhs += [both, both]
            total[...] += lax.dot_general(
                jnp.concatenate(lhs, axis=1), jnp.concatenate(rhs, axis=1), NT, preferred_element_type=jnp.float32
            )


def forward_kernel(blocks, has_before, hi_ref, lo_ref, *refs):
    count = len(blocks)
    total = refs[-1]
    total[...] = refs[count][...] if has_before else jnp.zeros_like(total)
    add_products(hi_ref, lo_ref, refs[:count], blocks, total)


def forward_part(rows, vecs, blocks, before=None, tokens=()):
    docs, q = rows[0].shape[1], vecs[0].shape[1]
    n = 4 * len(blocks)
    extra = [*tokens] if before is None else [before, *tokens]
    return pl.pallas_call(
        functools.partial(forward_kernel, blocks, before is not None),
        in_specs=[whole()] * (2 + len(vecs) + len(extra)),
        out_specs=whole(),
        out_shape=f32(docs, 2 * q),
        compiler_params=params(8),
        cost_estimate=cost(8 * docs * 256 * 256 * n, 4 * docs * 256 * n),
        name="forward_part",
    )(*rows, *vecs, *extra)


def product_kernel(blocks, hi_ref, lo_ref, vec, before, *refs):
    out, total, columns = refs[-3:]
    total[...] = before[...]
    add_products(hi_ref, lo_ref, (vec,), blocks, total)
    turned = total[...].T
    q = out.shape[0]
    product = turned[:q] + turned[q:]
    if len(refs) == 3:
        out[...] = product
        return
    _, z, _ = coords()
    *messages, alpha = refs[:5]
    columns[...] = row_to_column(alpha[...])
    scale = columns[pl.ds(pl.multiple_of(z * q, q), q), :][:, 0:1]
    for k, m in enumerate(messages):
        at = slice(k * m.shape[1], (k + 1) * m.shape[1])
        out[:, at] = product[:, at] - scale * m[q:, :]


def product_half(rows, vec, before, blocks, *left):
    docs, q = rows[0].shape[1], vec.shape[1]
    return pl.pallas_call(
        functools.partial(product_kernel, blocks),
        in_specs=[whole()] * (4 + len(left)),
        out_specs=whole(),
        out_shape=f32(q, docs),
        scratch_shapes=[pltpu.VMEM((docs, 2 * q), jnp.float32), pltpu.VMEM((4 * q, 128), jnp.float32)],
        compiler_params=params(8),
        cost_estimate=cost(8 * docs * 256 * 256 * 4, 16 * docs * 256),
        name="product_half",
    )(*rows, vec, before, *left)


def square_sums(value):
    q, n = value.shape
    sums = value[:, 0:128] * value[:, 0:128]
    for at in range(128, n, 128):
        sums = sums + value[:, at : at + 128] * value[:, at : at + 128]
    return jnp.sum(jnp.concatenate([sums] * (128 // q), axis=0).T, axis=0, keepdims=True)


def square_row(value, z, cols):
    row = square_sums(value)
    row = jnp.broadcast_to(jnp.concatenate([row] * (cols // 128), axis=1), (8, cols))
    lane = lax.broadcasted_iota(jnp.int32, (8, cols), 1)
    return jnp.where(lane // value.shape[0] == z, row, 0.0)


def row_to_column(row):
    return jnp.broadcast_to(row, (128, row.shape[1])).T


def left_half_kernel(mine, other, *refs):
    _, z, _ = coords()
    left = mine[...] + other[...]
    both, sums = refs[-2:]
    both[...] = split_rows(left)
    squares = square_row(left, z, sums.shape[1])
    sums[...] = refs[0][...] + squares if len(refs) == 4 else squares
    if len(refs) > 4:
        n = left.shape[1] // 4
        for k, out in enumerate(refs[:4]):
            out[...] = left[:, k * n : (k + 1) * n]


def left_half(mine, other, squares=None, token=None):
    q, docs = mine.shape
    extra = [] if squares is None else [squares, token]
    pieces = [f32(q, docs // 4)] * 4 if squares is None else []
    return pl.pallas_call(
        left_half_kernel,
        out_shape=pieces + [bf16(2 * q, docs), f32(8, 4 * q)],
        compiler_params=params(8),
        cost_estimate=cost(8 * q * docs, 16 * q * docs),
        name="left_half",
    )(mine, other, *extra)


def backward_kernel(first, blocks, parts, hi_ref, lo_ref, both_ref, *refs):
    out_ref = refs[-1]
    both = both_ref[...]
    q = both.shape[0] // 2
    twice = jnp.concatenate([both, both], axis=1)
    for b in range(blocks):
        got = jnp.dot(
            twice,
            jnp.concatenate([hi_ref[first + b], lo_ref[first + b]], axis=0),
            preferred_element_type=jnp.float32,
        )
        got = got[:q] + got[q:]
        if "before" in parts:
            got = got + refs[0][(first + b) * q : (first + b + 1) * q, :]
        out_ref[b * q : (b + 1) * q, :] = got
    if "tail" in parts:
        out_ref[blocks * q :, :] = refs[parts.index("tail")][...]


def backward_part(rows, both, first, blocks, before=None, tail=None, tokens=(), scale=64):
    q, docs = both.shape[0] // 2, both.shape[1]
    extra = {"before": before, "tail": tail, **{str(i): token for i, token in enumerate(tokens)}}
    extra = {name: value for name, value in extra.items() if value is not None}
    height = blocks * q + (0 if tail is None else tail.shape[0])
    return pl.pallas_call(
        functools.partial(backward_kernel, first, blocks, tuple(extra)),
        in_specs=[whole()] * (3 + len(extra)),
        out_specs=whole(),
        out_shape=f32(height, 256),
        compiler_params=params(8),
        cost_estimate=cost(8 * docs * 256 * 256 * blocks, 4 * docs * 256 * blocks, scale),
        name="backward_part",
    )(*rows, both, *extra.values())


def far_sum_kernel(near, far, beta, token, send_far, send_near, beta_core):
    n = near.shape[0] // 2
    beta_core[...] = beta[...] + far[2 * n :, :]
    send_far[...] = near[n:, :] + far[n : 2 * n, :]
    send_near[0:n, :] = near[0:n, :] + far[0:n, :]
    send_near[n:, :] = beta_core[...]


def far_sums(near, far, beta, token):
    rows = near.shape[0] // 2
    return pl.pallas_call(
        far_sum_kernel,
        out_shape=[f32(rows, 256), f32(rows + 8, 256), f32(8, 256)],
        compiler_params=params(8),
        cost_estimate=cost(near.size, near.size * 12),
        name="far_sums",
    )(near, far, beta, token)


def right_far_kernel(keep, peer, got, g2, g3):
    q = g2.shape[0]
    for k, g in ((2, g2), (3, g3)):
        rows = slice(k * q, (k + 1) * q)
        g[...] = (keep[rows, :] + peer[rows, :]) + got[(k - 2) * q : (k - 1) * q, :]


def right_far(keep, peer, got):
    q, rows = keep.shape[0] // 4, keep.shape[1]
    return pl.pallas_call(
        right_far_kernel,
        out_shape=[f32(q, rows)] * 2,
        compiler_params=params(8),
        cost_estimate=cost(rows * q * 4, rows * q * 32),
        name="right_far",
    )(keep, peer, got)


def right_norm_kernel(docs_total, keep, peer, got, beta_core, right, g2, g3, g0, g1, sums, columns):
    _, z, _ = coords()
    q = right.shape[1]
    beta_sums = beta_core[0:1, :] + got[2 * q : 2 * q + 1, :]
    columns[...] = row_to_column(jnp.sqrt(beta_sums / docs_total + epsilon))
    beta = columns[pl.ds(pl.multiple_of(z * q, q), q), :][:, 0:1]
    for k, g in enumerate((g0, g1)):
        rows = slice(k * q, (k + 1) * q)
        g[...] = (keep[rows, :] + peer[rows, :]) + got[rows, :]
    raws = [g[...] / beta - beta * right[k] for k, g in enumerate((g0, g1, g2, g3))]
    line = square_sums(jnp.concatenate(raws, axis=1))
    folded = beta_sums[:, :128] + beta_sums[:, 128:]
    folded = folded + jnp.concatenate([folded[:, q:], folded[:, :q]], axis=1)
    low = lax.broadcasted_iota(jnp.int32, line.shape, 1) < q
    sums[...] = jnp.broadcast_to(jnp.where(low, line, folded), sums.shape)


def right_norm(docs_total, keep, peer, got, beta_core, right, far):
    q, rows = keep.shape[0] // 4, keep.shape[1]
    g0, g1, sums = pl.pallas_call(
        functools.partial(right_norm_kernel, docs_total),
        out_shape=[f32(q, rows)] * 2 + [f32(32, 128)],
        scratch_shapes=[pltpu.VMEM((4 * q, 128), jnp.float32)],
        compiler_params=params(8),
        cost_estimate=cost(rows * q * 64, rows * q * 100, 64),
        name="right_norm",
    )(keep, peer, got, beta_core, right, *far)
    return g0, g1, sums.reshape(32, 1, 128)


def finish_kernel(docs_total, feat_total, g0, g1, g2, g3, squares, own, other, right, search, solution, phibar, rhobar,
                  left_out, right_out, search_out, solution_out, alpha_out, phibar_out, rhobar_out, turned):
    _, z, y = coords()
    q, half = turned.shape[1:]
    parts = [squares[i] for i in BACKWARDS]
    high = [jnp.concatenate([parts[8 * i][:, q:], parts[8 * i][:, :q]], axis=1) if i % 2 == 0 else parts[8 * i] for i in range(4)]
    while len(parts) > 4:
        parts = [a + b for a, b in zip(parts[::2], parts[1::2])]
    parts[1::2] = [jnp.concatenate([p[:, q:], p[:, :q]], axis=1) for p in parts[1::2]]
    low = lax.broadcasted_iota(jnp.int32, parts[0].shape, 1) < q
    alpha_sums, beta_sums = (
        jnp.concatenate([jnp.where(low, p[0], p[1]), jnp.where(low, p[2], p[3])], axis=1) for p in (parts, high)
    )
    alpha = jnp.sqrt(alpha_sums / feat_total + epsilon)
    beta = jnp.sqrt(beta_sums / docs_total + epsilon)
    for part, ref in ((y, own), (1 - y, other)):
        for k in range(4):
            turned[z ^ k] = ref[k]
        left_out[pl.ds(pl.multiple_of(part * half, half), half), :] = turned[...].reshape(-1, half).T / beta
    rho = jnp.sqrt(rhobar[...] * rhobar[...] + beta * beta)
    cosine = rhobar[...] / rho
    sine = beta / rho
    theta = sine * alpha
    phi = cosine * phibar[...]
    rhobar_out[...] = -cosine * alpha
    phibar_out[...] = sine * phibar[...]
    alpha_out[...] = alpha
    for k, g in enumerate((g0, g1, g2, g3)):
        turned[z ^ k] = g[...]
    got = turned[...].reshape(-1, half).T
    following = (got / beta - beta * right[...]) / alpha
    right_out[...] = following
    search_out[...] = following - (theta / rho) * search[...]
    solution_out[...] = solution[...] + (phi / rho) * search[...]


def finish(docs_total, feat_total, pieces, squares, own, other, right, search, solution, phibar, rhobar):
    rows, cols = right.shape
    return pl.pallas_call(
        functools.partial(finish_kernel, docs_total, feat_total),
        out_shape=[f32(2 * rows, cols)] + [f32(rows, cols)] * 3 + [f32(1, cols)] * 3,
        scratch_shapes=[pltpu.VMEM((4, cols // 4, rows), jnp.float32)],
        compiler_params=params(12),
        cost_estimate=cost(rows * cols * 16, rows * cols * 20),
        name="finish",
    )(*pieces, squares, own, other, right, search, solution, phibar, rhobar)


def swap(value, mask):
    return lax.ppermute(value, AXES, [(i, i ^ mask) for i in range(32)])


def along_z(values):
    got = {0: values[0]}
    for k in (2, 3, 1):
        got[k] = swap(values[k], k << Z_SHIFT)
    return [got[k] for k in range(4)]


def after(value, *earlier):
    return lax.optimization_barrier((value, *earlier))[0]


def by_columns(
    col_ids, col_vals, left_vec, right_vec, search_dir, solution_vec, alpha_prev, phibar, rhobar
):
    docs_total = left_vec.shape[0] * 16
    feat_total = right_vec.shape[0] * 32
    alpha_row, phibar_row, rhobar_row = (v.reshape(1, -1) for v in (alpha_prev, phibar, rhobar))

    stored, messages = prepare(col_ids.T, col_vals.T, right_vec, left_vec)
    entries = along_z([stored] * 4)
    messages = along_z([messages[0]] + [after(messages[1], entries[2]), messages[2], messages[3]])
    q = right_vec.shape[1] // 4

    rows1, token1 = build(entries, 1)
    own = stack(messages, q, "stack_right", token1)
    own_x = swap(own, X_BIT)
    own_peer = swap(own, CORE_BIT)
    rows0, token0 = build(entries, 0, own)
    total1 = forward_part(rows1, [own, own_peer], (0, 8), None, [token0])
    x_peer = swap(after(own_x, total1), CORE_BIT)
    total1 = forward_part(rows1, [own_x], (4,), total1)
    product1 = product_half(rows1, x_peer, total1, (12,))
    total0 = forward_part(rows0, [own, own_peer], (0, 8))
    total0 = forward_part(rows0, [own_x], (4,), total0)
    product0 = product_half(rows0, x_peer, total0, (12,), *messages, alpha_row)

    *lefts, both0, beta0 = left_half(product0, swap(product1, Y_BIT))
    partial = backward_part(rows0, both0, 0, 16)
    left_own = stack(along_z(lefts), q, "stack_left")
    both1, beta1 = left_half(product1, swap(product0, Y_BIT), beta0, partial)
    far = swap(backward_part(rows1, both1, 12, 4, partial, beta1), CORE_BIT)
    near = backward_part(rows1, both1, 4, 4, partial, None, [], 0.05)
    peer = backward_part(rows1, both1, 8, 4, partial, None, [near], 0.05)
    send_far, send_near, beta_core = far_sums(near, far, beta1, peer)
    got_far = swap(send_far, X_BIT)
    got_near = swap(send_near, X_BIT)
    keep = backward_part(rows1, both1, 0, 4, partial, None, [], 0.05)
    peer = swap(peer, CORE_BIT)

    g2, g3 = right_far(keep, peer, got_far)
    p2, p3 = swap(g2, 2 << Z_SHIFT), swap(g3, 3 << Z_SHIFT)
    g0, g1, sums = right_norm(docs_total, keep, peer, got_near, beta_core, own, (g2, g3))
    pieces = [g0, swap(g1, 1 << Z_SHIFT), p2, p3]
    left_other = swap(after(left_own, send_far), Y_BIT)
    squares = lax.all_to_all(after(sums, left_own), AXES, 0, 0, axis_index_groups=[BACKWARDS], tiled=True)
    left_next, right_next, search_next, solution_next, alpha_next, phibar_next, rhobar_next = finish(
        docs_total, feat_total, pieces, squares, left_own, left_other,
        right_vec, search_dir, solution_vec, phibar_row, rhobar_row,
    )
    return (
        left_next,
        right_next,
        search_next,
        solution_next,
        alpha_next.reshape(-1),
        phibar_next.reshape(-1),
        rhobar_next.reshape(-1),
    )


def forward(col_ids, col_vals, table):
    picked = table[col_ids]
    return jnp.sum(col_vals.astype(jnp.float32)[:, :, None] * picked, axis=1)


def backward(col_ids, col_vals, rows_in, width):
    terms = col_vals.astype(jnp.float32)[:, :, None] * rows_in[:, None, :]
    return jax.ops.segment_sum(
        terms.reshape(-1, rows_in.shape[1]), col_ids.reshape(-1), num_segments=width
    )


def by_blocks(
    col_ids, col_vals, left_vec, right_vec, search_dir, solution_vec, alpha_prev, phibar, rhobar
):
    n_feat = lax.axis_size("feat")
    n_doc = lax.axis_size("doc")
    docs_total = left_vec.shape[0] * n_doc
    feat_total = right_vec.shape[0] * n_doc * n_feat
    table = lax.all_gather(right_vec, "doc", axis=0, tiled=True)
    total = lax.psum(forward(col_ids, col_vals, table), "feat")
    left_raw = total - alpha_prev[None, :] * left_vec
    row_part = jnp.sum(left_raw * left_raw, axis=0)
    beta_norm = jnp.sqrt(lax.psum(row_part, "doc") / docs_total + epsilon)
    left_next = left_raw / beta_norm[None, :]
    feature_part = lax.psum_scatter(
        backward(col_ids, col_vals, left_next, table.shape[0]), "doc", scatter_dimension=0, tiled=True
    )
    right_raw = feature_part - beta_norm[None, :] * right_vec
    squares = lax.psum(jnp.sum(right_raw * right_raw, axis=0), AXES)
    alpha_next = jnp.sqrt(squares / feat_total + epsilon)
    right_next = right_raw / alpha_next[None, :]
    rho_val = jnp.sqrt(rhobar * rhobar + beta_norm * beta_norm)
    cosine = rhobar / rho_val
    sine_val = beta_norm / rho_val
    theta_val = sine_val * alpha_next
    phi_val = cosine * phibar
    solution_next = solution_vec + (phi_val / rho_val)[None, :] * search_dir
    search_next = right_next - (theta_val / rho_val)[None, :] * search_dir
    return (
        left_next,
        right_next,
        search_next,
        solution_next,
        alpha_next,
        sine_val * phibar,
        -cosine * alpha_next,
    )


def solution(mesh):
    small = mesh.shape["doc"] == 16 and mesh.shape["feat"] == 2
    rows = P(("feat", "doc"), None)
    return jax.shard_map(
        by_columns if small else by_blocks,
        mesh=mesh,
        in_specs=(P("doc", "feat"), P("doc", "feat"), P("doc", None), rows, rows, rows, P(), P(), P()),
        out_specs=(P("doc", None), rows, rows, rows, P(), P(), P()),
        check_vma=False,
    )
```

```python
import functools

import jax
import jax.numpy as jnp
from jax import lax
from jax.experimental import pallas as pl
from jax.experimental.pallas import tpu as pltpu
from jax.sharding import PartitionSpec as P

epsilon = 1e-06
AXES = ("doc", "feat")
MIB = 1024 * 1024


Y_BIT, CORE_BIT, X_BIT, Z_SHIFT = 1, 2, 4, 3
NT = (((1,), (1,)), ((), ()))


def coords():
    d = lax.axis_index("doc")
    y = lax.axis_index("feat")
    return d, d >> 2, y


def params(mib):
    return pltpu.CompilerParams(vmem_limit_bytes=mib * MIB)


def cost(flops, nbytes, scale=64):
    return pl.CostEstimate(flops=int(flops / scale), bytes_accessed=int(nbytes / scale), transcendentals=0)


def f32(*shape):
    return jax.ShapeDtypeStruct(shape, jnp.float32)


def bf16(*shape):
    return jax.ShapeDtypeStruct(shape, jnp.bfloat16)


def prepare_kernel(ids_hbm, vals_hbm, right_hbm, left_hbm, stored, m0, m1, m2, m3,
                   ids, vals, wide, right, left, turned, arrived):
    _, z, y = coords()
    q, rows = turned.shape[1:]
    moves = [(ids_hbm, ids), (vals_hbm, vals)]
    piece = rows // 4
    for src, first, dst in ((right_hbm, 0, right), (left_hbm, y * rows, left)):
        for i in range(4):
            at = pl.multiple_of(first + i * piece, piece)
            moves.append((src.at[pl.ds(at, piece), :], dst.at[i * piece : (i + 1) * piece, :]))
    copies = [pltpu.make_async_copy(src, dst, arrived.at[i]) for i, (src, dst) in enumerate(moves)]
    for copy in copies:
        copy.start()
    lines, count = stored.shape[0] // 2, ids.shape[0]
    for part, ref in enumerate((ids, vals)):
        copies[part].wait()
        wide[...] = ref[...].astype(jnp.float32).T
        for r in range(256 // count):
            stored[part * lines : (part + 1) * lines, r * count : (r + 1) * count] = wide[
                pl.ds(r, lines, stride=256 // count), :
            ]
    for part, ref in enumerate((right, left)):
        for copy in copies[2 + 4 * part : 6 + 4 * part]:
            copy.wait()
        turned[...] = ref[...].T.reshape(turned.shape)
        for k, out in enumerate((m0, m1, m2, m3)):
            out[part * q : (part + 1) * q, :] = turned[z ^ k]


def prepare(ids, vals, right, left):
    rows, cols = right.shape
    q = cols // 4
    got = pl.pallas_call(
        prepare_kernel,
        in_specs=[pl.BlockSpec(memory_space=pltpu.HBM)] * 4,
        out_specs=[whole()] * 5,
        out_shape=[pltpu.VMEM((ids.size // 128, 256), jnp.float32)] + [pltpu.VMEM((2 * q, rows), jnp.float32)] * 4,
        scratch_shapes=[
            pltpu.VMEM(ids.shape, jnp.int32),
            pltpu.VMEM(vals.shape, jnp.bfloat16),
            pltpu.VMEM(ids.shape[::-1], jnp.float32),
            pltpu.VMEM(right.shape, jnp.float32),
            pltpu.VMEM(right.shape, jnp.float32),
            pltpu.VMEM((4, q, rows), jnp.float32),
            pltpu.SemaphoreType.DMA((10,)),
        ],
        compiler_params=params(60),
        cost_estimate=cost(0, rows * cols * 16),
        name="prepare",
    )(ids, vals, right, left)
    return got[0], got[1:]


def stack_kernel(m0, m1, m2, m3, *refs):
    out = refs[-1]
    for k, m in enumerate((m0, m1, m2, m3)):
        out[k] = m[0 : out.shape[1], :]


def stack(messages, q, name, *tokens):
    rows = messages[0].shape[1]
    return pl.pallas_call(
        stack_kernel,
        out_shape=f32(4, q, rows),
        compiler_params=params(8),
        cost_estimate=cost(0, 32 * q * rows),
        name=name,
    )(*messages, *tokens)


def build_kernel(rel, e0, e1, e2, e3, *refs):
    hi_ref, lo_ref, token = refs[-3:]
    token[...] = jnp.zeros_like(token)
    d, _, y = coords()
    n = e0.shape[0] // 2
    iota = lax.broadcasted_iota(jnp.int32, (256, 256), 0).astype(jnp.float32).astype(jnp.bfloat16)
    lane_doc = lax.broadcasted_iota(jnp.int32, (8, 256), 1) >> 4
    one = jnp.ones((256, 256), jnp.bfloat16)
    zero = jnp.zeros((256, 256), jnp.bfloat16)

    def spread(row):
        wide = jnp.broadcast_to(row, (16, 256)).astype(jnp.bfloat16)
        return jnp.broadcast_to(wide[None], (16, 16, 256)).reshape(256, 256)

    for k, entries in enumerate((e0, e1, e2, e3)):

        @pl.loop(0, n // 16)
        def _(step, k=k, entries=entries):
            at = pl.multiple_of((y ^ rel) * (n // 2) + step * 8, 8)
            ids = entries[pl.ds(at, 8), :].astype(jnp.int32)
            vals = entries[pl.ds(n + at, 8), :]
            owner = (ids >> 8) ^ d
            block = ((owner & 1) << 3) | ((owner & 2) << 1) | (owner >> 2)
            code = (block * 16 + lane_doc).astype(jnp.float32)
            inner = (ids & 255).astype(jnp.float32)
            for t in range(8):
                pick = jnp.where(iota == spread(code[t : t + 1]), one, zero)
                weigh = jnp.where(iota == spread(inner[t : t + 1]), spread(vals[t : t + 1]), zero)
                dense = lax.dot_general(pick, weigh, NT, preferred_element_type=jnp.float32)
                high = dense.astype(jnp.bfloat16)
                low = (dense - high.astype(jnp.float32)).astype(jnp.bfloat16)
                docs = pl.ds(pl.multiple_of(k * 8 * n + step * 128 + 16 * t, 16), 16)
                hi_ref[:, docs, :] = high.reshape(16, 16, 256)
                lo_ref[:, docs, :] = low.reshape(16, 16, 256)


def whole():
    return pl.BlockSpec(memory_space=pltpu.VMEM)


def build(entries, rel, *tokens):
    docs = 4 * (entries[0].shape[0] // 4 * 16)
    *rows, token = pl.pallas_call(
        functools.partial(build_kernel, rel),
        in_specs=[whole()] * (4 + len(tokens)),
        out_specs=[whole()] * 3,
        out_shape=[pltpu.VMEM((16, docs, 256), jnp.bfloat16)] * 2 + [f32(8, 128)],
        compiler_params=params(8),
        cost_estimate=cost(2 * docs * 16 * 256 * 256, docs * 4096 * 4, 1 if rel else 64),
        name="dense_rows",
    )(*entries, *tokens)
    return rows, token


def split_rows(value):
    high = value.astype(jnp.bfloat16)
    low = (value - high.astype(jnp.float32)).astype(jnp.bfloat16)
    return jnp.concatenate([high, low], axis=0)


def add_products(hi_ref, lo_ref, vecs, blocks, total):
    for vec, first in zip(vecs, blocks):
        for pair in (0, 2):
            lhs, rhs = [], []
            for k in (pair, pair + 1):
                both = split_rows(vec[k])
                lhs += [hi_ref[first + k], lo_ref[first + k]]
                rhs += [both, both]
            total[...] += lax.dot_general(
                jnp.concatenate(lhs, axis=1), jnp.concatenate(rhs, axis=1), NT, preferred_element_type=jnp.float32
            )


def forward_kernel(blocks, has_before, hi_ref, lo_ref, *refs):
    count = len(blocks)
    total = refs[-1]
    total[...] = refs[count][...] if has_before else jnp.zeros_like(total)
    add_products(hi_ref, lo_ref, refs[:count], blocks, total)


def forward_part(rows, vecs, blocks, before=None, tokens=()):
    docs, q = rows[0].shape[1], vecs[0].shape[1]
    n = 4 * len(blocks)
    extra = [*tokens] if before is None else [before, *tokens]
    return pl.pallas_call(
        functools.partial(forward_kernel, blocks, before is not None),
        in_specs=[whole()] * (2 + len(vecs) + len(extra)),
        out_specs=whole(),
        out_shape=f32(docs, 2 * q),
        compiler_params=params(8),
        cost_estimate=cost(8 * docs * 256 * 256 * n, 4 * docs * 256 * n),
        name="forward_part",
    )(*rows, *vecs, *extra)


def product_kernel(blocks, hi_ref, lo_ref, vec, before, *refs):
    out, total, columns = refs[-3:]
    total[...] = before[...]
    add_products(hi_ref, lo_ref, (vec,), blocks, total)
    turned = total[...].T
    q = out.shape[0]
    product = turned[:q] + turned[q:]
    if len(refs) == 3:
        out[...] = product
        return
    _, z, _ = coords()
    *messages, alpha = refs[:5]
    columns[...] = row_to_column(alpha[...])
    scale = columns[pl.ds(pl.multiple_of(z * q, q), q), :][:, 0:1]
    for k, m in enumerate(messages):
        at = slice(k * m.shape[1], (k + 1) * m.shape[1])
        out[:, at] = product[:, at] - scale * m[q:, :]


def product_half(rows, vec, before, blocks, *left):
    docs, q = rows[0].shape[1], vec.shape[1]
    return pl.pallas_call(
        functools.partial(product_kernel, blocks),
        in_specs=[whole()] * (4 + len(left)),
        out_specs=whole(),
        out_shape=f32(q, docs),
        scratch_shapes=[pltpu.VMEM((docs, 2 * q), jnp.float32), pltpu.VMEM((4 * q, 128), jnp.float32)],
        compiler_params=params(8),
        cost_estimate=cost(8 * docs * 256 * 256 * 4, 16 * docs * 256),
        name="product_half",
    )(*rows, vec, before, *left)


def square_sums(value):
    q, n = value.shape
    sums = value[:, 0:128] * value[:, 0:128]
    for at in range(128, n, 128):
        sums = sums + value[:, at : at + 128] * value[:, at : at + 128]
    return jnp.sum(jnp.concatenate([sums] * (128 // q), axis=0).T, axis=0, keepdims=True)


def square_row(value, z, cols):
    row = square_sums(value)
    row = jnp.broadcast_to(jnp.concatenate([row] * (cols // 128), axis=1), (8, cols))
    lane = lax.broadcasted_iota(jnp.int32, (8, cols), 1)
    return jnp.where(lane // value.shape[0] == z, row, 0.0)


def row_to_column(row):
    return jnp.broadcast_to(row, (128, row.shape[1])).T


def left_half_kernel(mine, other, *refs):
    _, z, _ = coords()
    left = mine[...] + other[...]
    both, sums = refs[-2:]
    both[...] = split_rows(left)
    squares = square_row(left, z, sums.shape[1])
    sums[...] = refs[0][...] + squares if len(refs) == 4 else squares
    if len(refs) > 4:
        n = left.shape[1] // 4
        for k, out in enumerate(refs[:4]):
            out[...] = left[:, k * n : (k + 1) * n]


def left_half(mine, other, squares=None, token=None):
    q, docs = mine.shape
    extra = [] if squares is None else [squares, token]
    pieces = [f32(q, docs // 4)] * 4 if squares is None else []
    return pl.pallas_call(
        left_half_kernel,
        out_shape=pieces + [bf16(2 * q, docs), f32(8, 4 * q)],
        compiler_params=params(8),
        cost_estimate=cost(8 * q * docs, 16 * q * docs),
        name="left_half",
    )(mine, other, *extra)


def backward_kernel(first, blocks, parts, hi_ref, lo_ref, both_ref, *refs):
    out_ref = refs[-1]
    both = both_ref[...]
    q = both.shape[0] // 2
    twice = jnp.concatenate([both, both], axis=1)
    for b in range(blocks):
        got = jnp.dot(
            twice,
            jnp.concatenate([hi_ref[first + b], lo_ref[first + b]], axis=0),
            preferred_element_type=jnp.float32,
        )
        got = got[:q] + got[q:]
        if "before" in parts:
            got = got + refs[0][(first + b) * q : (first + b + 1) * q, :]
        out_ref[b * q : (b + 1) * q, :] = got
    if "tail" in parts:
        out_ref[blocks * q :, :] = refs[parts.index("tail")][...]


def backward_part(rows, both, first, blocks, before=None, tail=None, tokens=(), scale=64):
    q, docs = both.shape[0] // 2, both.shape[1]
    extra = {"before": before, "tail": tail, **{str(i): token for i, token in enumerate(tokens)}}
    extra = {name: value for name, value in extra.items() if value is not None}
    height = blocks * q + (0 if tail is None else tail.shape[0])
    return pl.pallas_call(
        functools.partial(backward_kernel, first, blocks, tuple(extra)),
        in_specs=[whole()] * (3 + len(extra)),
        out_specs=whole(),
        out_shape=f32(height, 256),
        compiler_params=params(8),
        cost_estimate=cost(8 * docs * 256 * 256 * blocks, 4 * docs * 256 * blocks, scale),
        name="backward_part",
    )(*rows, both, *extra.values())


def far_sum_kernel(near, far, beta, token, send_far, send_near, beta_core):
    n = near.shape[0] // 2
    beta_core[...] = beta[...] + far[2 * n :, :]
    send_far[...] = near[n:, :] + far[n : 2 * n, :]
    send_near[0:n, :] = near[0:n, :] + far[0:n, :]
    send_near[n:, :] = beta_core[...]


def far_sums(near, far, beta, token):
    rows = near.shape[0] // 2
    return pl.pallas_call(
        far_sum_kernel,
        out_shape=[f32(rows, 256), f32(rows + 8, 256), f32(8, 256)],
        compiler_params=params(8),
        cost_estimate=cost(near.size, near.size * 12),
        name="far_sums",
    )(near, far, beta, token)


def right_far_kernel(keep, peer, got, g2, g3):
    q = g2.shape[0]
    for k, g in ((2, g2), (3, g3)):
        rows = slice(k * q, (k + 1) * q)
        g[...] = (keep[rows, :] + peer[rows, :]) + got[(k - 2) * q : (k - 1) * q, :]


def right_far(keep, peer, got):
    q, rows = keep.shape[0] // 4, keep.shape[1]
    return pl.pallas_call(
        right_far_kernel,
        out_shape=[f32(q, rows)] * 2,
        compiler_params=params(8),
        cost_estimate=cost(rows * q * 4, rows * q * 32),
        name="right_far",
    )(keep, peer, got)


def right_norm_kernel(docs_total, keep, peer, got, beta_core, right, g2, g3, g0, g1, sums, columns):
    _, z, _ = coords()
    q = right.shape[1]
    beta_sums = beta_core[0:1, :] + got[2 * q : 2 * q + 1, :]
    columns[...] = row_to_column(jnp.sqrt(beta_sums / docs_total + epsilon))
    beta = columns[pl.ds(pl.multiple_of(z * q, q), q), :][:, 0:1]
    for k, g in enumerate((g0, g1)):
        rows = slice(k * q, (k + 1) * q)
        g[...] = (keep[rows, :] + peer[rows, :]) + got[rows, :]
    raws = [g[...] / beta - beta * right[k] for k, g in enumerate((g0, g1, g2, g3))]
    line = square_sums(jnp.concatenate(raws, axis=1))
    folded = beta_sums[:, :128] + beta_sums[:, 128:]
    folded = folded + jnp.concatenate([folded[:, q:], folded[:, :q]], axis=1)
    low = lax.broadcasted_iota(jnp.int32, line.shape, 1) < q
    sums[...] = jnp.broadcast_to(jnp.where(low, line, folded), sums.shape)


def right_norm(docs_total, keep, peer, got, beta_core, right, far):
    q, rows = keep.shape[0] // 4, keep.shape[1]
    g0, g1, sums = pl.pallas_call(
        functools.partial(right_norm_kernel, docs_total),
        out_shape=[f32(q, rows)] * 2 + [f32(32, 128)],
        scratch_shapes=[pltpu.VMEM((4 * q, 128), jnp.float32)],
        compiler_params=params(8),
        cost_estimate=cost(rows * q * 64, rows * q * 100, 64),
        name="right_norm",
    )(keep, peer, got, beta_core, right, *far)
    return g0, g1, sums.reshape(32, 1, 128)


def finish_kernel(docs_total, feat_total, g0, g1, g2, g3, squares, own, other, right, search, solution, phibar, rhobar,
                  left_hbm, right_hbm, search_hbm, solution_hbm, alpha_out, phibar_out, rhobar_out,
                  turned, left_out, right_out, search_out, solution_out, sent):
    _, z, y = coords()
    q, half = turned.shape[1:]
    parts = [squares[i] for i in range(32)]
    high = [jnp.concatenate([parts[8 * i][:, q:], parts[8 * i][:, :q]], axis=1) if i % 2 == 0 else parts[8 * i] for i in range(4)]
    while len(parts) > 4:
        parts = [a + b for a, b in zip(parts[::2], parts[1::2])]
    parts[1::2] = [jnp.concatenate([p[:, q:], p[:, :q]], axis=1) for p in parts[1::2]]
    low = lax.broadcasted_iota(jnp.int32, parts[0].shape, 1) < q
    alpha_sums, beta_sums = (
        jnp.concatenate([jnp.where(low, p[0], p[1]), jnp.where(low, p[2], p[3])], axis=1) for p in (parts, high)
    )
    alpha = jnp.sqrt(alpha_sums / feat_total + epsilon)
    beta = jnp.sqrt(beta_sums / docs_total + epsilon)
    copies = []

    def send(src, dst):
        copies.append(pltpu.make_async_copy(src, dst, sent.at[len(copies)]))
        copies[-1].start()

    rho = jnp.sqrt(rhobar[...] * rhobar[...] + beta * beta)
    cosine = rhobar[...] / rho
    sine = beta / rho
    theta = sine * alpha
    phi = cosine * phibar[...]
    rhobar_out[...] = -cosine * alpha
    phibar_out[...] = sine * phibar[...]
    alpha_out[...] = alpha
    solution_out[...] = solution[...] + (phi / rho) * search[...]
    send(solution_out, solution_hbm)
    for i, (part, ref) in enumerate(((y, own), (1 - y, other))):
        for k in range(4):
            turned[z ^ k] = ref[k]
        left_out[i] = turned[...].reshape(-1, half).T / beta
        send(left_out.at[i], left_hbm.at[pl.ds(pl.multiple_of(part * half, half), half), :])
    for k, g in enumerate((g0, g1, g2, g3)):
        turned[z ^ k] = g[...]
    got = turned[...].reshape(-1, half).T
    right_out[...] = (got / beta - beta * right[...]) / alpha
    send(right_out, right_hbm)
    search_out[...] = right_out[...] - (theta / rho) * search[...]
    send(search_out, search_hbm)
    for copy in copies:
        copy.wait()


def finish(docs_total, feat_total, pieces, squares, own, other, right, search, solution, phibar, rhobar):
    rows, cols = right.shape
    return pl.pallas_call(
        functools.partial(finish_kernel, docs_total, feat_total),
        in_specs=[whole()] * 12,
        out_specs=[pl.BlockSpec(memory_space=pltpu.HBM)] * 4 + [whole()] * 3,
        out_shape=[f32(2 * rows, cols)] + [f32(rows, cols)] * 3 + [f32(1, cols)] * 3,
        scratch_shapes=[
            pltpu.VMEM((4, cols // 4, rows), jnp.float32),
            pltpu.VMEM((2, rows, cols), jnp.float32),
            pltpu.VMEM((rows, cols), jnp.float32),
            pltpu.VMEM((rows, cols), jnp.float32),
            pltpu.VMEM((rows, cols), jnp.float32),
            pltpu.SemaphoreType.DMA((5,)),
        ],
        compiler_params=params(12),
        cost_estimate=cost(rows * cols * 16, rows * cols * 20),
        name="finish",
    )(*pieces, squares, own, other, right, search, solution, phibar, rhobar)


def swap(value, mask):
    return lax.ppermute(value, AXES, [(i, i ^ mask) for i in range(32)])


def along_z(values):
    got = {0: values[0]}
    for k in (2, 3, 1):
        got[k] = swap(values[k], k << Z_SHIFT)
    return [got[k] for k in range(4)]


def after(value, *earlier):
    return lax.optimization_barrier((value, *earlier))[0]


def by_columns(
    col_ids, col_vals, left_vec, right_vec, search_dir, solution_vec, alpha_prev, phibar, rhobar
):
    docs_total = left_vec.shape[0] * 16
    feat_total = right_vec.shape[0] * 32
    alpha_row, phibar_row, rhobar_row = (v.reshape(1, -1) for v in (alpha_prev, phibar, rhobar))

    stored, messages = prepare(col_ids.T, col_vals.T, right_vec, left_vec)
    entries = along_z([stored] * 4)
    messages = along_z([messages[0]] + [after(messages[1], entries[2]), messages[2], messages[3]])
    q = right_vec.shape[1] // 4

    rows1, token1 = build(entries, 1)
    own = stack(messages, q, "stack_right", token1)
    own_x = swap(own, X_BIT)
    own_peer = swap(own, CORE_BIT)
    rows0, token0 = build(entries, 0, own)
    total1 = forward_part(rows1, [own, own_peer], (0, 8), None, [token0])
    x_peer = swap(after(own_x, total1), CORE_BIT)
    total1 = forward_part(rows1, [own_x], (4,), total1)
    product1 = product_half(rows1, x_peer, total1, (12,))
    total0 = forward_part(rows0, [own, own_peer], (0, 8))
    total0 = forward_part(rows0, [own_x], (4,), total0)
    product0 = product_half(rows0, x_peer, total0, (12,), *messages, alpha_row)

    *lefts, both0, beta0 = left_half(product0, swap(product1, Y_BIT))
    partial = backward_part(rows0, both0, 0, 16)
    left_own = stack(along_z(lefts), q, "stack_left")
    both1, beta1 = left_half(product1, swap(product0, Y_BIT), beta0, partial)
    far = swap(backward_part(rows1, both1, 12, 4, partial, beta1), CORE_BIT)
    near = backward_part(rows1, both1, 4, 4, partial, None, [], 0.05)
    peer = backward_part(rows1, both1, 8, 4, partial, None, [near], 0.05)
    send_far, send_near, beta_core = far_sums(near, far, beta1, peer)
    got_far = swap(send_far, X_BIT)
    got_near = swap(send_near, X_BIT)
    keep = backward_part(rows1, both1, 0, 4, partial, None, [], 0.05)
    peer = swap(peer, CORE_BIT)

    g2, g3 = right_far(keep, peer, got_far)
    p2, p3 = swap(g2, 2 << Z_SHIFT), swap(g3, 3 << Z_SHIFT)
    g0, g1, sums = right_norm(docs_total, keep, peer, got_near, beta_core, own, (g2, g3))
    pieces = [g0, swap(g1, 1 << Z_SHIFT), p2, p3]
    left_other = swap(after(left_own, send_far), Y_BIT)
    squares = lax.all_to_all(after(sums, left_own), AXES, 0, 0, tiled=True)
    left_next, right_next, search_next, solution_next, alpha_next, phibar_next, rhobar_next = finish(
        docs_total, feat_total, pieces, squares, left_own, left_other,
        right_vec, search_dir, solution_vec, phibar_row, rhobar_row,
    )
    return (
        left_next,
        right_next,
        search_next,
        solution_next,
        alpha_next.reshape(-1),
        phibar_next.reshape(-1),
        rhobar_next.reshape(-1),
    )


def forward(col_ids, col_vals, table):
    picked = table[col_ids]
    return jnp.sum(col_vals.astype(jnp.float32)[:, :, None] * picked, axis=1)


def backward(col_ids, col_vals, rows_in, width):
    terms = col_vals.astype(jnp.float32)[:, :, None] * rows_in[:, None, :]
    return jax.ops.segment_sum(
        terms.reshape(-1, rows_in.shape[1]), col_ids.reshape(-1), num_segments=width
    )


def by_blocks(
    col_ids, col_vals, left_vec, right_vec, search_dir, solution_vec, alpha_prev, phibar, rhobar
):
    n_feat = lax.axis_size("feat")
    n_doc = lax.axis_size("doc")
    docs_total = left_vec.shape[0] * n_doc
    feat_total = right_vec.shape[0] * n_doc * n_feat
    table = lax.all_gather(right_vec, "doc", axis=0, tiled=True)
    total = lax.psum(forward(col_ids, col_vals, table), "feat")
    left_raw = total - alpha_prev[None, :] * left_vec
    row_part = jnp.sum(left_raw * left_raw, axis=0)
    beta_norm = jnp.sqrt(lax.psum(row_part, "doc") / docs_total + epsilon)
    left_next = left_raw / beta_norm[None, :]
    feature_part = lax.psum_scatter(
        backward(col_ids, col_vals, left_next, table.shape[0]), "doc", scatter_dimension=0, tiled=True
    )
    right_raw = feature_part - beta_norm[None, :] * right_vec
    squares = lax.psum(jnp.sum(right_raw * right_raw, axis=0), AXES)
    alpha_next = jnp.sqrt(squares / feat_total + epsilon)
    right_next = right_raw / alpha_next[None, :]
    rho_val = jnp.sqrt(rhobar * rhobar + beta_norm * beta_norm)
    cosine = rhobar / rho_val
    sine_val = beta_norm / rho_val
    theta_val = sine_val * alpha_next
    phi_val = cosine * phibar
    solution_next = solution_vec + (phi_val / rho_val)[None, :] * search_dir
    search_next = right_next - (theta_val / rho_val)[None, :] * search_dir
    return (
        left_next,
        right_next,
        search_next,
        solution_next,
        alpha_next,
        sine_val * phibar,
        -cosine * alpha_next,
    )


def solution(mesh):
    small = mesh.shape["doc"] == 16 and mesh.shape["feat"] == 2
    rows = P(("feat", "doc"), None)
    return jax.shard_map(
        by_columns if small else by_blocks,
        mesh=mesh,
        in_specs=(P("doc", "feat"), P("doc", "feat"), P("doc", None), rows, rows, rows, P(), P(), P()),
        out_specs=(P("doc", None), rows, rows, rows, P(), P(), P()),
        check_vma=False,
    )
```

```python
import functools

import jax
import jax.numpy as jnp
from jax import lax
from jax.experimental import pallas as pl
from jax.experimental.pallas import tpu as pltpu
from jax.sharding import PartitionSpec as P

epsilon = 1e-06
AXES = ("doc", "feat")
MIB = 1024 * 1024


Y_BIT, CORE_BIT, X_BIT, Z_SHIFT = 1, 2, 4, 3
NT = (((1,), (1,)), ((), ()))


def coords():
    d = lax.axis_index("doc")
    y = lax.axis_index("feat")
    return d, d >> 2, y


def params(mib):
    return pltpu.CompilerParams(vmem_limit_bytes=mib * MIB)


def cost(flops, nbytes, scale=64):
    return pl.CostEstimate(flops=int(flops / scale), bytes_accessed=int(nbytes / scale), transcendentals=0)


def f32(*shape):
    return jax.ShapeDtypeStruct(shape, jnp.float32)


def bf16(*shape):
    return jax.ShapeDtypeStruct(shape, jnp.bfloat16)


def prepare_kernel(ids_hbm, vals_hbm, right_hbm, left_hbm, stored, m0, m1, m2, m3,
                   ids, vals, wide, right, left, turned, arrived):
    _, z, y = coords()
    q, rows = turned.shape[1:]
    copies = [
        pltpu.make_async_copy(src, dst, arrived.at[i])
        for i, (src, dst) in enumerate((
            (ids_hbm, ids),
            (vals_hbm, vals),
            (right_hbm, right),
            (left_hbm.at[pl.ds(pl.multiple_of(y * rows, rows), rows), :], left),
        ))
    ]
    for copy in copies:
        copy.start()
    lines, count = stored.shape[0] // 2, ids.shape[0]
    for part, ref in enumerate((ids, vals)):
        copies[part].wait()
        wide[...] = ref[...].astype(jnp.float32).T
        for r in range(256 // count):
            stored[part * lines : (part + 1) * lines, r * count : (r + 1) * count] = wide[
                pl.ds(r, lines, stride=256 // count), :
            ]
    for part, ref in enumerate((right, left)):
        copies[2 + part].wait()
        turned[...] = ref[...].T.reshape(turned.shape)
        for k, out in enumerate((m0, m1, m2, m3)):
            out[part * q : (part + 1) * q, :] = turned[z ^ k]


def prepare(ids, vals, right, left):
    rows, cols = right.shape
    q = cols // 4
    got = pl.pallas_call(
        prepare_kernel,
        in_specs=[pl.BlockSpec(memory_space=pltpu.HBM)] * 4,
        out_specs=[whole()] * 5,
        out_shape=[pltpu.VMEM((ids.size // 128, 256), jnp.float32)] + [pltpu.VMEM((2 * q, rows), jnp.float32)] * 4,
        scratch_shapes=[
            pltpu.VMEM(ids.shape, jnp.int32),
            pltpu.VMEM(vals.shape, jnp.bfloat16),
            pltpu.VMEM(ids.shape[::-1], jnp.float32),
            pltpu.VMEM(right.shape, jnp.float32),
            pltpu.VMEM(right.shape, jnp.float32),
            pltpu.VMEM((4, q, rows), jnp.float32),
            pltpu.SemaphoreType.DMA((4,)),
        ],
        compiler_params=params(60),
        cost_estimate=cost(0, rows * cols * 16),
        name="prepare",
    )(ids, vals, right, left)
    return got[0], got[1:]


def stack_kernel(m0, m1, m2, m3, *refs):
    out = refs[-1]
    for k, m in enumerate((m0, m1, m2, m3)):
        out[k] = m[0 : out.shape[1], :]


def stack(messages, q, name, *tokens):
    rows = messages[0].shape[1]
    return pl.pallas_call(
        stack_kernel,
        out_shape=f32(4, q, rows),
        compiler_params=params(8),
        cost_estimate=cost(0, 32 * q * rows),
        name=name,
    )(*messages, *tokens)


def build_kernel(rel, e0, e1, e2, e3, *refs):
    hi_ref, lo_ref, token = refs[-3:]
    token[...] = jnp.zeros_like(token)
    d, _, y = coords()
    n = e0.shape[0] // 2
    iota = lax.broadcasted_iota(jnp.int32, (256, 256), 0).astype(jnp.float32).astype(jnp.bfloat16)
    lane_doc = lax.broadcasted_iota(jnp.int32, (8, 256), 1) >> 4
    one = jnp.ones((256, 256), jnp.bfloat16)
    zero = jnp.zeros((256, 256), jnp.bfloat16)

    def spread(row):
        wide = jnp.broadcast_to(row, (16, 256)).astype(jnp.bfloat16)
        return jnp.broadcast_to(wide[None], (16, 16, 256)).reshape(256, 256)

    for k, entries in enumerate((e0, e1, e2, e3)):

        @pl.loop(0, n // 16)
        def _(step, k=k, entries=entries):
            at = pl.multiple_of((y ^ rel) * (n // 2) + step * 8, 8)
            ids = entries[pl.ds(at, 8), :].astype(jnp.int32)
            vals = entries[pl.ds(n + at, 8), :]
            owner = (ids >> 8) ^ d
            block = ((owner & 1) << 3) | ((owner & 2) << 1) | (owner >> 2)
            code = (block * 16 + lane_doc).astype(jnp.float32)
            inner = (ids & 255).astype(jnp.float32)
            for t in range(8):
                pick = jnp.where(iota == spread(code[t : t + 1]), one, zero)
                weigh = jnp.where(iota == spread(inner[t : t + 1]), spread(vals[t : t + 1]), zero)
                dense = lax.dot_general(pick, weigh, NT, preferred_element_type=jnp.float32)
                high = dense.astype(jnp.bfloat16)
                low = (dense - high.astype(jnp.float32)).astype(jnp.bfloat16)
                docs = pl.ds(pl.multiple_of(k * 8 * n + step * 128 + 16 * t, 16), 16)
                hi_ref[:, docs, :] = high.reshape(16, 16, 256)
                lo_ref[:, docs, :] = low.reshape(16, 16, 256)


def whole():
    return pl.BlockSpec(memory_space=pltpu.VMEM)


def build(entries, rel, *tokens):
    docs = 4 * (entries[0].shape[0] // 4 * 16)
    *rows, token = pl.pallas_call(
        functools.partial(build_kernel, rel),
        in_specs=[whole()] * (4 + len(tokens)),
        out_specs=[whole()] * 3,
        out_shape=[pltpu.VMEM((16, docs, 256), jnp.bfloat16)] * 2 + [f32(8, 128)],
        compiler_params=params(8),
        cost_estimate=cost(2 * docs * 16 * 256 * 256, docs * 4096 * 4, 1 if rel else 64),
        name="dense_rows",
    )(*entries, *tokens)
    return rows, token


def split_rows(value):
    high = value.astype(jnp.bfloat16)
    low = (value - high.astype(jnp.float32)).astype(jnp.bfloat16)
    return jnp.concatenate([high, low], axis=0)


def add_products(hi_ref, lo_ref, vecs, blocks, total):
    for vec, first in zip(vecs, blocks):
        for pair in (0, 2):
            lhs, rhs = [], []
            for k in (pair, pair + 1):
                both = split_rows(vec[k])
                lhs += [hi_ref[first + k], lo_ref[first + k]]
                rhs += [both, both]
            total[...] += lax.dot_general(
                jnp.concatenate(lhs, axis=1), jnp.concatenate(rhs, axis=1), NT, preferred_element_type=jnp.float32
            )


def forward_kernel(blocks, has_before, hi_ref, lo_ref, *refs):
    count = len(blocks)
    total = refs[-1]
    total[...] = refs[count][...] if has_before else jnp.zeros_like(total)
    add_products(hi_ref, lo_ref, refs[:count], blocks, total)


def forward_part(rows, vecs, blocks, before=None, tokens=()):
    docs, q = rows[0].shape[1], vecs[0].shape[1]
    n = 4 * len(blocks)
    extra = [*tokens] if before is None else [before, *tokens]
    return pl.pallas_call(
        functools.partial(forward_kernel, blocks, before is not None),
        in_specs=[whole()] * (2 + len(vecs) + len(extra)),
        out_specs=whole(),
        out_shape=f32(docs, 2 * q),
        compiler_params=params(8),
        cost_estimate=cost(8 * docs * 256 * 256 * n, 4 * docs * 256 * n),
        name="forward_part",
    )(*rows, *vecs, *extra)


def product_kernel(blocks, hi_ref, lo_ref, vec, before, *refs):
    out, total, columns = refs[-3:]
    total[...] = before[...]
    add_products(hi_ref, lo_ref, (vec,), blocks, total)
    turned = total[...].T
    q = out.shape[0]
    product = turned[:q] + turned[q:]
    if len(refs) == 3:
        out[...] = product
        return
    _, z, _ = coords()
    *messages, alpha = refs[:5]
    columns[...] = row_to_column(alpha[...])
    scale = columns[pl.ds(pl.multiple_of(z * q, q), q), :][:, 0:1]
    for k, m in enumerate(messages):
        at = slice(k * m.shape[1], (k + 1) * m.shape[1])
        out[:, at] = product[:, at] - scale * m[q:, :]


def product_half(rows, vec, before, blocks, *left):
    docs, q = rows[0].shape[1], vec.shape[1]
    return pl.pallas_call(
        functools.partial(product_kernel, blocks),
        in_specs=[whole()] * (4 + len(left)),
        out_specs=whole(),
        out_shape=f32(q, docs),
        scratch_shapes=[pltpu.VMEM((docs, 2 * q), jnp.float32), pltpu.VMEM((4 * q, 128), jnp.float32)],
        compiler_params=params(8),
        cost_estimate=cost(8 * docs * 256 * 256 * 4, 16 * docs * 256),
        name="product_half",
    )(*rows, vec, before, *left)


def square_sums(value):
    q, n = value.shape
    sums = value[:, 0:128] * value[:, 0:128]
    for at in range(128, n, 128):
        sums = sums + value[:, at : at + 128] * value[:, at : at + 128]
    return jnp.sum(jnp.concatenate([sums] * (128 // q), axis=0).T, axis=0, keepdims=True)


def square_row(value, z, cols):
    row = square_sums(value)
    row = jnp.broadcast_to(jnp.concatenate([row] * (cols // 128), axis=1), (8, cols))
    lane = lax.broadcasted_iota(jnp.int32, (8, cols), 1)
    return jnp.where(lane // value.shape[0] == z, row, 0.0)


def row_to_column(row):
    return jnp.broadcast_to(row, (128, row.shape[1])).T


def left_half_kernel(mine, other, *refs):
    _, z, _ = coords()
    left = mine[...] + other[...]
    both, sums = refs[-2:]
    both[...] = split_rows(left)
    squares = square_row(left, z, sums.shape[1])
    sums[...] = refs[0][...] + squares if len(refs) == 4 else squares
    if len(refs) > 4:
        n = left.shape[1] // 4
        for k, out in enumerate(refs[:4]):
            out[...] = left[:, k * n : (k + 1) * n]


def left_half(mine, other, squares=None, token=None):
    q, docs = mine.shape
    extra = [] if squares is None else [squares, token]
    pieces = [f32(q, docs // 4)] * 4 if squares is None else []
    return pl.pallas_call(
        left_half_kernel,
        out_shape=pieces + [bf16(2 * q, docs), f32(8, 4 * q)],
        compiler_params=params(8),
        cost_estimate=cost(8 * q * docs, 16 * q * docs),
        name="left_half",
    )(mine, other, *extra)


def backward_kernel(first, blocks, parts, hi_ref, lo_ref, both_ref, *refs):
    out_ref = refs[-1]
    both = both_ref[...]
    q = both.shape[0] // 2
    twice = jnp.concatenate([both, both], axis=1)
    for b in range(blocks):
        got = jnp.dot(
            twice,
            jnp.concatenate([hi_ref[first + b], lo_ref[first + b]], axis=0),
            preferred_element_type=jnp.float32,
        )
        got = got[:q] + got[q:]
        if "before" in parts:
            got = got + refs[0][(first + b) * q : (first + b + 1) * q, :]
        out_ref[b * q : (b + 1) * q, :] = got
    if "tail" in parts:
        out_ref[blocks * q :, :] = refs[parts.index("tail")][...]


def backward_part(rows, both, first, blocks, before=None, tail=None, tokens=(), scale=64):
    q, docs = both.shape[0] // 2, both.shape[1]
    extra = {"before": before, "tail": tail, **{str(i): token for i, token in enumerate(tokens)}}
    extra = {name: value for name, value in extra.items() if value is not None}
    height = blocks * q + (0 if tail is None else tail.shape[0])
    return pl.pallas_call(
        functools.partial(backward_kernel, first, blocks, tuple(extra)),
        in_specs=[whole()] * (3 + len(extra)),
        out_specs=whole(),
        out_shape=f32(height, 256),
        compiler_params=params(8),
        cost_estimate=cost(8 * docs * 256 * 256 * blocks, 4 * docs * 256 * blocks, scale),
        name="backward_part",
    )(*rows, both, *extra.values())


def far_sum_kernel(near, far, beta, token, send_far, send_near, beta_core):
    n = near.shape[0] // 2
    beta_core[...] = beta[...] + far[2 * n :, :]
    send_far[...] = near[n:, :] + far[n : 2 * n, :]
    send_near[0:n, :] = near[0:n, :] + far[0:n, :]
    send_near[n:, :] = beta_core[...]


def far_sums(near, far, beta, token):
    rows = near.shape[0] // 2
    return pl.pallas_call(
        far_sum_kernel,
        out_shape=[f32(rows, 256), f32(rows + 8, 256), f32(8, 256)],
        compiler_params=params(8),
        cost_estimate=cost(near.size, near.size * 12),
        name="far_sums",
    )(near, far, beta, token)


def right_far_kernel(keep, peer, got, g2, g3):
    q = g2.shape[0]
    for k, g in ((2, g2), (3, g3)):
        rows = slice(k * q, (k + 1) * q)
        g[...] = (keep[rows, :] + peer[rows, :]) + got[(k - 2) * q : (k - 1) * q, :]


def right_far(keep, peer, got):
    q, rows = keep.shape[0] // 4, keep.shape[1]
    return pl.pallas_call(
        right_far_kernel,
        out_shape=[f32(q, rows)] * 2,
        compiler_params=params(8),
        cost_estimate=cost(rows * q * 4, rows * q * 32),
        name="right_far",
    )(keep, peer, got)


def right_norm_kernel(docs_total, keep, peer, got, beta_core, right, g2, g3, g0, g1, sums, columns):
    _, z, _ = coords()
    q = right.shape[1]
    beta_sums = beta_core[0:1, :] + got[2 * q : 2 * q + 1, :]
    columns[...] = row_to_column(jnp.sqrt(beta_sums / docs_total + epsilon))
    beta = columns[pl.ds(pl.multiple_of(z * q, q), q), :][:, 0:1]
    for k, g in enumerate((g0, g1)):
        rows = slice(k * q, (k + 1) * q)
        g[...] = (keep[rows, :] + peer[rows, :]) + got[rows, :]
    raws = [g[...] / beta - beta * right[k] for k, g in enumerate((g0, g1, g2, g3))]
    line = square_sums(jnp.concatenate(raws, axis=1))
    folded = beta_sums[:, :128] + beta_sums[:, 128:]
    folded = folded + jnp.concatenate([folded[:, q:], folded[:, :q]], axis=1)
    low = lax.broadcasted_iota(jnp.int32, line.shape, 1) < q
    sums[...] = jnp.broadcast_to(jnp.where(low, line, folded), sums.shape)


def right_norm(docs_total, keep, peer, got, beta_core, right, far):
    q, rows = keep.shape[0] // 4, keep.shape[1]
    g0, g1, sums = pl.pallas_call(
        functools.partial(right_norm_kernel, docs_total),
        out_shape=[f32(q, rows)] * 2 + [f32(32, 128)],
        scratch_shapes=[pltpu.VMEM((4 * q, 128), jnp.float32)],
        compiler_params=params(8),
        cost_estimate=cost(rows * q * 64, rows * q * 100, 64),
        name="right_norm",
    )(keep, peer, got, beta_core, right, *far)
    return g0, g1, sums.reshape(32, 1, 128)


def finish_kernel(docs_total, feat_total, g0, g1, g2, g3, squares, own, other, right, search, solution, phibar, rhobar,
                  left_out, right_out, search_out, solution_out, alpha_out, phibar_out, rhobar_out, turned):
    _, z, y = coords()
    q, half = turned.shape[1:]
    parts = [squares[i] for i in range(32)]
    high = [jnp.concatenate([parts[8 * i][:, q:], parts[8 * i][:, :q]], axis=1) if i % 2 == 0 else parts[8 * i] for i in range(4)]
    while len(parts) > 4:
        parts = [a + b for a, b in zip(parts[::2], parts[1::2])]
    parts[1::2] = [jnp.concatenate([p[:, q:], p[:, :q]], axis=1) for p in parts[1::2]]
    low = lax.broadcasted_iota(jnp.int32, parts[0].shape, 1) < q
    alpha_sums, beta_sums = (
        jnp.concatenate([jnp.where(low, p[0], p[1]), jnp.where(low, p[2], p[3])], axis=1) for p in (parts, high)
    )
    alpha = jnp.sqrt(alpha_sums / feat_total + epsilon)
    beta = jnp.sqrt(beta_sums / docs_total + epsilon)
    for part, ref in ((y, own), (1 - y, other)):
        for k in range(4):
            turned[z ^ k] = ref[k]
        left_out[pl.ds(pl.multiple_of(part * half, half), half), :] = turned[...].reshape(-1, half).T / beta
    rho = jnp.sqrt(rhobar[...] * rhobar[...] + beta * beta)
    cosine = rhobar[...] / rho
    sine = beta / rho
    theta = sine * alpha
    phi = cosine * phibar[...]
    rhobar_out[...] = -cosine * alpha
    phibar_out[...] = sine * phibar[...]
    alpha_out[...] = alpha
    for k, g in enumerate((g0, g1, g2, g3)):
        turned[z ^ k] = g[...]
    got = turned[...].reshape(-1, half).T
    following = (got / beta - beta * right[...]) / alpha
    right_out[...] = following
    search_out[...] = following - (theta / rho) * search[...]
    solution_out[...] = solution[...] + (phi / rho) * search[...]


def finish(docs_total, feat_total, pieces, squares, own, other, right, search, solution, phibar, rhobar):
    rows, cols = right.shape
    return pl.pallas_call(
        functools.partial(finish_kernel, docs_total, feat_total),
        out_shape=[f32(2 * rows, cols)] + [f32(rows, cols)] * 3 + [f32(1, cols)] * 3,
        scratch_shapes=[pltpu.VMEM((4, cols // 4, rows), jnp.float32)],
        compiler_params=params(12),
        cost_estimate=cost(rows * cols * 16, rows * cols * 20),
        name="finish",
    )(*pieces, squares, own, other, right, search, solution, phibar, rhobar)


def swap(value, mask):
    return lax.ppermute(value, AXES, [(i, i ^ mask) for i in range(32)])


def along_z(values):
    got = {0: values[0]}
    for k in (2, 3, 1):
        got[k] = swap(values[k], k << Z_SHIFT)
    return [got[k] for k in range(4)]


def after(value, *earlier):
    return lax.optimization_barrier((value, *earlier))[0]


def by_columns(
    col_ids, col_vals, left_vec, right_vec, search_dir, solution_vec, alpha_prev, phibar, rhobar
):
    docs_total = left_vec.shape[0] * 16
    feat_total = right_vec.shape[0] * 32
    alpha_row, phibar_row, rhobar_row = (v.reshape(1, -1) for v in (alpha_prev, phibar, rhobar))

    stored, messages = prepare(col_ids.T, col_vals.T, right_vec, left_vec)
    entries = along_z([stored] * 4)
    messages = along_z([messages[0]] + [after(messages[1], entries[1]), messages[2], messages[3]])
    q = right_vec.shape[1] // 4

    rows1, token1 = build(entries, 1)
    own = stack(messages, q, "stack_right", token1)
    own_x = swap(own, X_BIT)
    own_peer = swap(own, CORE_BIT)
    rows0, token0 = build(entries, 0, own)
    total1 = forward_part(rows1, [own, own_peer], (0, 8), None, [token0])
    x_peer = swap(after(own_x, total1), CORE_BIT)
    total1 = forward_part(rows1, [own_x], (4,), total1)
    product1 = product_half(rows1, x_peer, total1, (12,))
    total0 = forward_part(rows0, [own, own_peer], (0, 8))
    total0 = forward_part(rows0, [own_x], (4,), total0)
    product0 = product_half(rows0, x_peer, total0, (12,), *messages, alpha_row)

    *lefts, both0, beta0 = left_half(product0, swap(product1, Y_BIT))
    partial = backward_part(rows0, both0, 0, 16)
    left_own = stack(along_z(lefts), q, "stack_left")
    both1, beta1 = left_half(product1, swap(product0, Y_BIT), beta0, partial)
    far = swap(backward_part(rows1, both1, 12, 4, partial, beta1), CORE_BIT)
    near = backward_part(rows1, both1, 4, 4, partial, None, [], 0.05)
    peer = backward_part(rows1, both1, 8, 4, partial, None, [near], 0.05)
    send_far, send_near, beta_core = far_sums(near, far, beta1, peer)
    got_far = swap(send_far, X_BIT)
    got_near = swap(send_near, X_BIT)
    keep = backward_part(rows1, both1, 0, 4, partial, None, [], 0.05)
    peer = swap(peer, CORE_BIT)

    g2, g3 = right_far(keep, peer, got_far)
    p2, p3 = swap(g2, 2 << Z_SHIFT), swap(g3, 3 << Z_SHIFT)
    g0, g1, sums = right_norm(docs_total, keep, peer, got_near, beta_core, own, (g2, g3))
    pieces = [g0, swap(g1, 1 << Z_SHIFT), p2, p3]
    left_other = swap(after(left_own, send_far), Y_BIT)
    squares = lax.all_to_all(after(sums, left_own), AXES, 0, 0, tiled=True)
    left_next, right_next, search_next, solution_next, alpha_next, phibar_next, rhobar_next = finish(
        docs_total, feat_total, pieces, squares, left_own, left_other,
        right_vec, search_dir, solution_vec, phibar_row, rhobar_row,
    )
    return (
        left_next,
        right_next,
        search_next,
        solution_next,
        alpha_next.reshape(-1),
        phibar_next.reshape(-1),
        rhobar_next.reshape(-1),
    )


def forward(col_ids, col_vals, table):
    picked = table[col_ids]
    return jnp.sum(col_vals.astype(jnp.float32)[:, :, None] * picked, axis=1)


def backward(col_ids, col_vals, rows_in, width):
    terms = col_vals.astype(jnp.float32)[:, :, None] * rows_in[:, None, :]
    return jax.ops.segment_sum(
        terms.reshape(-1, rows_in.shape[1]), col_ids.reshape(-1), num_segments=width
    )


def by_blocks(
    col_ids, col_vals, left_vec, right_vec, search_dir, solution_vec, alpha_prev, phibar, rhobar
):
    n_feat = lax.axis_size("feat")
    n_doc = lax.axis_size("doc")
    docs_total = left_vec.shape[0] * n_doc
    feat_total = right_vec.shape[0] * n_doc * n_feat
    table = lax.all_gather(right_vec, "doc", axis=0, tiled=True)
    total = lax.psum(forward(col_ids, col_vals, table), "feat")
    left_raw = total - alpha_prev[None, :] * left_vec
    row_part = jnp.sum(left_raw * left_raw, axis=0)
    beta_norm = jnp.sqrt(lax.psum(row_part, "doc") / docs_total + epsilon)
    left_next = left_raw / beta_norm[None, :]
    feature_part = lax.psum_scatter(
        backward(col_ids, col_vals, left_next, table.shape[0]), "doc", scatter_dimension=0, tiled=True
    )
    right_raw = feature_part - beta_norm[None, :] * right_vec
    squares = lax.psum(jnp.sum(right_raw * right_raw, axis=0), AXES)
    alpha_next = jnp.sqrt(squares / feat_total + epsilon)
    right_next = right_raw / alpha_next[None, :]
    rho_val = jnp.sqrt(rhobar * rhobar + beta_norm * beta_norm)
    cosine = rhobar / rho_val
    sine_val = beta_norm / rho_val
    theta_val = sine_val * alpha_next
    phi_val = cosine * phibar
    solution_next = solution_vec + (phi_val / rho_val)[None, :] * search_dir
    search_next = right_next - (theta_val / rho_val)[None, :] * search_dir
    return (
        left_next,
        right_next,
        search_next,
        solution_next,
        alpha_next,
        sine_val * phibar,
        -cosine * alpha_next,
    )


def solution(mesh):
    small = mesh.shape["doc"] == 16 and mesh.shape["feat"] == 2
    rows = P(("feat", "doc"), None)
    return jax.shard_map(
        by_columns if small else by_blocks,
        mesh=mesh,
        in_specs=(P("doc", "feat"), P("doc", "feat"), P("doc", None), rows, rows, rows, P(), P(), P()),
        out_specs=(P("doc", None), rows, rows, rows, P(), P(), P()),
        check_vma=False,
    )
```

```python
import functools

import jax
import jax.numpy as jnp
from jax import lax
from jax.experimental import pallas as pl
from jax.experimental.pallas import tpu as pltpu
from jax.sharding import PartitionSpec as P

epsilon = 1e-06
AXES = ("doc", "feat")
MIB = 1024 * 1024


Y_BIT, CORE_BIT, X_BIT, Z_SHIFT = 1, 2, 4, 3
NT = (((1,), (1,)), ((), ()))


def coords():
    d = lax.axis_index("doc")
    y = lax.axis_index("feat")
    return d, d >> 2, y


def params(mib):
    return pltpu.CompilerParams(vmem_limit_bytes=mib * MIB)


def cost(flops, nbytes, scale=64):
    return pl.CostEstimate(flops=int(flops / scale), bytes_accessed=int(nbytes / scale), transcendentals=0)


def f32(*shape):
    return jax.ShapeDtypeStruct(shape, jnp.float32)


def bf16(*shape):
    return jax.ShapeDtypeStruct(shape, jnp.bfloat16)


def prepare_kernel(ids_hbm, vals_hbm, right_hbm, left_hbm, stored, m0, m1, m2, m3,
                   ids, vals, wide, right, left, turned, arrived):
    _, z, y = coords()
    q, rows = turned.shape[1:]
    copies = [
        pltpu.make_async_copy(src, dst, arrived.at[i])
        for i, (src, dst) in enumerate((
            (ids_hbm, ids),
            (vals_hbm, vals),
            (right_hbm, right),
            (left_hbm.at[pl.ds(pl.multiple_of(y * rows, rows), rows), :], left),
        ))
    ]
    for copy in copies:
        copy.start()
    lines, count = stored.shape[0] // 2, ids.shape[0]
    for part, ref in enumerate((ids, vals)):
        copies[part].wait()
        wide[...] = ref[...].astype(jnp.float32).T
        for r in range(256 // count):
            stored[part * lines : (part + 1) * lines, r * count : (r + 1) * count] = wide[
                pl.ds(r, lines, stride=256 // count), :
            ]
    for part, ref in enumerate((right, left)):
        copies[2 + part].wait()
        turned[...] = ref[...].T.reshape(turned.shape)
        for k, out in enumerate((m0, m1, m2, m3)):
            out[part * q : (part + 1) * q, :] = turned[z ^ k]


def prepare(ids, vals, right, left):
    rows, cols = right.shape
    q = cols // 4
    got = pl.pallas_call(
        prepare_kernel,
        in_specs=[pl.BlockSpec(memory_space=pltpu.HBM)] * 4,
        out_specs=[whole()] * 5,
        out_shape=[pltpu.VMEM((ids.size // 128, 256), jnp.float32)] + [pltpu.VMEM((2 * q, rows), jnp.float32)] * 4,
        scratch_shapes=[
            pltpu.VMEM(ids.shape, jnp.int32),
            pltpu.VMEM(vals.shape, jnp.bfloat16),
            pltpu.VMEM(ids.shape[::-1], jnp.float32),
            pltpu.VMEM(right.shape, jnp.float32),
            pltpu.VMEM(right.shape, jnp.float32),
            pltpu.VMEM((4, q, rows), jnp.float32),
            pltpu.SemaphoreType.DMA((4,)),
        ],
        compiler_params=params(60),
        cost_estimate=cost(0, rows * cols * 16),
        name="prepare",
    )(ids, vals, right, left)
    return got[0], got[1:]


def stack_kernel(m0, m1, m2, m3, *refs):
    out = refs[-1]
    for k, m in enumerate((m0, m1, m2, m3)):
        out[k] = m[0 : out.shape[1], :]


def stack(messages, q, name, *tokens):
    rows = messages[0].shape[1]
    return pl.pallas_call(
        stack_kernel,
        out_shape=f32(4, q, rows),
        compiler_params=params(8),
        cost_estimate=cost(0, 32 * q * rows),
        name=name,
    )(*messages, *tokens)


def build_kernel(rel, e0, e1, e2, e3, *refs):
    hi_ref, lo_ref, token = refs[-3:]
    token[...] = jnp.zeros_like(token)
    d, _, y = coords()
    n = e0.shape[0] // 2
    iota = lax.broadcasted_iota(jnp.int32, (256, 256), 0).astype(jnp.float32).astype(jnp.bfloat16)
    lane_doc = lax.broadcasted_iota(jnp.int32, (8, 256), 1) >> 4
    one = jnp.ones((256, 256), jnp.bfloat16)
    zero = jnp.zeros((256, 256), jnp.bfloat16)

    def spread(row):
        wide = jnp.broadcast_to(row, (16, 256)).astype(jnp.bfloat16)
        return jnp.broadcast_to(wide[None], (16, 16, 256)).reshape(256, 256)

    for k, entries in enumerate((e0, e1, e2, e3)):

        @pl.loop(0, n // 16)
        def _(step, k=k, entries=entries):
            at = pl.multiple_of((y ^ rel) * (n // 2) + step * 8, 8)
            ids = entries[pl.ds(at, 8), :].astype(jnp.int32)
            vals = entries[pl.ds(n + at, 8), :]
            owner = (ids >> 8) ^ d
            block = ((owner & 1) << 3) | ((owner & 2) << 1) | (owner >> 2)
            code = (block * 16 + lane_doc).astype(jnp.float32)
            inner = (ids & 255).astype(jnp.float32)
            for t in range(8):
                pick = jnp.where(iota == spread(code[t : t + 1]), one, zero)
                weigh = jnp.where(iota == spread(inner[t : t + 1]), spread(vals[t : t + 1]), zero)
                dense = lax.dot_general(pick, weigh, NT, preferred_element_type=jnp.float32)
                high = dense.astype(jnp.bfloat16)
                low = (dense - high.astype(jnp.float32)).astype(jnp.bfloat16)
                docs = pl.ds(pl.multiple_of(k * 8 * n + step * 128 + 16 * t, 16), 16)
                hi_ref[:, docs, :] = high.reshape(16, 16, 256)
                lo_ref[:, docs, :] = low.reshape(16, 16, 256)


def whole():
    return pl.BlockSpec(memory_space=pltpu.VMEM)


def build(entries, rel, *tokens):
    docs = 4 * (entries[0].shape[0] // 4 * 16)
    *rows, token = pl.pallas_call(
        functools.partial(build_kernel, rel),
        in_specs=[whole()] * (4 + len(tokens)),
        out_specs=[whole()] * 3,
        out_shape=[pltpu.VMEM((16, docs, 256), jnp.bfloat16)] * 2 + [f32(8, 128)],
        compiler_params=params(8),
        cost_estimate=cost(2 * docs * 16 * 256 * 256, docs * 4096 * 4, 1 if rel else 64),
        name="dense_rows",
    )(*entries, *tokens)
    return rows, token


def split_rows(value):
    high = value.astype(jnp.bfloat16)
    low = (value - high.astype(jnp.float32)).astype(jnp.bfloat16)
    return jnp.concatenate([high, low], axis=0)


def add_products(hi_ref, lo_ref, vecs, blocks, total):
    for vec, first in zip(vecs, blocks):
        for pair in (0, 2):
            lhs, rhs = [], []
            for k in (pair, pair + 1):
                both = split_rows(vec[k])
                lhs += [hi_ref[first + k], lo_ref[first + k]]
                rhs += [both, both]
            total[...] += lax.dot_general(
                jnp.concatenate(lhs, axis=1), jnp.concatenate(rhs, axis=1), NT, preferred_element_type=jnp.float32
            )


def forward_kernel(blocks, has_before, hi_ref, lo_ref, *refs):
    count = len(blocks)
    total = refs[-1]
    total[...] = refs[count][...] if has_before else jnp.zeros_like(total)
    add_products(hi_ref, lo_ref, refs[:count], blocks, total)


def forward_part(rows, vecs, blocks, before=None, tokens=()):
    docs, q = rows[0].shape[1], vecs[0].shape[1]
    n = 4 * len(blocks)
    extra = [*tokens] if before is None else [before, *tokens]
    return pl.pallas_call(
        functools.partial(forward_kernel, blocks, before is not None),
        in_specs=[whole()] * (2 + len(vecs) + len(extra)),
        out_specs=whole(),
        out_shape=f32(docs, 2 * q),
        compiler_params=params(8),
        cost_estimate=cost(8 * docs * 256 * 256 * n, 4 * docs * 256 * n),
        name="forward_part",
    )(*rows, *vecs, *extra)


def product_kernel(blocks, hi_ref, lo_ref, vec, before, *refs):
    out, total, columns = refs[-3:]
    total[...] = before[...]
    add_products(hi_ref, lo_ref, (vec,), blocks, total)
    turned = total[...].T
    q = out.shape[0]
    product = turned[:q] + turned[q:]
    if len(refs) == 3:
        out[...] = product
        return
    _, z, _ = coords()
    *messages, alpha = refs[:5]
    columns[...] = row_to_column(alpha[...])
    scale = columns[pl.ds(pl.multiple_of(z * q, q), q), :][:, 0:1]
    for k, m in enumerate(messages):
        at = slice(k * m.shape[1], (k + 1) * m.shape[1])
        out[:, at] = product[:, at] - scale * m[q:, :]


def product_half(rows, vec, before, blocks, *left):
    docs, q = rows[0].shape[1], vec.shape[1]
    return pl.pallas_call(
        functools.partial(product_kernel, blocks),
        in_specs=[whole()] * (4 + len(left)),
        out_specs=whole(),
        out_shape=f32(q, docs),
        scratch_shapes=[pltpu.VMEM((docs, 2 * q), jnp.float32), pltpu.VMEM((4 * q, 128), jnp.float32)],
        compiler_params=params(8),
        cost_estimate=cost(8 * docs * 256 * 256 * 4, 16 * docs * 256),
        name="product_half",
    )(*rows, vec, before, *left)


def square_sums(value):
    q, n = value.shape
    sums = value[:, 0:128] * value[:, 0:128]
    for at in range(128, n, 128):
        sums = sums + value[:, at : at + 128] * value[:, at : at + 128]
    return jnp.sum(jnp.concatenate([sums] * (128 // q), axis=0).T, axis=0, keepdims=True)


def square_row(value, z, cols):
    row = square_sums(value)
    row = jnp.broadcast_to(jnp.concatenate([row] * (cols // 128), axis=1), (8, cols))
    lane = lax.broadcasted_iota(jnp.int32, (8, cols), 1)
    return jnp.where(lane // value.shape[0] == z, row, 0.0)


def row_to_column(row):
    return jnp.broadcast_to(row, (128, row.shape[1])).T


def left_half_kernel(mine, other, *refs):
    _, z, _ = coords()
    left = mine[...] + other[...]
    both, sums = refs[-2:]
    both[...] = split_rows(left)
    squares = square_row(left, z, sums.shape[1])
    sums[...] = refs[0][...] + squares if len(refs) == 4 else squares
    if len(refs) > 4:
        n = left.shape[1] // 4
        for k, out in enumerate(refs[:4]):
            out[...] = left[:, k * n : (k + 1) * n]


def left_half(mine, other, squares=None, token=None):
    q, docs = mine.shape
    extra = [] if squares is None else [squares, token]
    pieces = [f32(q, docs // 4)] * 4 if squares is None else []
    return pl.pallas_call(
        left_half_kernel,
        out_shape=pieces + [bf16(2 * q, docs), f32(8, 4 * q)],
        compiler_params=params(8),
        cost_estimate=cost(8 * q * docs, 16 * q * docs),
        name="left_half",
    )(mine, other, *extra)


def backward_kernel(first, blocks, parts, hi_ref, lo_ref, both_ref, *refs):
    out_ref = refs[-1]
    both = both_ref[...]
    q = both.shape[0] // 2
    twice = jnp.concatenate([both, both], axis=1)
    for b in range(blocks):
        got = jnp.dot(
            twice,
            jnp.concatenate([hi_ref[first + b], lo_ref[first + b]], axis=0),
            preferred_element_type=jnp.float32,
        )
        got = got[:q] + got[q:]
        if "before" in parts:
            got = got + refs[0][(first + b) * q : (first + b + 1) * q, :]
        out_ref[b * q : (b + 1) * q, :] = got
    if "tail" in parts:
        out_ref[blocks * q :, :] = refs[parts.index("tail")][...]


def backward_part(rows, both, first, blocks, before=None, tail=None, tokens=(), scale=64):
    q, docs = both.shape[0] // 2, both.shape[1]
    extra = {"before": before, "tail": tail, **{str(i): token for i, token in enumerate(tokens)}}
    extra = {name: value for name, value in extra.items() if value is not None}
    height = blocks * q + (0 if tail is None else tail.shape[0])
    return pl.pallas_call(
        functools.partial(backward_kernel, first, blocks, tuple(extra)),
        in_specs=[whole()] * (3 + len(extra)),
        out_specs=whole(),
        out_shape=f32(height, 256),
        compiler_params=params(8),
        cost_estimate=cost(8 * docs * 256 * 256 * blocks, 4 * docs * 256 * blocks, scale),
        name="backward_part",
    )(*rows, both, *extra.values())


def far_sum_kernel(near, far, beta, token, send_far, send_near, beta_core):
    n = near.shape[0] // 2
    beta_core[...] = beta[...] + far[2 * n :, :]
    send_far[...] = near[n:, :] + far[n : 2 * n, :]
    send_near[0:n, :] = near[0:n, :] + far[0:n, :]
    send_near[n:, :] = beta_core[...]


def far_sums(near, far, beta, token):
    rows = near.shape[0] // 2
    return pl.pallas_call(
        far_sum_kernel,
        out_shape=[f32(rows, 256), f32(rows + 8, 256), f32(8, 256)],
        compiler_params=params(8),
        cost_estimate=cost(near.size, near.size * 12),
        name="far_sums",
    )(near, far, beta, token)


def right_far_kernel(keep, peer, got, g2, g3):
    q = g2.shape[0]
    for k, g in ((2, g2), (3, g3)):
        rows = slice(k * q, (k + 1) * q)
        g[...] = (keep[rows, :] + peer[rows, :]) + got[(k - 2) * q : (k - 1) * q, :]


def right_far(keep, peer, got):
    q, rows = keep.shape[0] // 4, keep.shape[1]
    return pl.pallas_call(
        right_far_kernel,
        out_shape=[f32(q, rows)] * 2,
        compiler_params=params(8),
        cost_estimate=cost(rows * q * 4, rows * q * 32),
        name="right_far",
    )(keep, peer, got)


def right_norm_kernel(docs_total, keep, peer, got, beta_core, right, g2, g3, g0, g1, sums, columns):
    _, z, _ = coords()
    q = right.shape[1]
    beta_sums = beta_core[0:1, :] + got[2 * q : 2 * q + 1, :]
    columns[...] = row_to_column(jnp.sqrt(beta_sums / docs_total + epsilon))
    beta = columns[pl.ds(pl.multiple_of(z * q, q), q), :][:, 0:1]
    for k, g in enumerate((g0, g1)):
        rows = slice(k * q, (k + 1) * q)
        g[...] = (keep[rows, :] + peer[rows, :]) + got[rows, :]
    raws = [g[...] / beta - beta * right[k] for k, g in enumerate((g0, g1, g2, g3))]
    line = square_sums(jnp.concatenate(raws, axis=1))
    folded = beta_sums[:, :128] + beta_sums[:, 128:]
    folded = folded + jnp.concatenate([folded[:, q:], folded[:, :q]], axis=1)
    low = lax.broadcasted_iota(jnp.int32, line.shape, 1) < q
    sums[...] = jnp.broadcast_to(jnp.where(low, line, folded), sums.shape)


def right_norm(docs_total, keep, peer, got, beta_core, right, far):
    q, rows = keep.shape[0] // 4, keep.shape[1]
    g0, g1, sums = pl.pallas_call(
        functools.partial(right_norm_kernel, docs_total),
        out_shape=[f32(q, rows)] * 2 + [f32(32, 128)],
        scratch_shapes=[pltpu.VMEM((4 * q, 128), jnp.float32)],
        compiler_params=params(8),
        cost_estimate=cost(rows * q * 64, rows * q * 100, 64),
        name="right_norm",
    )(keep, peer, got, beta_core, right, *far)
    return g0, g1, sums.reshape(32, 1, 128)


def finish_kernel(docs_total, feat_total, g0, g1, g2, g3, squares, own, other, right, search, solution, phibar, rhobar,
                  left_out, right_out, search_out, solution_out, alpha_out, phibar_out, rhobar_out, turned):
    _, z, y = coords()
    q, half = turned.shape[1:]
    parts = [squares[i] for i in range(32)]
    high = [jnp.concatenate([parts[8 * i][:, q:], parts[8 * i][:, :q]], axis=1) if i % 2 == 0 else parts[8 * i] for i in range(4)]
    while len(parts) > 4:
        parts = [a + b for a, b in zip(parts[::2], parts[1::2])]
    parts[1::2] = [jnp.concatenate([p[:, q:], p[:, :q]], axis=1) for p in parts[1::2]]
    low = lax.broadcasted_iota(jnp.int32, parts[0].shape, 1) < q
    alpha_sums, beta_sums = (
        jnp.concatenate([jnp.where(low, p[0], p[1]), jnp.where(low, p[2], p[3])], axis=1) for p in (parts, high)
    )
    alpha = jnp.sqrt(alpha_sums / feat_total + epsilon)
    beta = jnp.sqrt(beta_sums / docs_total + epsilon)
    for part, ref in ((y, own), (1 - y, other)):
        for k in range(4):
            turned[z ^ k] = ref[k]
        left_out[pl.ds(pl.multiple_of(part * half, half), half), :] = turned[...].reshape(-1, half).T / beta
    rho = jnp.sqrt(rhobar[...] * rhobar[...] + beta * beta)
    cosine = rhobar[...] / rho
    sine = beta / rho
    theta = sine * alpha
    phi = cosine * phibar[...]
    rhobar_out[...] = -cosine * alpha
    phibar_out[...] = sine * phibar[...]
    alpha_out[...] = alpha
    for k, g in enumerate((g0, g1, g2, g3)):
        turned[z ^ k] = g[...]
    got = turned[...].reshape(-1, half).T
    following = (got / beta - beta * right[...]) / alpha
    right_out[...] = following
    search_out[...] = following - (theta / rho) * search[...]
    solution_out[...] = solution[...] + (phi / rho) * search[...]


def finish(docs_total, feat_total, pieces, squares, own, other, right, search, solution, phibar, rhobar):
    rows, cols = right.shape
    return pl.pallas_call(
        functools.partial(finish_kernel, docs_total, feat_total),
        out_shape=[f32(2 * rows, cols)] + [f32(rows, cols)] * 3 + [f32(1, cols)] * 3,
        scratch_shapes=[pltpu.VMEM((4, cols // 4, rows), jnp.float32)],
        compiler_params=params(12),
        cost_estimate=cost(rows * cols * 16, rows * cols * 20),
        name="finish",
    )(*pieces, squares, own, other, right, search, solution, phibar, rhobar)


def swap(value, mask):
    return lax.ppermute(value, AXES, [(i, i ^ mask) for i in range(32)])


def along_z(values):
    got = {0: values[0]}
    for k in (2, 3, 1):
        got[k] = swap(values[k], k << Z_SHIFT)
    return [got[k] for k in range(4)]


def after(value, *earlier):
    return lax.optimization_barrier((value, *earlier))[0]


def by_columns(
    col_ids, col_vals, left_vec, right_vec, search_dir, solution_vec, alpha_prev, phibar, rhobar
):
    docs_total = left_vec.shape[0] * 16
    feat_total = right_vec.shape[0] * 32
    alpha_row, phibar_row, rhobar_row = (v.reshape(1, -1) for v in (alpha_prev, phibar, rhobar))

    stored, messages = prepare(col_ids.T, col_vals.T, right_vec, left_vec)
    entries = along_z([stored] * 4)
    messages = along_z([messages[0]] + [after(messages[1], entries[3]), messages[2], messages[3]])
    q = right_vec.shape[1] // 4

    rows1, token1 = build(entries, 1)
    own = stack(messages, q, "stack_right", token1)
    own_x = swap(own, X_BIT)
    own_peer = swap(own, CORE_BIT)
    rows0, token0 = build(entries, 0, own)
    total1 = forward_part(rows1, [own, own_peer], (0, 8), None, [token0])
    x_peer = swap(after(own_x, total1), CORE_BIT)
    total1 = forward_part(rows1, [own_x], (4,), total1)
    product1 = product_half(rows1, x_peer, total1, (12,))
    total0 = forward_part(rows0, [own, own_peer], (0, 8))
    total0 = forward_part(rows0, [own_x], (4,), total0)
    product0 = product_half(rows0, x_peer, total0, (12,), *messages, alpha_row)

    *lefts, both0, beta0 = left_half(product0, swap(product1, Y_BIT))
    partial = backward_part(rows0, both0, 0, 16)
    left_own = stack(along_z(lefts), q, "stack_left")
    both1, beta1 = left_half(product1, swap(product0, Y_BIT), beta0, partial)
    far = swap(backward_part(rows1, both1, 12, 4, partial, beta1), CORE_BIT)
    near = backward_part(rows1, both1, 4, 4, partial, None, [], 0.05)
    peer = backward_part(rows1, both1, 8, 4, partial, None, [near], 0.05)
    send_far, send_near, beta_core = far_sums(near, far, beta1, peer)
    got_far = swap(send_far, X_BIT)
    got_near = swap(send_near, X_BIT)
    keep = backward_part(rows1, both1, 0, 4, partial, None, [], 0.05)
    peer = swap(peer, CORE_BIT)

    g2, g3 = right_far(keep, peer, got_far)
    p2, p3 = swap(g2, 2 << Z_SHIFT), swap(g3, 3 << Z_SHIFT)
    g0, g1, sums = right_norm(docs_total, keep, peer, got_near, beta_core, own, (g2, g3))
    pieces = [g0, swap(g1, 1 << Z_SHIFT), p2, p3]
    left_other = swap(after(left_own, send_far), Y_BIT)
    squares = lax.all_to_all(after(sums, left_own), AXES, 0, 0, tiled=True)
    left_next, right_next, search_next, solution_next, alpha_next, phibar_next, rhobar_next = finish(
        docs_total, feat_total, pieces, squares, left_own, left_other,
        right_vec, search_dir, solution_vec, phibar_row, rhobar_row,
    )
    return (
        left_next,
        right_next,
        search_next,
        solution_next,
        alpha_next.reshape(-1),
        phibar_next.reshape(-1),
        rhobar_next.reshape(-1),
    )


def forward(col_ids, col_vals, table):
    picked = table[col_ids]
    return jnp.sum(col_vals.astype(jnp.float32)[:, :, None] * picked, axis=1)


def backward(col_ids, col_vals, rows_in, width):
    terms = col_vals.astype(jnp.float32)[:, :, None] * rows_in[:, None, :]
    return jax.ops.segment_sum(
        terms.reshape(-1, rows_in.shape[1]), col_ids.reshape(-1), num_segments=width
    )


def by_blocks(
    col_ids, col_vals, left_vec, right_vec, search_dir, solution_vec, alpha_prev, phibar, rhobar
):
    n_feat = lax.axis_size("feat")
    n_doc = lax.axis_size("doc")
    docs_total = left_vec.shape[0] * n_doc
    feat_total = right_vec.shape[0] * n_doc * n_feat
    table = lax.all_gather(right_vec, "doc", axis=0, tiled=True)
    total = lax.psum(forward(col_ids, col_vals, table), "feat")
    left_raw = total - alpha_prev[None, :] * left_vec
    row_part = jnp.sum(left_raw * left_raw, axis=0)
    beta_norm = jnp.sqrt(lax.psum(row_part, "doc") / docs_total + epsilon)
    left_next = left_raw / beta_norm[None, :]
    feature_part = lax.psum_scatter(
        backward(col_ids, col_vals, left_next, table.shape[0]), "doc", scatter_dimension=0, tiled=True
    )
    right_raw = feature_part - beta_norm[None, :] * right_vec
    squares = lax.psum(jnp.sum(right_raw * right_raw, axis=0), AXES)
    alpha_next = jnp.sqrt(squares / feat_total + epsilon)
    right_next = right_raw / alpha_next[None, :]
    rho_val = jnp.sqrt(rhobar * rhobar + beta_norm * beta_norm)
    cosine = rhobar / rho_val
    sine_val = beta_norm / rho_val
    theta_val = sine_val * alpha_next
    phi_val = cosine * phibar
    solution_next = solution_vec + (phi_val / rho_val)[None, :] * search_dir
    search_next = right_next - (theta_val / rho_val)[None, :] * search_dir
    return (
        left_next,
        right_next,
        search_next,
        solution_next,
        alpha_next,
        sine_val * phibar,
        -cosine * alpha_next,
    )


def solution(mesh):
    small = mesh.shape["doc"] == 16 and mesh.shape["feat"] == 2
    rows = P(("feat", "doc"), None)
    return jax.shard_map(
        by_columns if small else by_blocks,
        mesh=mesh,
        in_specs=(P("doc", "feat"), P("doc", "feat"), P("doc", None), rows, rows, rows, P(), P(), P()),
        out_specs=(P("doc", None), rows, rows, rows, P(), P(), P()),
        check_vma=False,
    )
```

```python
import functools

import jax
import jax.numpy as jnp
from jax import lax
from jax.experimental import pallas as pl
from jax.experimental.pallas import tpu as pltpu
from jax.sharding import PartitionSpec as P

epsilon = 1e-06
AXES = ("doc", "feat")
MIB = 1024 * 1024


Y_BIT, CORE_BIT, X_BIT, Z_SHIFT = 1, 2, 4, 3
NT = (((1,), (1,)), ((), ()))


def coords():
    d = lax.axis_index("doc")
    y = lax.axis_index("feat")
    return d, d >> 2, y


def params(mib):
    return pltpu.CompilerParams(vmem_limit_bytes=mib * MIB)


def cost(flops, nbytes, scale=64):
    return pl.CostEstimate(flops=int(flops / scale), bytes_accessed=int(nbytes / scale), transcendentals=0)


def f32(*shape):
    return jax.ShapeDtypeStruct(shape, jnp.float32)


def bf16(*shape):
    return jax.ShapeDtypeStruct(shape, jnp.bfloat16)


def prepare_kernel(ids_hbm, vals_hbm, right_hbm, left_hbm, stored, m0, m1, m2, m3,
                   ids, vals, wide, right, left, turned, arrived):
    _, z, y = coords()
    q, rows = turned.shape[1:]
    copies = [
        pltpu.make_async_copy(src, dst, arrived.at[i])
        for i, (src, dst) in enumerate((
            (ids_hbm, ids),
            (vals_hbm, vals),
            (right_hbm, right),
            (left_hbm.at[pl.ds(pl.multiple_of(y * rows, rows), rows), :], left),
        ))
    ]
    for copy in copies:
        copy.start()
    lines, count = stored.shape[0] // 2, ids.shape[0]
    for part, ref in enumerate((ids, vals)):
        copies[part].wait()
        wide[...] = ref[...].astype(jnp.float32).T
        for r in range(256 // count):
            stored[part * lines : (part + 1) * lines, r * count : (r + 1) * count] = wide[
                pl.ds(r, lines, stride=256 // count), :
            ]
    for part, ref in enumerate((right, left)):
        copies[2 + part].wait()
        turned[...] = ref[...].T.reshape(turned.shape)
        for k, out in enumerate((m0, m1, m2, m3)):
            out[part * q : (part + 1) * q, :] = turned[z ^ k]


def prepare(ids, vals, right, left):
    rows, cols = right.shape
    q = cols // 4
    got = pl.pallas_call(
        prepare_kernel,
        in_specs=[pl.BlockSpec(memory_space=pltpu.HBM)] * 4,
        out_specs=[whole()] * 5,
        out_shape=[pltpu.VMEM((ids.size // 128, 256), jnp.float32)] + [pltpu.VMEM((2 * q, rows), jnp.float32)] * 4,
        scratch_shapes=[
            pltpu.VMEM(ids.shape, jnp.int32),
            pltpu.VMEM(vals.shape, jnp.bfloat16),
            pltpu.VMEM(ids.shape[::-1], jnp.float32),
            pltpu.VMEM(right.shape, jnp.float32),
            pltpu.VMEM(right.shape, jnp.float32),
            pltpu.VMEM((4, q, rows), jnp.float32),
            pltpu.SemaphoreType.DMA((4,)),
        ],
        compiler_params=params(60),
        cost_estimate=cost(0, rows * cols * 16),
        name="prepare",
    )(ids, vals, right, left)
    return got[0], got[1:]


def stack_kernel(m0, m1, m2, m3, *refs):
    out = refs[-1]
    for k, m in enumerate((m0, m1, m2, m3)):
        out[k] = m[0 : out.shape[1], :]


def stack(messages, q, name, *tokens):
    rows = messages[0].shape[1]
    return pl.pallas_call(
        stack_kernel,
        out_shape=f32(4, q, rows),
        compiler_params=params(8),
        cost_estimate=cost(0, 32 * q * rows),
        name=name,
    )(*messages, *tokens)


def build_kernel(rel, e0, e1, e2, e3, *refs):
    hi_ref, lo_ref, token = refs[-3:]
    token[...] = jnp.zeros_like(token)
    d, _, y = coords()
    n = e0.shape[0] // 2
    iota = lax.broadcasted_iota(jnp.int32, (256, 256), 0).astype(jnp.float32).astype(jnp.bfloat16)
    lanes = lax.broadcasted_iota(jnp.int32, (256, 256), 1).astype(jnp.float32)
    lane_doc = lax.broadcasted_iota(jnp.int32, (8, 256), 1) >> 4
    one = jnp.ones((256, 256), jnp.bfloat16)
    zero = jnp.zeros((256, 256), jnp.bfloat16)

    def spread(row):
        wide = jnp.broadcast_to(row, (16, 256)).astype(jnp.bfloat16)
        return jnp.broadcast_to(wide[None], (16, 16, 256)).reshape(256, 256)

    for k, entries in enumerate((e0, e1, e2, e3)):

        @pl.loop(0, n // 16)
        def _(step, k=k, entries=entries):
            at = pl.multiple_of((y ^ rel) * (n // 2) + step * 8, 8)
            ids = entries[pl.ds(at, 8), :].astype(jnp.int32)
            vals = entries[pl.ds(n + at, 8), :]
            owner = (ids >> 8) ^ d
            block = ((owner & 1) << 3) | ((owner & 2) << 1) | (owner >> 2)
            code = (block * 16 + lane_doc).astype(jnp.float32)
            inner = (ids & 255).astype(jnp.float32)
            columns = jnp.concatenate([inner, vals] * 8, axis=0).T
            for t in range(8):
                pick = jnp.where(iota == spread(code[t : t + 1]), one, zero)
                weigh = jnp.where(lanes == columns[:, t : t + 1], columns[:, 8 + t : 9 + t], 0.0).astype(jnp.bfloat16)
                dense = jnp.dot(pick, weigh, preferred_element_type=jnp.float32)
                high = dense.astype(jnp.bfloat16)
                low = (dense - high.astype(jnp.float32)).astype(jnp.bfloat16)
                docs = pl.ds(pl.multiple_of(k * 8 * n + step * 128 + 16 * t, 16), 16)
                hi_ref[:, docs, :] = high.reshape(16, 16, 256)
                lo_ref[:, docs, :] = low.reshape(16, 16, 256)


def whole():
    return pl.BlockSpec(memory_space=pltpu.VMEM)


def build(entries, rel, *tokens):
    docs = 4 * (entries[0].shape[0] // 4 * 16)
    *rows, token = pl.pallas_call(
        functools.partial(build_kernel, rel),
        in_specs=[whole()] * (4 + len(tokens)),
        out_specs=[whole()] * 3,
        out_shape=[pltpu.VMEM((16, docs, 256), jnp.bfloat16)] * 2 + [f32(8, 128)],
        compiler_params=params(8),
        cost_estimate=cost(2 * docs * 16 * 256 * 256, docs * 4096 * 4, 1 if rel else 64),
        name="dense_rows",
    )(*entries, *tokens)
    return rows, token


def split_rows(value):
    high = value.astype(jnp.bfloat16)
    low = (value - high.astype(jnp.float32)).astype(jnp.bfloat16)
    return jnp.concatenate([high, low], axis=0)


def add_products(hi_ref, lo_ref, vecs, blocks, total):
    for vec, first in zip(vecs, blocks):
        for pair in (0, 2):
            lhs, rhs = [], []
            for k in (pair, pair + 1):
                both = split_rows(vec[k])
                lhs += [hi_ref[first + k], lo_ref[first + k]]
                rhs += [both, both]
            total[...] += lax.dot_general(
                jnp.concatenate(lhs, axis=1), jnp.concatenate(rhs, axis=1), NT, preferred_element_type=jnp.float32
            )


def forward_kernel(blocks, has_before, hi_ref, lo_ref, *refs):
    count = len(blocks)
    total = refs[-1]
    total[...] = refs[count][...] if has_before else jnp.zeros_like(total)
    add_products(hi_ref, lo_ref, refs[:count], blocks, total)


def forward_part(rows, vecs, blocks, before=None, tokens=()):
    docs, q = rows[0].shape[1], vecs[0].shape[1]
    n = 4 * len(blocks)
    extra = [*tokens] if before is None else [before, *tokens]
    return pl.pallas_call(
        functools.partial(forward_kernel, blocks, before is not None),
        in_specs=[whole()] * (2 + len(vecs) + len(extra)),
        out_specs=whole(),
        out_shape=f32(docs, 2 * q),
        compiler_params=params(8),
        cost_estimate=cost(8 * docs * 256 * 256 * n, 4 * docs * 256 * n),
        name="forward_part",
    )(*rows, *vecs, *extra)


def product_kernel(blocks, hi_ref, lo_ref, vec, before, *refs):
    out, total, columns = refs[-3:]
    total[...] = before[...]
    add_products(hi_ref, lo_ref, (vec,), blocks, total)
    turned = total[...].T
    q = out.shape[0]
    product = turned[:q] + turned[q:]
    if len(refs) == 3:
        out[...] = product
        return
    _, z, _ = coords()
    *messages, alpha = refs[:5]
    columns[...] = row_to_column(alpha[...])
    scale = columns[pl.ds(pl.multiple_of(z * q, q), q), :][:, 0:1]
    for k, m in enumerate(messages):
        at = slice(k * m.shape[1], (k + 1) * m.shape[1])
        out[:, at] = product[:, at] - scale * m[q:, :]


def product_half(rows, vec, before, blocks, *left):
    docs, q = rows[0].shape[1], vec.shape[1]
    return pl.pallas_call(
        functools.partial(product_kernel, blocks),
        in_specs=[whole()] * (4 + len(left)),
        out_specs=whole(),
        out_shape=f32(q, docs),
        scratch_shapes=[pltpu.VMEM((docs, 2 * q), jnp.float32), pltpu.VMEM((4 * q, 128), jnp.float32)],
        compiler_params=params(8),
        cost_estimate=cost(8 * docs * 256 * 256 * 4, 16 * docs * 256),
        name="product_half",
    )(*rows, vec, before, *left)


def square_sums(value):
    q, n = value.shape
    sums = value[:, 0:128] * value[:, 0:128]
    for at in range(128, n, 128):
        sums = sums + value[:, at : at + 128] * value[:, at : at + 128]
    return jnp.sum(jnp.concatenate([sums] * (128 // q), axis=0).T, axis=0, keepdims=True)


def square_row(value, z, cols):
    row = square_sums(value)
    row = jnp.broadcast_to(jnp.concatenate([row] * (cols // 128), axis=1), (8, cols))
    lane = lax.broadcasted_iota(jnp.int32, (8, cols), 1)
    return jnp.where(lane // value.shape[0] == z, row, 0.0)


def row_to_column(row):
    return jnp.broadcast_to(row, (128, row.shape[1])).T


def left_half_kernel(mine, other, *refs):
    _, z, _ = coords()
    left = mine[...] + other[...]
    both, sums = refs[-2:]
    both[...] = split_rows(left)
    squares = square_row(left, z, sums.shape[1])
    sums[...] = refs[0][...] + squares if len(refs) == 4 else squares
    if len(refs) > 4:
        n = left.shape[1] // 4
        for k, out in enumerate(refs[:4]):
            out[...] = left[:, k * n : (k + 1) * n]


def left_half(mine, other, squares=None, token=None):
    q, docs = mine.shape
    extra = [] if squares is None else [squares, token]
    pieces = [f32(q, docs // 4)] * 4 if squares is None else []
    return pl.pallas_call(
        left_half_kernel,
        out_shape=pieces + [bf16(2 * q, docs), f32(8, 4 * q)],
        compiler_params=params(8),
        cost_estimate=cost(8 * q * docs, 16 * q * docs),
        name="left_half",
    )(mine, other, *extra)


def backward_kernel(first, blocks, parts, hi_ref, lo_ref, both_ref, *refs):
    out_ref = refs[-1]
    both = both_ref[...]
    q = both.shape[0] // 2
    twice = jnp.concatenate([both, both], axis=1)
    for b in range(blocks):
        got = jnp.dot(
            twice,
            jnp.concatenate([hi_ref[first + b], lo_ref[first + b]], axis=0),
            preferred_element_type=jnp.float32,
        )
        got = got[:q] + got[q:]
        if "before" in parts:
            got = got + refs[0][(first + b) * q : (first + b + 1) * q, :]
        out_ref[b * q : (b + 1) * q, :] = got
    if "tail" in parts:
        out_ref[blocks * q :, :] = refs[parts.index("tail")][...]


def backward_part(rows, both, first, blocks, before=None, tail=None, tokens=(), scale=64):
    q, docs = both.shape[0] // 2, both.shape[1]
    extra = {"before": before, "tail": tail, **{str(i): token for i, token in enumerate(tokens)}}
    extra = {name: value for name, value in extra.items() if value is not None}
    height = blocks * q + (0 if tail is None else tail.shape[0])
    return pl.pallas_call(
        functools.partial(backward_kernel, first, blocks, tuple(extra)),
        in_specs=[whole()] * (3 + len(extra)),
        out_specs=whole(),
        out_shape=f32(height, 256),
        compiler_params=params(8),
        cost_estimate=cost(8 * docs * 256 * 256 * blocks, 4 * docs * 256 * blocks, scale),
        name="backward_part",
    )(*rows, both, *extra.values())


def far_sum_kernel(near, far, beta, token, send_far, send_near, beta_core):
    n = near.shape[0] // 2
    beta_core[...] = beta[...] + far[2 * n :, :]
    send_far[...] = near[n:, :] + far[n : 2 * n, :]
    send_near[0:n, :] = near[0:n, :] + far[0:n, :]
    send_near[n:, :] = beta_core[...]


def far_sums(near, far, beta, token):
    rows = near.shape[0] // 2
    return pl.pallas_call(
        far_sum_kernel,
        out_shape=[f32(rows, 256), f32(rows + 8, 256), f32(8, 256)],
        compiler_params=params(8),
        cost_estimate=cost(near.size, near.size * 12),
        name="far_sums",
    )(near, far, beta, token)


def right_far_kernel(keep, peer, got, g2, g3):
    q = g2.shape[0]
    for k, g in ((2, g2), (3, g3)):
        rows = slice(k * q, (k + 1) * q)
        g[...] = (keep[rows, :] + peer[rows, :]) + got[(k - 2) * q : (k - 1) * q, :]


def right_far(keep, peer, got):
    q, rows = keep.shape[0] // 4, keep.shape[1]
    return pl.pallas_call(
        right_far_kernel,
        out_shape=[f32(q, rows)] * 2,
        compiler_params=params(8),
        cost_estimate=cost(rows * q * 4, rows * q * 32),
        name="right_far",
    )(keep, peer, got)


def right_norm_kernel(docs_total, keep, peer, got, beta_core, right, g2, g3, g0, g1, sums, columns):
    _, z, _ = coords()
    q = right.shape[1]
    beta_sums = beta_core[0:1, :] + got[2 * q : 2 * q + 1, :]
    columns[...] = row_to_column(jnp.sqrt(beta_sums / docs_total + epsilon))
    beta = columns[pl.ds(pl.multiple_of(z * q, q), q), :][:, 0:1]
    for k, g in enumerate((g0, g1)):
        rows = slice(k * q, (k + 1) * q)
        g[...] = (keep[rows, :] + peer[rows, :]) + got[rows, :]
    raws = [g[...] / beta - beta * right[k] for k, g in enumerate((g0, g1, g2, g3))]
    line = square_sums(jnp.concatenate(raws, axis=1))
    folded = beta_sums[:, :128] + beta_sums[:, 128:]
    folded = folded + jnp.concatenate([folded[:, q:], folded[:, :q]], axis=1)
    low = lax.broadcasted_iota(jnp.int32, line.shape, 1) < q
    sums[...] = jnp.broadcast_to(jnp.where(low, line, folded), sums.shape)


def right_norm(docs_total, keep, peer, got, beta_core, right, far):
    q, rows = keep.shape[0] // 4, keep.shape[1]
    g0, g1, sums = pl.pallas_call(
        functools.partial(right_norm_kernel, docs_total),
        out_shape=[f32(q, rows)] * 2 + [f32(32, 128)],
        scratch_shapes=[pltpu.VMEM((4 * q, 128), jnp.float32)],
        compiler_params=params(8),
        cost_estimate=cost(rows * q * 64, rows * q * 100, 64),
        name="right_norm",
    )(keep, peer, got, beta_core, right, *far)
    return g0, g1, sums.reshape(32, 1, 128)


def finish_kernel(docs_total, feat_total, g0, g1, g2, g3, squares, own, other, right, search, solution, phibar, rhobar,
                  left_out, right_out, search_out, solution_out, alpha_out, phibar_out, rhobar_out, turned):
    _, z, y = coords()
    q, half = turned.shape[1:]
    parts = [squares[i] for i in range(32)]
    high = [jnp.concatenate([parts[8 * i][:, q:], parts[8 * i][:, :q]], axis=1) if i % 2 == 0 else parts[8 * i] for i in range(4)]
    while len(parts) > 4:
        parts = [a + b for a, b in zip(parts[::2], parts[1::2])]
    parts[1::2] = [jnp.concatenate([p[:, q:], p[:, :q]], axis=1) for p in parts[1::2]]
    low = lax.broadcasted_iota(jnp.int32, parts[0].shape, 1) < q
    alpha_sums, beta_sums = (
        jnp.concatenate([jnp.where(low, p[0], p[1]), jnp.where(low, p[2], p[3])], axis=1) for p in (parts, high)
    )
    alpha = jnp.sqrt(alpha_sums / feat_total + epsilon)
    beta = jnp.sqrt(beta_sums / docs_total + epsilon)
    for part, ref in ((y, own), (1 - y, other)):
        for k in range(4):
            turned[z ^ k] = ref[k]
        left_out[pl.ds(pl.multiple_of(part * half, half), half), :] = turned[...].reshape(-1, half).T / beta
    rho = jnp.sqrt(rhobar[...] * rhobar[...] + beta * beta)
    cosine = rhobar[...] / rho
    sine = beta / rho
    theta = sine * alpha
    phi = cosine * phibar[...]
    rhobar_out[...] = -cosine * alpha
    phibar_out[...] = sine * phibar[...]
    alpha_out[...] = alpha
    for k, g in enumerate((g0, g1, g2, g3)):
        turned[z ^ k] = g[...]
    got = turned[...].reshape(-1, half).T
    following = (got / beta - beta * right[...]) / alpha
    right_out[...] = following
    search_out[...] = following - (theta / rho) * search[...]
    solution_out[...] = solution[...] + (phi / rho) * search[...]


def finish(docs_total, feat_total, pieces, squares, own, other, right, search, solution, phibar, rhobar):
    rows, cols = right.shape
    return pl.pallas_call(
        functools.partial(finish_kernel, docs_total, feat_total),
        out_shape=[f32(2 * rows, cols)] + [f32(rows, cols)] * 3 + [f32(1, cols)] * 3,
        scratch_shapes=[pltpu.VMEM((4, cols // 4, rows), jnp.float32)],
        compiler_params=params(12),
        cost_estimate=cost(rows * cols * 16, rows * cols * 20),
        name="finish",
    )(*pieces, squares, own, other, right, search, solution, phibar, rhobar)


def swap(value, mask):
    return lax.ppermute(value, AXES, [(i, i ^ mask) for i in range(32)])


def along_z(values):
    got = {0: values[0]}
    for k in (2, 3, 1):
        got[k] = swap(values[k], k << Z_SHIFT)
    return [got[k] for k in range(4)]


def after(value, *earlier):
    return lax.optimization_barrier((value, *earlier))[0]


def by_columns(
    col_ids, col_vals, left_vec, right_vec, search_dir, solution_vec, alpha_prev, phibar, rhobar
):
    docs_total = left_vec.shape[0] * 16
    feat_total = right_vec.shape[0] * 32
    alpha_row, phibar_row, rhobar_row = (v.reshape(1, -1) for v in (alpha_prev, phibar, rhobar))

    stored, messages = prepare(col_ids.T, col_vals.T, right_vec, left_vec)
    entries = along_z([stored] * 4)
    messages = along_z([messages[0]] + [after(messages[1], entries[3]), messages[2], messages[3]])
    q = right_vec.shape[1] // 4

    rows1, token1 = build(entries, 1)
    own = stack(messages, q, "stack_right", token1)
    own_x = swap(own, X_BIT)
    own_peer = swap(own, CORE_BIT)
    rows0, token0 = build(entries, 0, own)
    total1 = forward_part(rows1, [own, own_peer], (0, 8), None, [token0])
    x_peer = swap(after(own_x, total1), CORE_BIT)
    total1 = forward_part(rows1, [own_x], (4,), total1)
    product1 = product_half(rows1, x_peer, total1, (12,))
    total0 = forward_part(rows0, [own, own_peer], (0, 8))
    total0 = forward_part(rows0, [own_x], (4,), total0)
    product0 = product_half(rows0, x_peer, total0, (12,), *messages, alpha_row)

    *lefts, both0, beta0 = left_half(product0, swap(product1, Y_BIT))
    partial = backward_part(rows0, both0, 0, 16)
    left_own = stack(along_z(lefts), q, "stack_left")
    both1, beta1 = left_half(product1, swap(product0, Y_BIT), beta0, partial)
    far = swap(backward_part(rows1, both1, 12, 4, partial, beta1), CORE_BIT)
    near = backward_part(rows1, both1, 4, 4, partial, None, [], 0.05)
    peer = backward_part(rows1, both1, 8, 4, partial, None, [near], 0.05)
    send_far, send_near, beta_core = far_sums(near, far, beta1, peer)
    got_far = swap(send_far, X_BIT)
    got_near = swap(send_near, X_BIT)
    keep = backward_part(rows1, both1, 0, 4, partial, None, [], 0.05)
    peer = swap(peer, CORE_BIT)

    g2, g3 = right_far(keep, peer, got_far)
    p2, p3 = swap(g2, 2 << Z_SHIFT), swap(g3, 3 << Z_SHIFT)
    g0, g1, sums = right_norm(docs_total, keep, peer, got_near, beta_core, own, (g2, g3))
    pieces = [g0, swap(g1, 1 << Z_SHIFT), p2, p3]
    left_other = swap(after(left_own, send_far), Y_BIT)
    squares = lax.all_to_all(after(sums, left_own), AXES, 0, 0, tiled=True)
    left_next, right_next, search_next, solution_next, alpha_next, phibar_next, rhobar_next = finish(
        docs_total, feat_total, pieces, squares, left_own, left_other,
        right_vec, search_dir, solution_vec, phibar_row, rhobar_row,
    )
    return (
        left_next,
        right_next,
        search_next,
        solution_next,
        alpha_next.reshape(-1),
        phibar_next.reshape(-1),
        rhobar_next.reshape(-1),
    )


def forward(col_ids, col_vals, table):
    picked = table[col_ids]
    return jnp.sum(col_vals.astype(jnp.float32)[:, :, None] * picked, axis=1)


def backward(col_ids, col_vals, rows_in, width):
    terms = col_vals.astype(jnp.float32)[:, :, None] * rows_in[:, None, :]
    return jax.ops.segment_sum(
        terms.reshape(-1, rows_in.shape[1]), col_ids.reshape(-1), num_segments=width
    )


def by_blocks(
    col_ids, col_vals, left_vec, right_vec, search_dir, solution_vec, alpha_prev, phibar, rhobar
):
    n_feat = lax.axis_size("feat")
    n_doc = lax.axis_size("doc")
    docs_total = left_vec.shape[0] * n_doc
    feat_total = right_vec.shape[0] * n_doc * n_feat
    table = lax.all_gather(right_vec, "doc", axis=0, tiled=True)
    total = lax.psum(forward(col_ids, col_vals, table), "feat")
    left_raw = total - alpha_prev[None, :] * left_vec
    row_part = jnp.sum(left_raw * left_raw, axis=0)
    beta_norm = jnp.sqrt(lax.psum(row_part, "doc") / docs_total + epsilon)
    left_next = left_raw / beta_norm[None, :]
    feature_part = lax.psum_scatter(
        backward(col_ids, col_vals, left_next, table.shape[0]), "doc", scatter_dimension=0, tiled=True
    )
    right_raw = feature_part - beta_norm[None, :] * right_vec
    squares = lax.psum(jnp.sum(right_raw * right_raw, axis=0), AXES)
    alpha_next = jnp.sqrt(squares / feat_total + epsilon)
    right_next = right_raw / alpha_next[None, :]
    rho_val = jnp.sqrt(rhobar * rhobar + beta_norm * beta_norm)
    cosine = rhobar / rho_val
    sine_val = beta_norm / rho_val
    theta_val = sine_val * alpha_next
    phi_val = cosine * phibar
    solution_next = solution_vec + (phi_val / rho_val)[None, :] * search_dir
    search_next = right_next - (theta_val / rho_val)[None, :] * search_dir
    return (
        left_next,
        right_next,
        search_next,
        solution_next,
        alpha_next,
        sine_val * phibar,
        -cosine * alpha_next,
    )


def solution(mesh):
    small = mesh.shape["doc"] == 16 and mesh.shape["feat"] == 2
    rows = P(("feat", "doc"), None)
    return jax.shard_map(
        by_columns if small else by_blocks,
        mesh=mesh,
        in_specs=(P("doc", "feat"), P("doc", "feat"), P("doc", None), rows, rows, rows, P(), P(), P()),
        out_specs=(P("doc", None), rows, rows, rows, P(), P(), P()),
        check_vma=False,
    )
```

```python
import functools

import jax
import jax.numpy as jnp
from jax import lax
from jax.experimental import pallas as pl
from jax.experimental.pallas import tpu as pltpu
from jax.sharding import PartitionSpec as P

epsilon = 1e-06
AXES = ("doc", "feat")
MIB = 1024 * 1024


Y_BIT, CORE_BIT, X_BIT, Z_SHIFT = 1, 2, 4, 3
NT = (((1,), (1,)), ((), ()))


def coords():
    d = lax.axis_index("doc")
    y = lax.axis_index("feat")
    return d, d >> 2, y


def params(mib):
    return pltpu.CompilerParams(vmem_limit_bytes=mib * MIB)


def cost(flops, nbytes, scale=64):
    return pl.CostEstimate(flops=int(flops / scale), bytes_accessed=int(nbytes / scale), transcendentals=0)


def f32(*shape):
    return jax.ShapeDtypeStruct(shape, jnp.float32)


def bf16(*shape):
    return jax.ShapeDtypeStruct(shape, jnp.bfloat16)


def prepare_kernel(ids_hbm, vals_hbm, right_hbm, left_hbm, stored, m0, m1, m2, m3,
                   ids, vals, wide, right, left, turned, arrived):
    _, z, y = coords()
    q, rows = turned.shape[1:]
    copies = [
        pltpu.make_async_copy(src, dst, arrived.at[i])
        for i, (src, dst) in enumerate((
            (ids_hbm, ids),
            (vals_hbm, vals),
            (right_hbm, right),
            (left_hbm.at[pl.ds(pl.multiple_of(y * rows, rows), rows), :], left),
        ))
    ]
    for copy in copies:
        copy.start()
    lines, count = stored.shape[0] // 2, ids.shape[0]
    for part, ref in enumerate((ids, vals)):
        copies[part].wait()
        wide[...] = ref[...].astype(jnp.float32).T
        for r in range(256 // count):
            stored[part * lines : (part + 1) * lines, r * count : (r + 1) * count] = wide[
                pl.ds(r, lines, stride=256 // count), :
            ]
    for part, ref in enumerate((right, left)):
        copies[2 + part].wait()
        turned[...] = ref[...].T.reshape(turned.shape)
        for k, out in enumerate((m0, m1, m2, m3)):
            out[part * q : (part + 1) * q, :] = turned[z ^ k]


def prepare(ids, vals, right, left):
    rows, cols = right.shape
    q = cols // 4
    got = pl.pallas_call(
        prepare_kernel,
        in_specs=[pl.BlockSpec(memory_space=pltpu.HBM)] * 4,
        out_specs=[whole()] * 5,
        out_shape=[pltpu.VMEM((ids.size // 128, 256), jnp.float32)] + [pltpu.VMEM((2 * q, rows), jnp.float32)] * 4,
        scratch_shapes=[
            pltpu.VMEM(ids.shape, jnp.int32),
            pltpu.VMEM(vals.shape, jnp.bfloat16),
            pltpu.VMEM(ids.shape[::-1], jnp.float32),
            pltpu.VMEM(right.shape, jnp.float32),
            pltpu.VMEM(right.shape, jnp.float32),
            pltpu.VMEM((4, q, rows), jnp.float32),
            pltpu.SemaphoreType.DMA((4,)),
        ],
        compiler_params=params(60),
        cost_estimate=cost(0, rows * cols * 16),
        name="prepare",
    )(ids, vals, right, left)
    return got[0], got[1:]


def stack_kernel(m0, m1, m2, m3, *refs):
    out = refs[-1]
    for k, m in enumerate((m0, m1, m2, m3)):
        out[k] = m[0 : out.shape[1], :]


def stack(messages, q, name, *tokens):
    rows = messages[0].shape[1]
    return pl.pallas_call(
        stack_kernel,
        out_shape=f32(4, q, rows),
        compiler_params=params(8),
        cost_estimate=cost(0, 32 * q * rows),
        name=name,
    )(*messages, *tokens)


def build_kernel(rel, e0, e1, e2, e3, *refs):
    hi_ref, lo_ref, token = refs[-3:]
    token[...] = jnp.zeros_like(token)
    d, _, y = coords()
    n = e0.shape[0] // 2
    iota = lax.broadcasted_iota(jnp.int32, (256, 256), 0).astype(jnp.float32).astype(jnp.bfloat16)
    lane_doc = lax.broadcasted_iota(jnp.int32, (8, 256), 1) >> 4
    one = jnp.ones((256, 256), jnp.bfloat16)
    zero = jnp.zeros((256, 256), jnp.bfloat16)

    def spread(row):
        wide = jnp.broadcast_to(row, (16, 256)).astype(jnp.bfloat16)
        return jnp.broadcast_to(wide[None], (16, 16, 256)).reshape(256, 256)

    for k, entries in enumerate((e0, e1, e2, e3)):

        @pl.loop(0, n // 16)
        def _(step, k=k, entries=entries):
            at = pl.multiple_of((y ^ rel) * (n // 2) + step * 8, 8)
            ids = entries[pl.ds(at, 8), :].astype(jnp.int32)
            vals = entries[pl.ds(n + at, 8), :]
            owner = (ids >> 8) ^ d
            block = ((owner & 1) << 3) | ((owner & 2) << 1) | (owner >> 2)
            code = (block * 16 + lane_doc).astype(jnp.float32)
            inner = (ids & 255).astype(jnp.float32)
            for t in range(8):
                pick = jnp.where(iota == spread(code[t : t + 1]), one, zero)
                weigh = jnp.where(iota == spread(inner[t : t + 1]), spread(vals[t : t + 1]), zero)
                dense = lax.dot_general(pick, weigh, NT, preferred_element_type=jnp.float32)
                high = dense.astype(jnp.bfloat16)
                low = (dense - high.astype(jnp.float32)).astype(jnp.bfloat16)
                docs = pl.ds(pl.multiple_of(k * 8 * n + step * 128 + 16 * t, 16), 16)
                hi_ref[:, docs, :] = high.reshape(16, 16, 256)
                lo_ref[:, docs, :] = low.reshape(16, 16, 256)


def whole():
    return pl.BlockSpec(memory_space=pltpu.VMEM)


def build(entries, rel, *tokens):
    docs = 4 * (entries[0].shape[0] // 4 * 16)
    *rows, token = pl.pallas_call(
        functools.partial(build_kernel, rel),
        in_specs=[whole()] * (4 + len(tokens)),
        out_specs=[whole()] * 3,
        out_shape=[pltpu.VMEM((16, docs, 256), jnp.bfloat16)] * 2 + [f32(8, 128)],
        compiler_params=params(8),
        cost_estimate=cost(2 * docs * 16 * 256 * 256, docs * 4096 * 4, 1 if rel else 64),
        name="dense_rows",
    )(*entries, *tokens)
    return rows, token


def split_rows(value):
    high = value.astype(jnp.bfloat16)
    low = (value - high.astype(jnp.float32)).astype(jnp.bfloat16)
    return jnp.concatenate([high, low], axis=0)


def add_products(hi_ref, lo_ref, vecs, blocks, total):
    for vec, first in zip(vecs, blocks):
        for pair in (0, 2):
            lhs, rhs = [], []
            for k in (pair, pair + 1):
                both = split_rows(vec[k])
                lhs += [hi_ref[first + k], lo_ref[first + k]]
                rhs += [both, both]
            total[...] += lax.dot_general(
                jnp.concatenate(lhs, axis=1), jnp.concatenate(rhs, axis=1), NT, preferred_element_type=jnp.float32
            )


def forward_kernel(blocks, has_before, hi_ref, lo_ref, *refs):
    count = len(blocks)
    total = refs[-1]
    total[...] = refs[count][...] if has_before else jnp.zeros_like(total)
    add_products(hi_ref, lo_ref, refs[:count], blocks, total)


def forward_part(rows, vecs, blocks, before=None, tokens=()):
    docs, q = rows[0].shape[1], vecs[0].shape[1]
    n = 4 * len(blocks)
    extra = [*tokens] if before is None else [before, *tokens]
    return pl.pallas_call(
        functools.partial(forward_kernel, blocks, before is not None),
        in_specs=[whole()] * (2 + len(vecs) + len(extra)),
        out_specs=whole(),
        out_shape=f32(docs, 2 * q),
        compiler_params=params(8),
        cost_estimate=cost(8 * docs * 256 * 256 * n, 4 * docs * 256 * n),
        name="forward_part",
    )(*rows, *vecs, *extra)


def product_kernel(blocks, hi_ref, lo_ref, vec, before, *refs):
    out, total, columns = refs[-3:]
    total[...] = before[...]
    add_products(hi_ref, lo_ref, (vec,), blocks, total)
    turned = total[...].T
    q = out.shape[0]
    product = turned[:q] + turned[q:]
    if len(refs) == 3:
        out[...] = product
        return
    _, z, _ = coords()
    *messages, alpha = refs[:5]
    columns[...] = row_to_column(alpha[...])
    scale = columns[pl.ds(pl.multiple_of(z * q, q), q), :][:, 0:1]
    for k, m in enumerate(messages):
        at = slice(k * m.shape[1], (k + 1) * m.shape[1])
        out[:, at] = product[:, at] - scale * m[q:, :]


def product_half(rows, vec, before, blocks, *left):
    docs, q = rows[0].shape[1], vec.shape[1]
    return pl.pallas_call(
        functools.partial(product_kernel, blocks),
        in_specs=[whole()] * (4 + len(left)),
        out_specs=whole(),
        out_shape=f32(q, docs),
        scratch_shapes=[pltpu.VMEM((docs, 2 * q), jnp.float32), pltpu.VMEM((4 * q, 128), jnp.float32)],
        compiler_params=params(8),
        cost_estimate=cost(8 * docs * 256 * 256 * 4, 16 * docs * 256),
        name="product_half",
    )(*rows, vec, before, *left)


def square_sums(value):
    q, n = value.shape
    sums = value[:, 0:128] * value[:, 0:128]
    for at in range(128, n, 128):
        sums = sums + value[:, at : at + 128] * value[:, at : at + 128]
    return jnp.sum(jnp.concatenate([sums] * (128 // q), axis=0).T, axis=0, keepdims=True)


def square_row(value, z, cols):
    row = square_sums(value)
    row = jnp.broadcast_to(jnp.concatenate([row] * (cols // 128), axis=1), (8, cols))
    lane = lax.broadcasted_iota(jnp.int32, (8, cols), 1)
    return jnp.where(lane // value.shape[0] == z, row, 0.0)


def row_to_column(row):
    return jnp.broadcast_to(row, (128, row.shape[1])).T


def left_half_kernel(mine, other, *refs):
    _, z, _ = coords()
    left = mine[...] + other[...]
    both, sums = refs[-2:]
    both[...] = split_rows(left)
    squares = square_row(left, z, sums.shape[1])
    sums[...] = refs[0][...] + squares if len(refs) == 4 else squares
    if len(refs) > 4:
        n = left.shape[1] // 4
        for k, out in enumerate(refs[:4]):
            out[...] = left[:, k * n : (k + 1) * n]


def left_half(mine, other, squares=None, token=None):
    q, docs = mine.shape
    extra = [] if squares is None else [squares, token]
    pieces = [f32(q, docs // 4)] * 4 if squares is None else []
    return pl.pallas_call(
        left_half_kernel,
        out_shape=pieces + [bf16(2 * q, docs), f32(8, 4 * q)],
        compiler_params=params(8),
        cost_estimate=cost(8 * q * docs, 16 * q * docs),
        name="left_half",
    )(mine, other, *extra)


def backward_kernel(first, blocks, parts, hi_ref, lo_ref, both_ref, *refs):
    out_ref = refs[-1]
    both = both_ref[...]
    q = both.shape[0] // 2
    twice = jnp.concatenate([both, both], axis=1)
    for b in range(blocks):
        got = jnp.dot(
            twice,
            jnp.concatenate([hi_ref[first + b], lo_ref[first + b]], axis=0),
            preferred_element_type=jnp.float32,
        )
        got = got[:q] + got[q:]
        if "before" in parts:
            got = got + refs[0][(first + b) * q : (first + b + 1) * q, :]
        out_ref[b * q : (b + 1) * q, :] = got
    if "tail" in parts:
        out_ref[blocks * q :, :] = refs[parts.index("tail")][...]


def backward_part(rows, both, first, blocks, before=None, tail=None, tokens=(), scale=64):
    q, docs = both.shape[0] // 2, both.shape[1]
    extra = {"before": before, "tail": tail, **{str(i): token for i, token in enumerate(tokens)}}
    extra = {name: value for name, value in extra.items() if value is not None}
    height = blocks * q + (0 if tail is None else tail.shape[0])
    return pl.pallas_call(
        functools.partial(backward_kernel, first, blocks, tuple(extra)),
        in_specs=[whole()] * (3 + len(extra)),
        out_specs=whole(),
        out_shape=f32(height, 256),
        compiler_params=params(8),
        cost_estimate=cost(8 * docs * 256 * 256 * blocks, 4 * docs * 256 * blocks, scale),
        name="backward_part",
    )(*rows, both, *extra.values())


def far_sum_kernel(near, far, beta, token, send_far, send_near, beta_core):
    n = near.shape[0] // 2
    beta_core[...] = beta[...] + far[2 * n :, :]
    send_far[...] = near[n:, :] + far[n : 2 * n, :]
    send_near[0:n, :] = near[0:n, :] + far[0:n, :]
    send_near[n:, :] = beta_core[...]


def far_sums(near, far, beta, token):
    rows = near.shape[0] // 2
    return pl.pallas_call(
        far_sum_kernel,
        out_shape=[f32(rows, 256), f32(rows + 8, 256), f32(8, 256)],
        compiler_params=params(8),
        cost_estimate=cost(near.size, near.size * 12),
        name="far_sums",
    )(near, far, beta, token)


def right_far_kernel(keep, peer, got, g2, g3):
    q = g2.shape[0] - 8
    for k, g in ((2, g2), (3, g3)):
        g[q:, :] = jnp.zeros_like(g[q:, :])
        rows = slice(k * q, (k + 1) * q)
        g[0:q, :] = (keep[rows, :] + peer[rows, :]) + got[(k - 2) * q : (k - 1) * q, :]


def right_far(keep, peer, got):
    q, rows = keep.shape[0] // 4, keep.shape[1]
    return pl.pallas_call(
        right_far_kernel,
        out_shape=[f32(q + 8, rows)] * 2,
        compiler_params=params(8),
        cost_estimate=cost(rows * q * 4, rows * q * 32),
        name="right_far",
    )(keep, peer, got)


def right_norm_kernel(docs_total, keep, peer, got, beta_core, right, g2, g3, g0, g1, sums, columns):
    _, z, _ = coords()
    q = right.shape[1]
    beta_sums = beta_core[0:1, :] + got[2 * q : 2 * q + 1, :]
    columns[...] = row_to_column(jnp.sqrt(beta_sums / docs_total + epsilon))
    beta = columns[pl.ds(pl.multiple_of(z * q, q), q), :][:, 0:1]
    for k, g in enumerate((g0, g1)):
        rows = slice(k * q, (k + 1) * q)
        g[...] = (keep[rows, :] + peer[rows, :]) + got[rows, :]
    raws = [g[0:q, :] / beta - beta * right[k] for k, g in enumerate((g0, g1, g2, g3))]
    line = square_sums(jnp.concatenate(raws, axis=1))
    folded = beta_sums[:, :128] + beta_sums[:, 128:]
    folded = folded + jnp.concatenate([folded[:, q:], folded[:, :q]], axis=1)
    low = lax.broadcasted_iota(jnp.int32, line.shape, 1) < q
    sums[...] = jnp.broadcast_to(jnp.where(low, line, folded), sums.shape)


def right_norm(docs_total, keep, peer, got, beta_core, right, far):
    q, rows = keep.shape[0] // 4, keep.shape[1]
    g0, g1, sums = pl.pallas_call(
        functools.partial(right_norm_kernel, docs_total),
        out_shape=[f32(q, rows)] * 2 + [f32(32, 128)],
        scratch_shapes=[pltpu.VMEM((4 * q, 128), jnp.float32)],
        compiler_params=params(8),
        cost_estimate=cost(rows * q * 64, rows * q * 100, 64),
        name="right_norm",
    )(keep, peer, got, beta_core, right, *far)
    return g0, g1, sums.reshape(32, 1, 128)


def finish_kernel(docs_total, feat_total, g0, g1, g2, g3, squares, own, other, right, search, solution, phibar, rhobar,
                  left_out, right_out, search_out, solution_out, alpha_out, phibar_out, rhobar_out, turned):
    _, z, y = coords()
    q, half = turned.shape[1:]
    parts = [squares[i] for i in range(32)]
    high = [jnp.concatenate([parts[8 * i][:, q:], parts[8 * i][:, :q]], axis=1) if i % 2 == 0 else parts[8 * i] for i in range(4)]
    while len(parts) > 4:
        parts = [a + b for a, b in zip(parts[::2], parts[1::2])]
    parts[1::2] = [jnp.concatenate([p[:, q:], p[:, :q]], axis=1) for p in parts[1::2]]
    low = lax.broadcasted_iota(jnp.int32, parts[0].shape, 1) < q
    alpha_sums, beta_sums = (
        jnp.concatenate([jnp.where(low, p[0], p[1]), jnp.where(low, p[2], p[3])], axis=1) for p in (parts, high)
    )
    alpha = jnp.sqrt(alpha_sums / feat_total + epsilon)
    beta = jnp.sqrt(beta_sums / docs_total + epsilon)
    for part, ref in ((y, own), (1 - y, other)):
        for k in range(4):
            turned[z ^ k] = ref[k]
        left_out[pl.ds(pl.multiple_of(part * half, half), half), :] = turned[...].reshape(-1, half).T / beta
    rho = jnp.sqrt(rhobar[...] * rhobar[...] + beta * beta)
    cosine = rhobar[...] / rho
    sine = beta / rho
    theta = sine * alpha
    phi = cosine * phibar[...]
    rhobar_out[...] = -cosine * alpha
    phibar_out[...] = sine * phibar[...]
    alpha_out[...] = alpha
    for k, g in enumerate((g0, g1, g2, g3)):
        turned[z ^ k] = g[0:q, :]
    got = turned[...].reshape(-1, half).T
    following = (got / beta - beta * right[...]) / alpha
    right_out[...] = following
    search_out[...] = following - (theta / rho) * search[...]
    solution_out[...] = solution[...] + (phi / rho) * search[...]


def finish(docs_total, feat_total, pieces, squares, own, other, right, search, solution, phibar, rhobar):
    rows, cols = right.shape
    return pl.pallas_call(
        functools.partial(finish_kernel, docs_total, feat_total),
        out_shape=[f32(2 * rows, cols)] + [f32(rows, cols)] * 3 + [f32(1, cols)] * 3,
        scratch_shapes=[pltpu.VMEM((4, cols // 4, rows), jnp.float32)],
        compiler_params=params(12),
        cost_estimate=cost(rows * cols * 16, rows * cols * 20),
        name="finish",
    )(*pieces, squares, own, other, right, search, solution, phibar, rhobar)


def swap(value, mask):
    return lax.ppermute(value, AXES, [(i, i ^ mask) for i in range(32)])


def along_z(values):
    got = {0: values[0]}
    for k in (2, 3, 1):
        got[k] = swap(values[k], k << Z_SHIFT)
    return [got[k] for k in range(4)]


def after(value, *earlier):
    return lax.optimization_barrier((value, *earlier))[0]


def by_columns(
    col_ids, col_vals, left_vec, right_vec, search_dir, solution_vec, alpha_prev, phibar, rhobar
):
    docs_total = left_vec.shape[0] * 16
    feat_total = right_vec.shape[0] * 32
    alpha_row, phibar_row, rhobar_row = (v.reshape(1, -1) for v in (alpha_prev, phibar, rhobar))

    stored, messages = prepare(col_ids.T, col_vals.T, right_vec, left_vec)
    entries = along_z([stored] * 4)
    messages = along_z([messages[0]] + [after(messages[1], entries[3]), messages[2], messages[3]])
    q = right_vec.shape[1] // 4

    rows1, token1 = build(entries, 1)
    own = stack(messages, q, "stack_right", token1)
    own_x = swap(own, X_BIT)
    own_peer = swap(own, CORE_BIT)
    rows0, token0 = build(entries, 0, own)
    total1 = forward_part(rows1, [own, own_peer], (0, 8), None, [token0])
    x_peer = swap(after(own_x, total1), CORE_BIT)
    total1 = forward_part(rows1, [own_x], (4,), total1)
    product1 = product_half(rows1, x_peer, total1, (12,))
    total0 = forward_part(rows0, [own, own_peer], (0, 8))
    total0 = forward_part(rows0, [own_x], (4,), total0)
    product0 = product_half(rows0, x_peer, total0, (12,), *messages, alpha_row)

    *lefts, both0, beta0 = left_half(product0, swap(product1, Y_BIT))
    partial = backward_part(rows0, both0, 0, 16)
    left_own = stack(along_z(lefts), q, "stack_left")
    both1, beta1 = left_half(product1, swap(product0, Y_BIT), beta0, partial)
    far = swap(backward_part(rows1, both1, 12, 4, partial, beta1), CORE_BIT)
    near = backward_part(rows1, both1, 4, 4, partial, None, [], 0.05)
    peer = backward_part(rows1, both1, 8, 4, partial, None, [near], 0.05)
    send_far, send_near, beta_core = far_sums(near, far, beta1, peer)
    got_far = swap(send_far, X_BIT)
    got_near = swap(send_near, X_BIT)
    keep = backward_part(rows1, both1, 0, 4, partial, None, [], 0.05)
    peer = swap(after(peer, send_far), CORE_BIT)

    g2, g3 = right_far(keep, peer, got_far)
    p2, p3 = swap(g2, 2 << Z_SHIFT), swap(g3, 3 << Z_SHIFT)
    g0, g1, sums = right_norm(docs_total, keep, peer, got_near, beta_core, own, (g2, g3))
    pieces = [g0, swap(g1, 1 << Z_SHIFT), p2, p3]
    left_other = swap(after(left_own, send_far), Y_BIT)
    squares = lax.all_to_all(after(sums, left_own), AXES, 0, 0, tiled=True)
    left_next, right_next, search_next, solution_next, alpha_next, phibar_next, rhobar_next = finish(
        docs_total, feat_total, pieces, squares, left_own, left_other,
        right_vec, search_dir, solution_vec, phibar_row, rhobar_row,
    )
    return (
        left_next,
        right_next,
        search_next,
        solution_next,
        alpha_next.reshape(-1),
        phibar_next.reshape(-1),
        rhobar_next.reshape(-1),
    )


def forward(col_ids, col_vals, table):
    picked = table[col_ids]
    return jnp.sum(col_vals.astype(jnp.float32)[:, :, None] * picked, axis=1)


def backward(col_ids, col_vals, rows_in, width):
    terms = col_vals.astype(jnp.float32)[:, :, None] * rows_in[:, None, :]
    return jax.ops.segment_sum(
        terms.reshape(-1, rows_in.shape[1]), col_ids.reshape(-1), num_segments=width
    )


def by_blocks(
    col_ids, col_vals, left_vec, right_vec, search_dir, solution_vec, alpha_prev, phibar, rhobar
):
    n_feat = lax.axis_size("feat")
    n_doc = lax.axis_size("doc")
    docs_total = left_vec.shape[0] * n_doc
    feat_total = right_vec.shape[0] * n_doc * n_feat
    table = lax.all_gather(right_vec, "doc", axis=0, tiled=True)
    total = lax.psum(forward(col_ids, col_vals, table), "feat")
    left_raw = total - alpha_prev[None, :] * left_vec
    row_part = jnp.sum(left_raw * left_raw, axis=0)
    beta_norm = jnp.sqrt(lax.psum(row_part, "doc") / docs_total + epsilon)
    left_next = left_raw / beta_norm[None, :]
    feature_part = lax.psum_scatter(
        backward(col_ids, col_vals, left_next, table.shape[0]), "doc", scatter_dimension=0, tiled=True
    )
    right_raw = feature_part - beta_norm[None, :] * right_vec
    squares = lax.psum(jnp.sum(right_raw * right_raw, axis=0), AXES)
    alpha_next = jnp.sqrt(squares / feat_total + epsilon)
    right_next = right_raw / alpha_next[None, :]
    rho_val = jnp.sqrt(rhobar * rhobar + beta_norm * beta_norm)
    cosine = rhobar / rho_val
    sine_val = beta_norm / rho_val
    theta_val = sine_val * alpha_next
    phi_val = cosine * phibar
    solution_next = solution_vec + (phi_val / rho_val)[None, :] * search_dir
    search_next = right_next - (theta_val / rho_val)[None, :] * search_dir
    return (
        left_next,
        right_next,
        search_next,
        solution_next,
        alpha_next,
        sine_val * phibar,
        -cosine * alpha_next,
    )


def solution(mesh):
    small = mesh.shape["doc"] == 16 and mesh.shape["feat"] == 2
    rows = P(("feat", "doc"), None)
    return jax.shard_map(
        by_columns if small else by_blocks,
        mesh=mesh,
        in_specs=(P("doc", "feat"), P("doc", "feat"), P("doc", None), rows, rows, rows, P(), P(), P()),
        out_specs=(P("doc", None), rows, rows, rows, P(), P(), P()),
        check_vma=False,
    )
```
